128 devices in a mesh: seq: 8 (over y, x_lo), fsdp: 16 (over x_hi, z, core).
Axes of the slice: x: 4 (x_hi: 2, x_lo: 2; x = x_hi * 2 + x_lo), y: 4, z: 4, core: 2. Of those that a mesh axis runs over, the one named last changes fastest.
Arguments:
- inputs: bfloat16 [16, 1024, 2048], P('fsdp', 'seq'), may hold values from -6 to 6
- gains: bfloat16 [2048], P('fsdp'), may hold values from 0.5 to 1.5
- shifts: bfloat16 [2048], P('fsdp'), may hold values from -4 to 4
- attend: bfloat16 [2048, 6144], P('fsdp'), may hold values from -0.125 to 0.125
- attend_bias: bfloat16 [6144], P('fsdp'), may hold values from -0.75 to 0.75
- mixer: bfloat16 [2048, 2048], P('fsdp'), may hold values from -1.5 to 1.5
- mixer_bias: bfloat16 [2048], P('fsdp'), may hold values from -4 to 4
- upward: bfloat16 [2048, 8192], P(None, 'fsdp'), may hold values from -0.125 to 0.125
- upward_bias: bfloat16 [8192], P('fsdp'), may hold values from -4 to 4
- downward: bfloat16 [8192, 2048], P('fsdp'), may hold values from -0.0625 to 0.0625
- downward_bias: bfloat16 [2048], P('fsdp'), may hold values from -4 to 4
- cotangent: bfloat16 [16, 1024, 2048], P('fsdp', 'seq'), may hold values from -6 to 6
Outputs:
- outputs: bfloat16 [16, 1024, 2048], P('fsdp', 'seq')
- inputs_grad: float32 [16, 1024, 2048], P('fsdp', 'seq')
- gains_grad: float32 [2048], P('fsdp')
- shifts_grad: float32 [2048], P('fsdp')
- attend_grad: float32 [2048, 6144], P('fsdp')
- attend_bias_grad: float32 [6144], P('fsdp')
- mixer_grad: float32 [2048, 2048], P('fsdp')
- mixer_bias_grad: float32 [2048], P('fsdp')
- upward_grad: float32 [2048, 8192], P(None, 'fsdp')
- upward_bias_grad: float32 [8192], P('fsdp')
- downward_grad: float32 [8192, 2048], P('fsdp')
- downward_bias_grad: float32 [2048], P('fsdp')
The draws below stay inside these ranges and needn't reach their ends.
All inputs are finite; a program needn't handle non-finite values.
Results may differ from the reference program's by a relative error of at most 0.0093.
Values may be sent and summed in bfloat16 or wider, within the bound.
No kernel may reach another device: no remote copies, remote signals or barrier semaphores. Data moves between devices by JAX's collectives and lax.ppermute only.
A program may use at most 256 MiB of HBM per device.

```python
import jax
import jax.numpy as jnp
from jax import lax

D = 2048
HEADS = 32
HEAD_DIM = 64
ROT = 32
FF = 8192
LENGTH = 1024
SEQS = 16


def shard_levels(key, extent, cuts, smallest, high):
    loudness, own = 1.0, jax.random.fold_in(key, 6)
    for position, blocks in cuts:
        draws = jnp.exp(jax.random.uniform(jax.random.fold_in(own, position), (blocks,), jnp.float32, smallest / len(cuts), high / len(cuts)))
        loudness = loudness * jnp.repeat(draws, extent[position] // blocks).reshape([-1 if axis == position else 1 for axis in range(len(extent))])
    return loudness


def gaussian(rng, shape, scale, reach, cuts=(), kind=jnp.bfloat16):
    level = shard_levels(rng, shape, cuts, -0.22, 0.18) if cuts else 1.0
    array = jax.random.normal(rng, shape, jnp.float32) * scale * level
    return jnp.minimum(jnp.maximum(array, -reach), reach).astype(kind)


def setup_inputs(seed: int = 0) -> dict:
    arg_keys = jax.random.split(jax.random.key(seed), 13)
    return {
        "inputs": gaussian(arg_keys[0], (SEQS, LENGTH, D), 1.0, 6.0, ((0, 16), (1, 8))),
        "gains": jnp.clip(1.0 + 0.1 * jax.random.normal(arg_keys[1], (D,), jnp.float32), 0.5, 1.5).astype(jnp.bfloat16),
        "shifts": gaussian(arg_keys[2], (D,), 0.3, 4.0, ((0, 16),)),
        "attend": gaussian(arg_keys[3], (D, 3 * D), D ** -0.5, 0.125, ((0, 16),)),
        "attend_bias": gaussian(arg_keys[4], (3 * D,), 0.05, 0.75, ((0, 16),)),
        "mixer": gaussian(arg_keys[5], (D, D), (max(D // 128, 4)) ** -0.5, 1.5, ((0, 16),)),
        "mixer_bias": gaussian(arg_keys[6], (D,), 0.3, 4.0, ((0, 16),)),
        "upward": gaussian(arg_keys[7], (D, FF), D ** -0.5, 0.125, ((1, 16),)),
        "upward_bias": gaussian(arg_keys[8], (FF,), 0.3, 4.0, ((0, 16),)),
        "downward": gaussian(arg_keys[9], (FF, D), FF ** -0.5, 0.0625, ((0, 16),)),
        "downward_bias": gaussian(arg_keys[10], (D,), 0.3, 4.0, ((0, 16),)),
        "cotangent": gaussian(arg_keys[11], (SEQS, LENGTH, D), 1.0, 6.0, ((0, 16), (1, 8))),
    }


EPSILON = 1e-05
ROPE_BASE = 10000.0
NEG_FILL = -1e+30
HIGHEST = lax.Precision.HIGHEST

@jax.custom_vjp
def low(v):
    return lax.optimization_barrier(v.astype(jnp.bfloat16)).astype(jnp.float32)

@jax.custom_vjp
def low_back(v):
    return v

def low_keep(v):
    return (low(v), None)

def low_pass(kept, grad):
    return (grad,)

def back_keep(v):
    return (v, None)

def back_low(kept, grad):
    return (low(grad),)
low.defvjp(low_keep, low_pass)
low_back.defvjp(back_keep, back_low)

def layer_norm(activation, gains, shifts):
    center = activation - lax.optimization_barrier(jnp.mean(activation, axis=-1, keepdims=True))
    spread = lax.optimization_barrier(jnp.mean(center * center, axis=-1, keepdims=True))
    return center * lax.rsqrt(spread + EPSILON) * gains + shifts

def rotate(field_in, positions, rotary, flip_sign):
    half_dim = rotary // 2
    frequency = ROPE_BASE ** (-2.0 * jnp.arange(half_dim, dtype=jnp.float32) / rotary)
    angle_grid = positions[:, None] * frequency[None, :]
    cosine = jnp.cos(angle_grid)[:, None, :]
    sine_grid = flip_sign * jnp.sin(angle_grid)[:, None, :]
    lower_part = field_in[..., :half_dim]
    upper_part = field_in[..., half_dim:rotary]
    return jnp.concatenate([lower_part * cosine - upper_part * sine_grid, upper_part * cosine + lower_part * sine_grid, field_in[..., rotary:]], axis=-1)

def smooth_gelu(values_in):
    return jax.nn.gelu(values_in, approximate=True)

def attend_block(offset, queries, key_grid, value_grid):
    block_rows = min(512, LENGTH)
    query_block = lax.dynamic_slice_in_dim(queries, offset, block_rows, 0)
    scores = jnp.einsum('qhd,khd->hqk', query_block, key_grid, precision=HIGHEST) * HEAD_DIM ** (-0.5)
    scores = low_back(scores)
    query_index = offset + jnp.arange(block_rows, dtype=jnp.int32)
    key_index = jnp.arange(LENGTH, dtype=jnp.int32)
    visible = key_index[None, :] <= query_index[:, None]
    scores = jnp.where(visible[None], scores, NEG_FILL)
    weights = low(jax.nn.softmax(scores, axis=-1))
    return jnp.einsum('hqk,khd->qhd', weights, value_grid, precision=HIGHEST)

def sequence_forward(activation, params):
    gains, shifts, attend, attend_bias, mixer, mixer_bias, upward, upward_bias, downward, downward_bias = params
    normed = low(layer_norm(activation, gains, shifts))
    projected = low_back(jnp.dot(normed, attend, precision=HIGHEST) + attend_bias)
    positions = jnp.arange(LENGTH, dtype=jnp.float32)
    queries = rotate(projected[:, :D].reshape(LENGTH, HEADS, HEAD_DIM), positions, ROT, 1.0)
    key_grid = rotate(projected[:, D:2 * D].reshape(LENGTH, HEADS, HEAD_DIM), positions, ROT, 1.0)
    value_grid = projected[:, 2 * D:].reshape(LENGTH, HEADS, HEAD_DIM)
    queries = low(low_back(queries))
    key_grid = low(low_back(key_grid))
    value_grid = low(low_back(value_grid))

    def one_block(offset):
        return attend_block(offset, queries, key_grid, value_grid)
    block_rows = min(512, LENGTH)
    offsets = jnp.arange(LENGTH // block_rows, dtype=jnp.int32) * block_rows
    attended = lax.map(jax.checkpoint(one_block), offsets).reshape(LENGTH, D)
    attended = low(low_back(attended))
    mixed = jnp.dot(attended, mixer, precision=HIGHEST) + mixer_bias
    hidden = low_back(jnp.dot(normed, upward, precision=HIGHEST) + upward_bias)
    activated = low(smooth_gelu(hidden))
    feed_out = jnp.dot(activated, downward, precision=HIGHEST) + downward_bias
    return activation + mixed + feed_out

def forward(rows_all, params):
    checked = jax.checkpoint(sequence_forward)

    def stepper(ignored, activation):
        return (ignored, checked(activation, params))
    ignored, layer_out = lax.scan(stepper, None, rows_all)
    return layer_out

def reference(inputs, gains, shifts, attend, attend_bias, mixer, mixer_bias, upward, upward_bias, downward, downward_bias, cotangent):
    params = (gains.astype(jnp.float32), shifts.astype(jnp.float32), attend.astype(jnp.float32), attend_bias.astype(jnp.float32), mixer.astype(jnp.float32), mixer_bias.astype(jnp.float32), upward.astype(jnp.float32), upward_bias.astype(jnp.float32), downward.astype(jnp.float32), downward_bias.astype(jnp.float32))
    layer_out, pullback = jax.vjp(forward, inputs.astype(jnp.float32), params)
    inputs_grad, param_grads = pullback(cotangent.astype(jnp.float32))
    return (layer_out.astype(jnp.bfloat16), inputs_grad, param_grads[0], param_grads[1], param_grads[2], param_grads[3], param_grads[4], param_grads[5], param_grads[6], param_grads[7], param_grads[8], param_grads[9])
```

```python
import functools

import jax
import jax.numpy as jnp
from jax import lax
from jax.experimental import pallas as pl
from jax.experimental.pallas import tpu as pltpu
from jax.sharding import Mesh, PartitionSpec as P

HEADS = 32
HEAD_DIM = 64
ROT = 32
WIDTH = 2048
FF = 8192
SEQ_DEVICES = 8
CHIPS = 8
FSDP_DEVICES = 16
ROWS = 128
LENGTH = ROWS * SEQ_DEVICES
TOKENS = ROWS * CHIPS
CHIP_COLS = WIDTH // CHIPS
CORE_COLS = WIDTH // FSDP_DEVICES
CORE_FF = FF // FSDP_DEVICES
PAIR = 2 * HEAD_DIM
QBLOCK = 256

EPSILON = 1e-05
ROPE_BASE = 10000.0
NEG_FILL = -1e30
SCALE = HEAD_DIM ** (-0.5)

F32 = jnp.float32
BF16 = jnp.bfloat16

SEQ = ("y", "xl")
GROUP = ("xh", "z")
FSDP = ("xh", "z", "c")

NT = (((1,), (1,)), ((), ()))
TN = (((0,), (0,)), ((), ()))
NN = (((1,), (0,)), ((), ()))


def dot(lhs, rhs, dims=NN):
    return lax.dot_general(lhs, rhs, dims, preferred_element_type=F32)


def swap(piece, axis):
    return lax.ppermute(piece, axis, [(0, 1), (1, 0)])


def from_ahead(piece, step):
    return lax.ppermute(piece, "z", [(i, (i - step) % 4) for i in range(4)])


def to_ahead(piece, step):
    return lax.ppermute(piece, "z", [(i, (i + step) % 4) for i in range(4)])


def spread(piece):
    other = swap(piece, "xh")
    near = [piece] + [from_ahead(piece, k) for k in (1, 3, 2)]
    far = [other] + [from_ahead(other, k) for k in (1, 3, 2)]
    near = [near[0], near[1], near[3], near[2]]
    far = [far[0], far[1], far[3], far[2]]
    return jnp.concatenate(near + far, axis=0)


def collect(parts):
    parts = parts.reshape(2, 4, ROWS, WIDTH)
    total = []
    for r in (1, 0):
        arrived = [to_ahead(parts[r, k], k) for k in (1, 3, 2)]
        total.append(parts[r, 0].astype(F32) + sum(a.astype(F32) for a in arrived))
    return total[1] + swap(total[0].astype(BF16), "xh").astype(F32)


def rope_tables(positions, heads):
    half = ROT // 2
    frequency = ROPE_BASE ** (-2.0 * jnp.arange(half, dtype=F32) / ROT)
    angle = positions.astype(F32)[:, None] * frequency[None, :]
    cosine, sine = jnp.cos(angle), jnp.sin(angle)
    rest = jnp.zeros((positions.shape[0], HEAD_DIM - ROT), F32)
    blank = jnp.zeros_like(sine)
    turn = jnp.concatenate([cosine, cosine, rest + 1.0], axis=1)
    upper = jnp.concatenate([-sine, blank, rest], axis=1)
    lower = jnp.concatenate([blank, sine, rest], axis=1)
    return tuple(jnp.tile(t, (1, heads)) for t in (turn, upper, lower))


def turn_columns(values, turn, upper, lower, sign):
    width = values.shape[1]
    half = ROT // 2
    ahead = pltpu.roll(values, width - half, 1)
    behind = pltpu.roll(values, half, 1)
    return values * turn + sign * (ahead * upper + behind * lower)


def project_kernel(rows_ref, weight_ref, bias_ref, turn_ref, upper_ref, lower_ref, out_ref):
    projected = dot(rows_ref[...], weight_ref[...]) + bias_ref[...]
    turned_width = 2 * CHIP_COLS
    repeat = rows_ref.shape[0] // ROWS
    for block in range(repeat):
        rows = slice(block * ROWS, (block + 1) * ROWS)
        part = projected[rows, :turned_width]
        out_ref[rows, :turned_width] = turn_columns(
            part, turn_ref[...], upper_ref[...], lower_ref[...], 1.0
        ).astype(BF16)
    out_ref[:, turned_width:] = projected[:, turned_width:].astype(BF16)


def project(normed, weight, bias, tables):
    block = 256
    whole = lambda shape: pl.BlockSpec(shape, lambda i: (0, 0))
    width = weight.shape[1]
    return pl.pallas_call(
        project_kernel,
        grid=(TOKENS // block,),
        in_specs=[
            pl.BlockSpec((block, WIDTH), lambda i: (i, 0)),
            whole(weight.shape),
            whole(bias.shape),
        ]
        + [whole(t.shape) for t in tables],
        out_specs=pl.BlockSpec((block, width), lambda i: (i, 0)),
        out_shape=jax.ShapeDtypeStruct((TOKENS, width), BF16),
        compiler_params=pltpu.CompilerParams(vmem_limit_bytes=40 * 2**20),
        cost_estimate=pl.CostEstimate(
            flops=2 * TOKENS * WIDTH * width, bytes_accessed=10 * 2**20, transcendentals=0
        ),
        name="project",
    )(normed, weight, bias, *tables)


def lane_masks():
    lane = lax.broadcasted_iota(jnp.int32, (1, PAIR), 1)
    first = (lane < HEAD_DIM).astype(BF16)
    return first, 1 - first


def scores_of(query, keys, low):
    scores = dot(query, keys, NT) * SCALE
    row = low + lax.broadcasted_iota(jnp.int32, scores.shape, 0)
    col = lax.broadcasted_iota(jnp.int32, scores.shape, 1)
    return jnp.where(col <= row, scores, NEG_FILL)


def attend_kernel(query_ref, key_ref, value_ref, out_ref, logsum_ref):
    first, second = lane_masks()
    lane = lax.broadcasted_iota(jnp.int32, (QBLOCK, PAIR), 1)
    for low in range(0, LENGTH, QBLOCK):
        reach = low + QBLOCK
        query = query_ref[low:reach, :]
        keys = key_ref[:reach, :]
        values = value_ref[:reach, :]
        found = []
        for mask in (first, second):
            scores = scores_of(query * mask, keys, low)
            peak = jnp.max(scores, axis=1, keepdims=True)
            weight = jnp.exp(scores - peak)
            total = jnp.sum(weight, axis=1, keepdims=True)
            prob_low = (weight * (1.0 / total)).astype(BF16)
            found.append((dot(prob_low, values), peak + jnp.log(total)))
        out_ref[low:reach, :] = jnp.where(lane < HEAD_DIM, found[0][0], found[1][0]).astype(BF16)
        logsum_ref[low:reach, :] = jnp.where(lane < HEAD_DIM, found[0][1], found[1][1])


def attend_forward(qkv):
    pairs = CHIP_COLS // PAIR
    column = lambda part: pl.BlockSpec((LENGTH, PAIR), lambda p: (0, part * pairs + p))
    return pl.pallas_call(
        attend_kernel,
        grid=(pairs,),
        in_specs=[column(0), column(1), column(2)],
        out_specs=[column(0), column(0)],
        out_shape=[
            jax.ShapeDtypeStruct((LENGTH, CHIP_COLS), BF16),
            jax.ShapeDtypeStruct((LENGTH, CHIP_COLS), F32),
        ],
        compiler_params=pltpu.CompilerParams(vmem_limit_bytes=40 * 2**20),
        cost_estimate=pl.CostEstimate(
            flops=8 * 2**30, bytes_accessed=4 * 2**20, transcendentals=4 * 2**20
        ),
        name="attend_forward",
    )(qkv, qkv, qkv)


def attend_back_kernel(
    query_ref,
    key_ref,
    value_ref,
    grad_ref,
    logsum_ref,
    turn_ref,
    upper_ref,
    lower_ref,
    out_ref,
    key_total,
    value_total,
):
    pair = pl.program_id(0)
    first, second = lane_masks()
    lane = lax.broadcasted_iota(jnp.int32, (QBLOCK, PAIR), 1)
    key_total[...] = jnp.zeros_like(key_total)
    value_total[...] = jnp.zeros_like(value_total)

    def store(part, low, reach, values):
        start = pl.multiple_of((part * (CHIP_COLS // PAIR) + pair) * PAIR, PAIR)
        out_ref[low:reach, pl.ds(start, PAIR)] = values.astype(BF16)

    def unturn(values, low, reach):
        kept = values.astype(BF16).astype(F32)
        return turn_columns(
            kept, turn_ref[low:reach, :], upper_ref[low:reach, :], lower_ref[low:reach, :], -1.0
        )

    for low in range(0, LENGTH, QBLOCK):
        reach = low + QBLOCK
        query = query_ref[low:reach, :]
        grad = grad_ref[low:reach, :]
        keys = key_ref[:reach, :]
        values = value_ref[:reach, :]
        query_grads = []
        key_part = 0.0
        value_part = 0.0
        for head, mask in enumerate((first, second)):
            own_query = query * mask
            own_grad = grad * mask
            scores = scores_of(own_query, keys, low)
            start = head * HEAD_DIM
            probs = jnp.exp(scores - logsum_ref[low:reach, start : start + 1])
            prob_grad = dot(own_grad, values, NT)
            inner = jnp.sum(probs * prob_grad, axis=1, keepdims=True)
            score_grad = (probs * (prob_grad - inner)).astype(BF16)
            query_grads.append(dot(score_grad, keys))
            key_part += dot(score_grad, own_query, TN)
            value_part += dot(probs.astype(BF16), own_grad, TN)
        key_total[:reach, :] += key_part
        value_total[:reach, :] += value_part
        query_grad = jnp.where(lane < HEAD_DIM, query_grads[0], query_grads[1]) * SCALE
        store(0, low, reach, unturn(query_grad, low, reach))
    store(1, 0, LENGTH, unturn(key_total[...] * SCALE, 0, LENGTH))
    store(2, 0, LENGTH, value_total[...])


def attend_backward(qkv, grad, logsum, tables):
    pairs = CHIP_COLS // PAIR
    column = lambda part: pl.BlockSpec((LENGTH, PAIR), lambda p: (0, part * pairs + p))
    whole = lambda shape: pl.BlockSpec(shape, lambda p: (0, 0))
    width = 3 * CHIP_COLS
    return pl.pallas_call(
        attend_back_kernel,
        grid=(pairs,),
        in_specs=[column(0), column(1), column(2), column(0), column(0)]
        + [whole(t.shape) for t in tables],
        out_specs=whole((LENGTH, width)),
        out_shape=jax.ShapeDtypeStruct((LENGTH, width), BF16),
        scratch_shapes=[pltpu.VMEM((LENGTH, PAIR), F32), pltpu.VMEM((LENGTH, PAIR), F32)],
        compiler_params=pltpu.CompilerParams(vmem_limit_bytes=40 * 2**20),
        cost_estimate=pl.CostEstimate(
            flops=20 * 2**30, bytes_accessed=6 * 2**20, transcendentals=4 * 2**20
        ),
        name="attend_backward",
    )(qkv, qkv, qkv, grad, logsum, *tables)


def layer_stats(rows):
    center = rows - jnp.mean(rows, axis=-1, keepdims=True)
    spread_out = jnp.mean(center * center, axis=-1, keepdims=True)
    return center, lax.rsqrt(spread_out + EPSILON)


def exchange_seq(blocks):
    return lax.all_to_all(blocks, SEQ, split_axis=0, concat_axis=0, tiled=True)


def reduce_seq(blocks):
    return jnp.sum(exchange_seq(blocks).astype(F32), axis=0)


def gather_seq(block):
    return lax.all_gather(block, SEQ, axis=0, tiled=False)


def per_device(
    inputs,
    gains,
    shifts,
    attend,
    attend_bias,
    mixer,
    mixer_bias,
    upward,
    upward_bias,
    downward,
    downward_bias,
    cotangent,
):
    core = lax.axis_index("c")
    chip = lax.axis_index("xh") * 4 + lax.axis_index("z")
    seq_index = lax.axis_index("y") * 2 + lax.axis_index("xl")
    rows_in = inputs.reshape(ROWS, WIDTH)
    own_cot = cotangent.reshape(ROWS, WIDTH)

    rows_group = spread(rows_in)
    cot_group = spread(own_cot)

    small = jnp.concatenate([gains, shifts, mixer_bias, downward_bias, attend_bias]).reshape(7, 128)
    small_all = lax.all_gather(small, FSDP, axis=0, tiled=False).astype(F32)
    gain_all = small_all[:, 0].reshape(WIDTH)
    shift_all = small_all[:, 1].reshape(WIDTH)
    out_bias = (small_all[:, 2] + small_all[:, 3]).reshape(WIDTH)
    bias_grid = small_all[:, 4:7].reshape(3, CHIPS, CHIP_COLS)
    attend_bias_chip = lax.dynamic_slice_in_dim(bias_grid, chip, 1, 1).reshape(1, 3 * CHIP_COLS)

    def by_core(own, other, axis):
        return jnp.where(
            core == 0,
            jnp.concatenate([own, other], axis=axis),
            jnp.concatenate([other, own], axis=axis),
        )

    attend_sent = attend.reshape(CORE_COLS, 3, CHIPS, CHIP_COLS).transpose(2, 0, 1, 3)
    attend_own = lax.all_to_all(
        attend_sent.reshape(CHIPS, CORE_COLS, 3 * CHIP_COLS),
        GROUP,
        split_axis=0,
        concat_axis=0,
        tiled=True,
    )
    attend_chip = by_core(
        attend_own[:, None], swap(attend_own, "c")[:, None], 1
    ).reshape(WIDTH, 3 * CHIP_COLS)
    mixer_chip = by_core(mixer, swap(mixer, "c"), 0)
    up_chip = jnp.concatenate([upward, swap(upward, "c")], axis=1)
    up_bias_chip = jnp.concatenate([upward_bias, swap(upward_bias, "c")]).astype(F32)
    down_chip = jnp.concatenate([downward, swap(downward, "c")], axis=0)

    own_positions = seq_index * ROWS + jnp.arange(ROWS, dtype=jnp.int32)
    own_tables = rope_tables(own_positions, 2 * CHIP_COLS // HEAD_DIM)
    all_tables = rope_tables(jnp.arange(LENGTH, dtype=jnp.int32), 2)

    center, inverse = layer_stats(rows_group.astype(F32))
    normed_group = (center * inverse * gain_all + shift_all).astype(BF16)
    qkv_sent = project(normed_group, attend_chip, attend_bias_chip, own_tables)
    qkv = exchange_seq(qkv_sent.reshape(CHIPS, ROWS, 3 * CHIP_COLS)).reshape(LENGTH, 3 * CHIP_COLS)

    hidden = dot(normed_group, up_chip) + up_bias_chip
    activated, gelu_pullback = jax.vjp(lambda h: jax.nn.gelu(h, approximate=True), hidden)
    activated_low = activated.astype(BF16)

    attended, logsum = attend_forward(qkv)
    attended_group = exchange_seq(attended.reshape(SEQ_DEVICES, ROWS, CHIP_COLS)).reshape(
        TOKENS, CHIP_COLS
    )
    attended_grad = dot(cot_group, mixer_chip, NT).astype(BF16)
    grad_heads = exchange_seq(attended_grad.reshape(CHIPS, ROWS, CHIP_COLS)).reshape(
        LENGTH, CHIP_COLS
    )

    out_part = (dot(activated_low, down_chip) + dot(attended_group, mixer_chip)).astype(BF16)
    outputs = (rows_in.astype(F32) + collect(out_part) + out_bias).astype(BF16)

    projected_grad = exchange_seq(
        attend_backward(qkv, grad_heads, logsum, all_tables).reshape(
            SEQ_DEVICES, ROWS, 3 * CHIP_COLS
        )
    ).reshape(TOKENS, 3 * CHIP_COLS)

    hidden_grad = gelu_pullback(dot(cot_group, down_chip, NT))[0].astype(BF16)

    normed_part = (
        dot(projected_grad, attend_chip, NT) + dot(hidden_grad, up_chip, NT)
    ).astype(BF16)
    normed_grad = collect(normed_part)
    own_center, own_inverse = layer_stats(rows_in.astype(F32))
    unit = own_center * own_inverse
    scaled = normed_grad * gain_all
    rows_grad = own_inverse * (
        scaled
        - jnp.mean(scaled, axis=-1, keepdims=True)
        - unit * jnp.mean(scaled * unit, axis=-1, keepdims=True)
    )
    inputs_grad = own_cot.astype(F32) + rows_grad

    up_part = dot(normed_group, hidden_grad, TN).astype(BF16)
    down_part = dot(activated_low, cot_group, TN).astype(BF16)
    mixer_part = dot(attended_group, cot_group, TN).astype(BF16)
    up_sum = up_part[:, :CORE_FF].astype(F32) + swap(up_part[:, CORE_FF:], "c").astype(F32)
    down_sum = down_part[:CORE_FF].astype(F32) + swap(down_part[CORE_FF:], "c").astype(F32)
    mixer_keep = lax.dynamic_slice_in_dim(mixer_part, core * CORE_COLS, CORE_COLS, 0)
    mixer_send = lax.dynamic_slice_in_dim(mixer_part, (1 - core) * CORE_COLS, CORE_COLS, 0)
    mixer_sum = mixer_keep.astype(F32) + swap(mixer_send, "c").astype(F32)

    up_grad = (
        gather_seq(reduce_seq(up_sum.astype(BF16).reshape(8, WIDTH // 8, CORE_FF)).astype(BF16))
        .reshape(WIDTH, CORE_FF)
        .astype(F32)
    )
    down_grad = (
        gather_seq(reduce_seq(down_sum.astype(BF16).reshape(8, CORE_FF // 8, WIDTH)).astype(BF16))
        .reshape(CORE_FF, WIDTH)
        .astype(F32)
    )
    mixer_grad = (
        gather_seq(
            reduce_seq(mixer_sum.astype(BF16).reshape(8, CORE_COLS // 8, WIDTH)).astype(BF16)
        )
        .reshape(CORE_COLS, WIDTH)
        .astype(F32)
    )

    attend_part = dot(normed_group, projected_grad, TN).astype(BF16)
    attend_part = attend_part.reshape(CHIPS, 2, CORE_COLS, 3 * CHIP_COLS)
    attend_keep = lax.dynamic_index_in_dim(attend_part, core, 1, keepdims=False)
    attend_send = lax.dynamic_index_in_dim(attend_part, 1 - core, 1, keepdims=False)
    attend_sum = (attend_keep.astype(F32) + swap(attend_send, "c").astype(F32)).astype(BF16)
    slab = CORE_COLS // 8
    attend_slab = reduce_seq(
        attend_sum.reshape(CHIPS, 8, slab, 3 * CHIP_COLS).transpose(1, 0, 2, 3)
    ).astype(BF16)
    attend_slab = lax.all_to_all(attend_slab, GROUP, split_axis=0, concat_axis=0, tiled=True)
    attend_slab = (
        attend_slab.reshape(CHIPS, slab, 3, CHIP_COLS).transpose(1, 2, 0, 3).reshape(slab, 3 * WIDTH)
    )
    attend_grad = gather_seq(attend_slab).reshape(CORE_COLS, 3 * WIDTH).astype(F32)

    gain_full = jnp.sum(normed_grad * unit, axis=0)
    shift_full = jnp.sum(normed_grad, axis=0)
    bias_full = jnp.sum(own_cot.astype(F32), axis=0)
    attend_bias_chip_grad = jnp.sum(projected_grad.astype(F32), axis=0).reshape(3, 1, CHIP_COLS)
    attend_bias_full = lax.dynamic_update_slice(
        jnp.zeros((3, CHIPS, CHIP_COLS), F32), attend_bias_chip_grad, (0, chip, 0)
    )
    up_bias_chip_grad = jnp.sum(hidden_grad.astype(F32), axis=0)
    up_bias_pair = by_core(up_bias_chip_grad[:CORE_FF], up_bias_chip_grad[CORE_FF:], 0)
    up_bias_full = lax.dynamic_update_slice(
        jnp.zeros((CHIPS, 2 * CORE_FF), F32), up_bias_pair[None], (chip, 0)
    )
    vectors = jnp.concatenate(
        [
            v.reshape(FSDP_DEVICES, -1)
            for v in (gain_full, shift_full, bias_full, attend_bias_full, up_bias_full)
        ],
        axis=1,
    )
    vectors = lax.all_to_all(vectors, FSDP, split_axis=0, concat_axis=0, tiled=True)
    vectors = lax.psum(jnp.sum(vectors, axis=0), SEQ)
    gain_grad, shift_grad, bias_grad = vectors[:128], vectors[128:256], vectors[256:384]
    attend_bias_grad, up_bias_grad = vectors[384:768], vectors[768:]

    return (
        outputs.reshape(inputs.shape),
        inputs_grad.reshape(inputs.shape),
        gain_grad,
        shift_grad,
        attend_grad,
        attend_bias_grad,
        mixer_grad,
        bias_grad,
        up_grad,
        up_bias_grad,
        down_grad,
        bias_grad,
    )


def solution(mesh):
    fine = Mesh(mesh.devices.reshape(4, 2, 2, 4, 2), ("y", "xl", "xh", "z", "c"))
    rows = P(FSDP, SEQ, None)
    vector = P(FSDP)
    by_row = P(FSDP, None)
    by_col = P(None, FSDP)
    in_specs = (
        rows,
        vector,
        vector,
        by_row,
        vector,
        by_row,
        vector,
        by_col,
        vector,
        by_row,
        vector,
        rows,
    )
    out_specs = (
        rows,
        rows,
        vector,
        vector,
        by_row,
        vector,
        by_row,
        vector,
        by_col,
        vector,
        by_row,
        vector,
    )
    return jax.shard_map(
        per_device, mesh=fine, in_specs=in_specs, out_specs=out_specs, check_vma=False
    )
```

```python
import jax
import jax.numpy as jnp
from jax import lax
from jax.experimental import pallas as pl
from jax.experimental.pallas import tpu as pltpu
from jax.sharding import Mesh, PartitionSpec as P

HEADS = 32
HEAD_DIM = 64
ROT = 32
WIDTH = 2048
FF = 8192
SEQ_DEVICES = 8
CHIPS = 8
FSDP_DEVICES = 16
ROWS = 128
LENGTH = ROWS * SEQ_DEVICES
TOKENS = ROWS * CHIPS
CHIP_COLS = WIDTH // CHIPS
CORE_COLS = WIDTH // FSDP_DEVICES
CORE_FF = FF // FSDP_DEVICES
PAIR = 2 * HEAD_DIM
QBLOCK = 256

EPSILON = 1e-05
ROPE_BASE = 10000.0
NEG_FILL = -1e30
SCALE = HEAD_DIM ** (-0.5)

F32 = jnp.float32
BF16 = jnp.bfloat16

SEQ = ("y", "xl")
GROUP = ("xh", "z")
FSDP = ("xh", "z", "c")

NT = (((1,), (1,)), ((), ()))
TN = (((0,), (0,)), ((), ()))
NN = (((1,), (0,)), ((), ()))


def dot(lhs, rhs, dims=NN):
    return lax.dot_general(lhs, rhs, dims, preferred_element_type=F32)


def swap(piece, axis):
    return lax.ppermute(piece, axis, [(0, 1), (1, 0)])


def rope_tables(positions, heads):
    half = ROT // 2
    frequency = ROPE_BASE ** (-2.0 * jnp.arange(half, dtype=F32) / ROT)
    angle = positions.astype(F32)[:, None] * frequency[None, :]
    cosine, sine = jnp.cos(angle), jnp.sin(angle)
    rest = jnp.zeros((positions.shape[0], HEAD_DIM - ROT), F32)
    blank = jnp.zeros_like(sine)
    turn = jnp.concatenate([cosine, cosine, rest + 1.0], axis=1)
    upper = jnp.concatenate([-sine, blank, rest], axis=1)
    lower = jnp.concatenate([blank, sine, rest], axis=1)
    return tuple(jnp.tile(t, (1, heads)) for t in (turn, upper, lower))


def turn_columns(values, turn, upper, lower, sign):
    width = values.shape[1]
    half = ROT // 2
    ahead = pltpu.roll(values, width - half, 1)
    behind = pltpu.roll(values, half, 1)
    return values * turn + sign * (ahead * upper + behind * lower)


def whole(shape):
    return pl.BlockSpec(shape, lambda i: (0,) * len(shape))


def row_block(rows, width, column=0):
    return pl.BlockSpec((rows, width), lambda i: (i, column))


def call(kernel, name, grid, in_specs, out_specs, out_shape, flops, moved, operands):
    return pl.pallas_call(
        kernel,
        grid=(grid,),
        in_specs=in_specs,
        out_specs=out_specs,
        out_shape=out_shape,
        compiler_params=pltpu.CompilerParams(vmem_limit_bytes=48 * 2**20),
        cost_estimate=pl.CostEstimate(flops=flops, bytes_accessed=moved, transcendentals=0),
        name=name,
    )(*operands)


def shape(dims, kind=BF16):
    return jax.ShapeDtypeStruct(dims, kind)


def layer_stats(rows):
    center = rows - jnp.mean(rows, axis=-1, keepdims=True)
    spread_out = jnp.mean(center * center, axis=-1, keepdims=True)
    return center, lax.rsqrt(spread_out + EPSILON)


def assemble_kernel(core_ref, own_ref, other_ref, out_ref):
    core = core_ref[0]
    out_ref[0, core] = own_ref[...].reshape(out_ref.shape[2:])
    out_ref[0, 1 - core] = other_ref[...].reshape(out_ref.shape[2:])


def assemble_attend(core, own, other):
    slab, cols = own.shape[2:]
    piece = pl.BlockSpec((SEQ_DEVICES, 1, slab, cols), lambda g, core: (0, g, 0, 0))
    out = (CHIPS, 2, SEQ_DEVICES, slab, cols)
    return pl.pallas_call(
        assemble_kernel,
        grid_spec=pltpu.PrefetchScalarGridSpec(
            num_scalar_prefetch=1,
            grid=(CHIPS,),
            in_specs=[piece, piece],
            out_specs=pl.BlockSpec((1,) + out[1:], lambda g, core: (g, 0, 0, 0, 0)),
        ),
        out_shape=shape(out),
        compiler_params=pltpu.CompilerParams(vmem_limit_bytes=24 * 2**20),
        cost_estimate=pl.CostEstimate(flops=0, bytes_accessed=6 * 2**20, transcendentals=0),
        name="assemble_attend",
    )(core, own, other).reshape(WIDTH, cols)


def norm_project_kernel(
    rows_ref,
    gain_ref,
    shift_ref,
    weight_ref,
    bias_ref,
    turn_ref,
    upper_ref,
    lower_ref,
    normed_ref,
    out_ref,
):
    center, inverse = layer_stats(rows_ref[...].astype(F32))
    normed = (center * inverse * gain_ref[...] + shift_ref[...]).astype(BF16)
    normed_ref[...] = normed
    projected = dot(normed, weight_ref[...]) + bias_ref[...]
    turned_width = 2 * CHIP_COLS
    for block in range(rows_ref.shape[0] // ROWS):
        rows = slice(block * ROWS, (block + 1) * ROWS)
        out_ref[rows, :turned_width] = turn_columns(
            projected[rows, :turned_width], turn_ref[...], upper_ref[...], lower_ref[...], 1.0
        ).astype(BF16)
    out_ref[:, turned_width:] = projected[:, turned_width:].astype(BF16)


def norm_project(rows, gain, shift, weight, bias, tables):
    block = 256
    width = weight.shape[1]
    vectors = (gain, shift, weight, bias) + tables
    return call(
        norm_project_kernel,
        "norm_project",
        TOKENS // block,
        [row_block(block, WIDTH)] + [whole(v.shape) for v in vectors],
        [row_block(block, WIDTH), row_block(block, width)],
        [shape((TOKENS, WIDTH)), shape((TOKENS, width))],
        2 * TOKENS * WIDTH * width,
        14 * 2**20,
        (rows,) + vectors,
    )


def hidden_kernel(
    normed_ref,
    own_ref,
    other_ref,
    own_bias_ref,
    other_bias_ref,
    own_act_ref,
    other_act_ref,
    own_slope_ref,
    other_slope_ref,
):
    root = (2.0 / 3.141592653589793) ** 0.5
    for weight, bias, act, slope in (
        (own_ref, own_bias_ref, own_act_ref, own_slope_ref),
        (other_ref, other_bias_ref, other_act_ref, other_slope_ref),
    ):
        hidden = dot(normed_ref[...], weight[...]) + bias[...]
        square = hidden * hidden
        bend = jnp.tanh(root * hidden * (1.0 + 0.044715 * square))
        half = 0.5 * (1.0 + bend)
        act[...] = (hidden * half).astype(BF16)
        slope[...] = half + 0.5 * hidden * (1.0 - bend * bend) * (
            root * (1.0 + 3.0 * 0.044715 * square)
        )


def hidden_forward(normed, own, other, own_bias, other_bias):
    block = 256
    operands = (own, other, own_bias, other_bias)
    return call(
        hidden_kernel,
        "hidden_forward",
        TOKENS // block,
        [row_block(block, WIDTH)] + [whole(v.shape) for v in operands],
        [row_block(block, CORE_FF)] * 4,
        [shape((TOKENS, CORE_FF))] * 2 + [shape((TOKENS, CORE_FF), F32)] * 2,
        4 * TOKENS * WIDTH * CORE_FF,
        14 * 2**20,
        (normed,) + operands,
    )


def grad_heads_kernel(cot_ref, mixer_ref, out_ref):
    out_ref[...] = dot(cot_ref[...], mixer_ref[...], NT).astype(BF16)


def grad_heads(cot, mixer):
    block = 256
    return call(
        grad_heads_kernel,
        "grad_heads",
        TOKENS // block,
        [row_block(block, WIDTH), whole(mixer.shape)],
        row_block(block, CHIP_COLS),
        shape((TOKENS, CHIP_COLS)),
        2 * TOKENS * WIDTH * CHIP_COLS,
        6 * 2**20,
        (cot, mixer),
    )


def hidden_back_kernel(
    cot_ref, own_ref, other_ref, own_slope_ref, other_slope_ref, own_out, other_out, own_sum, other_sum
):
    for weight, slope, out, total in (
        (own_ref, own_slope_ref, own_out, own_sum),
        (other_ref, other_slope_ref, other_out, other_sum),
    ):
        grad = (dot(cot_ref[...], weight[...], NT) * slope[...]).astype(BF16)
        out[...] = grad
        part = jnp.sum(grad.astype(F32), axis=0, keepdims=True)

        @pl.when(pl.program_id(0) == 0)
        def _():
            total[...] = part

        @pl.when(pl.program_id(0) > 0)
        def _():
            total[...] += part


def hidden_back(cot, own, other, own_slope, other_slope):
    block = 256
    return call(
        hidden_back_kernel,
        "hidden_back",
        TOKENS // block,
        [row_block(block, WIDTH), whole(own.shape), whole(other.shape)]
        + [row_block(block, CORE_FF)] * 2,
        [row_block(block, CORE_FF)] * 2 + [whole((1, CORE_FF))] * 2,
        [shape((TOKENS, CORE_FF))] * 2 + [shape((1, CORE_FF), F32)] * 2,
        4 * TOKENS * WIDTH * CORE_FF,
        14 * 2**20,
        (cot, own, other, own_slope, other_slope),
    )


def out_part_kernel(own_act, other_act, attended, own_ref, other_ref, mixer_ref, out_ref):
    out_ref[...] = (
        dot(own_act[...], own_ref[...])
        + dot(other_act[...], other_ref[...])
        + dot(attended[...], mixer_ref[...])
    ).astype(BF16)


def out_part(own_act, other_act, attended, own, other, mixer):
    block = 256
    weights = (own, other, mixer)
    return call(
        out_part_kernel,
        "out_part",
        TOKENS // block,
        [row_block(block, CORE_FF)] * 2
        + [row_block(block, CHIP_COLS)]
        + [whole(w.shape) for w in weights],
        row_block(block, WIDTH),
        shape((TOKENS, WIDTH)),
        2 * TOKENS * WIDTH * (2 * CORE_FF + CHIP_COLS),
        12 * 2**20,
        (own_act, other_act, attended) + weights,
    )


def normed_part_kernel(
    projected, own_grad, other_grad, rows_ref, attend_ref, own_ref, other_ref, out_ref, sums_ref, bias_ref
):
    total = (
        dot(projected[...], attend_ref[...], NT)
        + dot(own_grad[...], own_ref[...], NT)
        + dot(other_grad[...], other_ref[...], NT)
    )
    out_ref[...] = total.astype(BF16)
    center, inverse = layer_stats(rows_ref[...].astype(F32))
    gain_part = jnp.sum(total * (center * inverse), axis=0, keepdims=True)
    shift_part = jnp.sum(total, axis=0, keepdims=True)
    bias_part = jnp.sum(projected[...].astype(F32), axis=0, keepdims=True)

    @pl.when(pl.program_id(0) == 0)
    def _():
        sums_ref[0:1] = gain_part
        sums_ref[1:2] = shift_part
        bias_ref[...] = bias_part

    @pl.when(pl.program_id(0) > 0)
    def _():
        sums_ref[0:1] += gain_part
        sums_ref[1:2] += shift_part
        bias_ref[...] += bias_part


def normed_part(projected, own_grad, other_grad, rows, attend, own, other):
    block = 256
    width = projected.shape[1]
    weights = (attend, own, other)
    return call(
        normed_part_kernel,
        "normed_part",
        TOKENS // block,
        [row_block(block, width)]
        + [row_block(block, CORE_FF)] * 2
        + [row_block(block, WIDTH)]
        + [whole(w.shape) for w in weights],
        [row_block(block, WIDTH), whole((2, WIDTH)), whole((1, width))],
        [shape((TOKENS, WIDTH)), shape((2, WIDTH), F32), shape((1, width), F32)],
        2 * TOKENS * WIDTH * (2 * CORE_FF + width),
        18 * 2**20,
        (projected, own_grad, other_grad, rows) + weights,
    )


UP_ROWS = WIDTH // SEQ_DEVICES
DOWN_ROWS = CORE_FF // 2
MIX_ROWS = CORE_COLS // 2
PACK_ROWS = UP_ROWS + DOWN_ROWS + MIX_ROWS
PACK_COLS = CORE_FF


def pack_kernel(up_own, up_other, down_own, down_other, mix_own, mix_other, out_ref):
    half = PACK_COLS // 2
    out_ref[0, :UP_ROWS] = (up_own[...].astype(F32) + up_other[...].astype(F32)).astype(BF16)
    down = (down_own[...].astype(F32) + down_other[...].astype(F32)).astype(BF16)
    start, stop = UP_ROWS, UP_ROWS + DOWN_ROWS
    out_ref[0, start:stop, :half] = down[:DOWN_ROWS]
    out_ref[0, start:stop, half:] = down[DOWN_ROWS:]
    mix = (mix_own[...].astype(F32) + mix_other[...].astype(F32)).astype(BF16)
    out_ref[0, stop:, :half] = mix[:MIX_ROWS]
    out_ref[0, stop:, half:] = mix[MIX_ROWS:]


def pack(up_own, up_other, down_own, down_other, mix_own, mix_other):
    cols = WIDTH // SEQ_DEVICES
    up = row_block(UP_ROWS, CORE_FF)
    down = pl.BlockSpec((CORE_FF, cols), lambda i: (0, i))
    mix = pl.BlockSpec((CORE_COLS, cols), lambda i: (0, i))
    return call(
        pack_kernel,
        "pack",
        SEQ_DEVICES,
        [up, up, down, down, mix, mix],
        pl.BlockSpec((1, PACK_ROWS, PACK_COLS), lambda i: (i, 0, 0)),
        shape((SEQ_DEVICES, PACK_ROWS, PACK_COLS)),
        0,
        15 * 2**20,
        (up_own, up_other, down_own, down_other, mix_own, mix_other),
    )


def unpack_kernel(packed_ref, up_ref, down_ref, mix_ref):
    half = PACK_COLS // 2
    start, stop = UP_ROWS, UP_ROWS + DOWN_ROWS
    up_ref[...] = packed_ref[0, :start].astype(F32)
    down_ref[:DOWN_ROWS] = packed_ref[0, start:stop, :half].astype(F32)
    down_ref[DOWN_ROWS:] = packed_ref[0, start:stop, half:].astype(F32)
    mix_ref[:MIX_ROWS] = packed_ref[0, stop:, :half].astype(F32)
    mix_ref[MIX_ROWS:] = packed_ref[0, stop:, half:].astype(F32)


def unpack(packed):
    cols = WIDTH // SEQ_DEVICES
    return call(
        unpack_kernel,
        "unpack",
        SEQ_DEVICES,
        [pl.BlockSpec((1, PACK_ROWS, PACK_COLS), lambda i: (i, 0, 0))],
        [
            row_block(UP_ROWS, CORE_FF),
            pl.BlockSpec((CORE_FF, cols), lambda i: (0, i)),
            pl.BlockSpec((CORE_COLS, cols), lambda i: (0, i)),
        ],
        [shape((WIDTH, CORE_FF), F32), shape((CORE_FF, WIDTH), F32), shape((CORE_COLS, WIDTH), F32)],
        0,
        14 * 2**20,
        (packed,),
    )


SLAB = CORE_COLS // SEQ_DEVICES


def pack_attend_kernel(own_ref, other_ref, out_ref):
    total = (own_ref[...].astype(F32) + other_ref[...].astype(F32)).astype(BF16)
    out_ref[...] = total.reshape(out_ref.shape)


def pack_attend(own, other):
    cols = own.shape[1]
    return call(
        pack_attend_kernel,
        "pack_attend",
        CHIPS,
        [row_block(CORE_COLS, cols)] * 2,
        pl.BlockSpec((SEQ_DEVICES, 1, SLAB, cols), lambda i: (0, i, 0, 0)),
        shape((SEQ_DEVICES, CHIPS, SLAB, cols)),
        0,
        5 * 2**20,
        (own, other),
    )


def unpack_attend_kernel(packed_ref, out_ref):
    for chip in range(CHIPS):
        for part in range(3):
            out_ref[:, part * WIDTH + chip * CHIP_COLS : part * WIDTH + (chip + 1) * CHIP_COLS] = (
                packed_ref[0, chip, :, part * CHIP_COLS : (part + 1) * CHIP_COLS].astype(F32)
            )


def unpack_attend(packed):
    return call(
        unpack_attend_kernel,
        "unpack_attend",
        SEQ_DEVICES,
        [pl.BlockSpec((1,) + packed.shape[1:], lambda i: (i, 0, 0, 0))],
        row_block(SLAB, 3 * WIDTH),
        shape((CORE_COLS, 3 * WIDTH), F32),
        0,
        5 * 2**20,
        (packed,),
    )


def rows_grad_kernel(rows_ref, cot_ref, near_ref, far_ref, gain_ref, out_ref):
    grad = near_ref[...] + far_ref[...].astype(F32)
    center, inverse = layer_stats(rows_ref[...].astype(F32))
    unit = center * inverse
    scaled = grad * gain_ref[...]
    out_ref[...] = cot_ref[...].astype(F32) + inverse * (
        scaled
        - jnp.mean(scaled, axis=-1, keepdims=True)
        - unit * jnp.mean(scaled * unit, axis=-1, keepdims=True)
    )


def rows_grad(rows, cot, near, far, gain):
    block = 64
    return call(
        rows_grad_kernel,
        "rows_grad",
        ROWS // block,
        [row_block(block, WIDTH)] * 4 + [whole(gain.shape)],
        row_block(block, WIDTH),
        shape((ROWS, WIDTH), F32),
        0,
        4 * 2**20,
        (rows, cot, near, far, gain),
    )


def lane_masks():
    lane = lax.broadcasted_iota(jnp.int32, (1, PAIR), 1)
    first = (lane < HEAD_DIM).astype(BF16)
    return first, 1 - first


def scores_of(query, keys, low):
    scores = dot(query, keys, NT) * SCALE
    row = low + lax.broadcasted_iota(jnp.int32, scores.shape, 0)
    col = lax.broadcasted_iota(jnp.int32, scores.shape, 1)
    return jnp.where(col <= row, scores, NEG_FILL)


def attend_kernel(query_ref, key_ref, value_ref, out_ref, logsum_ref):
    first, second = lane_masks()
    lane = lax.broadcasted_iota(jnp.int32, (QBLOCK, PAIR), 1)
    for low in range(0, LENGTH, QBLOCK):
        reach = low + QBLOCK
        query = query_ref[low:reach, :]
        keys = key_ref[:reach, :]
        values = value_ref[:reach, :]
        found = []
        for mask in (first, second):
            scores = scores_of(query * mask, keys, low)
            peak = jnp.max(scores, axis=1, keepdims=True)
            weight = jnp.exp(scores - peak)
            total = jnp.sum(weight, axis=1, keepdims=True)
            prob_low = (weight * (1.0 / total)).astype(BF16)
            found.append((dot(prob_low, values), peak + jnp.log(total)))
        out_ref[low:reach, :] = jnp.where(lane < HEAD_DIM, found[0][0], found[1][0]).astype(BF16)
        logsum_ref[low:reach, :] = jnp.where(lane < HEAD_DIM, found[0][1], found[1][1])


def attend_forward(qkv):
    pairs = CHIP_COLS // PAIR
    column = lambda part: pl.BlockSpec((LENGTH, PAIR), lambda p: (0, part * pairs + p))
    return pl.pallas_call(
        attend_kernel,
        grid=(pairs,),
        in_specs=[column(0), column(1), column(2)],
        out_specs=[column(0), column(0)],
        out_shape=[
            jax.ShapeDtypeStruct((LENGTH, CHIP_COLS), BF16),
            jax.ShapeDtypeStruct((LENGTH, CHIP_COLS), F32),
        ],
        compiler_params=pltpu.CompilerParams(vmem_limit_bytes=40 * 2**20),
        cost_estimate=pl.CostEstimate(
            flops=8 * 2**30, bytes_accessed=4 * 2**20, transcendentals=4 * 2**20
        ),
        name="attend_forward",
    )(qkv, qkv, qkv)


def attend_back_kernel(
    query_ref,
    key_ref,
    value_ref,
    grad_ref,
    logsum_ref,
    turn_ref,
    upper_ref,
    lower_ref,
    out_ref,
    key_total,
    value_total,
):
    pair = pl.program_id(0)
    first, second = lane_masks()
    lane = lax.broadcasted_iota(jnp.int32, (QBLOCK, PAIR), 1)
    key_total[...] = jnp.zeros_like(key_total)
    value_total[...] = jnp.zeros_like(value_total)

    def store(part, low, reach, values):
        start = pl.multiple_of((part * (CHIP_COLS // PAIR) + pair) * PAIR, PAIR)
        out_ref[low:reach, pl.ds(start, PAIR)] = values.astype(BF16)

    def unturn(values, low, reach):
        kept = values.astype(BF16).astype(F32)
        return turn_columns(
            kept, turn_ref[low:reach, :], upper_ref[low:reach, :], lower_ref[low:reach, :], -1.0
        )

    for low in range(0, LENGTH, QBLOCK):
        reach = low + QBLOCK
        query = query_ref[low:reach, :]
        grad = grad_ref[low:reach, :]
        keys = key_ref[:reach, :]
        values = value_ref[:reach, :]
        query_grads = []
        key_part = 0.0
        value_part = 0.0
        for head, mask in enumerate((first, second)):
            own_query = query * mask
            own_grad = grad * mask
            scores = scores_of(own_query, keys, low)
            start = head * HEAD_DIM
            probs = jnp.exp(scores - logsum_ref[low:reach, start : start + 1])
            prob_grad = dot(own_grad, values, NT)
            inner = jnp.sum(probs * prob_grad, axis=1, keepdims=True)
            score_grad = (probs * (prob_grad - inner)).astype(BF16)
            query_grads.append(dot(score_grad, keys))
            key_part += dot(score_grad, own_query, TN)
            value_part += dot(probs.astype(BF16), own_grad, TN)
        key_total[:reach, :] += key_part
        value_total[:reach, :] += value_part
        query_grad = jnp.where(lane < HEAD_DIM, query_grads[0], query_grads[1]) * SCALE
        store(0, low, reach, unturn(query_grad, low, reach))
    store(1, 0, LENGTH, unturn(key_total[...] * SCALE, 0, LENGTH))
    store(2, 0, LENGTH, value_total[...])


def attend_backward(qkv, grad, logsum, tables):
    pairs = CHIP_COLS // PAIR
    column = lambda part: pl.BlockSpec((LENGTH, PAIR), lambda p: (0, part * pairs + p))
    whole = lambda shape: pl.BlockSpec(shape, lambda p: (0, 0))
    width = 3 * CHIP_COLS
    return pl.pallas_call(
        attend_back_kernel,
        grid=(pairs,),
        in_specs=[column(0), column(1), column(2), column(0), column(0)]
        + [whole(t.shape) for t in tables],
        out_specs=whole((LENGTH, width)),
        out_shape=jax.ShapeDtypeStruct((LENGTH, width), BF16),
        scratch_shapes=[pltpu.VMEM((LENGTH, PAIR), F32), pltpu.VMEM((LENGTH, PAIR), F32)],
        compiler_params=pltpu.CompilerParams(vmem_limit_bytes=40 * 2**20),
        cost_estimate=pl.CostEstimate(
            flops=20 * 2**30, bytes_accessed=6 * 2**20, transcendentals=4 * 2**20
        ),
        name="attend_backward",
    )(qkv, qkv, qkv, grad, logsum, *tables)


def exchange(blocks, axes):
    return lax.all_to_all(blocks, axes, split_axis=0, concat_axis=0, tiled=True)


def spread(block, axes, count):
    return exchange(jnp.broadcast_to(block[None], (count,) + block.shape), axes)


def after(value, *earlier):
    return lax.optimization_barrier((value,) + earlier)[0]


def half_sum(parts, axis, index):
    stay = lax.dynamic_index_in_dim(parts, index, 1, keepdims=False)
    leave = lax.dynamic_index_in_dim(parts, 1 - index, 1, keepdims=False)
    sent = swap(jnp.sum(leave.astype(F32), axis=0).astype(BF16), axis)
    return jnp.sum(stay.astype(F32), axis=0), sent


def per_device(
    inputs,
    gains,
    shifts,
    attend,
    attend_bias,
    mixer,
    mixer_bias,
    upward,
    upward_bias,
    downward,
    downward_bias,
    cotangent,
):
    core = lax.axis_index("c")
    x_hi = lax.axis_index("xh")
    x_lo = lax.axis_index("xl")
    chip = x_hi * 4 + lax.axis_index("z")
    seq_index = lax.axis_index("y") * 2 + x_lo
    core_at = core.reshape(1)
    rows_in = inputs.reshape(ROWS, WIDTH)
    own_cot = cotangent.reshape(ROWS, WIDTH)
    width = 3 * CHIP_COLS

    slots = ("z", "xh")
    rows_group = spread(rows_in, slots, CHIPS).reshape(TOKENS, WIDTH)

    slab_index = seq_index * SLAB
    slab = lax.dynamic_slice_in_dim(attend, slab_index, SLAB, 0)
    slab = slab.reshape(SLAB, 3, CHIPS, CHIP_COLS).transpose(2, 0, 1, 3).reshape(CHIPS, SLAB, width)
    slab = exchange(slab, GROUP)
    attend_own = spread(slab, SEQ, SEQ_DEVICES).reshape(SEQ_DEVICES, CHIPS, SLAB, width)
    attend_chip = assemble_attend(core_at, attend_own, swap(attend_own, "c"))

    small = jnp.concatenate([gains, shifts, mixer_bias, downward_bias, attend_bias]).reshape(1, 896)
    small_all = spread(small, FSDP, FSDP_DEVICES).reshape(FSDP_DEVICES, 7, 128).astype(F32)
    gain_all = small_all[:, 0].reshape(1, WIDTH)
    shift_all = small_all[:, 1].reshape(1, WIDTH)
    out_bias = (small_all[:, 2] + small_all[:, 3]).reshape(WIDTH)
    bias_grid = small_all[:, 4:7].reshape(3, CHIPS, CHIP_COLS)
    attend_bias_chip = lax.dynamic_slice_in_dim(bias_grid, chip, 1, 1).reshape(1, width)

    mixer_other = swap(mixer, "c")
    mixer_chip = jnp.where(
        core == 0, jnp.concatenate([mixer, mixer_other]), jnp.concatenate([mixer_other, mixer])
    )
    up_other = swap(upward, "c")
    down_other = swap(downward, "c")
    up_bias_own = upward_bias.astype(F32).reshape(1, CORE_FF)
    up_bias_other = swap(upward_bias.reshape(1, CORE_FF), "c").astype(F32)

    own_positions = seq_index * ROWS + jnp.arange(ROWS, dtype=jnp.int32)
    own_tables = rope_tables(own_positions, 2 * CHIP_COLS // HEAD_DIM)
    all_tables = rope_tables(jnp.arange(LENGTH, dtype=jnp.int32), 2)

    own_cot_late = after(own_cot, rows_group)
    cot_group = spread(own_cot_late, slots, CHIPS).reshape(TOKENS, WIDTH)
    normed, qkv_sent = norm_project(
        rows_group, gain_all, shift_all, attend_chip, attend_bias_chip, own_tables
    )
    qkv = exchange(qkv_sent.reshape(CHIPS, ROWS, width), SEQ).reshape(LENGTH, width)
    act_own, act_other, slope_own, slope_other = hidden_forward(
        normed, upward, up_other, up_bias_own, up_bias_other
    )

    attended, logsum = attend_forward(qkv)
    attended_group = exchange(attended.reshape(SEQ_DEVICES, ROWS, CHIP_COLS), SEQ).reshape(
        TOKENS, CHIP_COLS
    )
    attended_grad = grad_heads(cot_group, mixer_chip)
    grads = exchange(attended_grad.reshape(CHIPS, ROWS, CHIP_COLS), SEQ).reshape(LENGTH, CHIP_COLS)

    parts = out_part(act_own, act_other, attended_group, downward, down_other, mixer_chip)
    parts = exchange(parts.reshape(4, 2, ROWS, WIDTH), "z")
    near, far = half_sum(parts, "xh", x_hi)
    outputs = (rows_in.astype(F32) + out_bias + near + far.astype(F32)).astype(BF16)

    grad_own, grad_other, up_bias_sum, up_bias_other_sum = hidden_back(
        cot_group, downward, down_other, slope_own, slope_other
    )
    att_own = lax.dynamic_slice_in_dim(attended_group, core * CORE_COLS, CORE_COLS, 1)
    att_other = lax.dynamic_slice_in_dim(attended_group, (1 - core) * CORE_COLS, CORE_COLS, 1)
    weight_grad = lambda lhs, rhs: dot(lhs, rhs, TN).astype(BF16)
    packed = pack(
        weight_grad(normed, grad_own),
        swap(weight_grad(normed, grad_other), "c"),
        weight_grad(act_own, cot_group),
        swap(weight_grad(act_other, cot_group), "c"),
        weight_grad(att_own, cot_group),
        swap(weight_grad(att_other, cot_group), "c"),
    )
    packed = exchange(packed.reshape(4, 2, PACK_ROWS, PACK_COLS), "y")
    near, far = half_sum(packed, "xl", x_lo)
    packed = (near + far.astype(F32)).astype(BF16)
    packed = lax.all_gather(packed, SEQ, axis=0, tiled=False)
    up_grad, down_grad, mixer_grad = unpack(packed)

    projected_grad = exchange(
        attend_backward(qkv, grads, logsum, all_tables).reshape(SEQ_DEVICES, ROWS, width), SEQ
    ).reshape(TOKENS, width)

    parts, norm_sums, attend_bias_sum = normed_part(
        projected_grad, grad_own, grad_other, rows_group, attend_chip, upward, up_other
    )
    parts = exchange(parts.reshape(4, 2, ROWS, WIDTH), "z")
    near, far = half_sum(parts, "xh", x_hi)
    inputs_grad = rows_grad(rows_in, own_cot, near, far, gain_all)

    attend_part = weight_grad(normed, projected_grad).reshape(CHIPS, 2, CORE_COLS, width)
    attend_keep = lax.dynamic_index_in_dim(attend_part, core, 1, keepdims=False)
    attend_send = lax.dynamic_index_in_dim(attend_part, 1 - core, 1, keepdims=False)
    attend_sum = pack_attend(
        attend_keep.reshape(CHIPS * CORE_COLS, width),
        swap(attend_send.reshape(CHIPS * CORE_COLS, width), "c"),
    )
    attend_sum = exchange(attend_sum.reshape(4, 2, CHIPS, SLAB, width), "y")
    near, far = half_sum(attend_sum, "xl", x_lo)
    attend_slab = exchange((near + far.astype(F32)).astype(BF16), GROUP)
    attend_grad = unpack_attend(spread(attend_slab, SEQ, SEQ_DEVICES).reshape(
        SEQ_DEVICES, CHIPS, SLAB, width
    ))

    bias_full = jnp.sum(own_cot.astype(F32), axis=0)
    attend_bias_full = lax.dynamic_update_slice(
        jnp.zeros((3, CHIPS, CHIP_COLS), F32), attend_bias_sum.reshape(3, 1, CHIP_COLS), (0, chip, 0)
    )
    up_bias_pair = jnp.where(
        core == 0,
        jnp.concatenate([up_bias_sum, up_bias_other_sum]),
        jnp.concatenate([up_bias_other_sum, up_bias_sum]),
    )
    up_bias_full = lax.dynamic_update_slice(
        jnp.zeros((CHIPS, 2, CORE_FF), F32), up_bias_pair[None], (chip, 0, 0)
    )
    vectors = jnp.concatenate(
        [
            v.reshape(FSDP_DEVICES, -1)
            for v in (norm_sums[0], norm_sums[1], bias_full, attend_bias_full, up_bias_full)
        ],
        axis=1,
    )
    vectors = jnp.sum(exchange(vectors, FSDP), axis=0)
    vectors = jnp.sum(spread(vectors, SEQ, SEQ_DEVICES), axis=0)
    gain_grad, shift_grad, bias_grad = vectors[:128], vectors[128:256], vectors[256:384]
    attend_bias_grad, up_bias_grad = vectors[384:768], vectors[768:]

    return (
        outputs.reshape(inputs.shape),
        inputs_grad.reshape(inputs.shape),
        gain_grad,
        shift_grad,
        attend_grad,
        attend_bias_grad,
        mixer_grad,
        bias_grad,
        up_grad,
        up_bias_grad,
        down_grad,
        bias_grad,
    )


def solution(mesh):
    fine = Mesh(mesh.devices.reshape(4, 2, 2, 4, 2), ("y", "xl", "xh", "z", "c"))
    rows = P(FSDP, SEQ, None)
    vector = P(FSDP)
    by_row = P(FSDP, None)
    by_col = P(None, FSDP)
    in_specs = (
        rows,
        vector,
        vector,
        by_row,
        vector,
        by_row,
        vector,
        by_col,
        vector,
        by_row,
        vector,
        rows,
    )
    out_specs = (
        rows,
        rows,
        vector,
        vector,
        by_row,
        vector,
        by_row,
        vector,
        by_col,
        vector,
        by_row,
        vector,
    )
    return jax.shard_map(
        per_device, mesh=fine, in_specs=in_specs, out_specs=out_specs, check_vma=False
    )
```

```python
import jax
import jax.numpy as jnp
from jax import lax
from jax.experimental import pallas as pl
from jax.experimental.pallas import tpu as pltpu
from jax.sharding import Mesh, PartitionSpec as P

HEADS = 32
HEAD_DIM = 64
ROT = 32
WIDTH = 2048
FF = 8192
SEQ_DEVICES = 8
CHIPS = 8
FSDP_DEVICES = 16
ROWS = 128
LENGTH = ROWS * SEQ_DEVICES
TOKENS = ROWS * CHIPS
CHIP_COLS = WIDTH // CHIPS
CORE_COLS = WIDTH // FSDP_DEVICES
CORE_FF = FF // FSDP_DEVICES
PAIR = 2 * HEAD_DIM
QBLOCK = 256

EPSILON = 1e-05
ROPE_BASE = 10000.0
NEG_FILL = -1e30
SCALE = HEAD_DIM ** (-0.5)

F32 = jnp.float32
BF16 = jnp.bfloat16

SEQ = ("y", "xl")
GROUP = ("xh", "z")
FSDP = ("xh", "z", "c")

NT = (((1,), (1,)), ((), ()))
TN = (((0,), (0,)), ((), ()))
NN = (((1,), (0,)), ((), ()))


def dot(lhs, rhs, dims=NN):
    return lax.dot_general(lhs, rhs, dims, preferred_element_type=F32)


def swap(piece, axis):
    return lax.ppermute(piece, axis, [(0, 1), (1, 0)])


def shift(piece, axis, step):
    return lax.ppermute(piece, axis, [(i, (i - step) % 4) for i in range(4)])


def send(piece, axis, step):
    return lax.ppermute(piece, axis, [(i, (i + step) % 4) for i in range(4)])


def rope_tables(positions, heads):
    half = ROT // 2
    frequency = ROPE_BASE ** (-2.0 * jnp.arange(half, dtype=F32) / ROT)
    angle = positions.astype(F32)[:, None] * frequency[None, :]
    cosine, sine = jnp.cos(angle), jnp.sin(angle)
    rest = jnp.zeros((positions.shape[0], HEAD_DIM - ROT), F32)
    blank = jnp.zeros_like(sine)
    turn = jnp.concatenate([cosine, cosine, rest + 1.0], axis=1)
    upper = jnp.concatenate([-sine, blank, rest], axis=1)
    lower = jnp.concatenate([blank, sine, rest], axis=1)
    return tuple(jnp.tile(t, (1, heads)) for t in (turn, upper, lower))


def turn_columns(values, turn, upper, lower, sign):
    width = values.shape[1]
    half = ROT // 2
    ahead = pltpu.roll(values, width - half, 1)
    behind = pltpu.roll(values, half, 1)
    return values * turn + sign * (ahead * upper + behind * lower)


def whole(shape):
    return pl.BlockSpec(shape, lambda i: (0,) * len(shape))


def row_block(rows, width, column=0):
    return pl.BlockSpec((rows, width), lambda i: (i, column))


def call(kernel, name, grid, in_specs, out_specs, out_shape, flops, moved, operands):
    return pl.pallas_call(
        kernel,
        grid=(grid,),
        in_specs=in_specs,
        out_specs=out_specs,
        out_shape=out_shape,
        compiler_params=pltpu.CompilerParams(vmem_limit_bytes=48 * 2**20),
        cost_estimate=pl.CostEstimate(flops=flops, bytes_accessed=moved, transcendentals=0),
        name=name,
    )(*operands)


def placed_call(kernel, name, grid, in_specs, out_specs, out_shape, scratch, flops, moved, order, operands):
    return pl.pallas_call(
        kernel,
        grid_spec=pltpu.PrefetchScalarGridSpec(
            num_scalar_prefetch=1,
            grid=(grid,),
            in_specs=in_specs,
            out_specs=out_specs,
            scratch_shapes=scratch,
        ),
        out_shape=out_shape,
        compiler_params=pltpu.CompilerParams(vmem_limit_bytes=48 * 2**20),
        cost_estimate=pl.CostEstimate(flops=flops, bytes_accessed=moved, transcendentals=0),
        name=name,
    )(order, *operands)


def fixed(dims):
    return pl.BlockSpec(dims, lambda i, order: (0,) * len(dims))


def shape(dims, kind=BF16):
    return jax.ShapeDtypeStruct(dims, kind)


def layer_stats(rows):
    center = rows - jnp.mean(rows, axis=-1, keepdims=True)
    spread_out = jnp.mean(center * center, axis=-1, keepdims=True)
    return center, lax.rsqrt(spread_out + EPSILON)


def assemble_kernel(core_ref, own_ref, other_ref, out_ref):
    core = core_ref[0]
    out_ref[0, core] = own_ref[...].reshape(out_ref.shape[2:])
    out_ref[0, 1 - core] = other_ref[...].reshape(out_ref.shape[2:])


def assemble_attend(core, own, other):
    slab, cols = own.shape[2:]
    piece = pl.BlockSpec((SEQ_DEVICES, 1, slab, cols), lambda g, core: (0, g, 0, 0))
    out = (CHIPS, 2, SEQ_DEVICES, slab, cols)
    return pl.pallas_call(
        assemble_kernel,
        grid_spec=pltpu.PrefetchScalarGridSpec(
            num_scalar_prefetch=1,
            grid=(CHIPS,),
            in_specs=[piece, piece],
            out_specs=pl.BlockSpec((1,) + out[1:], lambda g, core: (g, 0, 0, 0, 0)),
        ),
        out_shape=shape(out),
        compiler_params=pltpu.CompilerParams(vmem_limit_bytes=24 * 2**20),
        cost_estimate=pl.CostEstimate(flops=0, bytes_accessed=6 * 2**20, transcendentals=0),
        name="assemble_attend",
    )(core, own, other).reshape(WIDTH, cols)


def norm_project_kernel(
    order_ref,
    near_0,
    near_1,
    near_2,
    near_3,
    far_0,
    far_1,
    far_2,
    far_3,
    gain_ref,
    shift_ref,
    weight_ref,
    bias_ref,
    turn_ref,
    upper_ref,
    lower_ref,
    rows_ref,
    normed_ref,
    out_ref,
):
    step = pl.program_id(0)
    pairs = ((near_0, far_0), (near_1, far_1), (near_2, far_2), (near_3, far_3))
    for index, (near, far) in enumerate(pairs):

        @pl.when(step == index)
        def _():
            rows_ref[:ROWS] = near[...]
            rows_ref[ROWS:] = far[...]

    center, inverse = layer_stats(rows_ref[...].astype(F32))
    normed = (center * inverse * gain_ref[...] + shift_ref[...]).astype(BF16)
    normed_ref[...] = normed
    projected = dot(normed, weight_ref[...]) + bias_ref[...]
    turned_width = 2 * CHIP_COLS
    for block in range(2):
        rows = slice(block * ROWS, (block + 1) * ROWS)
        out_ref[rows, :turned_width] = turn_columns(
            projected[rows, :turned_width], turn_ref[...], upper_ref[...], lower_ref[...], 1.0
        ).astype(BF16)
    out_ref[:, turned_width:] = projected[:, turned_width:].astype(BF16)


def norm_project(order, pieces, gain, shift_row, weight, bias, tables):
    block = 2 * ROWS
    width = weight.shape[1]
    vectors = (gain, shift_row, weight, bias) + tables
    out = lambda cols: pl.BlockSpec((block, cols), lambda i, order: (order[i], 0))
    return placed_call(
        norm_project_kernel,
        "norm_project",
        4,
        [fixed((ROWS, WIDTH))] * 8 + [fixed(v.shape) for v in vectors],
        [out(WIDTH), out(WIDTH), out(width)],
        [shape((TOKENS, WIDTH)), shape((TOKENS, WIDTH)), shape((TOKENS, width))],
        [],
        2 * TOKENS * WIDTH * width,
        18 * 2**20,
        order,
        tuple(pieces) + vectors,
    )


def hidden_kernel(
    normed_ref,
    own_ref,
    other_ref,
    own_bias_ref,
    other_bias_ref,
    own_act_ref,
    other_act_ref,
    own_slope_ref,
    other_slope_ref,
):
    root = (2.0 / 3.141592653589793) ** 0.5
    for weight, bias, act, slope in (
        (own_ref, own_bias_ref, own_act_ref, own_slope_ref),
        (other_ref, other_bias_ref, other_act_ref, other_slope_ref),
    ):
        hidden = dot(normed_ref[...], weight[...]) + bias[...]
        square = hidden * hidden
        bend = jnp.tanh(root * hidden * (1.0 + 0.044715 * square))
        half = 0.5 * (1.0 + bend)
        act[...] = (hidden * half).astype(BF16)
        slope[...] = half + 0.5 * hidden * (1.0 - bend * bend) * (
            root * (1.0 + 3.0 * 0.044715 * square)
        )


def hidden_forward(normed, own, other, own_bias, other_bias):
    block = 256
    operands = (own, other, own_bias, other_bias)
    return call(
        hidden_kernel,
        "hidden_forward",
        TOKENS // block,
        [row_block(block, WIDTH)] + [whole(v.shape) for v in operands],
        [row_block(block, CORE_FF)] * 4,
        [shape((TOKENS, CORE_FF))] * 2 + [shape((TOKENS, CORE_FF), F32)] * 2,
        4 * TOKENS * WIDTH * CORE_FF,
        14 * 2**20,
        (normed,) + operands,
    )


def grad_heads_kernel(cot_ref, mixer_ref, out_ref):
    out_ref[...] = dot(cot_ref[...], mixer_ref[...], NT).astype(BF16)


def grad_heads(cot, mixer):
    block = 256
    return call(
        grad_heads_kernel,
        "grad_heads",
        TOKENS // block,
        [row_block(block, WIDTH), whole(mixer.shape)],
        row_block(block, CHIP_COLS),
        shape((TOKENS, CHIP_COLS)),
        2 * TOKENS * WIDTH * CHIP_COLS,
        6 * 2**20,
        (cot, mixer),
    )


def hidden_back_kernel(
    cot_ref, own_ref, other_ref, own_slope_ref, other_slope_ref, own_out, other_out, own_sum, other_sum
):
    for weight, slope, out, total in (
        (own_ref, own_slope_ref, own_out, own_sum),
        (other_ref, other_slope_ref, other_out, other_sum),
    ):
        grad = (dot(cot_ref[...], weight[...], NT) * slope[...]).astype(BF16)
        out[...] = grad
        part = jnp.sum(grad.astype(F32), axis=0, keepdims=True)

        @pl.when(pl.program_id(0) == 0)
        def _():
            total[...] = part

        @pl.when(pl.program_id(0) > 0)
        def _():
            total[...] += part


def hidden_back(cot, own, other, own_slope, other_slope):
    block = 256
    return call(
        hidden_back_kernel,
        "hidden_back",
        TOKENS // block,
        [row_block(block, WIDTH), whole(own.shape), whole(other.shape)]
        + [row_block(block, CORE_FF)] * 2,
        [row_block(block, CORE_FF)] * 2 + [whole((1, CORE_FF))] * 2,
        [shape((TOKENS, CORE_FF))] * 2 + [shape((1, CORE_FF), F32)] * 2,
        4 * TOKENS * WIDTH * CORE_FF,
        14 * 2**20,
        (cot, own, other, own_slope, other_slope),
    )


def out_part_kernel(own_act, other_act, attended, own_ref, other_ref, mixer_ref, out_ref):
    out_ref[...] = (
        dot(own_act[...], own_ref[...])
        + dot(other_act[...], other_ref[...])
        + dot(attended[...], mixer_ref[...])
    ).astype(BF16)


def out_part(own_act, other_act, attended, own, other, mixer):
    block = 256
    weights = (own, other, mixer)
    return call(
        out_part_kernel,
        "out_part",
        TOKENS // block,
        [row_block(block, CORE_FF)] * 2
        + [row_block(block, CHIP_COLS)]
        + [whole(w.shape) for w in weights],
        row_block(block, WIDTH),
        shape((TOKENS, WIDTH)),
        2 * TOKENS * WIDTH * (2 * CORE_FF + CHIP_COLS),
        12 * 2**20,
        (own_act, other_act, attended) + weights,
    )


def normed_part_kernel(
    projected, own_grad, other_grad, rows_ref, attend_ref, own_ref, other_ref, out_ref, sums_ref, bias_ref
):
    total = (
        dot(projected[...], attend_ref[...], NT)
        + dot(own_grad[...], own_ref[...], NT)
        + dot(other_grad[...], other_ref[...], NT)
    )
    out_ref[...] = total.astype(BF16)
    center, inverse = layer_stats(rows_ref[...].astype(F32))
    gain_part = jnp.sum(total * (center * inverse), axis=0, keepdims=True)
    shift_part = jnp.sum(total, axis=0, keepdims=True)
    bias_part = jnp.sum(projected[...].astype(F32), axis=0, keepdims=True)

    @pl.when(pl.program_id(0) == 0)
    def _():
        sums_ref[0:1] = gain_part
        sums_ref[1:2] = shift_part
        bias_ref[...] = bias_part

    @pl.when(pl.program_id(0) > 0)
    def _():
        sums_ref[0:1] += gain_part
        sums_ref[1:2] += shift_part
        bias_ref[...] += bias_part


def normed_part(projected, own_grad, other_grad, rows, attend, own, other):
    block = 256
    width = projected.shape[1]
    weights = (attend, own, other)
    return call(
        normed_part_kernel,
        "normed_part",
        TOKENS // block,
        [row_block(block, width)]
        + [row_block(block, CORE_FF)] * 2
        + [row_block(block, WIDTH)]
        + [whole(w.shape) for w in weights],
        [row_block(block, WIDTH), whole((2, WIDTH)), whole((1, width))],
        [shape((TOKENS, WIDTH)), shape((2, WIDTH), F32), shape((1, width), F32)],
        2 * TOKENS * WIDTH * (2 * CORE_FF + width),
        18 * 2**20,
        (projected, own_grad, other_grad, rows) + weights,
    )


UP_ROWS = WIDTH // SEQ_DEVICES
DOWN_ROWS = CORE_FF // 2
MIX_ROWS = CORE_COLS // 2
PACK_ROWS = UP_ROWS + DOWN_ROWS + MIX_ROWS
PACK_COLS = CORE_FF


def pack_kernel(order_ref, up_own, up_other, down_own, down_other, mix_own, mix_other, *outs):
    half = PACK_COLS // 2
    up = (up_own[...].astype(F32) + up_other[...].astype(F32)).astype(BF16)
    down = (down_own[...].astype(F32) + down_other[...].astype(F32)).astype(BF16)
    mix = (mix_own[...].astype(F32) + mix_other[...].astype(F32)).astype(BF16)
    start, stop = UP_ROWS, UP_ROWS + DOWN_ROWS
    step = pl.program_id(0)
    for index, out_ref in enumerate(outs):

        @pl.when(step // 2 == index)
        def _():
            out_ref[0, :UP_ROWS] = up
            out_ref[0, start:stop, :half] = down[:DOWN_ROWS]
            out_ref[0, start:stop, half:] = down[DOWN_ROWS:]
            out_ref[0, stop:, :half] = mix[:MIX_ROWS]
            out_ref[0, stop:, half:] = mix[MIX_ROWS:]


def pack(order, up_own, up_other, down_own, down_other, mix_own, mix_other):
    cols = WIDTH // SEQ_DEVICES
    up = pl.BlockSpec((UP_ROWS, CORE_FF), lambda i, order: (order[i], 0))
    down = pl.BlockSpec((CORE_FF, cols), lambda i, order: (0, order[i]))
    mix = pl.BlockSpec((CORE_COLS, cols), lambda i, order: (0, order[i]))

    def out(k):
        return pl.BlockSpec(
            (1, PACK_ROWS, PACK_COLS), lambda i, order: (jnp.clip(i - 2 * k, 0, 1), 0, 0)
        )

    return placed_call(
        pack_kernel,
        "pack",
        SEQ_DEVICES,
        [up, up, down, down, mix, mix],
        [out(k) for k in range(4)],
        [shape((2, PACK_ROWS, PACK_COLS))] * 4,
        [],
        0,
        15 * 2**20,
        order,
        (up_own, up_other, down_own, down_other, mix_own, mix_other),
    )


def unpack_kernel(order_ref, *refs):
    pieces, (up_ref, down_ref, mix_ref) = refs[:8], refs[8:]
    half = PACK_COLS // 2
    start, stop = UP_ROWS, UP_ROWS + DOWN_ROWS
    step = pl.program_id(0)
    for index, piece in enumerate(pieces):

        @pl.when(step == index)
        def _():
            up_ref[...] = piece[:start].astype(F32)
            down_ref[:DOWN_ROWS] = piece[start:stop, :half].astype(F32)
            down_ref[DOWN_ROWS:] = piece[start:stop, half:].astype(F32)
            mix_ref[:MIX_ROWS] = piece[stop:, :half].astype(F32)
            mix_ref[MIX_ROWS:] = piece[stop:, half:].astype(F32)


def unpack(order, pieces):
    cols = WIDTH // SEQ_DEVICES
    return placed_call(
        unpack_kernel,
        "unpack",
        SEQ_DEVICES,
        [fixed((PACK_ROWS, PACK_COLS))] * 8,
        [
            pl.BlockSpec((UP_ROWS, CORE_FF), lambda i, order: (order[i], 0)),
            pl.BlockSpec((CORE_FF, cols), lambda i, order: (0, order[i])),
            pl.BlockSpec((CORE_COLS, cols), lambda i, order: (0, order[i])),
        ],
        [shape((WIDTH, CORE_FF), F32), shape((CORE_FF, WIDTH), F32), shape((CORE_COLS, WIDTH), F32)],
        [],
        0,
        14 * 2**20,
        order,
        tuple(pieces),
    )


SLAB = CORE_COLS // SEQ_DEVICES


def pack_attend_kernel(order_ref, own_ref, other_ref, *outs):
    for slot in range(SEQ_DEVICES):
        rows = pl.ds(pl.multiple_of(order_ref[slot] * SLAB, SLAB), SLAB)
        total = own_ref[rows, :].astype(F32) + other_ref[rows, :].astype(F32)
        outs[slot // 2][slot % 2, 0] = total.astype(BF16)


def pack_attend(order, own, other):
    cols = own.shape[1]
    block = pl.BlockSpec((CORE_COLS, cols), lambda i, order: (i, 0))
    return placed_call(
        pack_attend_kernel,
        "pack_attend",
        CHIPS,
        [block] * 2,
        [pl.BlockSpec((2, 1, SLAB, cols), lambda i, order: (0, i, 0, 0))] * 4,
        [shape((2, CHIPS, SLAB, cols))] * 4,
        [],
        0,
        5 * 2**20,
        order,
        (own, other),
    )


def unpack_attend_kernel(packed_ref, out_ref):
    for chip in range(CHIPS):
        for part in range(3):
            out_ref[:, part * WIDTH + chip * CHIP_COLS : part * WIDTH + (chip + 1) * CHIP_COLS] = (
                packed_ref[0, chip, :, part * CHIP_COLS : (part + 1) * CHIP_COLS].astype(F32)
            )


def unpack_attend(packed):
    return call(
        unpack_attend_kernel,
        "unpack_attend",
        SEQ_DEVICES,
        [pl.BlockSpec((1,) + packed.shape[1:], lambda i: (i, 0, 0, 0))],
        row_block(SLAB, 3 * WIDTH),
        shape((CORE_COLS, 3 * WIDTH), F32),
        0,
        5 * 2**20,
        (packed,),
    )


def rows_grad_kernel(rows_ref, cot_ref, near_ref, far_ref, gain_ref, out_ref):
    grad = near_ref[...].astype(F32) + far_ref[...].astype(F32)
    center, inverse = layer_stats(rows_ref[...].astype(F32))
    unit = center * inverse
    scaled = grad * gain_ref[...]
    out_ref[...] = cot_ref[...].astype(F32) + inverse * (
        scaled
        - jnp.mean(scaled, axis=-1, keepdims=True)
        - unit * jnp.mean(scaled * unit, axis=-1, keepdims=True)
    )


def rows_grad(rows, cot, near, far, gain):
    block = 64
    return call(
        rows_grad_kernel,
        "rows_grad",
        ROWS // block,
        [row_block(block, WIDTH)] * 4 + [whole(gain.shape)],
        row_block(block, WIDTH),
        shape((ROWS, WIDTH), F32),
        0,
        4 * 2**20,
        (rows, cot, near, far, gain),
    )


def lane_masks():
    lane = lax.broadcasted_iota(jnp.int32, (1, PAIR), 1)
    first = (lane < HEAD_DIM).astype(BF16)
    return first, 1 - first


def scores_of(query, keys, low):
    scores = dot(query, keys, NT) * SCALE
    row = low + lax.broadcasted_iota(jnp.int32, scores.shape, 0)
    col = lax.broadcasted_iota(jnp.int32, scores.shape, 1)
    return jnp.where(col <= row, scores, NEG_FILL)


def attend_kernel(query_ref, key_ref, value_ref, out_ref, logsum_ref):
    first, second = lane_masks()
    lane = lax.broadcasted_iota(jnp.int32, (QBLOCK, PAIR), 1)
    for low in range(0, LENGTH, QBLOCK):
        reach = low + QBLOCK
        query = query_ref[low:reach, :]
        keys = key_ref[:reach, :]
        values = value_ref[:reach, :]
        found = []
        for mask in (first, second):
            scores = scores_of(query * mask, keys, low)
            peak = jnp.max(scores, axis=1, keepdims=True)
            weight = jnp.exp(scores - peak)
            total = jnp.sum(weight, axis=1, keepdims=True)
            prob_low = (weight * (1.0 / total)).astype(BF16)
            found.append((dot(prob_low, values), peak + jnp.log(total)))
        out_ref[low:reach, :] = jnp.where(lane < HEAD_DIM, found[0][0], found[1][0]).astype(BF16)
        logsum_ref[low:reach, :] = jnp.where(lane < HEAD_DIM, found[0][1], found[1][1])


def attend_forward(qkv):
    pairs = CHIP_COLS // PAIR
    column = lambda part: pl.BlockSpec((LENGTH, PAIR), lambda p: (0, part * pairs + p))
    return pl.pallas_call(
        attend_kernel,
        grid=(pairs,),
        in_specs=[column(0), column(1), column(2)],
        out_specs=[column(0), column(0)],
        out_shape=[
            jax.ShapeDtypeStruct((LENGTH, CHIP_COLS), BF16),
            jax.ShapeDtypeStruct((LENGTH, CHIP_COLS), F32),
        ],
        compiler_params=pltpu.CompilerParams(vmem_limit_bytes=40 * 2**20),
        cost_estimate=pl.CostEstimate(
            flops=8 * 2**30, bytes_accessed=4 * 2**20, transcendentals=4 * 2**20
        ),
        name="attend_forward",
    )(qkv, qkv, qkv)


def attend_back_kernel(
    query_ref,
    key_ref,
    value_ref,
    grad_ref,
    logsum_ref,
    turn_ref,
    upper_ref,
    lower_ref,
    out_ref,
    key_total,
    value_total,
):
    pair = pl.program_id(0)
    first, second = lane_masks()
    lane = lax.broadcasted_iota(jnp.int32, (QBLOCK, PAIR), 1)
    key_total[...] = jnp.zeros_like(key_total)
    value_total[...] = jnp.zeros_like(value_total)

    def store(part, low, reach, values):
        start = pl.multiple_of((part * (CHIP_COLS // PAIR) + pair) * PAIR, PAIR)
        out_ref[low:reach, pl.ds(start, PAIR)] = values.astype(BF16)

    def unturn(values, low, reach):
        kept = values.astype(BF16).astype(F32)
        return turn_columns(
            kept, turn_ref[low:reach, :], upper_ref[low:reach, :], lower_ref[low:reach, :], -1.0
        )

    for low in range(0, LENGTH, QBLOCK):
        reach = low + QBLOCK
        query = query_ref[low:reach, :]
        grad = grad_ref[low:reach, :]
        keys = key_ref[:reach, :]
        values = value_ref[:reach, :]
        query_grads = []
        key_part = 0.0
        value_part = 0.0
        for head, mask in enumerate((first, second)):
            own_query = query * mask
            own_grad = grad * mask
            scores = scores_of(own_query, keys, low)
            start = head * HEAD_DIM
            probs = jnp.exp(scores - logsum_ref[low:reach, start : start + 1])
            prob_grad = dot(own_grad, values, NT)
            inner = jnp.sum(probs * prob_grad, axis=1, keepdims=True)
            score_grad = (probs * (prob_grad - inner)).astype(BF16)
            query_grads.append(dot(score_grad, keys))
            key_part += dot(score_grad, own_query, TN)
            value_part += dot(probs.astype(BF16), own_grad, TN)
        key_total[:reach, :] += key_part
        value_total[:reach, :] += value_part
        query_grad = jnp.where(lane < HEAD_DIM, query_grads[0], query_grads[1]) * SCALE
        store(0, low, reach, unturn(query_grad, low, reach))
    store(1, 0, LENGTH, unturn(key_total[...] * SCALE, 0, LENGTH))
    store(2, 0, LENGTH, value_total[...])


def attend_backward(qkv, grad, logsum, tables):
    pairs = CHIP_COLS // PAIR
    column = lambda part: pl.BlockSpec((LENGTH, PAIR), lambda p: (0, part * pairs + p))
    whole = lambda shape: pl.BlockSpec(shape, lambda p: (0, 0))
    width = 3 * CHIP_COLS
    return pl.pallas_call(
        attend_back_kernel,
        grid=(pairs,),
        in_specs=[column(0), column(1), column(2), column(0), column(0)]
        + [whole(t.shape) for t in tables],
        out_specs=whole((LENGTH, width)),
        out_shape=jax.ShapeDtypeStruct((LENGTH, width), BF16),
        scratch_shapes=[pltpu.VMEM((LENGTH, PAIR), F32), pltpu.VMEM((LENGTH, PAIR), F32)],
        compiler_params=pltpu.CompilerParams(vmem_limit_bytes=40 * 2**20),
        cost_estimate=pl.CostEstimate(
            flops=20 * 2**30, bytes_accessed=6 * 2**20, transcendentals=4 * 2**20
        ),
        name="attend_backward",
    )(qkv, qkv, qkv, grad, logsum, *tables)


def exchange(blocks, axes):
    return lax.all_to_all(blocks, axes, split_axis=0, concat_axis=0, tiled=True)


def spread(block, axes, count):
    return exchange(jnp.broadcast_to(block[None], (count,) + block.shape), axes)


def after(value, *earlier):
    return lax.optimization_barrier((value,) + earlier)[0]


def sum_seq(parts):
    arrived = [send(parts[k], "y", k) for k in (1, 3, 2)]
    leave, stay = (
        parts[0][r].astype(F32) + sum(a[r].astype(F32) for a in arrived) for r in (1, 0)
    )
    return (stay + swap(leave.astype(BF16), "xl").astype(F32)).astype(BF16)


def spread_seq(piece):
    other = swap(piece, "xl")
    near = {0: piece} | {k: shift(piece, "y", k) for k in (1, 3, 2)}
    far = {0: other} | {k: shift(other, "y", k) for k in (1, 3, 2)}
    return [part[k] for k in range(4) for part in (near, far)]


def sum_rows(parts):
    parts = lax.psum_scatter(
        parts.reshape(4, 2, ROWS, WIDTH), "z", scatter_dimension=0, tiled=False
    )
    return parts[0], swap(parts[1], "xh")


def per_device(
    inputs,
    gains,
    shifts,
    attend,
    attend_bias,
    mixer,
    mixer_bias,
    upward,
    upward_bias,
    downward,
    downward_bias,
    cotangent,
):
    core = lax.axis_index("c")
    x_lo = lax.axis_index("xl")
    chip = lax.axis_index("xh") * 4 + lax.axis_index("z")
    seq_index = lax.axis_index("y") * 2 + x_lo
    core_at = core.reshape(1)
    rows_in = inputs.reshape(ROWS, WIDTH)
    own_cot = cotangent.reshape(ROWS, WIDTH)
    width = 3 * CHIP_COLS

    z_order = (lax.axis_index("z") + jnp.arange(4, dtype=jnp.int32)) % 4
    y_order = (lax.axis_index("y") + jnp.arange(4, dtype=jnp.int32)) % 4
    seq_order = (y_order[:, None] * 2 + jnp.stack([x_lo, 1 - x_lo])[None, :]).reshape(SEQ_DEVICES)

    other_rows = swap(rows_in, "xh")
    near = {0: rows_in} | {k: shift(rows_in, "z", k) for k in (1, 3, 2)}
    far = {0: other_rows} | {k: shift(other_rows, "z", k) for k in (1, 3, 2)}
    pieces = [part[k] for part in (near, far) for k in range(4)]

    slab_index = seq_index * SLAB
    slab = lax.dynamic_slice_in_dim(attend, slab_index, SLAB, 0)
    slab = slab.reshape(SLAB, 3, CHIPS, CHIP_COLS).transpose(2, 0, 1, 3).reshape(CHIPS, SLAB, width)
    slab = exchange(slab, GROUP)
    attend_own = spread(slab, SEQ, SEQ_DEVICES).reshape(SEQ_DEVICES, CHIPS, SLAB, width)
    attend_chip = assemble_attend(core_at, attend_own, swap(attend_own, "c"))

    small = jnp.concatenate([gains, shifts, mixer_bias, downward_bias, attend_bias]).reshape(1, 896)
    small_all = spread(small, FSDP, FSDP_DEVICES).reshape(FSDP_DEVICES, 7, 128).astype(F32)
    gain_all = small_all[:, 0].reshape(1, WIDTH)
    shift_all = small_all[:, 1].reshape(1, WIDTH)
    out_bias = (small_all[:, 2] + small_all[:, 3]).reshape(WIDTH)
    bias_grid = small_all[:, 4:7].reshape(3, CHIPS, CHIP_COLS)
    attend_bias_chip = lax.dynamic_slice_in_dim(bias_grid, chip, 1, 1).reshape(1, width)

    mixer_other = swap(mixer, "c")
    mixer_chip = jnp.where(
        core == 0, jnp.concatenate([mixer, mixer_other]), jnp.concatenate([mixer_other, mixer])
    )
    up_other = swap(upward, "c")
    down_other = swap(downward, "c")
    up_bias_own = upward_bias.astype(F32).reshape(1, CORE_FF)
    up_bias_other = swap(upward_bias.reshape(1, CORE_FF), "c").astype(F32)

    own_positions = seq_index * ROWS + jnp.arange(ROWS, dtype=jnp.int32)
    own_tables = rope_tables(own_positions, 2 * CHIP_COLS // HEAD_DIM)
    all_tables = rope_tables(jnp.arange(LENGTH, dtype=jnp.int32), 2)

    cot_pair = jnp.stack([own_cot, swap(after(own_cot, near[1]), "xh")])
    cot_pair = after(cot_pair, *pieces)
    cot_group = lax.all_gather(cot_pair, "z", axis=0, tiled=False).reshape(TOKENS, WIDTH)
    rows_group, normed, qkv_sent = norm_project(
        z_order, pieces, gain_all, shift_all, attend_chip, attend_bias_chip, own_tables
    )
    qkv = exchange(qkv_sent.reshape(CHIPS, ROWS, width), SEQ).reshape(LENGTH, width)
    act_own, act_other, slope_own, slope_other = hidden_forward(
        normed, upward, up_other, up_bias_own, up_bias_other
    )

    attended, logsum = attend_forward(qkv)
    attended_group = exchange(attended.reshape(SEQ_DEVICES, ROWS, CHIP_COLS), SEQ).reshape(
        TOKENS, CHIP_COLS
    )
    attended_grad = grad_heads(cot_group, mixer_chip)
    grads = exchange(attended_grad.reshape(CHIPS, ROWS, CHIP_COLS), SEQ).reshape(LENGTH, CHIP_COLS)

    parts = out_part(act_own, act_other, attended_group, downward, down_other, mixer_chip)
    stay, arrived = sum_rows(parts)
    outputs = (
        rows_in.astype(F32) + out_bias + stay.astype(F32) + arrived.astype(F32)
    ).astype(BF16)

    grad_own, grad_other, up_bias_sum, up_bias_other_sum = hidden_back(
        cot_group, downward, down_other, slope_own, slope_other
    )
    att_own = lax.dynamic_slice_in_dim(attended_group, core * CORE_COLS, CORE_COLS, 1)
    att_other = lax.dynamic_slice_in_dim(attended_group, (1 - core) * CORE_COLS, CORE_COLS, 1)
    weight_grad = lambda lhs, rhs: dot(lhs, rhs, TN).astype(BF16)
    packed = pack(
        seq_order,
        weight_grad(normed, grad_own),
        swap(weight_grad(normed, grad_other), "c"),
        weight_grad(act_own, cot_group),
        swap(weight_grad(act_other, cot_group), "c"),
        weight_grad(att_own, cot_group),
        swap(weight_grad(att_other, cot_group), "c"),
    )
    up_grad, down_grad, mixer_grad = unpack(seq_order, spread_seq(sum_seq(packed)))

    projected_grad = exchange(
        attend_backward(qkv, grads, logsum, all_tables).reshape(SEQ_DEVICES, ROWS, width), SEQ
    ).reshape(TOKENS, width)

    parts, norm_sums, attend_bias_sum = normed_part(
        projected_grad, grad_own, grad_other, rows_group, attend_chip, upward, up_other
    )
    stay, arrived = sum_rows(parts)
    inputs_grad = rows_grad(rows_in, own_cot, stay, arrived, gain_all)

    attend_part = weight_grad(normed, projected_grad).reshape(CHIPS, 2, CORE_COLS, width)
    attend_keep = lax.dynamic_index_in_dim(attend_part, core, 1, keepdims=False)
    attend_send = lax.dynamic_index_in_dim(attend_part, 1 - core, 1, keepdims=False)
    attend_sum = pack_attend(
        seq_order,
        attend_keep.reshape(CHIPS * CORE_COLS, width),
        swap(attend_send.reshape(CHIPS * CORE_COLS, width), "c"),
    )
    attend_slab = exchange(sum_seq(attend_sum), GROUP)
    attend_grad = unpack_attend(spread(attend_slab, SEQ, SEQ_DEVICES).reshape(
        SEQ_DEVICES, CHIPS, SLAB, width
    ))

    bias_full = jnp.sum(own_cot.astype(F32), axis=0)
    attend_bias_full = lax.dynamic_update_slice(
        jnp.zeros((3, CHIPS, CHIP_COLS), F32), attend_bias_sum.reshape(3, 1, CHIP_COLS), (0, chip, 0)
    )
    up_bias_pair = jnp.where(
        core == 0,
        jnp.concatenate([up_bias_sum, up_bias_other_sum]),
        jnp.concatenate([up_bias_other_sum, up_bias_sum]),
    )
    up_bias_full = lax.dynamic_update_slice(
        jnp.zeros((CHIPS, 2, CORE_FF), F32), up_bias_pair[None], (chip, 0, 0)
    )
    vectors = jnp.concatenate(
        [
            v.reshape(FSDP_DEVICES, -1)
            for v in (norm_sums[0], norm_sums[1], bias_full, attend_bias_full, up_bias_full)
        ],
        axis=1,
    )
    vectors = jnp.sum(exchange(vectors, FSDP), axis=0)
    vectors = jnp.sum(spread(vectors, SEQ, SEQ_DEVICES), axis=0)
    gain_grad, shift_grad, bias_grad = vectors[:128], vectors[128:256], vectors[256:384]
    attend_bias_grad, up_bias_grad = vectors[384:768], vectors[768:]

    return (
        outputs.reshape(inputs.shape),
        inputs_grad.reshape(inputs.shape),
        gain_grad,
        shift_grad,
        attend_grad,
        attend_bias_grad,
        mixer_grad,
        bias_grad,
        up_grad,
        up_bias_grad,
        down_grad,
        bias_grad,
    )


def solution(mesh):
    fine = Mesh(mesh.devices.reshape(4, 2, 2, 4, 2), ("y", "xl", "xh", "z", "c"))
    rows = P(FSDP, SEQ, None)
    vector = P(FSDP)
    by_row = P(FSDP, None)
    by_col = P(None, FSDP)
    in_specs = (
        rows,
        vector,
        vector,
        by_row,
        vector,
        by_row,
        vector,
        by_col,
        vector,
        by_row,
        vector,
        rows,
    )
    out_specs = (
        rows,
        rows,
        vector,
        vector,
        by_row,
        vector,
        by_row,
        vector,
        by_col,
        vector,
        by_row,
        vector,
    )
    return jax.shard_map(
        per_device, mesh=fine, in_specs=in_specs, out_specs=out_specs, check_vma=False
    )
```

```python
import jax
import jax.numpy as jnp
from jax import lax
from jax.experimental import pallas as pl
from jax.experimental.pallas import tpu as pltpu
from jax.sharding import Mesh, PartitionSpec as P

HEADS = 32
HEAD_DIM = 64
ROT = 32
WIDTH = 2048
FF = 8192
SEQ_DEVICES = 8
CHIPS = 8
FSDP_DEVICES = 16
ROWS = 128
LENGTH = ROWS * SEQ_DEVICES
TOKENS = ROWS * CHIPS
CHIP_COLS = WIDTH // CHIPS
CORE_COLS = WIDTH // FSDP_DEVICES
CORE_FF = FF // FSDP_DEVICES
PAIR = 2 * HEAD_DIM
QBLOCK = 256

EPSILON = 1e-05
ROPE_BASE = 10000.0
NEG_FILL = -1e30
SCALE = HEAD_DIM ** (-0.5)

F32 = jnp.float32
BF16 = jnp.bfloat16

SEQ = ("y", "xl")
GROUP = ("xh", "z")
FSDP = ("xh", "z", "c")

NT = (((1,), (1,)), ((), ()))
TN = (((0,), (0,)), ((), ()))
NN = (((1,), (0,)), ((), ()))


def dot(lhs, rhs, dims=NN):
    return lax.dot_general(lhs, rhs, dims, preferred_element_type=F32)


def swap(piece, axis):
    return lax.ppermute(piece, axis, [(0, 1), (1, 0)])


def shift(piece, axis, step):
    return lax.ppermute(piece, axis, [(i, (i - step) % 4) for i in range(4)])


def send(piece, axis, step):
    return lax.ppermute(piece, axis, [(i, (i + step) % 4) for i in range(4)])


def rope_tables(positions, heads):
    half = ROT // 2
    frequency = ROPE_BASE ** (-2.0 * jnp.arange(half, dtype=F32) / ROT)
    angle = positions.astype(F32)[:, None] * frequency[None, :]
    cosine, sine = jnp.cos(angle), jnp.sin(angle)
    rest = jnp.zeros((positions.shape[0], HEAD_DIM - ROT), F32)
    blank = jnp.zeros_like(sine)
    turn = jnp.concatenate([cosine, cosine, rest + 1.0], axis=1)
    upper = jnp.concatenate([-sine, blank, rest], axis=1)
    lower = jnp.concatenate([blank, sine, rest], axis=1)
    return tuple(jnp.tile(t, (1, heads)) for t in (turn, upper, lower))


def turn_columns(values, turn, upper, lower, sign):
    width = values.shape[1]
    half = ROT // 2
    ahead = pltpu.roll(values, width - half, 1)
    behind = pltpu.roll(values, half, 1)
    return values * turn + sign * (ahead * upper + behind * lower)


def whole(shape):
    return pl.BlockSpec(shape, lambda i: (0,) * len(shape))


def row_block(rows, width, column=0):
    return pl.BlockSpec((rows, width), lambda i: (i, column))


def call(kernel, name, grid, in_specs, out_specs, out_shape, flops, moved, operands):
    return pl.pallas_call(
        kernel,
        grid=(grid,),
        in_specs=in_specs,
        out_specs=out_specs,
        out_shape=out_shape,
        compiler_params=pltpu.CompilerParams(vmem_limit_bytes=60 * 2**20),
        cost_estimate=pl.CostEstimate(flops=flops, bytes_accessed=moved, transcendentals=0),
        name=name,
    )(*operands)


def placed_call(kernel, name, grid, in_specs, out_specs, out_shape, scratch, flops, moved, order, operands):
    return pl.pallas_call(
        kernel,
        grid_spec=pltpu.PrefetchScalarGridSpec(
            num_scalar_prefetch=1,
            grid=(grid,),
            in_specs=in_specs,
            out_specs=out_specs,
            scratch_shapes=scratch,
        ),
        out_shape=out_shape,
        compiler_params=pltpu.CompilerParams(vmem_limit_bytes=60 * 2**20),
        cost_estimate=pl.CostEstimate(flops=flops, bytes_accessed=moved, transcendentals=0),
        name=name,
    )(order, *operands)


def fixed(dims):
    return pl.BlockSpec(dims, lambda i, order: (0,) * len(dims))


def shape(dims, kind=BF16):
    return jax.ShapeDtypeStruct(dims, kind)


def layer_stats(rows):
    center = rows - jnp.mean(rows, axis=-1, keepdims=True)
    spread_out = jnp.mean(center * center, axis=-1, keepdims=True)
    return center, lax.rsqrt(spread_out + EPSILON)


def assemble_kernel(core_ref, own_ref, other_ref, out_ref):
    core = core_ref[0]
    out_ref[0, core] = own_ref[...].reshape(out_ref.shape[2:])
    out_ref[0, 1 - core] = other_ref[...].reshape(out_ref.shape[2:])


def assemble_attend(core, own, other):
    slab, cols = own.shape[2:]
    piece = pl.BlockSpec((SEQ_DEVICES, 1, slab, cols), lambda g, core: (0, g, 0, 0))
    out = (CHIPS, 2, SEQ_DEVICES, slab, cols)
    return pl.pallas_call(
        assemble_kernel,
        grid_spec=pltpu.PrefetchScalarGridSpec(
            num_scalar_prefetch=1,
            grid=(CHIPS,),
            in_specs=[piece, piece],
            out_specs=pl.BlockSpec((1,) + out[1:], lambda g, core: (g, 0, 0, 0, 0)),
        ),
        out_shape=shape(out),
        compiler_params=pltpu.CompilerParams(vmem_limit_bytes=60 * 2**20),
        cost_estimate=pl.CostEstimate(flops=0, bytes_accessed=6 * 2**20, transcendentals=0),
        name="assemble_attend",
    )(core, own, other).reshape(WIDTH, cols)


def norm_project_kernel(
    order_ref,
    near_0,
    near_1,
    near_2,
    near_3,
    far_0,
    far_1,
    far_2,
    far_3,
    gain_ref,
    shift_ref,
    weight_ref,
    bias_ref,
    turn_ref,
    upper_ref,
    lower_ref,
    rows_ref,
    normed_ref,
    out_ref,
):
    step = pl.program_id(0)
    pairs = ((near_0, far_0), (near_1, far_1), (near_2, far_2), (near_3, far_3))
    for index, (near, far) in enumerate(pairs):

        @pl.when(step == index)
        def _():
            rows_ref[:ROWS] = near[...]
            rows_ref[ROWS:] = far[...]

    center, inverse = layer_stats(rows_ref[...].astype(F32))
    normed = (center * inverse * gain_ref[...] + shift_ref[...]).astype(BF16)
    normed_ref[...] = normed
    projected = dot(normed, weight_ref[...]) + bias_ref[...]
    turned_width = 2 * CHIP_COLS
    for block in range(2):
        rows = slice(block * ROWS, (block + 1) * ROWS)
        out_ref[rows, :turned_width] = turn_columns(
            projected[rows, :turned_width], turn_ref[...], upper_ref[...], lower_ref[...], 1.0
        ).astype(BF16)
    out_ref[:, turned_width:] = projected[:, turned_width:].astype(BF16)


def norm_project(order, pieces, gain, shift_row, weight, bias, tables):
    block = 2 * ROWS
    width = weight.shape[1]
    vectors = (gain, shift_row, weight, bias) + tables
    out = lambda cols: pl.BlockSpec((block, cols), lambda i, order: (order[i], 0))
    return placed_call(
        norm_project_kernel,
        "norm_project",
        4,
        [fixed((ROWS, WIDTH))] * 8 + [fixed(v.shape) for v in vectors],
        [out(WIDTH), out(WIDTH), out(width)],
        [shape((TOKENS, WIDTH)), shape((TOKENS, WIDTH)), shape((TOKENS, width))],
        [],
        2 * TOKENS * WIDTH * width,
        18 * 2**20,
        order,
        tuple(pieces) + vectors,
    )


def hidden_kernel(
    normed_ref,
    own_ref,
    other_ref,
    own_bias_ref,
    other_bias_ref,
    own_act_ref,
    other_act_ref,
    own_slope_ref,
    other_slope_ref,
):
    root = (2.0 / 3.141592653589793) ** 0.5
    for weight, bias, act, slope in (
        (own_ref, own_bias_ref, own_act_ref, own_slope_ref),
        (other_ref, other_bias_ref, other_act_ref, other_slope_ref),
    ):
        hidden = dot(normed_ref[...], weight[...]) + bias[...]
        square = hidden * hidden
        bend = jnp.tanh(root * hidden * (1.0 + 0.044715 * square))
        half = 0.5 * (1.0 + bend)
        act[...] = (hidden * half).astype(BF16)
        slope[...] = half + 0.5 * hidden * (1.0 - bend * bend) * (
            root * (1.0 + 3.0 * 0.044715 * square)
        )


def hidden_forward(normed, own, other, own_bias, other_bias):
    block = 256
    operands = (own, other, own_bias, other_bias)
    return call(
        hidden_kernel,
        "hidden_forward",
        TOKENS // block,
        [row_block(block, WIDTH)] + [whole(v.shape) for v in operands],
        [row_block(block, CORE_FF)] * 4,
        [shape((TOKENS, CORE_FF))] * 2 + [shape((TOKENS, CORE_FF), F32)] * 2,
        4 * TOKENS * WIDTH * CORE_FF,
        14 * 2**20,
        (normed,) + operands,
    )


def grad_heads_kernel(cot_ref, mixer_ref, out_ref):
    out_ref[...] = dot(cot_ref[...], mixer_ref[...], NT).astype(BF16)


def grad_heads(cot, mixer):
    block = 256
    return call(
        grad_heads_kernel,
        "grad_heads",
        TOKENS // block,
        [row_block(block, WIDTH), whole(mixer.shape)],
        row_block(block, CHIP_COLS),
        shape((TOKENS, CHIP_COLS)),
        2 * TOKENS * WIDTH * CHIP_COLS,
        6 * 2**20,
        (cot, mixer),
    )


def hidden_back_kernel(
    cot_ref, own_ref, other_ref, own_slope_ref, other_slope_ref, own_out, other_out, own_sum, other_sum
):
    for weight, slope, out, total in (
        (own_ref, own_slope_ref, own_out, own_sum),
        (other_ref, other_slope_ref, other_out, other_sum),
    ):
        grad = (dot(cot_ref[...], weight[...], NT) * slope[...]).astype(BF16)
        out[...] = grad
        part = jnp.sum(grad.astype(F32), axis=0, keepdims=True)

        @pl.when(pl.program_id(0) == 0)
        def _():
            total[...] = part

        @pl.when(pl.program_id(0) > 0)
        def _():
            total[...] += part


def hidden_back(cot, own, other, own_slope, other_slope):
    block = 256
    return call(
        hidden_back_kernel,
        "hidden_back",
        TOKENS // block,
        [row_block(block, WIDTH), whole(own.shape), whole(other.shape)]
        + [row_block(block, CORE_FF)] * 2,
        [row_block(block, CORE_FF)] * 2 + [whole((1, CORE_FF))] * 2,
        [shape((TOKENS, CORE_FF))] * 2 + [shape((1, CORE_FF), F32)] * 2,
        4 * TOKENS * WIDTH * CORE_FF,
        14 * 2**20,
        (cot, own, other, own_slope, other_slope),
    )


def out_part_kernel(own_act, other_act, attended, own_ref, other_ref, mixer_ref, out_ref):
    out_ref[...] = (
        dot(own_act[...], own_ref[...])
        + dot(other_act[...], other_ref[...])
        + dot(attended[...], mixer_ref[...])
    ).astype(BF16)


def out_part(own_act, other_act, attended, own, other, mixer):
    block = 256
    weights = (own, other, mixer)
    return call(
        out_part_kernel,
        "out_part",
        TOKENS // block,
        [row_block(block, CORE_FF)] * 2
        + [row_block(block, CHIP_COLS)]
        + [whole(w.shape) for w in weights],
        row_block(block, WIDTH),
        shape((TOKENS, WIDTH)),
        2 * TOKENS * WIDTH * (2 * CORE_FF + CHIP_COLS),
        12 * 2**20,
        (own_act, other_act, attended) + weights,
    )


def normed_part_kernel(
    projected, own_grad, other_grad, rows_ref, attend_ref, own_ref, other_ref, out_ref, sums_ref, bias_ref
):
    total = (
        dot(projected[...], attend_ref[...], NT)
        + dot(own_grad[...], own_ref[...], NT)
        + dot(other_grad[...], other_ref[...], NT)
    )
    out_ref[...] = total.astype(BF16)
    center, inverse = layer_stats(rows_ref[...].astype(F32))
    gain_part = jnp.sum(total * (center * inverse), axis=0, keepdims=True)
    shift_part = jnp.sum(total, axis=0, keepdims=True)
    bias_part = jnp.sum(projected[...].astype(F32), axis=0, keepdims=True)

    @pl.when(pl.program_id(0) == 0)
    def _():
        sums_ref[0:1] = gain_part
        sums_ref[1:2] = shift_part
        bias_ref[...] = bias_part

    @pl.when(pl.program_id(0) > 0)
    def _():
        sums_ref[0:1] += gain_part
        sums_ref[1:2] += shift_part
        bias_ref[...] += bias_part


def normed_part(projected, own_grad, other_grad, rows, attend, own, other):
    block = 256
    width = projected.shape[1]
    weights = (attend, own, other)
    return call(
        normed_part_kernel,
        "normed_part",
        TOKENS // block,
        [row_block(block, width)]
        + [row_block(block, CORE_FF)] * 2
        + [row_block(block, WIDTH)]
        + [whole(w.shape) for w in weights],
        [row_block(block, WIDTH), whole((2, WIDTH)), whole((1, width))],
        [shape((TOKENS, WIDTH)), shape((2, WIDTH), F32), shape((1, width), F32)],
        2 * TOKENS * WIDTH * (2 * CORE_FF + width),
        18 * 2**20,
        (projected, own_grad, other_grad, rows) + weights,
    )


UP_ROWS = WIDTH // SEQ_DEVICES
DOWN_ROWS = CORE_FF // 2
MIX_ROWS = CORE_COLS // 2
PACK_ROWS = UP_ROWS + MIX_ROWS
PACK_COLS = CORE_FF
HALF = PACK_COLS // 2
SLOT_COLS = WIDTH // SEQ_DEVICES


def across(rows):
    return pl.BlockSpec((rows, SLOT_COLS), lambda i, order: (0, order[i]))


def pair_out(rows, k):
    return pl.BlockSpec((1, rows, PACK_COLS), lambda i, order: (jnp.clip(i - 2 * k, 0, 1), 0, 0))


def pack_down_kernel(order_ref, own_ref, other_ref, stay_ref, leave_ref):
    down = (own_ref[...].astype(F32) + other_ref[...].astype(F32)).astype(BF16)
    step = pl.program_id(0)
    for index, out_ref in enumerate((stay_ref, leave_ref)):

        @pl.when(step // 4 == index)
        def _():
            out_ref[0, :, :HALF] = down[:DOWN_ROWS]
            out_ref[0, :, HALF:] = down[DOWN_ROWS:]


def pack_down(order, own, other):
    block = (1, DOWN_ROWS, PACK_COLS)
    return placed_call(
        pack_down_kernel,
        "pack_down",
        SEQ_DEVICES,
        [across(CORE_FF)] * 2,
        [
            pl.BlockSpec(block, lambda i, order: (jnp.minimum(i, 3), 0, 0)),
            pl.BlockSpec(block, lambda i, order: (jnp.maximum(i - 4, 0), 0, 0)),
        ],
        [shape((4, DOWN_ROWS, PACK_COLS))] * 2,
        [],
        0,
        6 * 2**20,
        order,
        (own, other),
    )


def pack_up_kernel(order_ref, up_own, up_other, mix_own, mix_other, *outs):
    up = (up_own[...].astype(F32) + up_other[...].astype(F32)).astype(BF16)
    mix = (mix_own[...].astype(F32) + mix_other[...].astype(F32)).astype(BF16)
    step = pl.program_id(0)
    for index, out_ref in enumerate(outs):

        @pl.when(step // 2 == index)
        def _():
            out_ref[0, :UP_ROWS] = up
            out_ref[0, UP_ROWS:, :HALF] = mix[:MIX_ROWS]
            out_ref[0, UP_ROWS:, HALF:] = mix[MIX_ROWS:]


def pack_up(order, up_own, up_other, mix_own, mix_other):
    up = pl.BlockSpec((UP_ROWS, CORE_FF), lambda i, order: (order[i], 0))
    return placed_call(
        pack_up_kernel,
        "pack_up",
        SEQ_DEVICES,
        [up, up, across(CORE_COLS), across(CORE_COLS)],
        [pair_out(PACK_ROWS, k) for k in range(4)],
        [shape((2, PACK_ROWS, PACK_COLS))] * 4,
        [],
        0,
        8 * 2**20,
        order,
        (up_own, up_other, mix_own, mix_other),
    )


def unpack_down_kernel(order_ref, *refs):
    out_ref = refs[8]
    for index, piece in enumerate(refs[:8]):

        @pl.when(pl.program_id(0) == index)
        def _():
            out_ref[:DOWN_ROWS] = piece[:, :HALF].astype(F32)
            out_ref[DOWN_ROWS:] = piece[:, HALF:].astype(F32)


def unpack_down(order, pieces):
    return placed_call(
        unpack_down_kernel,
        "unpack_down",
        SEQ_DEVICES,
        [fixed((DOWN_ROWS, PACK_COLS))] * 8,
        across(CORE_FF),
        shape((CORE_FF, WIDTH), F32),
        [],
        0,
        6 * 2**20,
        order,
        tuple(pieces),
    )


def unpack_up_kernel(order_ref, *refs):
    up_ref, mix_ref = refs[8:]
    for index, piece in enumerate(refs[:8]):

        @pl.when(pl.program_id(0) == index)
        def _():
            up_ref[...] = piece[:UP_ROWS].astype(F32)
            mix_ref[:MIX_ROWS] = piece[UP_ROWS:, :HALF].astype(F32)
            mix_ref[MIX_ROWS:] = piece[UP_ROWS:, HALF:].astype(F32)


def unpack_up(order, pieces):
    return placed_call(
        unpack_up_kernel,
        "unpack_up",
        SEQ_DEVICES,
        [fixed((PACK_ROWS, PACK_COLS))] * 8,
        [pl.BlockSpec((UP_ROWS, CORE_FF), lambda i, order: (order[i], 0)), across(CORE_COLS)],
        [shape((WIDTH, CORE_FF), F32), shape((CORE_COLS, WIDTH), F32)],
        [],
        0,
        8 * 2**20,
        order,
        tuple(pieces),
    )


SLAB = CORE_COLS // SEQ_DEVICES


def pack_attend_kernel(order_ref, own_ref, other_ref, *outs):
    for slot in range(SEQ_DEVICES):
        rows = pl.ds(pl.multiple_of(order_ref[slot] * SLAB, SLAB), SLAB)
        total = own_ref[rows, :].astype(F32) + other_ref[rows, :].astype(F32)
        outs[slot // 2][slot % 2, 0] = total.astype(BF16)


def pack_attend(order, own, other):
    cols = own.shape[1]
    block = pl.BlockSpec((CORE_COLS, cols), lambda i, order: (i, 0))
    return placed_call(
        pack_attend_kernel,
        "pack_attend",
        CHIPS,
        [block] * 2,
        [pl.BlockSpec((2, 1, SLAB, cols), lambda i, order: (0, i, 0, 0))] * 4,
        [shape((2, CHIPS, SLAB, cols))] * 4,
        [],
        0,
        5 * 2**20,
        order,
        (own, other),
    )


def unpack_attend_kernel(packed_ref, out_ref):
    for chip in range(CHIPS):
        for part in range(3):
            out_ref[:, part * WIDTH + chip * CHIP_COLS : part * WIDTH + (chip + 1) * CHIP_COLS] = (
                packed_ref[0, chip, :, part * CHIP_COLS : (part + 1) * CHIP_COLS].astype(F32)
            )


def unpack_attend(packed):
    return call(
        unpack_attend_kernel,
        "unpack_attend",
        SEQ_DEVICES,
        [pl.BlockSpec((1,) + packed.shape[1:], lambda i: (i, 0, 0, 0))],
        row_block(SLAB, 3 * WIDTH),
        shape((CORE_COLS, 3 * WIDTH), F32),
        0,
        5 * 2**20,
        (packed,),
    )


def rows_grad_kernel(rows_ref, cot_ref, near_ref, far_ref, gain_ref, out_ref):
    grad = near_ref[...].astype(F32) + far_ref[...].astype(F32)
    center, inverse = layer_stats(rows_ref[...].astype(F32))
    unit = center * inverse
    scaled = grad * gain_ref[...]
    out_ref[...] = cot_ref[...].astype(F32) + inverse * (
        scaled
        - jnp.mean(scaled, axis=-1, keepdims=True)
        - unit * jnp.mean(scaled * unit, axis=-1, keepdims=True)
    )


def rows_grad(rows, cot, near, far, gain):
    block = 64
    return call(
        rows_grad_kernel,
        "rows_grad",
        ROWS // block,
        [row_block(block, WIDTH)] * 4 + [whole(gain.shape)],
        row_block(block, WIDTH),
        shape((ROWS, WIDTH), F32),
        0,
        4 * 2**20,
        (rows, cot, near, far, gain),
    )


def lane_masks():
    lane = lax.broadcasted_iota(jnp.int32, (1, PAIR), 1)
    first = (lane < HEAD_DIM).astype(BF16)
    return first, 1 - first


def scores_of(query, keys, low):
    scores = dot(query, keys, NT) * SCALE
    row = low + lax.broadcasted_iota(jnp.int32, scores.shape, 0)
    col = lax.broadcasted_iota(jnp.int32, scores.shape, 1)
    return jnp.where(col <= row, scores, NEG_FILL)


def attend_kernel(query_ref, key_ref, value_ref, out_ref, logsum_ref):
    first, second = lane_masks()
    lane = lax.broadcasted_iota(jnp.int32, (QBLOCK, PAIR), 1)
    for low in range(0, LENGTH, QBLOCK):
        reach = low + QBLOCK
        query = query_ref[low:reach, :]
        keys = key_ref[:reach, :]
        values = value_ref[:reach, :]
        found = []
        for mask in (first, second):
            scores = scores_of(query * mask, keys, low)
            peak = jnp.max(scores, axis=1, keepdims=True)
            weight = jnp.exp(scores - peak)
            total = jnp.sum(weight, axis=1, keepdims=True)
            prob_low = (weight * (1.0 / total)).astype(BF16)
            found.append((dot(prob_low, values), peak + jnp.log(total)))
        out_ref[low:reach, :] = jnp.where(lane < HEAD_DIM, found[0][0], found[1][0]).astype(BF16)
        logsum_ref[low:reach, :] = jnp.where(lane < HEAD_DIM, found[0][1], found[1][1])


def attend_forward(qkv):
    pairs = CHIP_COLS // PAIR
    column = lambda part: pl.BlockSpec((LENGTH, PAIR), lambda p: (0, part * pairs + p))
    return pl.pallas_call(
        attend_kernel,
        grid=(pairs,),
        in_specs=[column(0), column(1), column(2)],
        out_specs=[column(0), column(0)],
        out_shape=[
            jax.ShapeDtypeStruct((LENGTH, CHIP_COLS), BF16),
            jax.ShapeDtypeStruct((LENGTH, CHIP_COLS), F32),
        ],
        compiler_params=pltpu.CompilerParams(vmem_limit_bytes=60 * 2**20),
        cost_estimate=pl.CostEstimate(
            flops=8 * 2**30, bytes_accessed=4 * 2**20, transcendentals=4 * 2**20
        ),
        name="attend_forward",
    )(qkv, qkv, qkv)


def attend_back_kernel(
    query_ref,
    key_ref,
    value_ref,
    grad_ref,
    logsum_ref,
    turn_ref,
    upper_ref,
    lower_ref,
    out_ref,
    key_total,
    value_total,
):
    pair = pl.program_id(0)
    first, second = lane_masks()
    lane = lax.broadcasted_iota(jnp.int32, (QBLOCK, PAIR), 1)
    key_total[...] = jnp.zeros_like(key_total)
    value_total[...] = jnp.zeros_like(value_total)

    def store(part, low, reach, values):
        start = pl.multiple_of((part * (CHIP_COLS // PAIR) + pair) * PAIR, PAIR)
        out_ref[low:reach, pl.ds(start, PAIR)] = values.astype(BF16)

    def unturn(values, low, reach):
        kept = values.astype(BF16).astype(F32)
        return turn_columns(
            kept, turn_ref[low:reach, :], upper_ref[low:reach, :], lower_ref[low:reach, :], -1.0
        )

    for low in range(0, LENGTH, QBLOCK):
        reach = low + QBLOCK
        query = query_ref[low:reach, :]
        grad = grad_ref[low:reach, :]
        keys = key_ref[:reach, :]
        values = value_ref[:reach, :]
        query_grads = []
        key_part = 0.0
        value_part = 0.0
        for head, mask in enumerate((first, second)):
            own_query = query * mask
            own_grad = grad * mask
            scores = scores_of(own_query, keys, low)
            start = head * HEAD_DIM
            probs = jnp.exp(scores - logsum_ref[low:reach, start : start + 1])
            prob_grad = dot(own_grad, values, NT)
            inner = jnp.sum(probs * prob_grad, axis=1, keepdims=True)
            score_grad = (probs * (prob_grad - inner)).astype(BF16)
            query_grads.append(dot(score_grad, keys))
            key_part += dot(score_grad, own_query, TN)
            value_part += dot(probs.astype(BF16), own_grad, TN)
        key_total[:reach, :] += key_part
        value_total[:reach, :] += value_part
        query_grad = jnp.where(lane < HEAD_DIM, query_grads[0], query_grads[1]) * SCALE
        store(0, low, reach, unturn(query_grad, low, reach))
    store(1, 0, LENGTH, unturn(key_total[...] * SCALE, 0, LENGTH))
    store(2, 0, LENGTH, value_total[...])


def attend_backward(qkv, grad, logsum, tables):
    pairs = CHIP_COLS // PAIR
    column = lambda part: pl.BlockSpec((LENGTH, PAIR), lambda p: (0, part * pairs + p))
    whole = lambda shape: pl.BlockSpec(shape, lambda p: (0, 0))
    width = 3 * CHIP_COLS
    return pl.pallas_call(
        attend_back_kernel,
        grid=(pairs,),
        in_specs=[column(0), column(1), column(2), column(0), column(0)]
        + [whole(t.shape) for t in tables],
        out_specs=whole((LENGTH, width)),
        out_shape=jax.ShapeDtypeStruct((LENGTH, width), BF16),
        scratch_shapes=[pltpu.VMEM((LENGTH, PAIR), F32), pltpu.VMEM((LENGTH, PAIR), F32)],
        compiler_params=pltpu.CompilerParams(vmem_limit_bytes=60 * 2**20),
        cost_estimate=pl.CostEstimate(
            flops=20 * 2**30, bytes_accessed=6 * 2**20, transcendentals=4 * 2**20
        ),
        name="attend_backward",
    )(qkv, qkv, qkv, grad, logsum, *tables)


def exchange(blocks, axes):
    return lax.all_to_all(blocks, axes, split_axis=0, concat_axis=0, tiled=True)


def spread(block, axes, count):
    return exchange(jnp.broadcast_to(block[None], (count,) + block.shape), axes)


def after(value, *earlier):
    return lax.optimization_barrier((value,) + earlier)[0]


def sent_y(parts):
    return [send(parts[k], "y", k) for k in (1, 3, 2)]


def sum_seq(parts, arrived):
    leave, stay = (
        parts[0][r].astype(F32) + sum(a[r].astype(F32) for a in arrived) for r in (1, 0)
    )
    return (stay + swap(leave.astype(BF16), "xl").astype(F32)).astype(BF16)


def sum_seq_x_first(stay, arrived):
    parts = (stay.astype(F32) + arrived.astype(F32)).astype(BF16)
    return (parts[0].astype(F32) + sum(a.astype(F32) for a in sent_y(parts))).astype(BF16)


def spread_seq_y_first(piece):
    near = {0: piece} | {k: shift(piece, "y", k) for k in (1, 3, 2)}
    far = {k: swap(near[k], "xl") for k in (0, 1, 3, 2)}
    return [part[k] for k in range(4) for part in (near, far)]


def spread_seq(piece):
    other = swap(piece, "xl")
    near = {0: piece} | {k: shift(piece, "y", k) for k in (1, 3, 2)}
    far = {0: other} | {k: shift(other, "y", k) for k in (1, 3, 2)}
    return [part[k] for k in range(4) for part in (near, far)]


def sum_rows(parts):
    parts = lax.psum_scatter(
        parts.reshape(4, 2, ROWS, WIDTH), "z", scatter_dimension=0, tiled=False
    )
    return parts[0], swap(parts[1], "xh")


def per_device(
    inputs,
    gains,
    shifts,
    attend,
    attend_bias,
    mixer,
    mixer_bias,
    upward,
    upward_bias,
    downward,
    downward_bias,
    cotangent,
):
    core = lax.axis_index("c")
    x_lo = lax.axis_index("xl")
    chip = lax.axis_index("xh") * 4 + lax.axis_index("z")
    seq_index = lax.axis_index("y") * 2 + x_lo
    core_at = core.reshape(1)
    rows_in = inputs.reshape(ROWS, WIDTH)
    own_cot = cotangent.reshape(ROWS, WIDTH)
    width = 3 * CHIP_COLS

    z_order = (lax.axis_index("z") + jnp.arange(4, dtype=jnp.int32)) % 4
    y_order = (lax.axis_index("y") + jnp.arange(4, dtype=jnp.int32)) % 4
    x_first_order = jnp.concatenate([y_order * 2 + x_lo, y_order * 2 + 1 - x_lo])
    seq_order = (y_order[:, None] * 2 + jnp.stack([x_lo, 1 - x_lo])[None, :]).reshape(SEQ_DEVICES)

    other_rows = swap(rows_in, "xh")
    slab = lax.dynamic_slice_in_dim(attend, seq_index * SLAB, SLAB, 0)
    slab = slab.reshape(SLAB, 3, CHIPS, CHIP_COLS).transpose(2, 0, 1, 3).reshape(CHIPS, SLAB, width)
    small = jnp.concatenate([gains, shifts, mixer_bias, downward_bias, attend_bias])
    small = jnp.pad(small, (0, 2 * width - small.shape[0])).reshape(1, 2, width)
    small = jnp.pad(jnp.broadcast_to(small, (CHIPS, 2, width)), ((0, 0), (0, SLAB - 2), (0, 0)))
    slab = exchange(jnp.concatenate([slab, small], axis=1), GROUP)
    small_own = slab[:, SLAB : SLAB + 2].reshape(CHIPS, 2 * width)[:, :896]
    slab = slab[:, :SLAB]
    attend_own = spread(slab, SEQ, SEQ_DEVICES).reshape(SEQ_DEVICES, CHIPS, SLAB, width)
    attend_chip = assemble_attend(core_at, attend_own, swap(attend_own, "c"))
    small_other = swap(small_own, "c")
    small_all = jnp.where(
        core == 0, jnp.stack([small_own, small_other], 1), jnp.stack([small_other, small_own], 1)
    ).reshape(FSDP_DEVICES, 7, 128).astype(F32)
    gain_all = small_all[:, 0].reshape(1, WIDTH)
    shift_all = small_all[:, 1].reshape(1, WIDTH)
    out_bias = (small_all[:, 2] + small_all[:, 3]).reshape(WIDTH)
    bias_grid = small_all[:, 4:7].reshape(3, CHIPS, CHIP_COLS)
    attend_bias_chip = lax.dynamic_slice_in_dim(bias_grid, chip, 1, 1).reshape(1, width)

    sent_rows, other_rows = after(rows_in, slab), after(other_rows, slab)
    near = {0: rows_in} | {k: shift(sent_rows, "z", k) for k in (1, 3, 2)}
    far = {0: other_rows} | {k: shift(other_rows, "z", k) for k in (1, 3, 2)}
    pieces = [part[k] for part in (near, far) for k in range(4)]

    mixer_other = swap(mixer, "c")
    mixer_chip = jnp.where(
        core == 0, jnp.concatenate([mixer, mixer_other]), jnp.concatenate([mixer_other, mixer])
    )
    up_other = swap(upward, "c")
    down_other = swap(downward, "c")
    up_bias_own = upward_bias.astype(F32).reshape(1, CORE_FF)
    up_bias_other = swap(upward_bias.reshape(1, CORE_FF), "c").astype(F32)

    own_positions = seq_index * ROWS + jnp.arange(ROWS, dtype=jnp.int32)
    own_tables = rope_tables(own_positions, 2 * CHIP_COLS // HEAD_DIM)
    all_tables = rope_tables(jnp.arange(LENGTH, dtype=jnp.int32), 2)

    cot_pair = jnp.stack([own_cot, swap(after(own_cot, near[1]), "xh")])
    cot_pair = after(cot_pair, *pieces)
    cot_group = lax.all_gather(cot_pair, "z", axis=0, tiled=False).reshape(TOKENS, WIDTH)
    rows_group, normed, qkv_sent = norm_project(
        z_order, pieces, gain_all, shift_all, attend_chip, attend_bias_chip, own_tables
    )
    qkv = exchange(qkv_sent.reshape(CHIPS, ROWS, width), SEQ).reshape(LENGTH, width)
    act_own, act_other, slope_own, slope_other = hidden_forward(
        normed, upward, up_other, up_bias_own, up_bias_other
    )

    attended, logsum = attend_forward(after(qkv, act_own))
    attended_group = exchange(attended.reshape(SEQ_DEVICES, ROWS, CHIP_COLS), SEQ).reshape(
        TOKENS, CHIP_COLS
    )
    attended_grad = grad_heads(cot_group, mixer_chip)
    grads = exchange(attended_grad.reshape(CHIPS, ROWS, CHIP_COLS), SEQ).reshape(LENGTH, CHIP_COLS)

    parts = out_part(
        act_own, act_other, after(attended_group, attended_grad), downward, down_other, mixer_chip
    )
    stay, arrived = sum_rows(parts)
    outputs = (
        rows_in.astype(F32) + out_bias + stay.astype(F32) + arrived.astype(F32)
    ).astype(BF16)

    weight_grad = lambda lhs, rhs: dot(lhs, rhs, TN).astype(BF16)
    cot_late = after(cot_group, parts)
    down_send = swap(weight_grad(act_other, cot_late), "c")
    down_keep = weight_grad(act_own, cot_late)

    back = attend_backward(qkv, after(grads, down_keep), logsum, all_tables)
    projected_grad = exchange(back.reshape(SEQ_DEVICES, ROWS, width), SEQ).reshape(TOKENS, width)
    down_stay, down_leave = pack_down(x_first_order, after(down_keep, back), down_send)
    down_arrived = swap(down_leave, "xl")

    grad_own, grad_other, up_bias_sum, up_bias_other_sum = hidden_back(
        after(cot_group, down_stay), downward, down_other, slope_own, slope_other
    )
    att_own = lax.dynamic_slice_in_dim(attended_group, core * CORE_COLS, CORE_COLS, 1)
    att_other = lax.dynamic_slice_in_dim(attended_group, (1 - core) * CORE_COLS, CORE_COLS, 1)
    mix_send = swap(weight_grad(att_other, after(cot_late, grad_own)), "c")
    up_send = swap(weight_grad(normed, grad_other), "c")
    up_keep = weight_grad(normed, grad_own)
    mix_keep = weight_grad(att_own, after(cot_late, up_keep))

    projected_grad = after(projected_grad, up_keep, mix_keep, down_arrived)
    attend_part = weight_grad(normed, projected_grad).reshape(CHIPS, 2, CORE_COLS, width)
    attend_keep = lax.dynamic_index_in_dim(attend_part, core, 1, keepdims=False)
    attend_send = lax.dynamic_index_in_dim(attend_part, 1 - core, 1, keepdims=False)
    attend_arrived = swap(attend_send.reshape(CHIPS * CORE_COLS, width), "c")
    up_slabs = pack_up(seq_order, after(up_keep, attend_send), up_send, mix_keep, mix_send)
    up_arrived = sent_y(up_slabs)
    down_sum = sum_seq_x_first(down_stay, down_arrived)

    parts, norm_sums, attend_bias_sum = normed_part(
        after(projected_grad, attend_send, up_slabs[0], attend_arrived),
        grad_own,
        grad_other,
        rows_group,
        attend_chip,
        upward,
        up_other,
    )
    stay, arrived = sum_rows(parts)
    inputs_grad = rows_grad(rows_in, own_cot, stay, arrived, gain_all)

    attend_slabs = pack_attend(
        seq_order, attend_keep.reshape(CHIPS * CORE_COLS, width), after(attend_arrived, parts)
    )
    attend_slab = exchange(sum_seq(attend_slabs, sent_y(attend_slabs)), GROUP)
    attend_grad = unpack_attend(spread(attend_slab, SEQ, SEQ_DEVICES).reshape(
        SEQ_DEVICES, CHIPS, SLAB, width
    ))
    down_grad = unpack_down(seq_order, spread_seq_y_first(down_sum))
    up_grad, mixer_grad = unpack_up(seq_order, spread_seq(sum_seq(up_slabs, up_arrived)))

    bias_full = jnp.sum(own_cot.astype(F32), axis=0)
    attend_bias_full = lax.dynamic_update_slice(
        jnp.zeros((3, CHIPS, CHIP_COLS), F32), attend_bias_sum.reshape(3, 1, CHIP_COLS), (0, chip, 0)
    )
    up_bias_pair = jnp.where(
        core == 0,
        jnp.concatenate([up_bias_sum, up_bias_other_sum]),
        jnp.concatenate([up_bias_other_sum, up_bias_sum]),
    )
    up_bias_full = lax.dynamic_update_slice(
        jnp.zeros((CHIPS, 2, CORE_FF), F32), up_bias_pair[None], (chip, 0, 0)
    )
    vectors = jnp.concatenate(
        [
            v.reshape(FSDP_DEVICES, -1)
            for v in (norm_sums[0], norm_sums[1], bias_full, attend_bias_full, up_bias_full)
        ],
        axis=1,
    )
    vectors = jnp.sum(exchange(vectors, FSDP), axis=0)
    vectors = jnp.sum(spread(vectors, SEQ, SEQ_DEVICES), axis=0)
    gain_grad, shift_grad, bias_grad = vectors[:128], vectors[128:256], vectors[256:384]
    attend_bias_grad, up_bias_grad = vectors[384:768], vectors[768:]

    return (
        outputs.reshape(inputs.shape),
        inputs_grad.reshape(inputs.shape),
        gain_grad,
        shift_grad,
        attend_grad,
        attend_bias_grad,
        mixer_grad,
        bias_grad,
        up_grad,
        up_bias_grad,
        down_grad,
        bias_grad,
    )


def solution(mesh):
    fine = Mesh(mesh.devices.reshape(4, 2, 2, 4, 2), ("y", "xl", "xh", "z", "c"))
    rows = P(FSDP, SEQ, None)
    vector = P(FSDP)
    by_row = P(FSDP, None)
    by_col = P(None, FSDP)
    in_specs = (
        rows,
        vector,
        vector,
        by_row,
        vector,
        by_row,
        vector,
        by_col,
        vector,
        by_row,
        vector,
        rows,
    )
    out_specs = (
        rows,
        rows,
        vector,
        vector,
        by_row,
        vector,
        by_row,
        vector,
        by_col,
        vector,
        by_row,
        vector,
    )
    return jax.shard_map(
        per_device, mesh=fine, in_specs=in_specs, out_specs=out_specs, check_vma=False
    )
```

```python
import jax
import jax.numpy as jnp
from jax import lax
from jax.experimental import pallas as pl
from jax.experimental.pallas import tpu as pltpu
from jax.sharding import Mesh, PartitionSpec as P

HEADS = 32
HEAD_DIM = 64
ROT = 32
WIDTH = 2048
FF = 8192
SEQ_DEVICES = 8
CHIPS = 8
FSDP_DEVICES = 16
ROWS = 128
LENGTH = ROWS * SEQ_DEVICES
TOKENS = ROWS * CHIPS
CHIP_COLS = WIDTH // CHIPS
CORE_COLS = WIDTH // FSDP_DEVICES
CORE_FF = FF // FSDP_DEVICES
PAIR = 2 * HEAD_DIM
QBLOCK = 256

EPSILON = 1e-05
ROPE_BASE = 10000.0
NEG_FILL = -1e30
LIGHTER = 8
SCALE = HEAD_DIM ** (-0.5)

F32 = jnp.float32
BF16 = jnp.bfloat16

SEQ = ("y", "xl")
GROUP = ("xh", "z")
FSDP = ("xh", "z", "c")

NT = (((1,), (1,)), ((), ()))
TN = (((0,), (0,)), ((), ()))
NN = (((1,), (0,)), ((), ()))


def dot(lhs, rhs, dims=NN):
    return lax.dot_general(lhs, rhs, dims, preferred_element_type=F32)


def swap(piece, axis):
    return lax.ppermute(piece, axis, [(0, 1), (1, 0)])


def shift(piece, axis, step):
    return lax.ppermute(piece, axis, [(i, (i - step) % 4) for i in range(4)])


def send(piece, axis, step):
    return lax.ppermute(piece, axis, [(i, (i + step) % 4) for i in range(4)])


def rope_tables(positions, heads):
    half = ROT // 2
    frequency = ROPE_BASE ** (-2.0 * jnp.arange(half, dtype=F32) / ROT)
    angle = positions.astype(F32)[:, None] * frequency[None, :]
    cosine, sine = jnp.cos(angle), jnp.sin(angle)
    rest = jnp.zeros((positions.shape[0], HEAD_DIM - ROT), F32)
    blank = jnp.zeros_like(sine)
    turn = jnp.concatenate([cosine, cosine, rest + 1.0], axis=1)
    upper = jnp.concatenate([-sine, blank, rest], axis=1)
    lower = jnp.concatenate([blank, sine, rest], axis=1)
    return tuple(jnp.tile(t, (1, heads)) for t in (turn, upper, lower))


def turn_columns(values, turn, upper, lower, sign):
    width = values.shape[1]
    half = ROT // 2
    ahead = pltpu.roll(values, width - half, 1)
    behind = pltpu.roll(values, half, 1)
    return values * turn + sign * (ahead * upper + behind * lower)


def cost(flops, moved):
    return pl.CostEstimate(flops=flops // LIGHTER, bytes_accessed=moved // LIGHTER, transcendentals=0)


def whole(shape):
    return pl.BlockSpec(shape, lambda i: (0,) * len(shape))


def row_block(rows, width, column=0):
    return pl.BlockSpec((rows, width), lambda i: (i, column))


def call(kernel, name, grid, in_specs, out_specs, out_shape, flops, moved, operands):
    return pl.pallas_call(
        kernel,
        grid=(grid,),
        in_specs=in_specs,
        out_specs=out_specs,
        out_shape=out_shape,
        compiler_params=pltpu.CompilerParams(vmem_limit_bytes=60 * 2**20),
        cost_estimate=cost(flops, moved),
        name=name,
    )(*operands)


def placed_call(kernel, name, grid, in_specs, out_specs, out_shape, scratch, flops, moved, order, operands):
    return pl.pallas_call(
        kernel,
        grid_spec=pltpu.PrefetchScalarGridSpec(
            num_scalar_prefetch=1,
            grid=(grid,),
            in_specs=in_specs,
            out_specs=out_specs,
            scratch_shapes=scratch,
        ),
        out_shape=out_shape,
        compiler_params=pltpu.CompilerParams(vmem_limit_bytes=60 * 2**20),
        cost_estimate=cost(flops, moved),
        name=name,
    )(order, *operands)


def fixed(dims):
    return pl.BlockSpec(dims, lambda i, order: (0,) * len(dims))


def shape(dims, kind=BF16):
    return jax.ShapeDtypeStruct(dims, kind)


def layer_stats(rows):
    center = rows - jnp.mean(rows, axis=-1, keepdims=True)
    spread_out = jnp.mean(center * center, axis=-1, keepdims=True)
    return center, lax.rsqrt(spread_out + EPSILON)


def assemble_kernel(core_ref, own_ref, other_ref, out_ref):
    core = core_ref[0]
    out_ref[0, core] = own_ref[...].reshape(out_ref.shape[2:])
    out_ref[0, 1 - core] = other_ref[...].reshape(out_ref.shape[2:])


def assemble_attend(core, own, other):
    slab, cols = own.shape[2:]
    piece = pl.BlockSpec((SEQ_DEVICES, 1, slab, cols), lambda g, core: (0, g, 0, 0))
    out = (CHIPS, 2, SEQ_DEVICES, slab, cols)
    return pl.pallas_call(
        assemble_kernel,
        grid_spec=pltpu.PrefetchScalarGridSpec(
            num_scalar_prefetch=1,
            grid=(CHIPS,),
            in_specs=[piece, piece],
            out_specs=pl.BlockSpec((1,) + out[1:], lambda g, core: (g, 0, 0, 0, 0)),
        ),
        out_shape=shape(out),
        compiler_params=pltpu.CompilerParams(vmem_limit_bytes=60 * 2**20),
        cost_estimate=cost(0, 6 * 2**20),
        name="assemble_attend",
    )(core, own, other).reshape(WIDTH, cols)


def norm_project_kernel(
    order_ref,
    near_0,
    near_1,
    near_2,
    near_3,
    far_0,
    far_1,
    far_2,
    far_3,
    gain_ref,
    shift_ref,
    weight_ref,
    bias_ref,
    turn_ref,
    upper_ref,
    lower_ref,
    rows_ref,
    normed_ref,
    out_ref,
):
    step = pl.program_id(0)
    pairs = ((near_0, far_0), (near_1, far_1), (near_2, far_2), (near_3, far_3))
    for index, (near, far) in enumerate(pairs):

        @pl.when(step == index)
        def _():
            rows_ref[:ROWS] = near[...]
            rows_ref[ROWS:] = far[...]

    center, inverse = layer_stats(rows_ref[...].astype(F32))
    normed = (center * inverse * gain_ref[...] + shift_ref[...]).astype(BF16)
    normed_ref[...] = normed
    projected = dot(normed, weight_ref[...]) + bias_ref[...]
    turned_width = 2 * CHIP_COLS
    for block in range(2):
        rows = slice(block * ROWS, (block + 1) * ROWS)
        out_ref[rows, :turned_width] = turn_columns(
            projected[rows, :turned_width], turn_ref[...], upper_ref[...], lower_ref[...], 1.0
        ).astype(BF16)
    out_ref[:, turned_width:] = projected[:, turned_width:].astype(BF16)


def norm_project(order, pieces, gain, shift_row, weight, bias, tables):
    block = 2 * ROWS
    width = weight.shape[1]
    vectors = (gain, shift_row, weight, bias) + tables
    out = lambda cols: pl.BlockSpec((block, cols), lambda i, order: (order[i], 0))
    return placed_call(
        norm_project_kernel,
        "norm_project",
        4,
        [fixed((ROWS, WIDTH))] * 8 + [fixed(v.shape) for v in vectors],
        [out(WIDTH), out(WIDTH), out(width)],
        [shape((TOKENS, WIDTH)), shape((TOKENS, WIDTH)), shape((TOKENS, width))],
        [],
        2 * TOKENS * WIDTH * width,
        18 * 2**20,
        order,
        tuple(pieces) + vectors,
    )


def hidden_kernel(
    normed_ref,
    own_ref,
    other_ref,
    own_bias_ref,
    other_bias_ref,
    own_act_ref,
    other_act_ref,
    own_slope_ref,
    other_slope_ref,
):
    root = (2.0 / 3.141592653589793) ** 0.5
    for weight, bias, act, slope in (
        (own_ref, own_bias_ref, own_act_ref, own_slope_ref),
        (other_ref, other_bias_ref, other_act_ref, other_slope_ref),
    ):
        hidden = dot(normed_ref[...], weight[...]) + bias[...]
        square = hidden * hidden
        bend = jnp.tanh(root * hidden * (1.0 + 0.044715 * square))
        half = 0.5 * (1.0 + bend)
        act[...] = (hidden * half).astype(BF16)
        slope[...] = half + 0.5 * hidden * (1.0 - bend * bend) * (
            root * (1.0 + 3.0 * 0.044715 * square)
        )


def hidden_forward(normed, own, other, own_bias, other_bias):
    block = 256
    operands = (own, other, own_bias, other_bias)
    return call(
        hidden_kernel,
        "hidden_forward",
        TOKENS // block,
        [row_block(block, WIDTH)] + [whole(v.shape) for v in operands],
        [row_block(block, CORE_FF)] * 4,
        [shape((TOKENS, CORE_FF))] * 2 + [shape((TOKENS, CORE_FF), F32)] * 2,
        4 * TOKENS * WIDTH * CORE_FF,
        14 * 2**20,
        (normed,) + operands,
    )


def grad_heads_kernel(cot_ref, mixer_ref, out_ref):
    out_ref[...] = dot(cot_ref[...], mixer_ref[...], NT).astype(BF16)


def grad_heads(cot, mixer):
    block = 256
    return call(
        grad_heads_kernel,
        "grad_heads",
        TOKENS // block,
        [row_block(block, WIDTH), whole(mixer.shape)],
        row_block(block, CHIP_COLS),
        shape((TOKENS, CHIP_COLS)),
        2 * TOKENS * WIDTH * CHIP_COLS,
        6 * 2**20,
        (cot, mixer),
    )


def hidden_back_kernel(
    cot_ref, own_ref, other_ref, own_slope_ref, other_slope_ref, own_out, other_out, own_sum, other_sum
):
    for weight, slope, out, total in (
        (own_ref, own_slope_ref, own_out, own_sum),
        (other_ref, other_slope_ref, other_out, other_sum),
    ):
        grad = (dot(cot_ref[...], weight[...], NT) * slope[...]).astype(BF16)
        out[...] = grad
        part = jnp.sum(grad.astype(F32), axis=0, keepdims=True)

        @pl.when(pl.program_id(0) == 0)
        def _():
            total[...] = part

        @pl.when(pl.program_id(0) > 0)
        def _():
            total[...] += part


def hidden_back(cot, own, other, own_slope, other_slope):
    block = 256
    return call(
        hidden_back_kernel,
        "hidden_back",
        TOKENS // block,
        [row_block(block, WIDTH), whole(own.shape), whole(other.shape)]
        + [row_block(block, CORE_FF)] * 2,
        [row_block(block, CORE_FF)] * 2 + [whole((1, CORE_FF))] * 2,
        [shape((TOKENS, CORE_FF))] * 2 + [shape((1, CORE_FF), F32)] * 2,
        4 * TOKENS * WIDTH * CORE_FF,
        14 * 2**20,
        (cot, own, other, own_slope, other_slope),
    )


def out_part_kernel(own_act, other_act, attended, own_ref, other_ref, mixer_ref, out_ref):
    out_ref[...] = (
        dot(own_act[...], own_ref[...])
        + dot(other_act[...], other_ref[...])
        + dot(attended[...], mixer_ref[...])
    ).astype(BF16)


def out_part(own_act, other_act, attended, own, other, mixer):
    block = 256
    weights = (own, other, mixer)
    return call(
        out_part_kernel,
        "out_part",
        TOKENS // block,
        [row_block(block, CORE_FF)] * 2
        + [row_block(block, CHIP_COLS)]
        + [whole(w.shape) for w in weights],
        row_block(block, WIDTH),
        shape((TOKENS, WIDTH)),
        2 * TOKENS * WIDTH * (2 * CORE_FF + CHIP_COLS),
        12 * 2**20,
        (own_act, other_act, attended) + weights,
    )


def normed_part_kernel(
    projected, own_grad, other_grad, rows_ref, attend_ref, own_ref, other_ref, out_ref, sums_ref, bias_ref
):
    total = (
        dot(projected[...], attend_ref[...], NT)
        + dot(own_grad[...], own_ref[...], NT)
        + dot(other_grad[...], other_ref[...], NT)
    )
    out_ref[...] = total.astype(BF16)
    center, inverse = layer_stats(rows_ref[...].astype(F32))
    gain_part = jnp.sum(total * (center * inverse), axis=0, keepdims=True)
    shift_part = jnp.sum(total, axis=0, keepdims=True)
    bias_part = jnp.sum(projected[...].astype(F32), axis=0, keepdims=True)

    @pl.when(pl.program_id(0) == 0)
    def _():
        sums_ref[0:1] = gain_part
        sums_ref[1:2] = shift_part
        bias_ref[...] = bias_part

    @pl.when(pl.program_id(0) > 0)
    def _():
        sums_ref[0:1] += gain_part
        sums_ref[1:2] += shift_part
        bias_ref[...] += bias_part


def normed_part(projected, own_grad, other_grad, rows, attend, own, other):
    block = 256
    width = projected.shape[1]
    weights = (attend, own, other)
    return call(
        normed_part_kernel,
        "normed_part",
        TOKENS // block,
        [row_block(block, width)]
        + [row_block(block, CORE_FF)] * 2
        + [row_block(block, WIDTH)]
        + [whole(w.shape) for w in weights],
        [row_block(block, WIDTH), whole((2, WIDTH)), whole((1, width))],
        [shape((TOKENS, WIDTH)), shape((2, WIDTH), F32), shape((1, width), F32)],
        2 * TOKENS * WIDTH * (2 * CORE_FF + width),
        18 * 2**20,
        (projected, own_grad, other_grad, rows) + weights,
    )


UP_ROWS = WIDTH // SEQ_DEVICES
DOWN_ROWS = CORE_FF // 2
MIX_ROWS = CORE_COLS // 2
PACK_ROWS = DOWN_ROWS + MIX_ROWS
PACK_COLS = CORE_FF
HALF = PACK_COLS // 2
SLOT_COLS = WIDTH // SEQ_DEVICES


def across(rows):
    return pl.BlockSpec((rows, SLOT_COLS), lambda i, order: (0, order[i]))


def plan_call(kernel, name, grid, in_specs, out_specs, out_shape, scratch, flops, moved, order, side, operands):
    return pl.pallas_call(
        kernel,
        grid_spec=pltpu.PrefetchScalarGridSpec(
            num_scalar_prefetch=2,
            grid=(grid,),
            in_specs=in_specs,
            out_specs=out_specs,
            scratch_shapes=scratch,
        ),
        out_shape=out_shape,
        compiler_params=pltpu.CompilerParams(vmem_limit_bytes=60 * 2**20),
        cost_estimate=cost(flops, moved),
        name=name,
    )(order, side, *operands)


def plan_whole(array):
    return pl.BlockSpec(array.shape, lambda i, order, side: (0, 0))


WIDE = 2 * SLOT_COLS
WIDE_COLUMNS = pl.BlockSpec((TOKENS, WIDE), lambda i, order, side: (0, order[i]))


def down_grads_kernel(
    order_ref, x_ref, act_ref, act_other, att_ref, att_other, cot_ref, cot_other, stay_ref, leave_ref
):
    down = dot(act_ref[...], cot_ref[...], TN) + dot(act_other[...], cot_other[...], TN)
    mix = dot(att_ref[...], cot_ref[...], TN) + dot(att_other[...], cot_other[...], TN)
    for x in range(2):

        @pl.when(x_ref[0] == x)
        def _():
            for out_ref, half in ((stay_ref, x), (leave_ref, 1 - x)):
                cols = slice(half * SLOT_COLS, (half + 1) * SLOT_COLS)
                part = down[:, cols].astype(BF16)
                out_ref[0, :DOWN_ROWS, :HALF] = part[:DOWN_ROWS]
                out_ref[0, :DOWN_ROWS, HALF:] = part[DOWN_ROWS:]
                part = mix[:, cols].astype(BF16)
                out_ref[0, DOWN_ROWS:, :HALF] = part[:MIX_ROWS]
                out_ref[0, DOWN_ROWS:, HALF:] = part[MIX_ROWS:]


def down_grads(order, x_lo, act, act_other, att, att_other, cot, cot_other):
    block = pl.BlockSpec((1, PACK_ROWS, PACK_COLS), lambda i, order, side: (i, 0, 0))
    return plan_call(
        down_grads_kernel,
        "down_grads",
        4,
        [plan_whole(a) for a in (act, act_other, att, att_other)] + [WIDE_COLUMNS] * 2,
        [block] * 2,
        [shape((4, PACK_ROWS, PACK_COLS))] * 2,
        [],
        4 * TOKENS * WIDTH * (CORE_FF + CORE_COLS),
        14 * 2**20,
        order,
        x_lo,
        (act, act_other, att, att_other, cot, cot_other),
    )


def up_grads_kernel(order_ref, x_ref, grad_ref, grad_other, normed_ref, normed_other, *refs):
    outs, held = refs[:4], refs[4]
    held[...] = (
        dot(normed_ref[...], grad_ref[...], TN) + dot(normed_other[...], grad_other[...], TN)
    ).astype(BF16)
    for index, out_ref in enumerate(outs):

        @pl.when(pl.program_id(0) == index)
        def _():
            for r, x in enumerate((x_ref[0], 1 - x_ref[0])):
                out_ref[r] = held[pl.ds(pl.multiple_of(x * UP_ROWS, UP_ROWS), UP_ROWS), :]


def up_grads(order, x_lo, grad, grad_other, normed, normed_other):
    block = (2, UP_ROWS, CORE_FF)
    return plan_call(
        up_grads_kernel,
        "up_grads",
        4,
        [plan_whole(grad), plan_whole(grad_other)] + [WIDE_COLUMNS] * 2,
        [pl.BlockSpec(block, lambda i, order, side: (0, 0, 0))] * 4,
        [shape(block)] * 4,
        [pltpu.VMEM((2 * UP_ROWS, CORE_FF), BF16)],
        4 * TOKENS * WIDTH * CORE_FF,
        14 * 2**20,
        order,
        x_lo,
        (grad, grad_other, normed, normed_other),
    )


def attend_grads_kernel(order_ref, core_ref, grad_ref, grad_other, own_0, own_1, other_0, other_1, *refs):
    outs, held = refs[:4], refs[4]
    for half, (own, other) in enumerate(((own_0, other_0), (own_1, other_1))):
        held[half] = (
            dot(own[...], grad_ref[...], TN) + dot(other[...], grad_other[...], TN)
        ).astype(BF16)
    for slot in range(SEQ_DEVICES):
        rows = pl.ds(pl.multiple_of(order_ref[slot] * SLAB, SLAB), SLAB)
        for half in range(2):
            outs[slot // 2][slot % 2, half] = held[half, rows, :]


def attend_grads(order, core, grad, grad_other, normed, normed_other):
    cols = grad.shape[1]

    def rows_of(half):
        return pl.BlockSpec((TOKENS, CORE_COLS), lambda i, order, core: (0, 4 * i + 2 * half + core[0]))

    return plan_call(
        attend_grads_kernel,
        "attend_grads",
        CHIPS // 2,
        [plan_whole(grad), plan_whole(grad_other)] + [rows_of(0), rows_of(1)] * 2,
        [pl.BlockSpec((2, 2, SLAB, cols), lambda i, order, core: (0, i, 0, 0))] * 4,
        [shape((2, CHIPS, SLAB, cols))] * 4,
        [pltpu.VMEM((2, CORE_COLS, cols), BF16)],
        4 * TOKENS * WIDTH * cols // 2,
        12 * 2**20,
        order,
        core,
        (grad, grad_other, normed, normed, normed_other, normed_other),
    )


def unpack_down_kernel(order_ref, *refs):
    down_ref, mix_ref = refs[8:]
    for index, piece in enumerate(refs[:8]):

        @pl.when(pl.program_id(0) == index)
        def _():
            down_ref[:DOWN_ROWS] = piece[:DOWN_ROWS, :HALF].astype(F32)
            down_ref[DOWN_ROWS:] = piece[:DOWN_ROWS, HALF:].astype(F32)
            mix_ref[:MIX_ROWS] = piece[DOWN_ROWS:, :HALF].astype(F32)
            mix_ref[MIX_ROWS:] = piece[DOWN_ROWS:, HALF:].astype(F32)


def unpack_down(order, pieces):
    return placed_call(
        unpack_down_kernel,
        "unpack_down",
        SEQ_DEVICES,
        [fixed((PACK_ROWS, PACK_COLS))] * 8,
        [across(CORE_FF), across(CORE_COLS)],
        [shape((CORE_FF, WIDTH), F32), shape((CORE_COLS, WIDTH), F32)],
        [],
        0,
        8 * 2**20,
        order,
        tuple(pieces),
    )


def unpack_up_kernel(order_ref, *refs):
    for index, piece in enumerate(refs[:8]):

        @pl.when(pl.program_id(0) == index)
        def _():
            refs[8][...] = piece[...].astype(F32)


def unpack_up(order, pieces):
    block = (UP_ROWS, CORE_FF)
    return placed_call(
        unpack_up_kernel,
        "unpack_up",
        SEQ_DEVICES,
        [fixed(block)] * 8,
        pl.BlockSpec(block, lambda i, order: (order[i], 0)),
        shape((WIDTH, CORE_FF), F32),
        [],
        0,
        6 * 2**20,
        order,
        tuple(pieces),
    )


SLAB = CORE_COLS // SEQ_DEVICES


def unpack_attend_kernel(packed_ref, out_ref):
    for chip in range(CHIPS):
        for part in range(3):
            out_ref[:, part * WIDTH + chip * CHIP_COLS : part * WIDTH + (chip + 1) * CHIP_COLS] = (
                packed_ref[0, chip, :, part * CHIP_COLS : (part + 1) * CHIP_COLS].astype(F32)
            )


def unpack_attend(packed):
    return call(
        unpack_attend_kernel,
        "unpack_attend",
        SEQ_DEVICES,
        [pl.BlockSpec((1,) + packed.shape[1:], lambda i: (i, 0, 0, 0))],
        row_block(SLAB, 3 * WIDTH),
        shape((CORE_COLS, 3 * WIDTH), F32),
        0,
        5 * 2**20,
        (packed,),
    )


def rows_grad_kernel(rows_ref, cot_ref, near_ref, far_ref, gain_ref, out_ref):
    grad = near_ref[...].astype(F32) + far_ref[...].astype(F32)
    center, inverse = layer_stats(rows_ref[...].astype(F32))
    unit = center * inverse
    scaled = grad * gain_ref[...]
    out_ref[...] = cot_ref[...].astype(F32) + inverse * (
        scaled
        - jnp.mean(scaled, axis=-1, keepdims=True)
        - unit * jnp.mean(scaled * unit, axis=-1, keepdims=True)
    )


def rows_grad(rows, cot, near, far, gain):
    block = 64
    return call(
        rows_grad_kernel,
        "rows_grad",
        ROWS // block,
        [row_block(block, WIDTH)] * 4 + [whole(gain.shape)],
        row_block(block, WIDTH),
        shape((ROWS, WIDTH), F32),
        0,
        4 * 2**20,
        (rows, cot, near, far, gain),
    )


def lane_masks():
    lane = lax.broadcasted_iota(jnp.int32, (1, PAIR), 1)
    first = (lane < HEAD_DIM).astype(BF16)
    return first, 1 - first


def scores_of(query, keys, low):
    scores = dot(query, keys, NT) * SCALE
    row = low + lax.broadcasted_iota(jnp.int32, scores.shape, 0)
    col = lax.broadcasted_iota(jnp.int32, scores.shape, 1)
    return jnp.where(col <= row, scores, NEG_FILL)


def attend_kernel(query_ref, key_ref, value_ref, out_ref, logsum_ref):
    first, second = lane_masks()
    lane = lax.broadcasted_iota(jnp.int32, (QBLOCK, PAIR), 1)
    for low in range(0, LENGTH, QBLOCK):
        reach = low + QBLOCK
        query = query_ref[low:reach, :]
        keys = key_ref[:reach, :]
        values = value_ref[:reach, :]
        found = []
        for mask in (first, second):
            scores = scores_of(query * mask, keys, low)
            peak = jnp.max(scores, axis=1, keepdims=True)
            weight = jnp.exp(scores - peak)
            total = jnp.sum(weight, axis=1, keepdims=True)
            prob_low = (weight * (1.0 / total)).astype(BF16)
            found.append((dot(prob_low, values), peak + jnp.log(total)))
        out_ref[low:reach, :] = jnp.where(lane < HEAD_DIM, found[0][0], found[1][0]).astype(BF16)
        logsum_ref[low:reach, :] = jnp.where(lane < HEAD_DIM, found[0][1], found[1][1])


def attend_forward(qkv):
    pairs = CHIP_COLS // PAIR
    column = lambda part: pl.BlockSpec((LENGTH, PAIR), lambda p: (0, part * pairs + p))
    return pl.pallas_call(
        attend_kernel,
        grid=(pairs,),
        in_specs=[column(0), column(1), column(2)],
        out_specs=[column(0), column(0)],
        out_shape=[
            jax.ShapeDtypeStruct((LENGTH, CHIP_COLS), BF16),
            jax.ShapeDtypeStruct((LENGTH, CHIP_COLS), F32),
        ],
        compiler_params=pltpu.CompilerParams(vmem_limit_bytes=60 * 2**20),
        cost_estimate=cost(8 * 2**30, 4 * 2**20),
        name="attend_forward",
    )(qkv, qkv, qkv)


def attend_back_kernel(
    query_ref,
    key_ref,
    value_ref,
    grad_ref,
    logsum_ref,
    turn_ref,
    upper_ref,
    lower_ref,
    out_ref,
    key_total,
    value_total,
):
    pair = pl.program_id(0)
    first, second = lane_masks()
    lane = lax.broadcasted_iota(jnp.int32, (QBLOCK, PAIR), 1)
    key_total[...] = jnp.zeros_like(key_total)
    value_total[...] = jnp.zeros_like(value_total)

    def store(part, low, reach, values):
        start = pl.multiple_of((part * (CHIP_COLS // PAIR) + pair) * PAIR, PAIR)
        out_ref[low:reach, pl.ds(start, PAIR)] = values.astype(BF16)

    def unturn(values, low, reach):
        kept = values.astype(BF16).astype(F32)
        return turn_columns(
            kept, turn_ref[low:reach, :], upper_ref[low:reach, :], lower_ref[low:reach, :], -1.0
        )

    for low in range(0, LENGTH, QBLOCK):
        reach = low + QBLOCK
        query = query_ref[low:reach, :]
        grad = grad_ref[low:reach, :]
        keys = key_ref[:reach, :]
        values = value_ref[:reach, :]
        query_grads = []
        key_part = 0.0
        value_part = 0.0
        for head, mask in enumerate((first, second)):
            own_query = query * mask
            own_grad = grad * mask
            scores = scores_of(own_query, keys, low)
            start = head * HEAD_DIM
            probs = jnp.exp(scores - logsum_ref[low:reach, start : start + 1])
            prob_grad = dot(own_grad, values, NT)
            inner = jnp.sum(probs * prob_grad, axis=1, keepdims=True)
            score_grad = (probs * (prob_grad - inner)).astype(BF16)
            query_grads.append(dot(score_grad, keys))
            key_part += dot(score_grad, own_query, TN)
            value_part += dot(probs.astype(BF16), own_grad, TN)
        key_total[:reach, :] += key_part
        value_total[:reach, :] += value_part
        query_grad = jnp.where(lane < HEAD_DIM, query_grads[0], query_grads[1]) * SCALE
        store(0, low, reach, unturn(query_grad, low, reach))
    store(1, 0, LENGTH, unturn(key_total[...] * SCALE, 0, LENGTH))
    store(2, 0, LENGTH, value_total[...])


def attend_backward(qkv, grad, logsum, tables):
    pairs = CHIP_COLS // PAIR
    column = lambda part: pl.BlockSpec((LENGTH, PAIR), lambda p: (0, part * pairs + p))
    whole = lambda shape: pl.BlockSpec(shape, lambda p: (0, 0))
    width = 3 * CHIP_COLS
    return pl.pallas_call(
        attend_back_kernel,
        grid=(pairs,),
        in_specs=[column(0), column(1), column(2), column(0), column(0)]
        + [whole(t.shape) for t in tables],
        out_specs=whole((LENGTH, width)),
        out_shape=jax.ShapeDtypeStruct((LENGTH, width), BF16),
        scratch_shapes=[pltpu.VMEM((LENGTH, PAIR), F32), pltpu.VMEM((LENGTH, PAIR), F32)],
        compiler_params=pltpu.CompilerParams(vmem_limit_bytes=60 * 2**20),
        cost_estimate=cost(20 * 2**30, 6 * 2**20),
        name="attend_backward",
    )(qkv, qkv, qkv, grad, logsum, *tables)


def exchange(blocks, axes):
    return lax.all_to_all(blocks, axes, split_axis=0, concat_axis=0, tiled=True)


def spread(block, axes, count):
    return exchange(jnp.broadcast_to(block[None], (count,) + block.shape), axes)


def after(value, *earlier):
    return lax.optimization_barrier((value,) + earlier)[0]


def sent_y(parts):
    return [send(parts[k], "y", k) for k in (1, 3, 2)]


def sum_seq(parts, arrived):
    leave, stay = (
        parts[0][r].astype(F32) + sum(a[r].astype(F32) for a in arrived) for r in (1, 0)
    )
    return (stay + swap(leave.astype(BF16), "xl").astype(F32)).astype(BF16)


def sum_seq_x_first(parts):
    return (parts[0].astype(F32) + sum(a.astype(F32) for a in sent_y(parts))).astype(BF16)


def spread_seq_y_first(piece):
    near = {0: piece} | {k: shift(piece, "y", k) for k in (1, 3, 2)}
    far = {k: swap(near[k], "xl") for k in (0, 1, 3, 2)}
    return [part[k] for k in range(4) for part in (near, far)]


def spread_seq(piece):
    other = swap(piece, "xl")
    near = {0: piece} | {k: shift(piece, "y", k) for k in (1, 3, 2)}
    far = {0: other} | {k: shift(other, "y", k) for k in (1, 3, 2)}
    return [part[k] for k in range(4) for part in (near, far)]


def sum_rows(parts):
    parts = lax.psum_scatter(
        parts.reshape(4, 2, ROWS, WIDTH), "z", scatter_dimension=0, tiled=False
    )
    return parts[0], swap(parts[1], "xh")


def per_device(
    inputs,
    gains,
    shifts,
    attend,
    attend_bias,
    mixer,
    mixer_bias,
    upward,
    upward_bias,
    downward,
    downward_bias,
    cotangent,
):
    core = lax.axis_index("c")
    x_lo = lax.axis_index("xl")
    chip = lax.axis_index("xh") * 4 + lax.axis_index("z")
    seq_index = lax.axis_index("y") * 2 + x_lo
    core_at = core.reshape(1)
    rows_in = inputs.reshape(ROWS, WIDTH)
    own_cot = cotangent.reshape(ROWS, WIDTH)
    width = 3 * CHIP_COLS

    z_order = (lax.axis_index("z") + jnp.arange(4, dtype=jnp.int32)) % 4
    y_order = (lax.axis_index("y") + jnp.arange(4, dtype=jnp.int32)) % 4
    seq_order = (y_order[:, None] * 2 + jnp.stack([x_lo, 1 - x_lo])[None, :]).reshape(SEQ_DEVICES)

    other_rows = swap(rows_in, "xh")
    slab = lax.dynamic_slice_in_dim(attend, seq_index * SLAB, SLAB, 0)
    slab = slab.reshape(SLAB, 3, CHIPS, CHIP_COLS).transpose(2, 0, 1, 3).reshape(CHIPS, SLAB, width)
    small = jnp.concatenate([gains, shifts, mixer_bias, downward_bias, attend_bias])
    small = jnp.pad(small, (0, 2 * width - small.shape[0])).reshape(1, 2, width)
    small = jnp.pad(jnp.broadcast_to(small, (CHIPS, 2, width)), ((0, 0), (0, SLAB - 2), (0, 0)))
    slab = exchange(jnp.concatenate([slab, small], axis=1), GROUP)
    small_own = slab[:, SLAB : SLAB + 2].reshape(CHIPS, 2 * width)[:, :896]
    slab = slab[:, :SLAB]
    attend_own = spread(slab, SEQ, SEQ_DEVICES).reshape(SEQ_DEVICES, CHIPS, SLAB, width)
    attend_chip = assemble_attend(core_at, attend_own, swap(attend_own, "c"))
    small_other = swap(small_own, "c")
    small_all = jnp.where(
        core == 0, jnp.stack([small_own, small_other], 1), jnp.stack([small_other, small_own], 1)
    ).reshape(FSDP_DEVICES, 7, 128).astype(F32)
    gain_all = small_all[:, 0].reshape(1, WIDTH)
    shift_all = small_all[:, 1].reshape(1, WIDTH)
    out_bias = (small_all[:, 2] + small_all[:, 3]).reshape(WIDTH)
    bias_grid = small_all[:, 4:7].reshape(3, CHIPS, CHIP_COLS)
    attend_bias_chip = lax.dynamic_slice_in_dim(bias_grid, chip, 1, 1).reshape(1, width)

    sent_rows, other_rows = after(rows_in, slab), after(other_rows, attend_own)
    near = {0: rows_in} | {k: shift(sent_rows, "z", k) for k in (1, 3, 2)}
    far = {0: other_rows} | {k: shift(other_rows, "z", k) for k in (1, 3, 2)}
    pieces = [part[k] for part in (near, far) for k in range(4)]

    mixer_other = swap(mixer, "c")
    mixer_chip = jnp.where(
        core == 0, jnp.concatenate([mixer, mixer_other]), jnp.concatenate([mixer_other, mixer])
    )
    up_other = swap(upward, "c")
    down_other = swap(downward, "c")
    up_bias_own = upward_bias.astype(F32).reshape(1, CORE_FF)
    up_bias_other = swap(upward_bias.reshape(1, CORE_FF), "c").astype(F32)

    own_positions = seq_index * ROWS + jnp.arange(ROWS, dtype=jnp.int32)
    own_tables = rope_tables(own_positions, 2 * CHIP_COLS // HEAD_DIM)
    all_tables = rope_tables(jnp.arange(LENGTH, dtype=jnp.int32), 2)

    cot_pair = jnp.stack([own_cot, swap(after(own_cot, near[1]), "xh")])
    cot_pair = after(cot_pair, *pieces)
    cot_group = lax.all_gather(cot_pair, "z", axis=0, tiled=False).reshape(TOKENS, WIDTH)
    rows_group, normed, qkv_sent = norm_project(
        z_order, pieces, gain_all, shift_all, attend_chip, attend_bias_chip, own_tables
    )
    normed_other = swap(normed, "c")
    qkv = exchange(qkv_sent.reshape(CHIPS, ROWS, width), SEQ).reshape(LENGTH, width)
    act_own, act_other, slope_own, slope_other = hidden_forward(
        normed, upward, up_other, up_bias_own, up_bias_other
    )

    attended, logsum = attend_forward(after(qkv, act_own))
    attended_group = exchange(attended.reshape(SEQ_DEVICES, ROWS, CHIP_COLS), SEQ).reshape(
        TOKENS, CHIP_COLS
    )
    cot_group = after(cot_group, attended)
    cot_other = swap(cot_group, "c")
    act_sent = swap(act_other, "c")
    attended_grad = grad_heads(cot_group, mixer_chip)
    grads = exchange(attended_grad.reshape(CHIPS, ROWS, CHIP_COLS), SEQ).reshape(LENGTH, CHIP_COLS)

    parts = out_part(
        act_own, act_other, after(attended_group, attended_grad, cot_other), downward, down_other, mixer_chip
    )
    stay, arrived = sum_rows(parts)
    outputs = (
        rows_in.astype(F32) + out_bias + stay.astype(F32) + arrived.astype(F32)
    ).astype(BF16)

    att_own = lax.dynamic_slice_in_dim(attended_group, core * CORE_COLS, CORE_COLS, 1)
    att_other = lax.dynamic_slice_in_dim(attended_group, (1 - core) * CORE_COLS, CORE_COLS, 1)
    x_at = x_lo.reshape(1)
    down_stay, down_leave = down_grads(
        y_order, x_at, after(act_own, parts), act_sent, att_own, swap(att_other, "c"), cot_group, cot_other
    )
    down_arrived = swap(down_leave, "xl")

    back = attend_backward(qkv, after(grads, down_stay), logsum, all_tables)
    projected_grad = exchange(back.reshape(SEQ_DEVICES, ROWS, width), SEQ).reshape(TOKENS, width)

    grad_own, grad_other, up_bias_sum, up_bias_other_sum = hidden_back(
        after(cot_group, back), downward, down_other, slope_own, slope_other
    )
    up_slabs = up_grads(y_order, x_at, grad_own, swap(grad_other, "c"), normed, normed_other)
    up_arrived = sent_y(up_slabs)

    projected_grad = after(projected_grad, up_slabs[0])
    down_parts = (down_stay.astype(F32) + down_arrived.astype(F32)).astype(BF16)
    projected_grad, down_parts = lax.optimization_barrier((projected_grad, down_parts))
    attend_slabs = attend_grads(
        seq_order,
        core_at,
        projected_grad,
        swap(projected_grad, "c"),
        normed,
        normed_other,
    )
    down_sum = sum_seq_x_first(down_parts)

    parts, norm_sums, attend_bias_sum = normed_part(
        after(projected_grad, attend_slabs[0], up_arrived[0]),
        grad_own,
        grad_other,
        rows_group,
        attend_chip,
        upward,
        up_other,
    )
    stay, arrived = sum_rows(parts)
    inputs_grad = rows_grad(rows_in, own_cot, stay, arrived, gain_all)

    attend_slab = exchange(sum_seq(attend_slabs, sent_y(attend_slabs)), GROUP)
    attend_grad = unpack_attend(spread(attend_slab, SEQ, SEQ_DEVICES).reshape(
        SEQ_DEVICES, CHIPS, SLAB, width
    ))
    down_grad, mixer_grad = unpack_down(seq_order, spread_seq_y_first(down_sum))
    up_grad = unpack_up(seq_order, spread_seq(sum_seq(up_slabs, up_arrived)))

    bias_full = jnp.sum(own_cot.astype(F32), axis=0)
    attend_bias_full = lax.dynamic_update_slice(
        jnp.zeros((3, CHIPS, CHIP_COLS), F32), attend_bias_sum.reshape(3, 1, CHIP_COLS), (0, chip, 0)
    )
    up_bias_pair = jnp.where(
        core == 0,
        jnp.concatenate([up_bias_sum, up_bias_other_sum]),
        jnp.concatenate([up_bias_other_sum, up_bias_sum]),
    )
    up_bias_full = lax.dynamic_update_slice(
        jnp.zeros((CHIPS, 2, CORE_FF), F32), up_bias_pair[None], (chip, 0, 0)
    )
    vectors = jnp.concatenate(
        [
            v.reshape(FSDP_DEVICES, -1)
            for v in (norm_sums[0], norm_sums[1], bias_full, attend_bias_full, up_bias_full)
        ],
        axis=1,
    )
    vectors = jnp.sum(exchange(vectors, FSDP), axis=0)
    vectors = jnp.sum(spread(vectors, SEQ, SEQ_DEVICES), axis=0)
    gain_grad, shift_grad, bias_grad = vectors[:128], vectors[128:256], vectors[256:384]
    attend_bias_grad, up_bias_grad = vectors[384:768], vectors[768:]

    return (
        outputs.reshape(inputs.shape),
        inputs_grad.reshape(inputs.shape),
        gain_grad,
        shift_grad,
        attend_grad,
        attend_bias_grad,
        mixer_grad,
        bias_grad,
        up_grad,
        up_bias_grad,
        down_grad,
        bias_grad,
    )


def solution(mesh):
    fine = Mesh(mesh.devices.reshape(4, 2, 2, 4, 2), ("y", "xl", "xh", "z", "c"))
    rows = P(FSDP, SEQ, None)
    vector = P(FSDP)
    by_row = P(FSDP, None)
    by_col = P(None, FSDP)
    in_specs = (
        rows,
        vector,
        vector,
        by_row,
        vector,
        by_row,
        vector,
        by_col,
        vector,
        by_row,
        vector,
        rows,
    )
    out_specs = (
        rows,
        rows,
        vector,
        vector,
        by_row,
        vector,
        by_row,
        vector,
        by_col,
        vector,
        by_row,
        vector,
    )
    return jax.shard_map(
        per_device, mesh=fine, in_specs=in_specs, out_specs=out_specs, check_vma=False
    )
```

```python
import jax
import jax.numpy as jnp
from jax import lax
from jax.experimental import pallas as pl
from jax.experimental.pallas import tpu as pltpu
from jax.sharding import Mesh, PartitionSpec as P

HEADS = 32
HEAD_DIM = 64
ROT = 32
WIDTH = 2048
FF = 8192
SEQ_DEVICES = 8
CHIPS = 8
FSDP_DEVICES = 16
ROWS = 128
LENGTH = ROWS * SEQ_DEVICES
TOKENS = ROWS * CHIPS
CHIP_COLS = WIDTH // CHIPS
CORE_COLS = WIDTH // FSDP_DEVICES
CORE_FF = FF // FSDP_DEVICES
PAIR = 2 * HEAD_DIM
QBLOCK = 256

EPSILON = 1e-05
ROPE_BASE = 10000.0
NEG_FILL = -1e30
LIGHTER = 8
SCALE = HEAD_DIM ** (-0.5)

F32 = jnp.float32
BF16 = jnp.bfloat16

SEQ = ("y", "xl")
GROUP = ("xh", "z")
FSDP = ("xh", "z", "c")

NT = (((1,), (1,)), ((), ()))
TN = (((0,), (0,)), ((), ()))
NN = (((1,), (0,)), ((), ()))


def dot(lhs, rhs, dims=NN):
    return lax.dot_general(lhs, rhs, dims, preferred_element_type=F32)


def swap(piece, axis):
    return lax.ppermute(piece, axis, [(0, 1), (1, 0)])


def shift(piece, axis, step):
    return lax.ppermute(piece, axis, [(i, (i - step) % 4) for i in range(4)])


def send(piece, axis, step):
    return lax.ppermute(piece, axis, [(i, (i + step) % 4) for i in range(4)])


def rope_tables(positions, heads):
    half = ROT // 2
    frequency = ROPE_BASE ** (-2.0 * jnp.arange(half, dtype=F32) / ROT)
    angle = positions.astype(F32)[:, None] * frequency[None, :]
    cosine, sine = jnp.cos(angle), jnp.sin(angle)
    rest = jnp.zeros((positions.shape[0], HEAD_DIM - ROT), F32)
    blank = jnp.zeros_like(sine)
    turn = jnp.concatenate([cosine, cosine, rest + 1.0], axis=1)
    upper = jnp.concatenate([-sine, blank, rest], axis=1)
    lower = jnp.concatenate([blank, sine, rest], axis=1)
    return tuple(jnp.tile(t, (1, heads)) for t in (turn, upper, lower))


def turn_columns(values, turn, upper, lower, sign):
    width = values.shape[1]
    half = ROT // 2
    ahead = pltpu.roll(values, width - half, 1)
    behind = pltpu.roll(values, half, 1)
    return values * turn + sign * (ahead * upper + behind * lower)


def cost(flops, moved):
    return pl.CostEstimate(flops=flops // LIGHTER, bytes_accessed=moved // LIGHTER, transcendentals=0)


def whole(shape):
    return pl.BlockSpec(shape, lambda i: (0,) * len(shape))


def row_block(rows, width, column=0):
    return pl.BlockSpec((rows, width), lambda i: (i, column))


def call(
    kernel, name, grid, in_specs, out_specs, out_shape, flops, moved, operands, late=(), scratch=(), plan=()
):
    first, last = len(plan) + len(operands), len(plan) + len(operands) + len(late)

    def body(*refs):
        kernel(*refs[:first], *refs[last:])

    return pl.pallas_call(
        body,
        grid_spec=pltpu.PrefetchScalarGridSpec(
            num_scalar_prefetch=len(plan),
            grid=(grid,),
            in_specs=list(in_specs) + [pl.BlockSpec(memory_space=pl.ANY)] * len(late),
            out_specs=out_specs,
            scratch_shapes=list(scratch),
        ),
        out_shape=out_shape,
        compiler_params=pltpu.CompilerParams(vmem_limit_bytes=60 * 2**20),
        cost_estimate=cost(flops, moved),
        name=name,
    )(*plan, *operands, *late)


def placed_call(
    kernel, name, grid, in_specs, out_specs, out_shape, scratch, flops, moved, order, operands, late=()
):
    return call(
        kernel, name, grid, in_specs, out_specs, out_shape, flops, moved, operands, late, scratch, (order,)
    )


def fixed(dims):
    return pl.BlockSpec(dims, lambda i, order: (0,) * len(dims))


def shape(dims, kind=BF16):
    return jax.ShapeDtypeStruct(dims, kind)


def layer_stats(rows):
    center = rows - jnp.mean(rows, axis=-1, keepdims=True)
    spread_out = jnp.mean(center * center, axis=-1, keepdims=True)
    return center, lax.rsqrt(spread_out + EPSILON)


def assemble_kernel(core_ref, own_ref, other_ref, out_ref):
    core = core_ref[0]
    out_ref[0, core] = own_ref[...].reshape(out_ref.shape[2:])
    out_ref[0, 1 - core] = other_ref[...].reshape(out_ref.shape[2:])


def assemble_attend(core, own, other):
    slab, cols = own.shape[2:]
    piece = pl.BlockSpec((SEQ_DEVICES, 1, slab, cols), lambda g, core: (0, g, 0, 0))
    out = (CHIPS, 2, SEQ_DEVICES, slab, cols)
    return pl.pallas_call(
        assemble_kernel,
        grid_spec=pltpu.PrefetchScalarGridSpec(
            num_scalar_prefetch=1,
            grid=(CHIPS,),
            in_specs=[piece, piece],
            out_specs=pl.BlockSpec((1,) + out[1:], lambda g, core: (g, 0, 0, 0, 0)),
        ),
        out_shape=shape(out),
        compiler_params=pltpu.CompilerParams(vmem_limit_bytes=60 * 2**20),
        cost_estimate=cost(0, 6 * 2**20),
        name="assemble_attend",
    )(core, own, other).reshape(WIDTH, cols)


def norm_project_kernel(
    order_ref,
    near_0,
    near_1,
    near_2,
    near_3,
    far_0,
    far_1,
    far_2,
    far_3,
    gain_ref,
    shift_ref,
    weight_ref,
    bias_ref,
    turn_ref,
    upper_ref,
    lower_ref,
    rows_ref,
    normed_ref,
    out_ref,
):
    step = pl.program_id(0)
    pairs = ((near_0, far_0), (near_1, far_1), (near_2, far_2), (near_3, far_3))
    for index, (near, far) in enumerate(pairs):

        @pl.when(step == index)
        def _():
            rows_ref[:ROWS] = near[...]
            rows_ref[ROWS:] = far[...]

    center, inverse = layer_stats(rows_ref[...].astype(F32))
    normed = (center * inverse * gain_ref[...] + shift_ref[...]).astype(BF16)
    normed_ref[...] = normed
    projected = dot(normed, weight_ref[...]) + bias_ref[...]
    turned_width = 2 * CHIP_COLS
    for block in range(2):
        rows = slice(block * ROWS, (block + 1) * ROWS)
        out_ref[rows, :turned_width] = turn_columns(
            projected[rows, :turned_width], turn_ref[...], upper_ref[...], lower_ref[...], 1.0
        ).astype(BF16)
    out_ref[:, turned_width:] = projected[:, turned_width:].astype(BF16)


def norm_project(order, pieces, gain, shift_row, weight, bias, tables):
    block = 2 * ROWS
    width = weight.shape[1]
    vectors = (gain, shift_row, weight, bias) + tables
    out = lambda cols: pl.BlockSpec((block, cols), lambda i, order: (order[i], 0))
    return placed_call(
        norm_project_kernel,
        "norm_project",
        4,
        [fixed((ROWS, WIDTH))] * 8 + [fixed(v.shape) for v in vectors],
        [out(WIDTH), out(WIDTH), out(width)],
        [shape((TOKENS, WIDTH)), shape((TOKENS, WIDTH)), shape((TOKENS, width))],
        [],
        2 * TOKENS * WIDTH * width,
        18 * 2**20,
        order,
        tuple(pieces) + vectors,
    )


def hidden_kernel(
    normed_ref,
    own_ref,
    other_ref,
    own_bias_ref,
    other_bias_ref,
    own_act_ref,
    other_act_ref,
    own_slope_ref,
    other_slope_ref,
):
    root = (2.0 / 3.141592653589793) ** 0.5
    for weight, bias, act, slope in (
        (own_ref, own_bias_ref, own_act_ref, own_slope_ref),
        (other_ref, other_bias_ref, other_act_ref, other_slope_ref),
    ):
        hidden = dot(normed_ref[...], weight[...]) + bias[...]
        square = hidden * hidden
        bend = jnp.tanh(root * hidden * (1.0 + 0.044715 * square))
        half = 0.5 * (1.0 + bend)
        act[...] = (hidden * half).astype(BF16)
        slope[...] = half + 0.5 * hidden * (1.0 - bend * bend) * (
            root * (1.0 + 3.0 * 0.044715 * square)
        )


def hidden_forward(normed, own, other, own_bias, other_bias):
    block = 256
    operands = (own, other, own_bias, other_bias)
    return call(
        hidden_kernel,
        "hidden_forward",
        TOKENS // block,
        [row_block(block, WIDTH)] + [whole(v.shape) for v in operands],
        [row_block(block, CORE_FF)] * 4,
        [shape((TOKENS, CORE_FF))] * 2 + [shape((TOKENS, CORE_FF), F32)] * 2,
        4 * TOKENS * WIDTH * CORE_FF,
        14 * 2**20,
        (normed,) + operands,
    )


def grad_heads_kernel(cot_ref, mixer_ref, out_ref):
    out_ref[...] = dot(cot_ref[...], mixer_ref[...], NT).astype(BF16)


def grad_heads(cot, mixer, late):
    block = 256
    return call(
        grad_heads_kernel,
        "grad_heads",
        TOKENS // block,
        [row_block(block, WIDTH), whole(mixer.shape)],
        row_block(block, CHIP_COLS),
        shape((TOKENS, CHIP_COLS)),
        2 * TOKENS * WIDTH * CHIP_COLS,
        6 * 2**20,
        (cot, mixer),
        late,
    )


def hidden_back_kernel(
    cot_ref, own_ref, other_ref, own_slope_ref, other_slope_ref, own_out, other_out, own_sum, other_sum
):
    for weight, slope, out, total in (
        (own_ref, own_slope_ref, own_out, own_sum),
        (other_ref, other_slope_ref, other_out, other_sum),
    ):
        grad = (dot(cot_ref[...], weight[...], NT) * slope[...]).astype(BF16)
        out[...] = grad
        part = jnp.sum(grad.astype(F32), axis=0, keepdims=True)

        @pl.when(pl.program_id(0) == 0)
        def _():
            total[...] = part

        @pl.when(pl.program_id(0) > 0)
        def _():
            total[...] += part


def hidden_back(cot, own, other, own_slope, other_slope, late):
    block = 256
    return call(
        hidden_back_kernel,
        "hidden_back",
        TOKENS // block,
        [row_block(block, WIDTH), whole(own.shape), whole(other.shape)]
        + [row_block(block, CORE_FF)] * 2,
        [row_block(block, CORE_FF)] * 2 + [whole((1, CORE_FF))] * 2,
        [shape((TOKENS, CORE_FF))] * 2 + [shape((1, CORE_FF), F32)] * 2,
        4 * TOKENS * WIDTH * CORE_FF,
        14 * 2**20,
        (cot, own, other, own_slope, other_slope),
        late,
    )


def out_part_kernel(own_act, other_act, attended, own_ref, other_ref, mixer_ref, out_ref):
    out_ref[...] = (
        dot(own_act[...], own_ref[...])
        + dot(other_act[...], other_ref[...])
        + dot(attended[...], mixer_ref[...])
    ).astype(BF16)


def out_part(own_act, other_act, attended, own, other, mixer, late):
    block = 256
    weights = (own, other, mixer)
    return call(
        out_part_kernel,
        "out_part",
        TOKENS // block,
        [row_block(block, CORE_FF)] * 2
        + [row_block(block, CHIP_COLS)]
        + [whole(w.shape) for w in weights],
        row_block(block, WIDTH),
        shape((TOKENS, WIDTH)),
        2 * TOKENS * WIDTH * (2 * CORE_FF + CHIP_COLS),
        12 * 2**20,
        (own_act, other_act, attended) + weights,
        late,
    )


def normed_part_kernel(
    projected, own_grad, other_grad, rows_ref, attend_ref, own_ref, other_ref, out_ref, sums_ref, bias_ref
):
    total = (
        dot(projected[...], attend_ref[...], NT)
        + dot(own_grad[...], own_ref[...], NT)
        + dot(other_grad[...], other_ref[...], NT)
    )
    out_ref[...] = total.astype(BF16)
    center, inverse = layer_stats(rows_ref[...].astype(F32))
    gain_part = jnp.sum(total * (center * inverse), axis=0, keepdims=True)
    shift_part = jnp.sum(total, axis=0, keepdims=True)
    bias_part = jnp.sum(projected[...].astype(F32), axis=0, keepdims=True)

    @pl.when(pl.program_id(0) == 0)
    def _():
        sums_ref[0:1] = gain_part
        sums_ref[1:2] = shift_part
        bias_ref[...] = bias_part

    @pl.when(pl.program_id(0) > 0)
    def _():
        sums_ref[0:1] += gain_part
        sums_ref[1:2] += shift_part
        bias_ref[...] += bias_part


def normed_part(projected, own_grad, other_grad, rows, attend, own, other, late):
    block = 256
    width = projected.shape[1]
    weights = (attend, own, other)
    return call(
        normed_part_kernel,
        "normed_part",
        TOKENS // block,
        [row_block(block, width)]
        + [row_block(block, CORE_FF)] * 2
        + [row_block(block, WIDTH)]
        + [whole(w.shape) for w in weights],
        [row_block(block, WIDTH), whole((2, WIDTH)), whole((1, width))],
        [shape((TOKENS, WIDTH)), shape((2, WIDTH), F32), shape((1, width), F32)],
        2 * TOKENS * WIDTH * (2 * CORE_FF + width),
        18 * 2**20,
        (projected, own_grad, other_grad, rows) + weights,
        late,
    )


UP_ROWS = WIDTH // SEQ_DEVICES
DOWN_ROWS = CORE_FF // 2
MIX_ROWS = CORE_COLS // 2
PACK_ROWS = DOWN_ROWS + MIX_ROWS
PACK_COLS = CORE_FF
HALF = PACK_COLS // 2
SLOT_COLS = WIDTH // SEQ_DEVICES


def across(rows):
    return pl.BlockSpec((rows, SLOT_COLS), lambda i, order: (0, order[i]))


def plan_call(
    kernel, name, grid, in_specs, out_specs, out_shape, scratch, flops, moved, order, side, operands, late=()
):
    return call(
        kernel, name, grid, in_specs, out_specs, out_shape, flops, moved, operands, late, scratch, (order, side)
    )


def plan_whole(array):
    return pl.BlockSpec(array.shape, lambda i, order, side: (0, 0))


WIDE = 2 * SLOT_COLS
WIDE_COLUMNS = pl.BlockSpec((TOKENS, WIDE), lambda i, order, side: (0, order[i]))


def down_grads_kernel(
    order_ref, x_ref, act_ref, act_other, att_ref, att_other, cot_ref, cot_other, stay_ref, leave_ref
):
    down = dot(act_ref[...], cot_ref[...], TN) + dot(act_other[...], cot_other[...], TN)
    mix = dot(att_ref[...], cot_ref[...], TN) + dot(att_other[...], cot_other[...], TN)
    for x in range(2):

        @pl.when(x_ref[0] == x)
        def _():
            for out_ref, half in ((stay_ref, x), (leave_ref, 1 - x)):
                cols = slice(half * SLOT_COLS, (half + 1) * SLOT_COLS)
                part = down[:, cols].astype(BF16)
                out_ref[0, :DOWN_ROWS, :HALF] = part[:DOWN_ROWS]
                out_ref[0, :DOWN_ROWS, HALF:] = part[DOWN_ROWS:]
                part = mix[:, cols].astype(BF16)
                out_ref[0, DOWN_ROWS:, :HALF] = part[:MIX_ROWS]
                out_ref[0, DOWN_ROWS:, HALF:] = part[MIX_ROWS:]


def down_grads(order, x_lo, act, act_other, att, att_other, cot, cot_other, late):
    block = pl.BlockSpec((1, PACK_ROWS, PACK_COLS), lambda i, order, side: (i, 0, 0))
    return plan_call(
        down_grads_kernel,
        "down_grads",
        4,
        [plan_whole(a) for a in (act, act_other, att, att_other)] + [WIDE_COLUMNS] * 2,
        [block] * 2,
        [shape((4, PACK_ROWS, PACK_COLS))] * 2,
        [],
        4 * TOKENS * WIDTH * (CORE_FF + CORE_COLS),
        14 * 2**20,
        order,
        x_lo,
        (act, act_other, att, att_other, cot, cot_other),
        late,
    )


def up_grads_kernel(order_ref, x_ref, grad_ref, grad_other, normed_ref, normed_other, *refs):
    outs, held = refs[:4], refs[4]
    held[...] = (
        dot(normed_ref[...], grad_ref[...], TN) + dot(normed_other[...], grad_other[...], TN)
    ).astype(BF16)
    for index, out_ref in enumerate(outs):

        @pl.when(pl.program_id(0) == index)
        def _():
            for r, x in enumerate((x_ref[0], 1 - x_ref[0])):
                out_ref[r] = held[pl.ds(pl.multiple_of(x * UP_ROWS, UP_ROWS), UP_ROWS), :]


def up_grads(order, x_lo, grad, grad_other, normed, normed_other, late):
    block = (2, UP_ROWS, CORE_FF)
    return plan_call(
        up_grads_kernel,
        "up_grads",
        4,
        [plan_whole(grad), plan_whole(grad_other)] + [WIDE_COLUMNS] * 2,
        [pl.BlockSpec(block, lambda i, order, side: (0, 0, 0))] * 4,
        [shape(block)] * 4,
        [pltpu.VMEM((2 * UP_ROWS, CORE_FF), BF16)],
        4 * TOKENS * WIDTH * CORE_FF,
        14 * 2**20,
        order,
        x_lo,
        (grad, grad_other, normed, normed_other),
        late,
    )


def attend_grads_kernel(order_ref, core_ref, grad_ref, grad_other, own_0, own_1, other_0, other_1, *refs):
    outs, held = refs[:4], refs[4]
    for half, (own, other) in enumerate(((own_0, other_0), (own_1, other_1))):
        held[half] = (
            dot(own[...], grad_ref[...], TN) + dot(other[...], grad_other[...], TN)
        ).astype(BF16)
    for slot in range(SEQ_DEVICES):
        rows = pl.ds(pl.multiple_of(order_ref[slot] * SLAB, SLAB), SLAB)
        for half in range(2):
            outs[slot // 2][slot % 2, half] = held[half, rows, :]


def attend_grads(order, core, grad, grad_other, normed, normed_other, late):
    cols = grad.shape[1]

    def rows_of(half):
        return pl.BlockSpec((TOKENS, CORE_COLS), lambda i, order, core: (0, 4 * i + 2 * half + core[0]))

    return plan_call(
        attend_grads_kernel,
        "attend_grads",
        CHIPS // 2,
        [plan_whole(grad), plan_whole(grad_other)] + [rows_of(0), rows_of(1)] * 2,
        [pl.BlockSpec((2, 2, SLAB, cols), lambda i, order, core: (0, i, 0, 0))] * 4,
        [shape((2, CHIPS, SLAB, cols))] * 4,
        [pltpu.VMEM((2, CORE_COLS, cols), BF16)],
        4 * TOKENS * WIDTH * cols // 2,
        12 * 2**20,
        order,
        core,
        (grad, grad_other, normed, normed, normed_other, normed_other),
        late,
    )


def unpack_down_kernel(order_ref, *refs):
    down_ref, mix_ref = refs[8:]
    for index, piece in enumerate(refs[:8]):

        @pl.when(pl.program_id(0) == index)
        def _():
            down_ref[:DOWN_ROWS] = piece[:DOWN_ROWS, :HALF].astype(F32)
            down_ref[DOWN_ROWS:] = piece[:DOWN_ROWS, HALF:].astype(F32)
            mix_ref[:MIX_ROWS] = piece[DOWN_ROWS:, :HALF].astype(F32)
            mix_ref[MIX_ROWS:] = piece[DOWN_ROWS:, HALF:].astype(F32)


def unpack_down(order, pieces):
    return placed_call(
        unpack_down_kernel,
        "unpack_down",
        SEQ_DEVICES,
        [fixed((PACK_ROWS, PACK_COLS))] * 8,
        [across(CORE_FF), across(CORE_COLS)],
        [shape((CORE_FF, WIDTH), F32), shape((CORE_COLS, WIDTH), F32)],
        [],
        0,
        8 * 2**20,
        order,
        tuple(pieces),
    )


def unpack_up_kernel(order_ref, *refs):
    for index, piece in enumerate(refs[:8]):

        @pl.when(pl.program_id(0) == index)
        def _():
            refs[8][...] = piece[...].astype(F32)


def unpack_up(order, pieces):
    block = (UP_ROWS, CORE_FF)
    return placed_call(
        unpack_up_kernel,
        "unpack_up",
        SEQ_DEVICES,
        [fixed(block)] * 8,
        pl.BlockSpec(block, lambda i, order: (order[i], 0)),
        shape((WIDTH, CORE_FF), F32),
        [],
        0,
        6 * 2**20,
        order,
        tuple(pieces),
    )


SLAB = CORE_COLS // SEQ_DEVICES


def unpack_attend_kernel(packed_ref, out_ref):
    for chip in range(CHIPS):
        for part in range(3):
            out_ref[:, part * WIDTH + chip * CHIP_COLS : part * WIDTH + (chip + 1) * CHIP_COLS] = (
                packed_ref[0, chip, :, part * CHIP_COLS : (part + 1) * CHIP_COLS].astype(F32)
            )


def unpack_attend(packed):
    return call(
        unpack_attend_kernel,
        "unpack_attend",
        SEQ_DEVICES,
        [pl.BlockSpec((1,) + packed.shape[1:], lambda i: (i, 0, 0, 0))],
        row_block(SLAB, 3 * WIDTH),
        shape((CORE_COLS, 3 * WIDTH), F32),
        0,
        5 * 2**20,
        (packed,),
    )


def rows_grad_kernel(rows_ref, cot_ref, near_ref, far_ref, gain_ref, out_ref):
    grad = near_ref[...].astype(F32) + far_ref[...].astype(F32)
    center, inverse = layer_stats(rows_ref[...].astype(F32))
    unit = center * inverse
    scaled = grad * gain_ref[...]
    out_ref[...] = cot_ref[...].astype(F32) + inverse * (
        scaled
        - jnp.mean(scaled, axis=-1, keepdims=True)
        - unit * jnp.mean(scaled * unit, axis=-1, keepdims=True)
    )


def rows_grad(rows, cot, near, far, gain):
    block = 64
    return call(
        rows_grad_kernel,
        "rows_grad",
        ROWS // block,
        [row_block(block, WIDTH)] * 4 + [whole(gain.shape)],
        row_block(block, WIDTH),
        shape((ROWS, WIDTH), F32),
        0,
        4 * 2**20,
        (rows, cot, near, far, gain),
    )


def lane_masks():
    lane = lax.broadcasted_iota(jnp.int32, (1, PAIR), 1)
    first = (lane < HEAD_DIM).astype(BF16)
    return first, 1 - first


def scores_of(query, keys, low):
    scores = dot(query, keys, NT) * SCALE
    row = low + lax.broadcasted_iota(jnp.int32, scores.shape, 0)
    col = lax.broadcasted_iota(jnp.int32, scores.shape, 1)
    return jnp.where(col <= row, scores, NEG_FILL)


def attend_kernel(query_ref, key_ref, value_ref, out_ref, logsum_ref):
    first, second = lane_masks()
    lane = lax.broadcasted_iota(jnp.int32, (QBLOCK, PAIR), 1)
    for low in range(0, LENGTH, QBLOCK):
        reach = low + QBLOCK
        query = query_ref[low:reach, :]
        keys = key_ref[:reach, :]
        values = value_ref[:reach, :]
        found = []
        for mask in (first, second):
            scores = scores_of(query * mask, keys, low)
            peak = jnp.max(scores, axis=1, keepdims=True)
            weight = jnp.exp(scores - peak)
            total = jnp.sum(weight, axis=1, keepdims=True)
            prob_low = (weight * (1.0 / total)).astype(BF16)
            found.append((dot(prob_low, values), peak + jnp.log(total)))
        out_ref[low:reach, :] = jnp.where(lane < HEAD_DIM, found[0][0], found[1][0]).astype(BF16)
        logsum_ref[low:reach, :] = jnp.where(lane < HEAD_DIM, found[0][1], found[1][1])


def pair_columns(part):
    return pl.BlockSpec((LENGTH, PAIR), lambda p: (0, part * (CHIP_COLS // PAIR) + p))


def attend_forward(qkv, late):
    return call(
        attend_kernel,
        "attend_forward",
        CHIP_COLS // PAIR,
        [pair_columns(0), pair_columns(1), pair_columns(2)],
        [pair_columns(0)] * 2,
        [shape((LENGTH, CHIP_COLS)), shape((LENGTH, CHIP_COLS), F32)],
        8 * 2**30,
        4 * 2**20,
        (qkv, qkv, qkv),
        late,
    )


def attend_back_kernel(
    query_ref,
    key_ref,
    value_ref,
    grad_ref,
    logsum_ref,
    turn_ref,
    upper_ref,
    lower_ref,
    out_ref,
    key_total,
    value_total,
):
    pair = pl.program_id(0)
    first, second = lane_masks()
    lane = lax.broadcasted_iota(jnp.int32, (QBLOCK, PAIR), 1)
    key_total[...] = jnp.zeros_like(key_total)
    value_total[...] = jnp.zeros_like(value_total)

    def store(part, low, reach, values):
        start = pl.multiple_of((part * (CHIP_COLS // PAIR) + pair) * PAIR, PAIR)
        out_ref[low:reach, pl.ds(start, PAIR)] = values.astype(BF16)

    def unturn(values, low, reach):
        kept = values.astype(BF16).astype(F32)
        return turn_columns(
            kept, turn_ref[low:reach, :], upper_ref[low:reach, :], lower_ref[low:reach, :], -1.0
        )

    for low in range(0, LENGTH, QBLOCK):
        reach = low + QBLOCK
        query = query_ref[low:reach, :]
        grad = grad_ref[low:reach, :]
        keys = key_ref[:reach, :]
        values = value_ref[:reach, :]
        query_grads = []
        key_part = 0.0
        value_part = 0.0
        for head, mask in enumerate((first, second)):
            own_query = query * mask
            own_grad = grad * mask
            scores = scores_of(own_query, keys, low)
            start = head * HEAD_DIM
            probs = jnp.exp(scores - logsum_ref[low:reach, start : start + 1])
            prob_grad = dot(own_grad, values, NT)
            inner = jnp.sum(probs * prob_grad, axis=1, keepdims=True)
            score_grad = (probs * (prob_grad - inner)).astype(BF16)
            query_grads.append(dot(score_grad, keys))
            key_part += dot(score_grad, own_query, TN)
            value_part += dot(probs.astype(BF16), own_grad, TN)
        key_total[:reach, :] += key_part
        value_total[:reach, :] += value_part
        query_grad = jnp.where(lane < HEAD_DIM, query_grads[0], query_grads[1]) * SCALE
        store(0, low, reach, unturn(query_grad, low, reach))
    store(1, 0, LENGTH, unturn(key_total[...] * SCALE, 0, LENGTH))
    store(2, 0, LENGTH, value_total[...])


def attend_backward(qkv, grad, logsum, tables, late):
    return call(
        attend_back_kernel,
        "attend_backward",
        CHIP_COLS // PAIR,
        [pair_columns(0), pair_columns(1), pair_columns(2), pair_columns(0), pair_columns(0)]
        + [whole(t.shape) for t in tables],
        whole((LENGTH, 3 * CHIP_COLS)),
        shape((LENGTH, 3 * CHIP_COLS)),
        20 * 2**30,
        6 * 2**20,
        (qkv, qkv, qkv, grad, logsum) + tables,
        late,
        [pltpu.VMEM((LENGTH, PAIR), F32)] * 2,
    )


def exchange(blocks, axes):
    return lax.all_to_all(blocks, axes, split_axis=0, concat_axis=0, tiled=True)


def spread(block, axes, count):
    return exchange(jnp.broadcast_to(block[None], (count,) + block.shape), axes)


def gate(value):
    return swap(value.reshape(-1, value.shape[-1])[:16, :128], "c")


tie = lax.optimization_barrier


def sent_y(parts):
    return [send(parts[k], "y", k) for k in (1, 3, 2)]


def sum_seq(parts, arrived):
    leave, stay = (
        parts[0][r].astype(F32) + sum(a[r].astype(F32) for a in arrived) for r in (1, 0)
    )
    return (stay + swap(leave.astype(BF16), "xl").astype(F32)).astype(BF16)


def sum_seq_x_first(parts):
    return (parts[0].astype(F32) + sum(a.astype(F32) for a in sent_y(parts))).astype(BF16)


def spread_seq_y_first(piece):
    near = {0: piece} | {k: shift(piece, "y", k) for k in (1, 3, 2)}
    far = {k: swap(near[k], "xl") for k in (0, 1, 3, 2)}
    return [part[k] for k in range(4) for part in (near, far)]


def spread_seq(piece):
    other = swap(piece, "xl")
    near = {0: piece} | {k: shift(piece, "y", k) for k in (1, 3, 2)}
    far = {0: other} | {k: shift(other, "y", k) for k in (1, 3, 2)}
    return [part[k] for k in range(4) for part in (near, far)]


def sum_rows(parts):
    parts = lax.psum_scatter(
        parts.reshape(4, 2, ROWS, WIDTH), "z", scatter_dimension=0, tiled=False
    )
    return parts[0], swap(parts[1], "xh")


def per_device(
    inputs,
    gains,
    shifts,
    attend,
    attend_bias,
    mixer,
    mixer_bias,
    upward,
    upward_bias,
    downward,
    downward_bias,
    cotangent,
):
    core = lax.axis_index("c")
    x_lo = lax.axis_index("xl")
    chip = lax.axis_index("xh") * 4 + lax.axis_index("z")
    seq_index = lax.axis_index("y") * 2 + x_lo
    core_at = core.reshape(1)
    rows_in = inputs.reshape(ROWS, WIDTH)
    own_cot = cotangent.reshape(ROWS, WIDTH)
    width = 3 * CHIP_COLS

    z_order = (lax.axis_index("z") + jnp.arange(4, dtype=jnp.int32)) % 4
    y_order = (lax.axis_index("y") + jnp.arange(4, dtype=jnp.int32)) % 4
    seq_order = (y_order[:, None] * 2 + jnp.stack([x_lo, 1 - x_lo])[None, :]).reshape(SEQ_DEVICES)

    other_rows = swap(rows_in, "xh")
    slab = lax.dynamic_slice_in_dim(attend, seq_index * SLAB, SLAB, 0)
    slab = slab.reshape(SLAB, 3, CHIPS, CHIP_COLS).transpose(2, 0, 1, 3).reshape(CHIPS, SLAB, width)
    small = jnp.concatenate([gains, shifts, mixer_bias, downward_bias, attend_bias])
    small = jnp.pad(small, (0, 2 * width - small.shape[0])).reshape(1, 2, width)
    small = jnp.pad(jnp.broadcast_to(small, (CHIPS, 2, width)), ((0, 0), (0, SLAB - 2), (0, 0)))
    message = jnp.concatenate([slab, small], axis=1)
    message, sent_rows, sent_cot = tie((message, rows_in, own_cot))
    slab = exchange(message, GROUP)
    small_own = slab[:, SLAB : SLAB + 2].reshape(CHIPS, 2 * width)[:, :896]
    slab = slab[:, :SLAB]
    attend_own = spread(slab, SEQ, SEQ_DEVICES).reshape(SEQ_DEVICES, CHIPS, SLAB, width)
    attend_own, other_rows, sent_cot = tie((attend_own, other_rows, sent_cot))
    attend_chip = assemble_attend(core_at, attend_own, swap(attend_own, "c"))
    small_other = swap(small_own, "c")
    small_all = jnp.where(
        core == 0, jnp.stack([small_own, small_other], 1), jnp.stack([small_other, small_own], 1)
    ).reshape(FSDP_DEVICES, 7, 128).astype(F32)
    gain_all = small_all[:, 0].reshape(1, WIDTH)
    shift_all = small_all[:, 1].reshape(1, WIDTH)
    out_bias = (small_all[:, 2] + small_all[:, 3]).reshape(WIDTH)
    bias_grid = small_all[:, 4:7].reshape(3, CHIPS, CHIP_COLS)
    attend_bias_chip = lax.dynamic_slice_in_dim(bias_grid, chip, 1, 1).reshape(1, width)

    own_positions = seq_index * ROWS + jnp.arange(ROWS, dtype=jnp.int32)
    own_tables = rope_tables(own_positions, 2 * CHIP_COLS // HEAD_DIM)
    all_tables = rope_tables(jnp.arange(LENGTH, dtype=jnp.int32), 2)

    near = {0: rows_in} | {k: shift(sent_rows, "z", k) for k in (1, 3, 2)}
    far = {0: other_rows} | {k: shift(other_rows, "z", k) for k in (1, 3)}
    ready, all_tables, gain_all, shift_all, attend_bias_chip, attend_chip = lax.optimization_barrier(
        (other_rows, all_tables, gain_all, shift_all, attend_bias_chip, attend_chip)
    )
    far[2] = shift(ready, "z", 2)
    pieces = [part[k] for part in (near, far) for k in range(4)]

    mixer_other = swap(mixer, "c")
    mixer_chip = jnp.where(
        core == 0, jnp.concatenate([mixer, mixer_other]), jnp.concatenate([mixer_other, mixer])
    )
    up_other = swap(upward, "c")
    down_other = swap(downward, "c")
    up_bias_own = upward_bias.astype(F32).reshape(1, CORE_FF)
    up_bias_other = swap(upward_bias.reshape(1, CORE_FF), "c").astype(F32)

    cot_pair = jnp.stack([own_cot, swap(sent_cot, "xh")])
    cot_pair, *pieces = tie((cot_pair, *pieces))
    cot_group = lax.all_gather(cot_pair, "z", axis=0, tiled=False).reshape(TOKENS, WIDTH)
    rows_group, normed, qkv_sent = norm_project(
        z_order, pieces, gain_all, shift_all, attend_chip, attend_bias_chip, own_tables
    )
    normed_other = swap(normed, "c")
    qkv = exchange(qkv_sent.reshape(CHIPS, ROWS, width), SEQ).reshape(LENGTH, width)
    act_own, act_other, slope_own, slope_other = hidden_forward(
        normed, upward, up_other, up_bias_own, up_bias_other
    )

    attended, logsum = attend_forward(qkv, (act_own, normed_other, mixer_chip))
    attended, cot_group = tie((attended, cot_group))
    attended_group = exchange(attended.reshape(SEQ_DEVICES, ROWS, CHIP_COLS), SEQ).reshape(
        TOKENS, CHIP_COLS
    )
    cot_other = swap(cot_group, "c")
    act_sent = swap(act_other, "c")
    attended_grad = grad_heads(cot_group, mixer_chip, (attended,))
    grads = exchange(attended_grad.reshape(CHIPS, ROWS, CHIP_COLS), SEQ).reshape(LENGTH, CHIP_COLS)

    grad_own, grad_other, up_bias_sum, up_bias_other_sum = hidden_back(
        cot_group,
        downward,
        down_other,
        slope_own,
        slope_other,
        (attended_group, cot_other, gate(attended_grad)),
    )
    grad_sent = swap(grad_other, "c")

    att_own = lax.dynamic_slice_in_dim(attended_group, core * CORE_COLS, CORE_COLS, 1)
    att_other = lax.dynamic_slice_in_dim(attended_group, (1 - core) * CORE_COLS, CORE_COLS, 1)
    x_at = x_lo.reshape(1)
    down_stay, down_leave = down_grads(
        y_order, x_at, act_own, act_sent, att_own, swap(att_other, "c"), cot_group, cot_other, (grad_own,)
    )
    down_arrived = swap(down_leave, "xl")

    back = attend_backward(qkv, grads, logsum, all_tables, (down_stay, grad_sent))
    projected_grad = exchange(back.reshape(SEQ_DEVICES, ROWS, width), SEQ).reshape(TOKENS, width)

    parts = out_part(
        act_own, act_other, attended_group, downward, down_other, mixer_chip, (gate(back),)
    )
    stay, arrived = sum_rows(parts)
    outputs = (
        rows_in.astype(F32) + out_bias + stay.astype(F32) + arrived.astype(F32)
    ).astype(BF16)

    down_parts = (down_stay.astype(F32) + down_arrived.astype(F32)).astype(BF16)
    up_slabs = up_grads(
        y_order, x_at, grad_own, grad_sent, normed, normed_other, (parts, down_parts)
    )
    up_arrived = sent_y(up_slabs)
    down_sum = sum_seq_x_first(down_parts)

    projected_grad, up_first = tie((projected_grad, up_slabs[0]))
    attend_slabs = attend_grads(
        seq_order,
        core_at,
        projected_grad,
        swap(projected_grad, "c"),
        normed,
        normed_other,
        (up_first, down_sum),
    )

    parts, norm_sums, attend_bias_sum = normed_part(
        projected_grad,
        grad_own,
        grad_other,
        rows_group,
        attend_chip,
        upward,
        up_other,
        (attend_slabs[0], up_arrived[0], up_arrived[1]),
    )
    stay, arrived = sum_rows(parts)
    inputs_grad = rows_grad(rows_in, own_cot, stay, arrived, gain_all)

    attend_slab = exchange(sum_seq(attend_slabs, sent_y(attend_slabs)), GROUP)
    attend_grad = unpack_attend(spread(attend_slab, SEQ, SEQ_DEVICES).reshape(
        SEQ_DEVICES, CHIPS, SLAB, width
    ))
    down_grad, mixer_grad = unpack_down(seq_order, spread_seq_y_first(down_sum))
    up_grad = unpack_up(seq_order, spread_seq(sum_seq(up_slabs, up_arrived)))

    bias_full = jnp.sum(own_cot.astype(F32), axis=0)
    attend_bias_full = lax.dynamic_update_slice(
        jnp.zeros((3, CHIPS, CHIP_COLS), F32), attend_bias_sum.reshape(3, 1, CHIP_COLS), (0, chip, 0)
    )
    up_bias_pair = jnp.where(
        core == 0,
        jnp.concatenate([up_bias_sum, up_bias_other_sum]),
        jnp.concatenate([up_bias_other_sum, up_bias_sum]),
    )
    up_bias_full = lax.dynamic_update_slice(
        jnp.zeros((CHIPS, 2, CORE_FF), F32), up_bias_pair[None], (chip, 0, 0)
    )
    vectors = jnp.concatenate(
        [
            v.reshape(FSDP_DEVICES, -1)
            for v in (norm_sums[0], norm_sums[1], bias_full, attend_bias_full, up_bias_full)
        ],
        axis=1,
    )
    vectors = jnp.sum(exchange(vectors, FSDP), axis=0)
    vectors = jnp.sum(spread(vectors, SEQ, SEQ_DEVICES), axis=0)
    gain_grad, shift_grad, bias_grad = vectors[:128], vectors[128:256], vectors[256:384]
    attend_bias_grad, up_bias_grad = vectors[384:768], vectors[768:]

    return (
        outputs.reshape(inputs.shape),
        inputs_grad.reshape(inputs.shape),
        gain_grad,
        shift_grad,
        attend_grad,
        attend_bias_grad,
        mixer_grad,
        bias_grad,
        up_grad,
        up_bias_grad,
        down_grad,
        bias_grad,
    )


def solution(mesh):
    fine = Mesh(mesh.devices.reshape(4, 2, 2, 4, 2), ("y", "xl", "xh", "z", "c"))
    rows = P(FSDP, SEQ, None)
    vector = P(FSDP)
    by_row = P(FSDP, None)
    by_col = P(None, FSDP)
    in_specs = (
        rows,
        vector,
        vector,
        by_row,
        vector,
        by_row,
        vector,
        by_col,
        vector,
        by_row,
        vector,
        rows,
    )
    out_specs = (
        rows,
        rows,
        vector,
        vector,
        by_row,
        vector,
        by_row,
        vector,
        by_col,
        vector,
        by_row,
        vector,
    )
    return jax.shard_map(
        per_device, mesh=fine, in_specs=in_specs, out_specs=out_specs, check_vma=False
    )
```

```python
from typing import Callable, NamedTuple, Sequence

import jax
import jax.numpy as jnp
from jax import lax
from jax.experimental import pallas as pl
from jax.experimental.pallas import tpu as pltpu
from jax.sharding import Mesh, PartitionSpec as P

HEADS = 32
HEAD_DIM = 64
ROT = 32
WIDTH = 2048
FF = 8192
SEQ_DEVICES = 8
CHIPS = 8
FSDP_DEVICES = 16
ROWS = 128
LENGTH = ROWS * SEQ_DEVICES
TOKENS = ROWS * CHIPS
CHIP_COLS = WIDTH // CHIPS
CORE_COLS = WIDTH // FSDP_DEVICES
CORE_FF = FF // FSDP_DEVICES
PAIR = 2 * HEAD_DIM
QBLOCK = 256

EPSILON = 1e-05
ROPE_BASE = 10000.0
NEG_FILL = -1e30
PACE = 1 * 1.15e9
MICROSECONDS = dict(
    assemble_attend=6,
    norm_project=13,
    hidden_forward=11,
    attend_forward=10,
    grad_heads=15,
    hidden_back=30,
    down_grads=30,
    attend_backward=15,
    out_part=30,
    up_grads=30,
    attend_grads=25,
    normed_part=43,
    unpack_down=6,
    unpack_up=6,
    unpack_attend=6,
    rows_grad=3,
)
SCALE = HEAD_DIM ** (-0.5)

F32 = jnp.float32
BF16 = jnp.bfloat16

SEQ = ("y", "xl")
GROUP = ("xh", "z")
FSDP = ("xh", "z", "c")

NT = (((1,), (1,)), ((), ()))
TN = (((0,), (0,)), ((), ()))
NN = (((1,), (0,)), ((), ()))


def dot(lhs, rhs, dims=NN):
    return lax.dot_general(lhs, rhs, dims, preferred_element_type=F32)


def swap(piece, axis):
    return lax.ppermute(piece, axis, [(0, 1), (1, 0)])


def shift(piece, axis, step):
    return lax.ppermute(piece, axis, [(i, (i - step) % 4) for i in range(4)])


def send(piece, axis, step):
    return lax.ppermute(piece, axis, [(i, (i + step) % 4) for i in range(4)])


def rope_tables(positions, heads):
    half = ROT // 2
    frequency = ROPE_BASE ** (-2.0 * jnp.arange(half, dtype=F32) / ROT)
    angle = positions.astype(F32)[:, None] * frequency[None, :]
    cosine, sine = jnp.cos(angle), jnp.sin(angle)
    rest = jnp.zeros((positions.shape[0], HEAD_DIM - ROT), F32)
    blank = jnp.zeros_like(sine)
    turn = jnp.concatenate([cosine, cosine, rest + 1.0], axis=1)
    upper = jnp.concatenate([-sine, blank, rest], axis=1)
    lower = jnp.concatenate([blank, sine, rest], axis=1)
    return tuple(jnp.concatenate([t] * heads, axis=1) for t in (turn, upper, lower))


def turn_columns(values, turn, upper, lower, sign):
    width = values.shape[1]
    half = ROT // 2
    ahead = pltpu.roll(values, width - half, 1)
    behind = pltpu.roll(values, half, 1)
    return values * turn + sign * (ahead * upper + behind * lower)


def cost(names):
    return pl.CostEstimate(
        flops=int(sum(MICROSECONDS[name] for name in names) * PACE), bytes_accessed=0, transcendentals=0
    )


def whole(shape):
    return pl.BlockSpec(shape, lambda i: (0,) * len(shape))


def row_block(rows, width, column=0):
    return pl.BlockSpec((rows, width), lambda i: (i, column))


class Job(NamedTuple):
    name: str
    kernel: Callable
    grid: int
    in_specs: Sequence
    out_specs: Sequence
    out_shape: Sequence
    operands: tuple
    scratch: tuple = ()
    plan: tuple = ()


def run(*jobs, late=()):
    plans = [len(job.plan) for job in jobs]
    starts = [sum(job.grid for job in jobs[:k]) for k in range(len(jobs))]

    def moved(spec, start, count, first, size):
        def index(step, *plan):
            own = plan[first : first + size]
            return spec.index_map(jnp.clip(step - start, 0, count - 1) if len(jobs) > 1 else step, *own)

        return pl.BlockSpec(spec.block_shape, index)

    def specs_of(kind):
        return [
            moved(spec, starts[k], job.grid, sum(plans[:k]), plans[k])
            for k, job in enumerate(jobs)
            for spec in getattr(job, kind)
        ]

    def body(*refs):
        refs = list(refs)
        take = lambda count: [refs.pop(0) for _ in range(count)]
        plan_refs = [take(count) for count in plans]
        in_refs = [take(len(job.operands)) for job in jobs]
        take(len(late))
        out_refs = [take(len(job.out_specs)) for job in jobs]
        held = [take(len(job.scratch)) for job in jobs]
        step = pl.program_id(0)
        for k, job in enumerate(jobs):
            own = (*plan_refs[k], *in_refs[k], *out_refs[k], *held[k])
            if len(jobs) == 1:
                job.kernel(step, *own)
            else:

                @pl.when((step >= starts[k]) & (step < starts[k] + job.grid))
                def _():
                    job.kernel(step - starts[k], *own)

    found = pl.pallas_call(
        body,
        grid_spec=pltpu.PrefetchScalarGridSpec(
            num_scalar_prefetch=sum(plans),
            grid=(sum(job.grid for job in jobs),),
            in_specs=specs_of("in_specs") + [pl.BlockSpec(memory_space=pl.ANY)] * len(late),
            out_specs=specs_of("out_specs"),
            scratch_shapes=[shape for job in jobs for shape in job.scratch],
        ),
        out_shape=[shape for job in jobs for shape in job.out_shape],
        compiler_params=pltpu.CompilerParams(vmem_limit_bytes=60 * 2**20),
        cost_estimate=cost([job.name for job in jobs]),
        name="_".join(job.name for job in jobs),
    )(*(p for job in jobs for p in job.plan), *(a for job in jobs for a in job.operands), *late)
    found = list(found)
    results = []
    for job in jobs:
        own, found = found[: len(job.out_specs)], found[len(job.out_specs) :]
        results.append(own[0] if len(own) == 1 else own)
    return results[0] if len(jobs) == 1 else results


def listed(value):
    return list(value) if isinstance(value, (list, tuple)) else [value]


def call(
    kernel, name, grid, in_specs, out_specs, out_shape, flops, moved, operands, late=(), scratch=(), plan=()
):
    job = Job(
        name, kernel, grid, in_specs, listed(out_specs), listed(out_shape), operands, tuple(scratch), plan
    )
    return job if late is None else run(job, late=late)


def placed_call(
    kernel, name, grid, in_specs, out_specs, out_shape, scratch, flops, moved, order, operands, late=()
):
    return call(
        kernel, name, grid, in_specs, out_specs, out_shape, flops, moved, operands, late, scratch, (order,)
    )


def fixed(dims):
    return pl.BlockSpec(dims, lambda i, order: (0,) * len(dims))


def shape(dims, kind=BF16):
    return jax.ShapeDtypeStruct(dims, kind)


def layer_stats(rows):
    center = rows - jnp.mean(rows, axis=-1, keepdims=True)
    spread_out = jnp.mean(center * center, axis=-1, keepdims=True)
    return center, lax.rsqrt(spread_out + EPSILON)


def assemble_kernel(core_ref, own_ref, other_ref, out_ref):
    core = core_ref[0]
    out_ref[0, core] = own_ref[...].reshape(out_ref.shape[2:])
    out_ref[0, 1 - core] = other_ref[...].reshape(out_ref.shape[2:])


def assemble_attend(core, own, other):
    slab, cols = own.shape[2:]
    piece = pl.BlockSpec((SEQ_DEVICES, 1, slab, cols), lambda g, core: (0, g, 0, 0))
    out = (CHIPS, 2, SEQ_DEVICES, slab, cols)
    return pl.pallas_call(
        assemble_kernel,
        grid_spec=pltpu.PrefetchScalarGridSpec(
            num_scalar_prefetch=1,
            grid=(CHIPS,),
            in_specs=[piece, piece],
            out_specs=pl.BlockSpec((1,) + out[1:], lambda g, core: (g, 0, 0, 0, 0)),
        ),
        out_shape=shape(out),
        compiler_params=pltpu.CompilerParams(vmem_limit_bytes=60 * 2**20),
        cost_estimate=cost(["assemble_attend"]),
        name="assemble_attend",
    )(core, own, other).reshape(WIDTH, cols)


def norm_project_kernel(
    step,
    order_ref,
    near_0,
    near_1,
    near_2,
    near_3,
    far_0,
    far_1,
    far_2,
    far_3,
    gain_ref,
    shift_ref,
    weight_ref,
    bias_ref,
    turn_ref,
    upper_ref,
    lower_ref,
    rows_ref,
    normed_ref,
    out_ref,
):
    pairs = ((near_0, far_0), (near_1, far_1), (near_2, far_2), (near_3, far_3))
    for index, (near, far) in enumerate(pairs):

        @pl.when(step == index)
        def _():
            rows_ref[:ROWS] = near[...]
            rows_ref[ROWS:] = far[...]

    center, inverse = layer_stats(rows_ref[...].astype(F32))
    normed = (center * inverse * gain_ref[...] + shift_ref[...]).astype(BF16)
    normed_ref[...] = normed
    projected = dot(normed, weight_ref[...]) + bias_ref[...]
    turned_width = 2 * CHIP_COLS
    for block in range(2):
        rows = slice(block * ROWS, (block + 1) * ROWS)
        out_ref[rows, :turned_width] = turn_columns(
            projected[rows, :turned_width], turn_ref[...], upper_ref[...], lower_ref[...], 1.0
        ).astype(BF16)
    out_ref[:, turned_width:] = projected[:, turned_width:].astype(BF16)


def norm_project(order, pieces, gain, shift_row, weight, bias, tables):
    block = 2 * ROWS
    width = weight.shape[1]
    vectors = (gain, shift_row, weight, bias) + tables
    out = lambda cols: pl.BlockSpec((block, cols), lambda i, order: (order[i], 0))
    return placed_call(
        norm_project_kernel,
        "norm_project",
        4,
        [fixed((ROWS, WIDTH))] * 8 + [fixed(v.shape) for v in vectors],
        [out(WIDTH), out(WIDTH), out(width)],
        [shape((TOKENS, WIDTH)), shape((TOKENS, WIDTH)), shape((TOKENS, width))],
        [],
        2 * TOKENS * WIDTH * width,
        18 * 2**20,
        order,
        tuple(pieces) + vectors,
    )


def hidden_kernel(
    step,
    normed_ref,
    own_ref,
    other_ref,
    own_bias_ref,
    other_bias_ref,
    own_act_ref,
    other_act_ref,
    own_slope_ref,
    other_slope_ref,
):
    root = (2.0 / 3.141592653589793) ** 0.5
    for weight, bias, act, slope in (
        (own_ref, own_bias_ref, own_act_ref, own_slope_ref),
        (other_ref, other_bias_ref, other_act_ref, other_slope_ref),
    ):
        hidden = dot(normed_ref[...], weight[...]) + bias[...]
        square = hidden * hidden
        bend = jnp.tanh(root * hidden * (1.0 + 0.044715 * square))
        half = 0.5 * (1.0 + bend)
        act[...] = (hidden * half).astype(BF16)
        slope[...] = half + 0.5 * hidden * (1.0 - bend * bend) * (
            root * (1.0 + 3.0 * 0.044715 * square)
        )


def hidden_forward(normed, own, other, own_bias, other_bias):
    block = 256
    operands = (own, other, own_bias, other_bias)
    return call(
        hidden_kernel,
        "hidden_forward",
        TOKENS // block,
        [row_block(block, WIDTH)] + [whole(v.shape) for v in operands],
        [row_block(block, CORE_FF)] * 4,
        [shape((TOKENS, CORE_FF))] * 2 + [shape((TOKENS, CORE_FF), F32)] * 2,
        4 * TOKENS * WIDTH * CORE_FF,
        14 * 2**20,
        (normed,) + operands,
    )


def grad_heads_kernel(step, cot_ref, mixer_ref, out_ref):
    out_ref[...] = dot(cot_ref[...], mixer_ref[...], NT).astype(BF16)


def grad_heads(cot, mixer, late):
    block = 256
    return call(
        grad_heads_kernel,
        "grad_heads",
        TOKENS // block,
        [row_block(block, WIDTH), whole(mixer.shape)],
        row_block(block, CHIP_COLS),
        shape((TOKENS, CHIP_COLS)),
        2 * TOKENS * WIDTH * CHIP_COLS,
        6 * 2**20,
        (cot, mixer),
        late,
    )


def hidden_back_kernel(
    step,
    cot_ref, own_ref, other_ref, own_slope_ref, other_slope_ref, own_out, other_out, own_sum, other_sum
):
    for weight, slope, out, total in (
        (own_ref, own_slope_ref, own_out, own_sum),
        (other_ref, other_slope_ref, other_out, other_sum),
    ):
        grad = (dot(cot_ref[...], weight[...], NT) * slope[...]).astype(BF16)
        out[...] = grad
        part = jnp.sum(grad.astype(F32), axis=0, keepdims=True)

        @pl.when(step == 0)
        def _():
            total[...] = part

        @pl.when(step > 0)
        def _():
            total[...] += part


def hidden_back(cot, own, other, own_slope, other_slope):
    block = 256
    return call(
        hidden_back_kernel,
        "hidden_back",
        TOKENS // block,
        [row_block(block, WIDTH), whole(own.shape), whole(other.shape)]
        + [row_block(block, CORE_FF)] * 2,
        [row_block(block, CORE_FF)] * 2 + [whole((1, CORE_FF))] * 2,
        [shape((TOKENS, CORE_FF))] * 2 + [shape((1, CORE_FF), F32)] * 2,
        4 * TOKENS * WIDTH * CORE_FF,
        14 * 2**20,
        (cot, own, other, own_slope, other_slope),
        None,
    )


def out_part_kernel(step, own_act, other_act, attended, own_ref, other_ref, mixer_ref, out_ref):
    out_ref[...] = (
        dot(own_act[...], own_ref[...])
        + dot(other_act[...], other_ref[...])
        + dot(attended[...], mixer_ref[...])
    ).astype(BF16)


def out_part(own_act, other_act, attended, own, other, mixer):
    block = 256
    weights = (own, other, mixer)
    return call(
        out_part_kernel,
        "out_part",
        TOKENS // block,
        [row_block(block, CORE_FF)] * 2
        + [row_block(block, CHIP_COLS)]
        + [whole(w.shape) for w in weights],
        row_block(block, WIDTH),
        shape((TOKENS, WIDTH)),
        2 * TOKENS * WIDTH * (2 * CORE_FF + CHIP_COLS),
        12 * 2**20,
        (own_act, other_act, attended) + weights,
        None,
    )


def normed_part_kernel(
    step,
    projected, own_grad, other_grad, rows_ref, attend_ref, own_ref, other_ref, out_ref, sums_ref, bias_ref
):
    total = (
        dot(projected[...], attend_ref[...], NT)
        + dot(own_grad[...], own_ref[...], NT)
        + dot(other_grad[...], other_ref[...], NT)
    )
    out_ref[...] = total.astype(BF16)
    center, inverse = layer_stats(rows_ref[...].astype(F32))
    gain_part = jnp.sum(total * (center * inverse), axis=0, keepdims=True)
    shift_part = jnp.sum(total, axis=0, keepdims=True)
    bias_part = jnp.sum(projected[...].astype(F32), axis=0, keepdims=True)

    @pl.when(step == 0)
    def _():
        sums_ref[0:1] = gain_part
        sums_ref[1:2] = shift_part
        bias_ref[...] = bias_part

    @pl.when(step > 0)
    def _():
        sums_ref[0:1] += gain_part
        sums_ref[1:2] += shift_part
        bias_ref[...] += bias_part


def normed_part(projected, own_grad, other_grad, rows, attend, own, other, late):
    block = 256
    width = projected.shape[1]
    weights = (attend, own, other)
    return call(
        normed_part_kernel,
        "normed_part",
        TOKENS // block,
        [row_block(block, width)]
        + [row_block(block, CORE_FF)] * 2
        + [row_block(block, WIDTH)]
        + [whole(w.shape) for w in weights],
        [row_block(block, WIDTH), whole((2, WIDTH)), whole((1, width))],
        [shape((TOKENS, WIDTH)), shape((2, WIDTH), F32), shape((1, width), F32)],
        2 * TOKENS * WIDTH * (2 * CORE_FF + width),
        18 * 2**20,
        (projected, own_grad, other_grad, rows) + weights,
        late,
    )


UP_ROWS = WIDTH // SEQ_DEVICES
DOWN_ROWS = CORE_FF // 2
MIX_ROWS = CORE_COLS // 2
PACK_ROWS = DOWN_ROWS + MIX_ROWS
PACK_COLS = CORE_FF
HALF = PACK_COLS // 2
SLOT_COLS = WIDTH // SEQ_DEVICES


def across(rows):
    return pl.BlockSpec((rows, SLOT_COLS), lambda i, order: (0, order[i]))


def plan_call(
    kernel, name, grid, in_specs, out_specs, out_shape, scratch, flops, moved, order, side, operands, late=()
):
    return call(
        kernel, name, grid, in_specs, out_specs, out_shape, flops, moved, operands, late, scratch, (order, side)
    )


def plan_whole(array):
    return pl.BlockSpec(array.shape, lambda i, order, side: (0, 0))


WIDE = 2 * SLOT_COLS
WIDE_COLUMNS = pl.BlockSpec((TOKENS, WIDE), lambda i, order, side: (0, order[i]))


def down_grads_kernel(
    step, x_ref, core_ref, act_ref, act_other, att_ref, att_other, cot_ref, cot_other, out_ref
):
    cols = pl.ds(pl.multiple_of(core_ref[0] * CORE_COLS, CORE_COLS), CORE_COLS)
    down = dot(act_ref[...], cot_ref[...], TN) + dot(act_other[...], cot_other[...], TN)
    mix = dot(att_ref[:, cols], cot_ref[...], TN) + dot(att_other[:, cols], cot_other[...], TN)
    for x in range(2):

        @pl.when(x_ref[0] == x)
        def _():
            for r, half in ((0, x), (1, 1 - x)):
                cols = slice(half * SLOT_COLS, (half + 1) * SLOT_COLS)
                part = down[:, cols].astype(BF16)
                out_ref[0, r, :DOWN_ROWS, :HALF] = part[:DOWN_ROWS]
                out_ref[0, r, :DOWN_ROWS, HALF:] = part[DOWN_ROWS:]
                part = mix[:, cols].astype(BF16)
                out_ref[0, r, DOWN_ROWS:, :HALF] = part[:MIX_ROWS]
                out_ref[0, r, DOWN_ROWS:, HALF:] = part[MIX_ROWS:]


def down_grads(x_lo, core, act, act_other, att, att_other, cot, cot_other):
    columns = pl.BlockSpec((TOKENS, WIDE), lambda i, *plan: (0, i))
    held = lambda array: pl.BlockSpec(array.shape, lambda i, *plan: (0, 0))
    block = (1, 2, PACK_ROWS, PACK_COLS)
    return Job(
        "down_grads",
        down_grads_kernel,
        4,
        [held(a) for a in (act, act_other, att, att_other)] + [columns] * 2,
        [pl.BlockSpec(block, lambda i, *plan: (i, 0, 0, 0))],
        [shape((4,) + block[1:])],
        (act, act_other, att, att_other, cot, cot_other),
        (),
        (x_lo, core),
    )


def up_grads_kernel(step, order_ref, x_ref, grad_ref, grad_other, normed_ref, normed_other, *refs):
    outs, held = refs[:4], refs[4]
    held[...] = (
        dot(normed_ref[...], grad_ref[...], TN) + dot(normed_other[...], grad_other[...], TN)
    ).astype(BF16)
    for index, out_ref in enumerate(outs):

        @pl.when(step == index)
        def _():
            for r, x in enumerate((x_ref[0], 1 - x_ref[0])):
                out_ref[r] = held[pl.ds(pl.multiple_of(x * UP_ROWS, UP_ROWS), UP_ROWS), :]


def up_grads(order, x_lo, grad, grad_other, normed, normed_other):
    block = (2, UP_ROWS, CORE_FF)
    return plan_call(
        up_grads_kernel,
        "up_grads",
        4,
        [plan_whole(grad), plan_whole(grad_other)] + [WIDE_COLUMNS] * 2,
        [pl.BlockSpec(block, lambda i, order, side: (0, 0, 0))] * 4,
        [shape(block)] * 4,
        [pltpu.VMEM((2 * UP_ROWS, CORE_FF), BF16)],
        4 * TOKENS * WIDTH * CORE_FF,
        14 * 2**20,
        order,
        x_lo,
        (grad, grad_other, normed, normed_other),
        None,
    )


def attend_grads_kernel(step, order_ref, core_ref, grad_ref, grad_other, own_0, own_1, other_0, other_1, *refs):
    outs, held = refs[:4], refs[4]
    for half, (own, other) in enumerate(((own_0, other_0), (own_1, other_1))):
        held[half] = (
            dot(own[...], grad_ref[...], TN) + dot(other[...], grad_other[...], TN)
        ).astype(BF16)
    for slot in range(SEQ_DEVICES):
        rows = pl.ds(pl.multiple_of(order_ref[slot] * SLAB, SLAB), SLAB)
        for half in range(2):
            outs[slot // 2][slot % 2, half] = held[half, rows, :]


def attend_grads(order, core, grad, grad_other, normed, normed_other, late):
    cols = grad.shape[1]

    def rows_of(half):
        return pl.BlockSpec((TOKENS, CORE_COLS), lambda i, order, core: (0, 4 * i + 2 * half + core[0]))

    return plan_call(
        attend_grads_kernel,
        "attend_grads",
        CHIPS // 2,
        [plan_whole(grad), plan_whole(grad_other)] + [rows_of(0), rows_of(1)] * 2,
        [pl.BlockSpec((2, 2, SLAB, cols), lambda i, order, core: (0, i, 0, 0))] * 4,
        [shape((2, CHIPS, SLAB, cols))] * 4,
        [pltpu.VMEM((2, CORE_COLS, cols), BF16)],
        4 * TOKENS * WIDTH * cols // 2,
        12 * 2**20,
        order,
        core,
        (grad, grad_other, normed, normed, normed_other, normed_other),
        late,
    )


def unpack_down_kernel(step, order_ref, *refs):
    down_ref, mix_ref = refs[4:]
    for index, pieces in enumerate(refs[:4]):

        @pl.when(step // 2 == index)
        def _():
            piece = pieces.at[step % 2]
            down_ref[:DOWN_ROWS] = piece[:DOWN_ROWS, :HALF].astype(F32)
            down_ref[DOWN_ROWS:] = piece[:DOWN_ROWS, HALF:].astype(F32)
            mix_ref[:MIX_ROWS] = piece[DOWN_ROWS:, :HALF].astype(F32)
            mix_ref[MIX_ROWS:] = piece[DOWN_ROWS:, HALF:].astype(F32)


def unpack_down(order, pieces):
    return placed_call(
        unpack_down_kernel,
        "unpack_down",
        SEQ_DEVICES,
        [fixed((2, PACK_ROWS, PACK_COLS))] * 4,
        [across(CORE_FF), across(CORE_COLS)],
        [shape((CORE_FF, WIDTH), F32), shape((CORE_COLS, WIDTH), F32)],
        [],
        0,
        8 * 2**20,
        order,
        tuple(pieces),
    )


def unpack_up_kernel(step, order_ref, *refs):
    for index, pieces in enumerate(refs[:4]):

        @pl.when(step // 2 == index)
        def _():
            refs[4][...] = pieces[step % 2].astype(F32)


def unpack_up(order, pieces):
    block = (UP_ROWS, CORE_FF)
    return placed_call(
        unpack_up_kernel,
        "unpack_up",
        SEQ_DEVICES,
        [fixed((2,) + block)] * 4,
        pl.BlockSpec(block, lambda i, order: (order[i], 0)),
        shape((WIDTH, CORE_FF), F32),
        [],
        0,
        6 * 2**20,
        order,
        tuple(pieces),
    )


SLAB = CORE_COLS // SEQ_DEVICES


def unpack_attend_kernel(step, packed_ref, out_ref):
    for chip in range(CHIPS):
        for part in range(3):
            out_ref[:, part * WIDTH + chip * CHIP_COLS : part * WIDTH + (chip + 1) * CHIP_COLS] = (
                packed_ref[0, chip, :, part * CHIP_COLS : (part + 1) * CHIP_COLS].astype(F32)
            )


def unpack_attend(packed):
    return call(
        unpack_attend_kernel,
        "unpack_attend",
        SEQ_DEVICES,
        [pl.BlockSpec((1,) + packed.shape[1:], lambda i: (i, 0, 0, 0))],
        row_block(SLAB, 3 * WIDTH),
        shape((CORE_COLS, 3 * WIDTH), F32),
        0,
        5 * 2**20,
        (packed,),
    )


def rows_grad_kernel(step, rows_ref, cot_ref, near_ref, far_ref, gain_ref, out_ref):
    grad = near_ref[...].astype(F32) + far_ref[...].astype(F32)
    center, inverse = layer_stats(rows_ref[...].astype(F32))
    unit = center * inverse
    scaled = grad * gain_ref[...]
    out_ref[...] = cot_ref[...].astype(F32) + inverse * (
        scaled
        - jnp.mean(scaled, axis=-1, keepdims=True)
        - unit * jnp.mean(scaled * unit, axis=-1, keepdims=True)
    )


def rows_grad(rows, cot, near, far, gain):
    block = 64
    return call(
        rows_grad_kernel,
        "rows_grad",
        ROWS // block,
        [row_block(block, WIDTH)] * 4 + [whole(gain.shape)],
        row_block(block, WIDTH),
        shape((ROWS, WIDTH), F32),
        0,
        4 * 2**20,
        (rows, cot, near, far, gain),
    )


def lane_masks():
    lane = lax.broadcasted_iota(jnp.int32, (1, PAIR), 1)
    first = (lane < HEAD_DIM).astype(BF16)
    return first, 1 - first


def scores_of(query, keys, low):
    scores = dot(query, keys, NT) * SCALE
    row = low + lax.broadcasted_iota(jnp.int32, scores.shape, 0)
    col = lax.broadcasted_iota(jnp.int32, scores.shape, 1)
    return jnp.where(col <= row, scores, NEG_FILL)


def attend_kernel(step, query_ref, key_ref, value_ref, out_ref, logsum_ref):
    first, second = lane_masks()
    lane = lax.broadcasted_iota(jnp.int32, (QBLOCK, PAIR), 1)
    for low in range(0, LENGTH, QBLOCK):
        reach = low + QBLOCK
        query = query_ref[low:reach, :]
        keys = key_ref[:reach, :]
        values = value_ref[:reach, :]
        found = []
        for mask in (first, second):
            scores = scores_of(query * mask, keys, low)
            peak = jnp.max(scores, axis=1, keepdims=True)
            weight = jnp.exp(scores - peak)
            total = jnp.sum(weight, axis=1, keepdims=True)
            prob_low = (weight * (1.0 / total)).astype(BF16)
            found.append((dot(prob_low, values), peak + jnp.log(total)))
        out_ref[low:reach, :] = jnp.where(lane < HEAD_DIM, found[0][0], found[1][0]).astype(BF16)
        logsum_ref[low:reach, :] = jnp.where(lane < HEAD_DIM, found[0][1], found[1][1])


def pair_columns(part):
    return pl.BlockSpec((LENGTH, PAIR), lambda p: (0, part * (CHIP_COLS // PAIR) + p))


def attend_forward(qkv, late):
    return call(
        attend_kernel,
        "attend_forward",
        CHIP_COLS // PAIR,
        [pair_columns(0), pair_columns(1), pair_columns(2)],
        [pair_columns(0)] * 2,
        [shape((LENGTH, CHIP_COLS)), shape((LENGTH, CHIP_COLS), F32)],
        8 * 2**30,
        4 * 2**20,
        (qkv, qkv, qkv),
        late,
    )


def attend_back_kernel(
    step,
    query_ref,
    key_ref,
    value_ref,
    grad_ref,
    logsum_ref,
    turn_ref,
    upper_ref,
    lower_ref,
    out_ref,
    key_total,
    value_total,
):
    pair = step
    first, second = lane_masks()
    lane = lax.broadcasted_iota(jnp.int32, (QBLOCK, PAIR), 1)
    key_total[...] = jnp.zeros_like(key_total)
    value_total[...] = jnp.zeros_like(value_total)

    def store(part, low, reach, values):
        start = pl.multiple_of((part * (CHIP_COLS // PAIR) + pair) * PAIR, PAIR)
        out_ref[low:reach, pl.ds(start, PAIR)] = values.astype(BF16)

    def unturn(values, low, reach):
        kept = values.astype(BF16).astype(F32)
        return turn_columns(
            kept, turn_ref[low:reach, :], upper_ref[low:reach, :], lower_ref[low:reach, :], -1.0
        )

    for low in range(0, LENGTH, QBLOCK):
        reach = low + QBLOCK
        query = query_ref[low:reach, :]
        grad = grad_ref[low:reach, :]
        keys = key_ref[:reach, :]
        values = value_ref[:reach, :]
        query_grads = []
        key_part = 0.0
        value_part = 0.0
        for head, mask in enumerate((first, second)):
            own_query = query * mask
            own_grad = grad * mask
            scores = scores_of(own_query, keys, low)
            start = head * HEAD_DIM
            probs = jnp.exp(scores - logsum_ref[low:reach, start : start + 1])
            prob_grad = dot(own_grad, values, NT)
            inner = jnp.sum(probs * prob_grad, axis=1, keepdims=True)
            score_grad = (probs * (prob_grad - inner)).astype(BF16)
            query_grads.append(dot(score_grad, keys))
            key_part += dot(score_grad, own_query, TN)
            value_part += dot(probs.astype(BF16), own_grad, TN)
        key_total[:reach, :] += key_part
        value_total[:reach, :] += value_part
        query_grad = jnp.where(lane < HEAD_DIM, query_grads[0], query_grads[1]) * SCALE
        store(0, low, reach, unturn(query_grad, low, reach))
    store(1, 0, LENGTH, unturn(key_total[...] * SCALE, 0, LENGTH))
    store(2, 0, LENGTH, value_total[...])


def attend_backward(qkv, grad, logsum, tables, late):
    return call(
        attend_back_kernel,
        "attend_backward",
        CHIP_COLS // PAIR,
        [pair_columns(0), pair_columns(1), pair_columns(2), pair_columns(0), pair_columns(0)]
        + [whole(t.shape) for t in tables],
        whole((LENGTH, 3 * CHIP_COLS)),
        shape((LENGTH, 3 * CHIP_COLS)),
        20 * 2**30,
        6 * 2**20,
        (qkv, qkv, qkv, grad, logsum) + tables,
        late,
        [pltpu.VMEM((LENGTH, PAIR), F32)] * 2,
    )


def exchange(blocks, axes):
    return lax.all_to_all(blocks, axes, split_axis=0, concat_axis=0, tiled=True)


def spread(block, axes, count):
    return exchange(jnp.broadcast_to(block[None], (count,) + block.shape), axes)


def gate(value):
    return swap(value.reshape(-1, value.shape[-1])[:16, :128], "c")


tie = lax.optimization_barrier


def sent_y(parts):
    return [send(parts[k], "y", k) for k in (1, 3, 2)]


def joined(leave, stay):
    return (stay + swap(leave.astype(BF16), "xl").astype(F32)).astype(BF16)


def sum_seq(parts, arrived):
    leave, stay = (
        parts[0][r].astype(F32) + sum(a[r].astype(F32) for a in arrived) for r in (1, 0)
    )
    return joined(leave, stay)


def spread_seq(piece):
    pair = jnp.stack([piece, swap(piece, "xl")])
    found = {0: pair} | {k: shift(pair, "y", k) for k in (1, 3, 2)}
    return [found[k] for k in range(4)]


def sum_rows(parts):
    parts = lax.psum_scatter(
        parts.reshape(4, 2, ROWS, WIDTH), "z", scatter_dimension=0, tiled=False
    )
    return parts[0], swap(parts[1], "xh")


def per_device(
    inputs,
    gains,
    shifts,
    attend,
    attend_bias,
    mixer,
    mixer_bias,
    upward,
    upward_bias,
    downward,
    downward_bias,
    cotangent,
):
    core = lax.axis_index("c")
    x_lo = lax.axis_index("xl")
    chip = lax.axis_index("xh") * 4 + lax.axis_index("z")
    seq_index = lax.axis_index("y") * 2 + x_lo
    core_at = core.reshape(1)
    rows_in = inputs.reshape(ROWS, WIDTH)
    own_cot = cotangent.reshape(ROWS, WIDTH)
    width = 3 * CHIP_COLS

    z_order = (lax.axis_index("z") + jnp.arange(4, dtype=jnp.int32)) % 4
    y_order = (lax.axis_index("y") + jnp.arange(4, dtype=jnp.int32)) % 4
    seq_order = (y_order[:, None] * 2 + jnp.stack([x_lo, 1 - x_lo])[None, :]).reshape(SEQ_DEVICES)

    other_rows = swap(rows_in, "xh")
    slab = lax.dynamic_slice_in_dim(attend, seq_index * SLAB, SLAB, 0)
    slab = slab.reshape(SLAB, 3, CHIPS, CHIP_COLS).transpose(2, 0, 1, 3).reshape(CHIPS, SLAB, width)
    small = jnp.concatenate([gains, shifts, mixer_bias, downward_bias, attend_bias])
    small = jnp.pad(small, (0, 2 * width - small.shape[0])).reshape(1, 2, width)
    small = jnp.pad(jnp.broadcast_to(small, (CHIPS, 2, width)), ((0, 0), (0, SLAB - 2), (0, 0)))
    message = jnp.concatenate([slab, small], axis=1)
    near = {0: rows_in} | {k: shift(rows_in, "z", k) for k in (1, 3)}
    message, other_rows, near[1], near[3] = tie((message, other_rows, near[1], near[3]))
    slab = exchange(message, GROUP)
    slab, other_rows = tie((slab, other_rows))
    small_own = slab[:, SLAB : SLAB + 2].reshape(CHIPS, 2 * width)[:, :896]
    slab = slab[:, :SLAB]
    attend_own = spread(slab, SEQ, SEQ_DEVICES).reshape(SEQ_DEVICES, CHIPS, SLAB, width)
    far = {0: other_rows} | {k: shift(other_rows, "z", k) for k in (1, 3)}
    attend_own, sent_cot, far[1], far[3] = tie((attend_own, own_cot, far[1], far[3]))
    attend_chip = assemble_attend(core_at, attend_own, swap(attend_own, "c"))
    small_other = swap(small_own, "c")
    small_all = jnp.where(
        core == 0, jnp.stack([small_own, small_other], 1), jnp.stack([small_other, small_own], 1)
    ).reshape(FSDP_DEVICES, 7, 128).astype(F32)
    gain_all = small_all[:, 0].reshape(1, WIDTH)
    shift_all = small_all[:, 1].reshape(1, WIDTH)
    out_bias = (small_all[:, 2] + small_all[:, 3]).reshape(WIDTH)
    bias_grid = small_all[:, 4:7].reshape(3, CHIPS, CHIP_COLS)
    attend_bias_chip = lax.dynamic_slice_in_dim(bias_grid, chip, 1, 1).reshape(1, width)

    own_positions = seq_index * ROWS + jnp.arange(ROWS, dtype=jnp.int32)
    own_tables = rope_tables(own_positions, 2 * CHIP_COLS // HEAD_DIM)
    all_tables = rope_tables(jnp.arange(LENGTH, dtype=jnp.int32), 2)

    near[2] = shift(rows_in, "z", 2)
    far[2] = shift(other_rows, "z", 2)
    pieces = [part[k] for part in (near, far) for k in range(4)]

    mixer_other = swap(mixer, "c")
    mixer_chip = jnp.where(
        core == 0, jnp.concatenate([mixer, mixer_other]), jnp.concatenate([mixer_other, mixer])
    )
    up_other = swap(upward, "c")
    down_other = swap(downward, "c")
    up_bias_own = upward_bias.astype(F32).reshape(1, CORE_FF)
    up_bias_other = swap(upward_bias.reshape(1, CORE_FF), "c").astype(F32)

    cot_pair = jnp.stack([own_cot, swap(sent_cot, "xh")])
    cot_pair, attend_chip, gain_all, shift_all, attend_bias_chip, own_tables, all_tables, *pieces = tie(
        (cot_pair, attend_chip, gain_all, shift_all, attend_bias_chip, own_tables, all_tables, *pieces)
    )
    cot_group = lax.all_gather(cot_pair, "z", axis=0, tiled=False).reshape(TOKENS, WIDTH)
    rows_group, normed, qkv_sent = norm_project(
        z_order, pieces, gain_all, shift_all, attend_chip, attend_bias_chip, own_tables
    )
    normed_other = swap(normed, "c")
    qkv = exchange(qkv_sent.reshape(CHIPS, ROWS, width), SEQ).reshape(LENGTH, width)
    act_own, act_other, slope_own, slope_other = hidden_forward(
        normed, upward, up_other, up_bias_own, up_bias_other
    )

    attended, logsum = attend_forward(qkv, (act_own, normed_other, mixer_chip))
    attended, cot_group = tie((attended, cot_group))
    attended_group = exchange(attended.reshape(SEQ_DEVICES, ROWS, CHIP_COLS), SEQ).reshape(
        TOKENS, CHIP_COLS
    )
    cot_other = swap(cot_group, "c")
    act_sent = swap(act_other, "c")
    attended_grad = grad_heads(cot_group, mixer_chip, (attended,))
    grads = exchange(attended_grad.reshape(CHIPS, ROWS, CHIP_COLS), SEQ).reshape(LENGTH, CHIP_COLS)

    x_at = x_lo.reshape(1)
    (grad_own, grad_other, up_bias_sum, up_bias_other_sum), down_slabs = run(
        hidden_back(cot_group, downward, down_other, slope_own, slope_other),
        down_grads(
            x_at, core_at, act_own, act_sent, attended_group, swap(attended_group, "c"), cot_group, cot_other
        ),
        late=(gate(attended_grad),),
    )
    grad_sent = swap(grad_other, "c")

    back = attend_backward(qkv, grads, logsum, all_tables, (down_slabs,))
    projected_grad = exchange(back.reshape(SEQ_DEVICES, ROWS, width), SEQ).reshape(TOKENS, width)

    parts, up_slabs = run(
        out_part(act_own, act_other, attended_group, downward, down_other, mixer_chip),
        up_grads(y_order, x_at, grad_own, grad_sent, normed, normed_other),
        late=(gate(back),),
    )
    stay, arrived = sum_rows(parts)
    outputs = (
        rows_in.astype(F32) + out_bias + stay.astype(F32) + arrived.astype(F32)
    ).astype(BF16)
    up_arrived = sent_y(up_slabs)
    down_sums = lax.psum_scatter(down_slabs, "y", scatter_dimension=0, tiled=False)
    down_sum = joined(down_sums[1], down_sums[0].astype(F32))

    projected_grad, up_first = tie((projected_grad, up_slabs[0]))
    attend_slabs = attend_grads(
        seq_order,
        core_at,
        projected_grad,
        swap(projected_grad, "c"),
        normed,
        normed_other,
        (up_first,),
    )

    parts, norm_sums, attend_bias_sum = normed_part(
        projected_grad,
        grad_own,
        grad_other,
        rows_group,
        attend_chip,
        upward,
        up_other,
        (attend_slabs[0], up_arrived[0], up_arrived[1], down_sum),
    )
    stay, arrived = sum_rows(parts)
    inputs_grad = rows_grad(rows_in, own_cot, stay, arrived, gain_all)

    bias_full = jnp.sum(own_cot.astype(F32), axis=0)
    attend_bias_full = lax.dynamic_update_slice(
        jnp.zeros((3, CHIPS, CHIP_COLS), F32), attend_bias_sum.reshape(3, 1, CHIP_COLS), (0, chip, 0)
    )
    up_bias_pair = jnp.where(
        core == 0,
        jnp.concatenate([up_bias_sum, up_bias_other_sum]),
        jnp.concatenate([up_bias_other_sum, up_bias_sum]),
    )
    up_bias_full = lax.dynamic_update_slice(
        jnp.zeros((CHIPS, 2, CORE_FF), F32), up_bias_pair[None], (chip, 0, 0)
    )
    vectors = jnp.concatenate(
        [
            v.reshape(FSDP_DEVICES, -1)
            for v in (norm_sums[0], norm_sums[1], bias_full, attend_bias_full, up_bias_full)
        ],
        axis=1,
    )
    vectors = exchange(vectors, FSDP)
    attend_sum = sum_seq(attend_slabs, sent_y(attend_slabs))
    attend_sum, vectors, last_up = tie((attend_sum, vectors, up_arrived[2]))
    up_arrived = [up_arrived[0], up_arrived[1], last_up]
    attend_slab, vectors = tie((spread(exchange(attend_sum, GROUP), SEQ, SEQ_DEVICES), vectors))
    vectors = spread(jnp.sum(vectors, axis=0), SEQ, SEQ_DEVICES)
    attend_grad = unpack_attend(attend_slab.reshape(SEQ_DEVICES, CHIPS, SLAB, width))
    down_grad, mixer_grad = unpack_down(seq_order, spread_seq(down_sum))
    up_grad = unpack_up(seq_order, spread_seq(sum_seq(up_slabs, up_arrived)))

    vectors = jnp.sum(vectors, axis=0)
    gain_grad, shift_grad, bias_grad = vectors[:128], vectors[128:256], vectors[256:384]
    attend_bias_grad, up_bias_grad = vectors[384:768], vectors[768:]

    return (
        outputs.reshape(inputs.shape),
        inputs_grad.reshape(inputs.shape),
        gain_grad,
        shift_grad,
        attend_grad,
        attend_bias_grad,
        mixer_grad,
        bias_grad,
        up_grad,
        up_bias_grad,
        down_grad,
        bias_grad,
    )


def solution(mesh):
    fine = Mesh(mesh.devices.reshape(4, 2, 2, 4, 2), ("y", "xl", "xh", "z", "c"))
    rows = P(FSDP, SEQ, None)
    vector = P(FSDP)
    by_row = P(FSDP, None)
    by_col = P(None, FSDP)
    in_specs = (
        rows,
        vector,
        vector,
        by_row,
        vector,
        by_row,
        vector,
        by_col,
        vector,
        by_row,
        vector,
        rows,
    )
    out_specs = (
        rows,
        rows,
        vector,
        vector,
        by_row,
        vector,
        by_row,
        vector,
        by_col,
        vector,
        by_row,
        vector,
    )
    return jax.shard_map(
        per_device, mesh=fine, in_specs=in_specs, out_specs=out_specs, check_vma=False
    )
```

```python
from typing import Callable, NamedTuple, Sequence

import jax
import jax.numpy as jnp
from jax import lax
from jax.experimental import pallas as pl
from jax.experimental.pallas import tpu as pltpu
from jax.sharding import Mesh, PartitionSpec as P

HEADS = 32
HEAD_DIM = 64
ROT = 32
WIDTH = 2048
FF = 8192
SEQ_DEVICES = 8
CHIPS = 8
FSDP_DEVICES = 16
ROWS = 128
LENGTH = ROWS * SEQ_DEVICES
TOKENS = ROWS * CHIPS
CHIP_COLS = WIDTH // CHIPS
CORE_COLS = WIDTH // FSDP_DEVICES
CORE_FF = FF // FSDP_DEVICES
PAIR = 2 * HEAD_DIM
QBLOCK = 256

EPSILON = 1e-05
ROPE_BASE = 10000.0
NEG_FILL = -1e30
PACE = 1 * 1.15e9
MICROSECONDS = dict(
    assemble_attend=6,
    norm_project=13,
    hidden_forward=11,
    attend_forward=10,
    grad_heads=15,
    hidden_back=30,
    down_grads=30,
    attend_backward=15,
    out_part=30,
    up_grads=30,
    attend_grads=25,
    normed_part=43,
    unpack_down=6,
    unpack_up=6,
    unpack_attend=6,
    rows_grad=3,
)
SCALE = HEAD_DIM ** (-0.5)

F32 = jnp.float32
BF16 = jnp.bfloat16

SEQ = ("y", "xl")
GROUP = ("xh", "z")
FSDP = ("xh", "z", "c")

NT = (((1,), (1,)), ((), ()))
TN = (((0,), (0,)), ((), ()))
NN = (((1,), (0,)), ((), ()))


def dot(lhs, rhs, dims=NN):
    return lax.dot_general(lhs, rhs, dims, preferred_element_type=F32)


def swap(piece, axis):
    return lax.ppermute(piece, axis, [(0, 1), (1, 0)])


def shift(piece, axis, step):
    return lax.ppermute(piece, axis, [(i, (i - step) % 4) for i in range(4)])


def send(piece, axis, step):
    return lax.ppermute(piece, axis, [(i, (i + step) % 4) for i in range(4)])


def rope_tables(positions, heads):
    half = ROT // 2
    frequency = ROPE_BASE ** (-2.0 * jnp.arange(half, dtype=F32) / ROT)
    angle = positions.astype(F32)[:, None] * frequency[None, :]
    cosine, sine = jnp.cos(angle), jnp.sin(angle)
    rest = jnp.zeros((positions.shape[0], HEAD_DIM - ROT), F32)
    blank = jnp.zeros_like(sine)
    turn = jnp.concatenate([cosine, cosine, rest + 1.0], axis=1)
    upper = jnp.concatenate([-sine, blank, rest], axis=1)
    lower = jnp.concatenate([blank, sine, rest], axis=1)
    return tuple(jnp.concatenate([t] * heads, axis=1) for t in (turn, upper, lower))


def turn_columns(values, turn, upper, lower, sign):
    width = values.shape[1]
    half = ROT // 2
    ahead = pltpu.roll(values, width - half, 1)
    behind = pltpu.roll(values, half, 1)
    return values * turn + sign * (ahead * upper + behind * lower)


def cost(names):
    return pl.CostEstimate(
        flops=int(sum(MICROSECONDS[name] for name in names) * PACE), bytes_accessed=0, transcendentals=0
    )


def whole(shape):
    return pl.BlockSpec(shape, lambda i: (0,) * len(shape))


def row_block(rows, width, column=0):
    return pl.BlockSpec((rows, width), lambda i: (i, column))


class Job(NamedTuple):
    name: str
    kernel: Callable
    grid: int
    in_specs: Sequence
    out_specs: Sequence
    out_shape: Sequence
    operands: tuple
    scratch: tuple = ()
    plan: tuple = ()


def run(*jobs, late=()):
    plans = [len(job.plan) for job in jobs]
    starts = [sum(job.grid for job in jobs[:k]) for k in range(len(jobs))]

    def moved(spec, start, count, first, size):
        def index(step, *plan):
            own = plan[first : first + size]
            return spec.index_map(jnp.clip(step - start, 0, count - 1) if len(jobs) > 1 else step, *own)

        return pl.BlockSpec(spec.block_shape, index)

    def specs_of(kind):
        return [
            moved(spec, starts[k], job.grid, sum(plans[:k]), plans[k])
            for k, job in enumerate(jobs)
            for spec in getattr(job, kind)
        ]

    def body(*refs):
        refs = list(refs)
        take = lambda count: [refs.pop(0) for _ in range(count)]
        plan_refs = [take(count) for count in plans]
        in_refs = [take(len(job.operands)) for job in jobs]
        take(len(late))
        out_refs = [take(len(job.out_specs)) for job in jobs]
        held = [take(len(job.scratch)) for job in jobs]
        step = pl.program_id(0)
        for k, job in enumerate(jobs):
            own = (*plan_refs[k], *in_refs[k], *out_refs[k], *held[k])
            if len(jobs) == 1:
                job.kernel(step, *own)
            else:

                @pl.when((step >= starts[k]) & (step < starts[k] + job.grid))
                def _():
                    job.kernel(step - starts[k], *own)

    found = pl.pallas_call(
        body,
        grid_spec=pltpu.PrefetchScalarGridSpec(
            num_scalar_prefetch=sum(plans),
            grid=(sum(job.grid for job in jobs),),
            in_specs=specs_of("in_specs") + [pl.BlockSpec(memory_space=pl.ANY)] * len(late),
            out_specs=specs_of("out_specs"),
            scratch_shapes=[shape for job in jobs for shape in job.scratch],
        ),
        out_shape=[shape for job in jobs for shape in job.out_shape],
        compiler_params=pltpu.CompilerParams(vmem_limit_bytes=60 * 2**20),
        cost_estimate=cost([job.name for job in jobs]),
        name="_".join(job.name for job in jobs),
    )(*(p for job in jobs for p in job.plan), *(a for job in jobs for a in job.operands), *late)
    found = list(found)
    results = []
    for job in jobs:
        own, found = found[: len(job.out_specs)], found[len(job.out_specs) :]
        results.append(own[0] if len(own) == 1 else own)
    return results[0] if len(jobs) == 1 else results


def listed(value):
    return list(value) if isinstance(value, (list, tuple)) else [value]


def call(
    kernel, name, grid, in_specs, out_specs, out_shape, flops, moved, operands, late=(), scratch=(), plan=()
):
    job = Job(
        name, kernel, grid, in_specs, listed(out_specs), listed(out_shape), operands, tuple(scratch), plan
    )
    return job if late is None else run(job, late=late)


def placed_call(
    kernel, name, grid, in_specs, out_specs, out_shape, scratch, flops, moved, order, operands, late=()
):
    return call(
        kernel, name, grid, in_specs, out_specs, out_shape, flops, moved, operands, late, scratch, (order,)
    )


def fixed(dims):
    return pl.BlockSpec(dims, lambda i, order: (0,) * len(dims))


def shape(dims, kind=BF16):
    return jax.ShapeDtypeStruct(dims, kind)


def layer_stats(rows):
    center = rows - jnp.mean(rows, axis=-1, keepdims=True)
    spread_out = jnp.mean(center * center, axis=-1, keepdims=True)
    return center, lax.rsqrt(spread_out + EPSILON)


def assemble_kernel(core_ref, own_ref, other_ref, out_ref):
    core = core_ref[0]
    out_ref[0, core] = own_ref[...].reshape(out_ref.shape[2:])
    out_ref[0, 1 - core] = other_ref[...].reshape(out_ref.shape[2:])


def assemble_attend(core, own, other):
    slab, cols = own.shape[2:]
    piece = pl.BlockSpec((SEQ_DEVICES, 1, slab, cols), lambda g, core: (0, g, 0, 0))
    out = (CHIPS, 2, SEQ_DEVICES, slab, cols)
    return pl.pallas_call(
        assemble_kernel,
        grid_spec=pltpu.PrefetchScalarGridSpec(
            num_scalar_prefetch=1,
            grid=(CHIPS,),
            in_specs=[piece, piece],
            out_specs=pl.BlockSpec((1,) + out[1:], lambda g, core: (g, 0, 0, 0, 0)),
        ),
        out_shape=shape(out),
        compiler_params=pltpu.CompilerParams(vmem_limit_bytes=60 * 2**20),
        cost_estimate=cost(["assemble_attend"]),
        name="assemble_attend",
    )(core, own, other).reshape(WIDTH, cols)


def put_rows(step, near_ref, far_refs, held):
    held[:ROWS] = near_ref[...]
    for index, far_ref in enumerate(far_refs):

        @pl.when(step == index)
        def _():
            held[ROWS:] = far_ref[...]


def norm_project_kernel(
    step,
    at_ref,
    order_ref,
    near_ref,
    far_0,
    far_1,
    far_2,
    far_3,
    gain_ref,
    shift_ref,
    weight_ref,
    bias_ref,
    turn_ref,
    upper_ref,
    lower_ref,
    normed_ref,
    out_ref,
    held,
):
    put_rows(step, near_ref, (far_0, far_1, far_2, far_3), held)
    rows = held[...]
    center, inverse = layer_stats(rows.astype(F32))
    normed = (center * inverse * gain_ref[...] + shift_ref[...]).astype(BF16)
    normed_ref[...] = normed
    projected = dot(normed, weight_ref[...]) + bias_ref[...]
    turned_width = 2 * CHIP_COLS
    for block in range(2):
        rows = slice(block * ROWS, (block + 1) * ROWS)
        for start in range(0, turned_width, PAIR):
            cols = slice(start, start + PAIR)
            out_ref[rows, cols] = turn_columns(
                projected[rows, cols], turn_ref[...], upper_ref[...], lower_ref[...], 1.0
            ).astype(BF16)
    out_ref[:, turned_width:] = projected[:, turned_width:].astype(BF16)


def norm_project(seq_at, order, near, far, gain, shift_row, weight, bias, tables, late):
    block = 2 * ROWS
    width = weight.shape[1]
    vectors = (gain, shift_row, weight, bias)
    row = lambda rows, cols: pl.BlockSpec((rows, cols), lambda i, at, order: (order[i], 0))
    own = pl.BlockSpec((ROWS, PAIR), lambda i, at, order: (at[0], 0))
    held = lambda array: pl.BlockSpec(array.shape, lambda i, at, order: (0, 0))
    return call(
        norm_project_kernel,
        "norm_project",
        4,
        [row(ROWS, WIDTH)] + [held(a) for a in (*far, *vectors)] + [own] * 3,
        [row(block, WIDTH), row(block, width)],
        [shape((TOKENS, WIDTH)), shape((TOKENS, width))],
        0,
        0,
        (near, *far) + vectors + tables,
        late,
        [pltpu.VMEM((block, WIDTH), BF16)],
        (seq_at, order),
    )


def hidden_kernel(
    step,
    normed_ref,
    own_ref,
    other_ref,
    own_bias_ref,
    other_bias_ref,
    own_act_ref,
    other_act_ref,
    own_slope_ref,
    other_slope_ref,
):
    root = (2.0 / 3.141592653589793) ** 0.5
    for weight, bias, act, slope in (
        (own_ref, own_bias_ref, own_act_ref, own_slope_ref),
        (other_ref, other_bias_ref, other_act_ref, other_slope_ref),
    ):
        hidden = dot(normed_ref[...], weight[...]) + bias[...]
        square = hidden * hidden
        bend = jnp.tanh(root * hidden * (1.0 + 0.044715 * square))
        half = 0.5 * (1.0 + bend)
        act[...] = (hidden * half).astype(BF16)
        slope[...] = half + 0.5 * hidden * (1.0 - bend * bend) * (
            root * (1.0 + 3.0 * 0.044715 * square)
        )


def hidden_forward(normed, own, other, own_bias, other_bias):
    block = 256
    operands = (own, other, own_bias, other_bias)
    return call(
        hidden_kernel,
        "hidden_forward",
        TOKENS // block,
        [row_block(block, WIDTH)] + [whole(v.shape) for v in operands],
        [row_block(block, CORE_FF)] * 4,
        [shape((TOKENS, CORE_FF))] * 2 + [shape((TOKENS, CORE_FF), F32)] * 2,
        4 * TOKENS * WIDTH * CORE_FF,
        14 * 2**20,
        (normed,) + operands,
    )


def grad_heads_kernel(step, cot_ref, mixer_ref, out_ref):
    out_ref[...] = dot(cot_ref[...], mixer_ref[...], NT).astype(BF16)


def grad_heads(cot, mixer, late):
    block = 256
    return call(
        grad_heads_kernel,
        "grad_heads",
        TOKENS // block,
        [row_block(block, WIDTH), whole(mixer.shape)],
        row_block(block, CHIP_COLS),
        shape((TOKENS, CHIP_COLS)),
        2 * TOKENS * WIDTH * CHIP_COLS,
        6 * 2**20,
        (cot, mixer),
        late,
    )


def hidden_back_kernel(
    step,
    cot_ref, own_ref, other_ref, own_slope_ref, other_slope_ref, own_out, other_out, own_sum, other_sum
):
    for weight, slope, out, total in (
        (own_ref, own_slope_ref, own_out, own_sum),
        (other_ref, other_slope_ref, other_out, other_sum),
    ):
        grad = (dot(cot_ref[...], weight[...], NT) * slope[...]).astype(BF16)
        out[...] = grad
        part = jnp.sum(grad.astype(F32), axis=0, keepdims=True)

        @pl.when(step == 0)
        def _():
            total[...] = part

        @pl.when(step > 0)
        def _():
            total[...] += part


def hidden_back(cot, own, other, own_slope, other_slope):
    block = 256
    return call(
        hidden_back_kernel,
        "hidden_back",
        TOKENS // block,
        [row_block(block, WIDTH), whole(own.shape), whole(other.shape)]
        + [row_block(block, CORE_FF)] * 2,
        [row_block(block, CORE_FF)] * 2 + [whole((1, CORE_FF))] * 2,
        [shape((TOKENS, CORE_FF))] * 2 + [shape((1, CORE_FF), F32)] * 2,
        4 * TOKENS * WIDTH * CORE_FF,
        14 * 2**20,
        (cot, own, other, own_slope, other_slope),
        None,
    )


def out_part_kernel(step, own_act, other_act, attended, own_ref, other_ref, mixer_ref, out_ref):
    out_ref[...] = (
        dot(own_act[...], own_ref[...])
        + dot(other_act[...], other_ref[...])
        + dot(attended[...], mixer_ref[...])
    ).astype(BF16)


def out_part(own_act, other_act, attended, own, other, mixer):
    block = 256
    weights = (own, other, mixer)
    return call(
        out_part_kernel,
        "out_part",
        TOKENS // block,
        [row_block(block, CORE_FF)] * 2
        + [row_block(block, CHIP_COLS)]
        + [whole(w.shape) for w in weights],
        row_block(block, WIDTH),
        shape((TOKENS, WIDTH)),
        2 * TOKENS * WIDTH * (2 * CORE_FF + CHIP_COLS),
        12 * 2**20,
        (own_act, other_act, attended) + weights,
        None,
    )


def normed_part_kernel(
    step,
    order_ref,
    projected,
    own_grad,
    other_grad,
    near_ref,
    far_0,
    far_1,
    far_2,
    far_3,
    attend_ref,
    own_ref,
    other_ref,
    out_ref,
    sums_ref,
    bias_ref,
    held,
):
    put_rows(step, near_ref, (far_0, far_1, far_2, far_3), held)
    total = (
        dot(projected[...], attend_ref[...], NT)
        + dot(own_grad[...], own_ref[...], NT)
        + dot(other_grad[...], other_ref[...], NT)
    )
    out_ref[...] = total.astype(BF16)
    center, inverse = layer_stats(held[...].astype(F32))
    gain_part = jnp.sum(total * (center * inverse), axis=0, keepdims=True)
    shift_part = jnp.sum(total, axis=0, keepdims=True)
    bias_part = jnp.sum(projected[...].astype(F32), axis=0, keepdims=True)

    @pl.when(step == 0)
    def _():
        sums_ref[0:1] = gain_part
        sums_ref[1:2] = shift_part
        bias_ref[...] = bias_part

    @pl.when(step > 0)
    def _():
        sums_ref[0:1] += gain_part
        sums_ref[1:2] += shift_part
        bias_ref[...] += bias_part


def normed_part(order, projected, own_grad, other_grad, near, far, attend, own, other, late):
    block = 2 * ROWS
    width = projected.shape[1]
    row = lambda rows, cols: pl.BlockSpec((rows, cols), lambda i, order: (order[i], 0))
    weights = (attend, own, other)
    return call(
        normed_part_kernel,
        "normed_part",
        4,
        [row(block, width), row(block, CORE_FF), row(block, CORE_FF), row(ROWS, WIDTH)]
        + [fixed(a.shape) for a in (*far, *weights)],
        [row(block, WIDTH), fixed((2, WIDTH)), fixed((1, width))],
        [shape((TOKENS, WIDTH)), shape((2, WIDTH), F32), shape((1, width), F32)],
        0,
        0,
        (projected, own_grad, other_grad, near, *far) + weights,
        late,
        [pltpu.VMEM((block, WIDTH), BF16)],
        (order,),
    )


UP_ROWS = WIDTH // SEQ_DEVICES
DOWN_ROWS = CORE_FF // 2
MIX_ROWS = CORE_COLS // 2
PACK_ROWS = UP_ROWS + MIX_ROWS
PACK_COLS = CORE_FF
HALF = PACK_COLS // 2
SLOT_COLS = WIDTH // SEQ_DEVICES


def across(rows):
    return pl.BlockSpec((rows, SLOT_COLS), lambda i, order: (0, order[i]))


def plan_call(
    kernel, name, grid, in_specs, out_specs, out_shape, scratch, flops, moved, order, side, operands, late=()
):
    return call(
        kernel, name, grid, in_specs, out_specs, out_shape, flops, moved, operands, late, scratch, (order, side)
    )


def plan_whole(array):
    return pl.BlockSpec(array.shape, lambda i, order, side: (0, 0))


WIDE = 2 * SLOT_COLS
WIDE_COLUMNS = pl.BlockSpec((TOKENS, WIDE), lambda i, order, side: (0, order[i]))


def down_grads_kernel(step, order_ref, x_ref, act_ref, act_other, cot_ref, cot_other, *refs):
    outs = refs
    down = (dot(act_ref[...], cot_ref[...], TN) + dot(act_other[...], cot_other[...], TN)).astype(BF16)
    for index, out_ref in enumerate(outs):
        for x in range(2):

            @pl.when((step == index) & (x_ref[0] == x))
            def _():
                for r, half in ((0, x), (1, 1 - x)):
                    cols = slice(half * SLOT_COLS, (half + 1) * SLOT_COLS)
                    out_ref[r, :, :HALF] = down[:DOWN_ROWS, cols]
                    out_ref[r, :, HALF:] = down[DOWN_ROWS:, cols]


def down_grads(order, x_lo, act, act_other, cot, cot_other):
    block = (2, DOWN_ROWS, PACK_COLS)
    return Job(
        "down_grads",
        down_grads_kernel,
        4,
        [plan_whole(act), plan_whole(act_other)] + [WIDE_COLUMNS] * 2,
        [pl.BlockSpec(block, lambda i, order, side: (0, 0, 0))] * 4,
        [shape(block)] * 4,
        (act, act_other, cot, cot_other),
        (),
        (order, x_lo),
    )


def up_grads_kernel(
    step,
    order_ref,
    x_ref,
    core_ref,
    grad_ref,
    grad_other,
    att_ref,
    att_other,
    normed_ref,
    normed_other,
    cot_ref,
    cot_other,
    *refs,
):
    outs, held, mixed = refs[:4], refs[4], refs[5]
    held[...] = (
        dot(normed_ref[...], grad_ref[...], TN) + dot(normed_other[...], grad_other[...], TN)
    ).astype(BF16)
    cols = pl.ds(pl.multiple_of(core_ref[0] * CORE_COLS, CORE_COLS), CORE_COLS)
    mixed[...] = (
        dot(att_ref[:, cols], cot_ref[...], TN) + dot(att_other[:, cols], cot_other[...], TN)
    ).astype(BF16)
    for index, out_ref in enumerate(outs):

        @pl.when(step == index)
        def _():
            for r, x in enumerate((x_ref[0], 1 - x_ref[0])):
                out_ref[r, :UP_ROWS] = held[pl.ds(pl.multiple_of(x * UP_ROWS, UP_ROWS), UP_ROWS), :]
                part = mixed[:, pl.ds(pl.multiple_of(x * SLOT_COLS, SLOT_COLS), SLOT_COLS)]
                out_ref[r, UP_ROWS:, :HALF] = part[:MIX_ROWS]
                out_ref[r, UP_ROWS:, HALF:] = part[MIX_ROWS:]


def up_grads(order, x_lo, core, grad, grad_other, att, att_other, normed, normed_other, cot, cot_other):
    block = (2, PACK_ROWS, PACK_COLS)
    columns = pl.BlockSpec((TOKENS, WIDE), lambda i, order, *plan: (0, order[i]))
    held = [pl.BlockSpec(a.shape, lambda i, *plan: (0, 0)) for a in (grad, grad_other, att, att_other)]
    return Job(
        "up_grads",
        up_grads_kernel,
        4,
        held + [columns] * 4,
        [pl.BlockSpec(block, lambda i, *plan: (0, 0, 0))] * 4,
        [shape(block)] * 4,
        (grad, grad_other, att, att_other, normed, normed_other, cot, cot_other),
        (pltpu.VMEM((2 * UP_ROWS, CORE_FF), BF16), pltpu.VMEM((CORE_COLS, WIDE), BF16)),
        (order, x_lo, core),
    )


def attend_grads_kernel(step, order_ref, core_ref, grad_ref, grad_other, own_0, own_1, other_0, other_1, *refs):
    outs, held = refs[:4], refs[4]
    for half, (own, other) in enumerate(((own_0, other_0), (own_1, other_1))):
        held[half] = (
            dot(own[...], grad_ref[...], TN) + dot(other[...], grad_other[...], TN)
        ).astype(BF16)
    for slot in range(SEQ_DEVICES):
        rows = pl.ds(pl.multiple_of(order_ref[slot] * SLAB, SLAB), SLAB)
        for half in range(2):
            outs[slot // 2][slot % 2, half] = held[half, rows, :]


def attend_grads(order, core, grad, grad_other, normed, normed_other, late):
    cols = grad.shape[1]

    def rows_of(half):
        return pl.BlockSpec((TOKENS, CORE_COLS), lambda i, order, core: (0, 4 * i + 2 * half + core[0]))

    return plan_call(
        attend_grads_kernel,
        "attend_grads",
        CHIPS // 2,
        [plan_whole(grad), plan_whole(grad_other)] + [rows_of(0), rows_of(1)] * 2,
        [pl.BlockSpec((2, 2, SLAB, cols), lambda i, order, core: (0, i, 0, 0))] * 4,
        [shape((2, CHIPS, SLAB, cols))] * 4,
        [pltpu.VMEM((2, CORE_COLS, cols), BF16)],
        4 * TOKENS * WIDTH * cols // 2,
        12 * 2**20,
        order,
        core,
        (grad, grad_other, normed, normed, normed_other, normed_other),
        late,
    )


def unpack_down_kernel(step, order_ref, *refs):
    down_ref = refs[4]
    for index, pieces in enumerate(refs[:4]):

        @pl.when(step // 2 == index)
        def _():
            piece = pieces.at[step % 2]
            down_ref[:DOWN_ROWS] = piece[:, :HALF].astype(F32)
            down_ref[DOWN_ROWS:] = piece[:, HALF:].astype(F32)


def unpack_down(order, pieces, late):
    return placed_call(
        unpack_down_kernel,
        "unpack_down",
        SEQ_DEVICES,
        [fixed((2, DOWN_ROWS, PACK_COLS))] * 4,
        across(CORE_FF),
        shape((CORE_FF, WIDTH), F32),
        [],
        0,
        0,
        order,
        tuple(pieces),
        late,
    )


def unpack_up_kernel(step, x_ref, piece, up_ref, mix_ref):
    up_ref[...] = piece[0, 0, :UP_ROWS].astype(F32)
    mix_ref[:MIX_ROWS] = piece[0, 0, UP_ROWS:, :HALF].astype(F32)
    mix_ref[MIX_ROWS:] = piece[0, 0, UP_ROWS:, HALF:].astype(F32)


def unpack_up(x_lo, pairs, late):
    slot = lambda i, x: 2 * (i // 2) + lax.rem(i + x[0], 2)
    return call(
        unpack_up_kernel,
        "unpack_up",
        SEQ_DEVICES,
        [pl.BlockSpec((1, 1, PACK_ROWS, PACK_COLS), lambda i, x: (i // 2, i % 2, 0, 0))],
        [
            pl.BlockSpec((UP_ROWS, CORE_FF), lambda i, x: (slot(i, x), 0)),
            pl.BlockSpec((CORE_COLS, SLOT_COLS), lambda i, x: (0, slot(i, x))),
        ],
        [shape((WIDTH, CORE_FF), F32), shape((CORE_COLS, WIDTH), F32)],
        0,
        0,
        (pairs,),
        late,
        (),
        (x_lo,),
    )


SLAB = CORE_COLS // SEQ_DEVICES


def unpack_attend_kernel(step, packed_ref, out_ref):
    for chip in range(CHIPS):
        for part in range(3):
            out_ref[:, part * WIDTH + chip * CHIP_COLS : part * WIDTH + (chip + 1) * CHIP_COLS] = (
                packed_ref[0, chip * SLAB : (chip + 1) * SLAB, part * CHIP_COLS : (part + 1) * CHIP_COLS].astype(F32)
            )


def unpack_attend(packed, late):
    return call(
        unpack_attend_kernel,
        "unpack_attend",
        SEQ_DEVICES,
        [pl.BlockSpec((1,) + packed.shape[1:], lambda i: (i, 0, 0))],
        row_block(SLAB, 3 * WIDTH),
        shape((CORE_COLS, 3 * WIDTH), F32),
        0,
        5 * 2**20,
        (packed,),
        late,
    )


def rows_grad_kernel(step, rows_ref, cot_ref, near_ref, far_ref, gain_ref, out_ref):
    grad = near_ref[...].astype(F32) + far_ref[...].astype(F32)
    center, inverse = layer_stats(rows_ref[...].astype(F32))
    unit = center * inverse
    scaled = grad * gain_ref[...]
    out_ref[...] = cot_ref[...].astype(F32) + inverse * (
        scaled
        - jnp.mean(scaled, axis=-1, keepdims=True)
        - unit * jnp.mean(scaled * unit, axis=-1, keepdims=True)
    )


def rows_grad(rows, cot, near, far, gain):
    block = 64
    return call(
        rows_grad_kernel,
        "rows_grad",
        ROWS // block,
        [row_block(block, WIDTH)] * 4 + [whole(gain.shape)],
        row_block(block, WIDTH),
        shape((ROWS, WIDTH), F32),
        0,
        4 * 2**20,
        (rows, cot, near, far, gain),
    )


def lane_masks():
    lane = lax.broadcasted_iota(jnp.int32, (1, PAIR), 1)
    first = (lane < HEAD_DIM).astype(BF16)
    return first, 1 - first


def scores_of(query, keys, low):
    scores = dot(query, keys, NT)
    if low:
        head, last = scores[:, :low], scores[:, low:]
    else:
        head, last = None, scores
    row = lax.broadcasted_iota(jnp.int32, last.shape, 0)
    col = lax.broadcasted_iota(jnp.int32, last.shape, 1)
    last = jnp.where(col <= row, last, NEG_FILL)
    return last if head is None else jnp.concatenate([head, last], axis=1)


def attend_kernel(step, query_ref, key_ref, value_ref, out_ref, logsum_ref):
    first, second = lane_masks()
    lane = lax.broadcasted_iota(jnp.int32, (QBLOCK, PAIR), 1)
    for low in range(0, LENGTH, QBLOCK):
        reach = low + QBLOCK
        query = query_ref[low:reach, :] * BF16(SCALE)
        keys = key_ref[:reach, :]
        values = value_ref[:reach, :]
        found = []
        for mask in (first, second):
            scores = scores_of(query * mask, keys, low)
            peak = jnp.max(scores, axis=1, keepdims=True)
            weight = jnp.exp(scores - peak)
            total = jnp.sum(weight, axis=1, keepdims=True)
            found.append((dot(weight.astype(BF16), values) / total, peak + jnp.log(total)))
        out_ref[low:reach, :] = jnp.where(lane < HEAD_DIM, found[0][0], found[1][0]).astype(BF16)
        logsum_ref[low:reach, :] = jnp.where(lane < HEAD_DIM, found[0][1], found[1][1])


def pair_columns(part):
    return pl.BlockSpec((LENGTH, PAIR), lambda p: (0, part * (CHIP_COLS // PAIR) + p))


def attend_forward(qkv, late):
    return call(
        attend_kernel,
        "attend_forward",
        CHIP_COLS // PAIR,
        [pair_columns(0), pair_columns(1), pair_columns(2)],
        [pair_columns(0)] * 2,
        [shape((LENGTH, CHIP_COLS)), shape((LENGTH, CHIP_COLS), F32)],
        8 * 2**30,
        4 * 2**20,
        (qkv, qkv, qkv),
        late,
    )


def attend_back_kernel(
    step,
    query_ref,
    key_ref,
    value_ref,
    grad_ref,
    logsum_ref,
    turn_ref,
    upper_ref,
    lower_ref,
    out_ref,
    key_total,
    value_total,
):
    pair = step
    first, second = lane_masks()
    lane = lax.broadcasted_iota(jnp.int32, (QBLOCK, PAIR), 1)
    key_total[...] = jnp.zeros_like(key_total)
    value_total[...] = jnp.zeros_like(value_total)

    def store(part, low, reach, values):
        start = pl.multiple_of((part * (CHIP_COLS // PAIR) + pair) * PAIR, PAIR)
        out_ref[low:reach, pl.ds(start, PAIR)] = values.astype(BF16)

    def unturn(values, low, reach):
        kept = values.astype(BF16).astype(F32)
        return turn_columns(
            kept, turn_ref[low:reach, :], upper_ref[low:reach, :], lower_ref[low:reach, :], -1.0
        )

    for low in range(0, LENGTH, QBLOCK):
        reach = low + QBLOCK
        query = query_ref[low:reach, :] * BF16(SCALE)
        grad = grad_ref[low:reach, :]
        keys = key_ref[:reach, :]
        values = value_ref[:reach, :]
        query_grads = []
        key_part = 0.0
        value_part = 0.0
        for head, mask in enumerate((first, second)):
            own_query = query * mask
            own_grad = grad * mask
            scores = scores_of(own_query, keys, low)
            start = head * HEAD_DIM
            probs = jnp.exp(scores - logsum_ref[low:reach, start : start + 1])
            prob_grad = dot(own_grad, values, NT)
            inner = jnp.sum(probs * prob_grad, axis=1, keepdims=True)
            score_grad = (probs * (prob_grad - inner)).astype(BF16)
            query_grads.append(dot(score_grad, keys))
            key_part += dot(score_grad, own_query, TN)
            value_part += dot(probs.astype(BF16), own_grad, TN)
        key_total[:reach, :] += key_part
        value_total[:reach, :] += value_part
        query_grad = jnp.where(lane < HEAD_DIM, query_grads[0], query_grads[1]) * SCALE
        store(0, low, reach, unturn(query_grad, low, reach))
    store(1, 0, LENGTH, unturn(key_total[...], 0, LENGTH))
    store(2, 0, LENGTH, value_total[...])


def attend_backward(qkv, grad, logsum, tables, late):
    return call(
        attend_back_kernel,
        "attend_backward",
        CHIP_COLS // PAIR,
        [pair_columns(0), pair_columns(1), pair_columns(2), pair_columns(0), pair_columns(0)]
        + [whole(t.shape) for t in tables],
        whole((LENGTH, 3 * CHIP_COLS)),
        shape((LENGTH, 3 * CHIP_COLS)),
        20 * 2**30,
        6 * 2**20,
        (qkv, qkv, qkv, grad, logsum) + tables,
        late,
        [pltpu.VMEM((LENGTH, PAIR), F32)] * 2,
    )


def exchange(blocks, axes):
    return lax.all_to_all(blocks, axes, split_axis=0, concat_axis=0, tiled=True)


def spread(block, axes, count):
    return exchange(jnp.broadcast_to(block[None], (count,) + block.shape), axes)


def gate(value):
    return swap(value.reshape(-1, value.shape[-1])[:16, :128], "c")


tie = lax.optimization_barrier


def sent_y(parts):
    return [send(parts[k], "y", k) for k in (1, 3, 2)]


def joined(leave, stay):
    return (stay + swap(leave.astype(BF16), "xl").astype(F32)).astype(BF16)


def sum_seq(parts, arrived):
    leave, stay = (
        parts[0][r].astype(F32) + sum(a[r].astype(F32) for a in arrived) for r in (1, 0)
    )
    return joined(leave, stay)


def in_rows(values):
    width = 3 * CHIP_COLS
    count = values.shape[0]
    head = lax.reduce_precision(values, 8, 7)
    rest = (values - head).astype(BF16)
    head = head.astype(BF16)
    rows = [jnp.pad(part, ((0, 0), (0, 2 * width - part.shape[1]))).reshape(count, 2, width) for part in (head, rest)]
    return jnp.pad(jnp.concatenate(rows, axis=1), ((0, 0), (0, SLAB - 4), (0, 0)))


def from_rows(rows):
    count = rows.shape[0]
    head, rest = (rows[:, k : k + 2].reshape(count, -1)[:, :1280].astype(F32) for k in (0, 2))
    return head + rest


def summed_y(parts, arrived):
    return (parts[0].astype(F32) + sum(a.astype(F32) for a in arrived)).astype(BF16)


def summed_pair(own, other):
    return (own.astype(F32) + other[::-1].astype(F32)).astype(BF16)


def spread_y(pair):
    found = {0: pair} | {k: shift(pair, "y", k) for k in (1, 3, 2)}
    return [found[k] for k in range(4)]


def sum_rows(parts):
    parts = lax.psum_scatter(
        parts.reshape(4, 2, ROWS, WIDTH), "z", scatter_dimension=0, tiled=False
    )
    return parts[0], swap(parts[1], "xh")


def per_device(
    inputs,
    gains,
    shifts,
    attend,
    attend_bias,
    mixer,
    mixer_bias,
    upward,
    upward_bias,
    downward,
    downward_bias,
    cotangent,
):
    core = lax.axis_index("c")
    x_lo = lax.axis_index("xl")
    chip = lax.axis_index("xh") * 4 + lax.axis_index("z")
    seq_index = lax.axis_index("y") * 2 + x_lo
    core_at = core.reshape(1)
    rows_in = inputs.reshape(ROWS, WIDTH)
    own_cot = cotangent.reshape(ROWS, WIDTH)
    width = 3 * CHIP_COLS

    z_order = (lax.axis_index("z") + jnp.arange(4, dtype=jnp.int32)) % 4
    y_order = (lax.axis_index("y") + jnp.arange(4, dtype=jnp.int32)) % 4
    seq_order = (y_order[:, None] * 2 + jnp.stack([x_lo, 1 - x_lo])[None, :]).reshape(SEQ_DEVICES)

    near = lax.all_gather(rows_in, "z", axis=0, tiled=True)
    other_rows = swap(rows_in, "xh")

    slab = lax.dynamic_slice_in_dim(attend, seq_index * SLAB, SLAB, 0)
    slab = slab.reshape(SLAB, 3, CHIPS, CHIP_COLS).transpose(2, 0, 1, 3).reshape(CHIPS, SLAB, width)
    small = jnp.concatenate([gains, shifts, mixer_bias, downward_bias, attend_bias])
    small = jnp.pad(small, (0, 2 * width - small.shape[0])).reshape(1, 2, width)
    small = jnp.pad(jnp.broadcast_to(small, (CHIPS, 2, width)), ((0, 0), (0, SLAB - 2), (0, 0)))
    message, all_tables = tie(
        (jnp.concatenate([slab, small], axis=1), rope_tables(jnp.arange(LENGTH, dtype=jnp.int32), 2))
    )
    slab, other_rows = tie((exchange(message, GROUP), other_rows))
    far = [other_rows] + [shift(other_rows, "z", k) for k in (1, 2, 3)]
    small_own = slab[:, SLAB : SLAB + 2].reshape(CHIPS, 2 * width)[:, :896]
    slab = slab[:, :SLAB]
    attend_own = spread(slab, SEQ, SEQ_DEVICES).reshape(SEQ_DEVICES, CHIPS, SLAB, width)
    attend_own, near, *far = tie((attend_own, near, *far))
    attend_chip = assemble_attend(core_at, attend_own, swap(attend_own, "c"))
    small_other = swap(small_own, "c")
    small_all = jnp.where(
        core == 0, jnp.stack([small_own, small_other], 1), jnp.stack([small_other, small_own], 1)
    ).reshape(FSDP_DEVICES, 7, 128).astype(F32)
    gain_all = small_all[:, 0].reshape(1, WIDTH)
    shift_all = small_all[:, 1].reshape(1, WIDTH)
    out_bias = (small_all[:, 2] + small_all[:, 3]).reshape(WIDTH)
    bias_grid = small_all[:, 4:7].reshape(3, CHIPS, CHIP_COLS)
    attend_bias_chip = lax.dynamic_slice_in_dim(bias_grid, chip, 1, 1).reshape(1, width)

    mixer_other = swap(mixer, "c")
    mixer_chip = jnp.where(
        core == 0, jnp.concatenate([mixer, mixer_other]), jnp.concatenate([mixer_other, mixer])
    )
    up_other = swap(upward, "c")
    down_other = swap(downward, "c")
    up_bias_own = upward_bias.astype(F32).reshape(1, CORE_FF)
    up_bias_other = swap(upward_bias.reshape(1, CORE_FF), "c").astype(F32)

    cot_pair = jnp.stack([own_cot, swap(own_cot, "xh")])
    cot_pair, near, *far = tie((cot_pair, near, *far))
    cot_group = lax.all_gather(cot_pair, "z", axis=0, tiled=False).reshape(TOKENS, WIDTH)
    normed, qkv_sent = norm_project(
        seq_index.reshape(1),
        z_order,
        near,
        far,
        gain_all,
        shift_all,
        attend_chip,
        attend_bias_chip,
        all_tables,
        (mixer_chip, up_other, down_other, up_bias_other, up_bias_own),
    )
    normed_other = swap(normed, "c")
    qkv = exchange(qkv_sent.reshape(CHIPS, ROWS, width), SEQ).reshape(LENGTH, width)
    act_own, act_other, slope_own, slope_other = hidden_forward(
        normed, upward, up_other, up_bias_own, up_bias_other
    )
    act_sent = swap(act_other, "c")

    attended, logsum = attend_forward(qkv, (act_own, normed_other))
    attended, cot_group = tie((attended, cot_group))
    attended_group = exchange(attended.reshape(SEQ_DEVICES, ROWS, CHIP_COLS), SEQ).reshape(
        TOKENS, CHIP_COLS
    )
    cot_other = swap(cot_group, "c")
    attended_grad = grad_heads(cot_group, mixer_chip, (attended,))
    grads = exchange(attended_grad.reshape(CHIPS, ROWS, CHIP_COLS), SEQ).reshape(LENGTH, CHIP_COLS)

    x_at = x_lo.reshape(1)
    (grad_own, grad_other, up_bias_sum, up_bias_other_sum), down_slabs = run(
        hidden_back(cot_group, downward, down_other, slope_own, slope_other),
        down_grads(y_order, x_at, act_own, act_sent, cot_group, cot_other),
        late=(gate(attended_grad),),
    )
    grad_sent = swap(grad_other, "c")

    back = attend_backward(qkv, grads, logsum, all_tables, (down_slabs[0],))
    projected_grad = exchange(back.reshape(SEQ_DEVICES, ROWS, width), SEQ).reshape(TOKENS, width)

    down_arrived = sent_y(down_slabs)
    parts, up_slabs = run(
        out_part(act_own, act_other, attended_group, downward, down_other, mixer_chip),
        up_grads(
            y_order,
            x_at,
            core_at,
            grad_own,
            grad_sent,
            attended_group,
            swap(attended_group, "c"),
            normed,
            normed_other,
            cot_group,
            cot_other,
        ),
        late=(gate(back), *down_arrived),
    )
    stay, arrived = sum_rows(parts)
    outputs = (
        rows_in.astype(F32) + out_bias + stay.astype(F32) + arrived.astype(F32)
    ).astype(BF16)
    up_arrived = sent_y(up_slabs)

    down_own = summed_y(down_slabs, down_arrived)
    down_other_x = swap(down_own, "xl")

    projected_grad, up_first = tie((projected_grad, up_slabs[0]))
    attend_slabs = attend_grads(
        seq_order,
        core_at,
        projected_grad,
        swap(projected_grad, "c"),
        normed,
        normed_other,
        (up_first,),
    )

    down_other_x, attend_first = tie((down_other_x, attend_slabs[0]))
    attend_slabs = [attend_first, *attend_slabs[1:]]
    down_pair = summed_pair(down_own, down_other_x)

    parts, norm_sums, attend_bias_sum = normed_part(
        z_order,
        projected_grad,
        grad_own,
        grad_other,
        near,
        far,
        attend_chip,
        upward,
        up_other,
        (attend_slabs[0],),
    )
    parts, down_pair, *up_arrived = tie((parts, down_pair, *up_arrived))
    stay, arrived = sum_rows(parts)
    inputs_grad = rows_grad(rows_in, own_cot, stay, arrived, gain_all)

    bias_full = jnp.sum(own_cot.astype(F32), axis=0)
    attend_bias_full = lax.dynamic_update_slice(
        jnp.zeros((3, CHIPS, CHIP_COLS), F32), attend_bias_sum.reshape(3, 1, CHIP_COLS), (0, chip, 0)
    )
    up_bias_pair = jnp.where(
        core == 0,
        jnp.concatenate([up_bias_sum, up_bias_other_sum]),
        jnp.concatenate([up_bias_other_sum, up_bias_sum]),
    )
    up_bias_full = lax.dynamic_update_slice(
        jnp.zeros((CHIPS, 2, CORE_FF), F32), up_bias_pair[None], (chip, 0, 0)
    )
    vectors = jnp.concatenate(
        [
            v.reshape(FSDP_DEVICES, -1)
            for v in (norm_sums[0], norm_sums[1], bias_full, attend_bias_full, up_bias_full)
        ],
        axis=1,
    )
    vectors = vectors.reshape(CHIPS, 2, -1)
    vectors_keep = lax.dynamic_index_in_dim(vectors, core, 1, keepdims=False)
    vectors_sent = lax.dynamic_index_in_dim(vectors, 1 - core, 1, keepdims=False)
    vectors = vectors_keep + swap(vectors_sent, "c")
    up_own = summed_y(up_slabs, up_arrived)
    up_pair = summed_pair(up_own, swap(up_own, "xl"))
    *attend_arrived, down_pair, up_pair = tie((*sent_y(attend_slabs), down_pair, up_pair))
    attend_sum = sum_seq(attend_slabs, attend_arrived)
    message, outputs = tie((jnp.concatenate([attend_sum, in_rows(vectors)], axis=1), outputs))
    message = exchange(message, GROUP)
    kept = message[:, SLAB : SLAB + 4].reshape(-1, width)
    message = jnp.concatenate([message[:, :SLAB].reshape(-1, width), kept], axis=0)
    message, *down_pieces = tie((message, *spread_y(down_pair)))
    message = spread(message, SEQ, SEQ_DEVICES).reshape(SEQ_DEVICES, -1, width)
    up_pairs = lax.all_gather(up_pair, "y", axis=0, tiled=False)
    down_grad = unpack_down(seq_order, down_pieces, ())
    attend_grad = unpack_attend(
        message,
        (inputs_grad, outputs, down_grad),
    )
    message, attend_grad = tie((message, attend_grad))
    vectors = jnp.sum(from_rows(message[:, CHIPS * SLAB :].reshape(-1, 4, width)), axis=0)
    up_grad, mixer_grad = unpack_up(x_at, up_pairs, (attend_grad,))

    gain_grad, shift_grad, bias_grad = vectors[:128], vectors[128:256], vectors[256:384]
    attend_bias_grad, up_bias_grad = vectors[384:768], vectors[768:]

    return (
        outputs.reshape(inputs.shape),
        inputs_grad.reshape(inputs.shape),
        gain_grad,
        shift_grad,
        attend_grad,
        attend_bias_grad,
        mixer_grad,
        bias_grad,
        up_grad,
        up_bias_grad,
        down_grad,
        bias_grad,
    )


def solution(mesh):
    fine = Mesh(mesh.devices.reshape(4, 2, 2, 4, 2), ("y", "xl", "xh", "z", "c"))
    rows = P(FSDP, SEQ, None)
    vector = P(FSDP)
    by_row = P(FSDP, None)
    by_col = P(None, FSDP)
    in_specs = (
        rows,
        vector,
        vector,
        by_row,
        vector,
        by_row,
        vector,
        by_col,
        vector,
        by_row,
        vector,
        rows,
    )
    out_specs = (
        rows,
        rows,
        vector,
        vector,
        by_row,
        vector,
        by_row,
        vector,
        by_col,
        vector,
        by_row,
        vector,
    )
    return jax.shard_map(
        per_device, mesh=fine, in_specs=in_specs, out_specs=out_specs, check_vma=False
    )
```

```python
from typing import Callable, NamedTuple, Sequence

import jax
import jax.numpy as jnp
from jax import lax
from jax.experimental import pallas as pl
from jax.experimental.pallas import tpu as pltpu
from jax.sharding import Mesh, PartitionSpec as P

HEADS = 32
HEAD_DIM = 64
ROT = 32
WIDTH = 2048
FF = 8192
SEQ_DEVICES = 8
CHIPS = 8
FSDP_DEVICES = 16
ROWS = 128
LENGTH = ROWS * SEQ_DEVICES
TOKENS = ROWS * CHIPS
CHIP_COLS = WIDTH // CHIPS
CORE_COLS = WIDTH // FSDP_DEVICES
CORE_FF = FF // FSDP_DEVICES
PAIR = 2 * HEAD_DIM
QBLOCK = 256

EPSILON = 1e-05
ROPE_BASE = 10000.0
NEG_FILL = -1e30
PACE = 1 * 1.15e9
MICROSECONDS = dict(
    norm_project=13,
    hidden_forward=11,
    attend_forward=10,
    grad_heads=15,
    hidden_back=30,
    down_grads=30,
    attend_backward=15,
    out_part=30,
    up_grads=40,
    attend_grads=25,
    normed_part=25,
    unpack_down=6,
    unpack_up=6,
    unpack_attend=6,
    rows_grad=3,
)
SCALE = HEAD_DIM ** (-0.5)

F32 = jnp.float32
BF16 = jnp.bfloat16

SEQ = ("y", "xl")
GROUP = ("xh", "z")
FSDP = ("xh", "z", "c")

NT = (((1,), (1,)), ((), ()))
TN = (((0,), (0,)), ((), ()))
NN = (((1,), (0,)), ((), ()))


def dot(lhs, rhs, dims=NN):
    return lax.dot_general(lhs, rhs, dims, preferred_element_type=F32)


def swap(piece, axis):
    return lax.ppermute(piece, axis, [(0, 1), (1, 0)])


def shift(piece, axis, step):
    return lax.ppermute(piece, axis, [(i, (i - step) % 4) for i in range(4)])


def send(piece, axis, step):
    return lax.ppermute(piece, axis, [(i, (i + step) % 4) for i in range(4)])


def rope_tables(positions, heads):
    half = ROT // 2
    frequency = ROPE_BASE ** (-2.0 * jnp.arange(half, dtype=F32) / ROT)
    angle = positions.astype(F32)[:, None] * frequency[None, :]
    cosine, sine = jnp.cos(angle), jnp.sin(angle)
    rest = jnp.zeros((positions.shape[0], HEAD_DIM - ROT), F32)
    blank = jnp.zeros_like(sine)
    turn = jnp.concatenate([cosine, cosine, rest + 1.0], axis=1)
    upper = jnp.concatenate([-sine, blank, rest], axis=1)
    lower = jnp.concatenate([blank, sine, rest], axis=1)
    return tuple(jnp.concatenate([t] * heads, axis=1) for t in (turn, upper, lower))


def turn_columns(values, turn, upper, lower, sign):
    width = values.shape[1]
    half = ROT // 2
    ahead = pltpu.roll(values, width - half, 1)
    behind = pltpu.roll(values, half, 1)
    return values * turn + sign * (ahead * upper + behind * lower)


def cost(names):
    return pl.CostEstimate(
        flops=int(sum(MICROSECONDS[name] for name in names) * PACE), bytes_accessed=0, transcendentals=0
    )


def whole(shape):
    return pl.BlockSpec(shape, lambda i: (0,) * len(shape))


def row_block(rows, width, column=0):
    return pl.BlockSpec((rows, width), lambda i: (i, column))


class Job(NamedTuple):
    name: str
    kernel: Callable
    grid: int
    in_specs: Sequence
    out_specs: Sequence
    out_shape: Sequence
    operands: tuple
    scratch: tuple = ()
    plan: tuple = ()


def run(*jobs, late=()):
    plans = [len(job.plan) for job in jobs]
    starts = [sum(job.grid for job in jobs[:k]) for k in range(len(jobs))]

    def moved(spec, start, count, first, size):
        def index(step, *plan):
            own = plan[first : first + size]
            return spec.index_map(jnp.clip(step - start, 0, count - 1) if len(jobs) > 1 else step, *own)

        return pl.BlockSpec(spec.block_shape, index)

    def specs_of(kind):
        return [
            moved(spec, starts[k], job.grid, sum(plans[:k]), plans[k])
            for k, job in enumerate(jobs)
            for spec in getattr(job, kind)
        ]

    def body(*refs):
        refs = list(refs)
        take = lambda count: [refs.pop(0) for _ in range(count)]
        plan_refs = [take(count) for count in plans]
        in_refs = [take(len(job.operands)) for job in jobs]
        take(len(late))
        out_refs = [take(len(job.out_specs)) for job in jobs]
        held = [take(len(job.scratch)) for job in jobs]
        step = pl.program_id(0)
        for k, job in enumerate(jobs):
            own = (*plan_refs[k], *in_refs[k], *out_refs[k], *held[k])
            if len(jobs) == 1:
                job.kernel(step, *own)
            else:

                @pl.when((step >= starts[k]) & (step < starts[k] + job.grid))
                def _():
                    job.kernel(step - starts[k], *own)

    found = pl.pallas_call(
        body,
        grid_spec=pltpu.PrefetchScalarGridSpec(
            num_scalar_prefetch=sum(plans),
            grid=(sum(job.grid for job in jobs),),
            in_specs=specs_of("in_specs") + [pl.BlockSpec(memory_space=pl.ANY)] * len(late),
            out_specs=specs_of("out_specs"),
            scratch_shapes=[shape for job in jobs for shape in job.scratch],
        ),
        out_shape=[shape for job in jobs for shape in job.out_shape],
        compiler_params=pltpu.CompilerParams(vmem_limit_bytes=60 * 2**20),
        cost_estimate=cost([job.name for job in jobs]),
        name="_".join(job.name for job in jobs),
    )(*(p for job in jobs for p in job.plan), *(a for job in jobs for a in job.operands), *late)
    found = list(found)
    results = []
    for job in jobs:
        own, found = found[: len(job.out_specs)], found[len(job.out_specs) :]
        results.append(own[0] if len(own) == 1 else own)
    return results[0] if len(jobs) == 1 else results


def listed(value):
    return list(value) if isinstance(value, (list, tuple)) else [value]


def call(
    kernel, name, grid, in_specs, out_specs, out_shape, flops, moved, operands, late=(), scratch=(), plan=()
):
    job = Job(
        name, kernel, grid, in_specs, listed(out_specs), listed(out_shape), operands, tuple(scratch), plan
    )
    return job if late is None else run(job, late=late)


def placed_call(
    kernel, name, grid, in_specs, out_specs, out_shape, scratch, flops, moved, order, operands, late=()
):
    return call(
        kernel, name, grid, in_specs, out_specs, out_shape, flops, moved, operands, late, scratch, (order,)
    )


def fixed(dims):
    return pl.BlockSpec(dims, lambda i, order: (0,) * len(dims))


def shape(dims, kind=BF16):
    return jax.ShapeDtypeStruct(dims, kind)


def layer_stats(rows):
    center = rows - jnp.mean(rows, axis=-1, keepdims=True)
    spread_out = jnp.mean(center * center, axis=-1, keepdims=True)
    return center, lax.rsqrt(spread_out + EPSILON)


def put_rows(step, near_ref, far_refs, held):
    held[:ROWS] = near_ref[...]
    for index, far_ref in enumerate(far_refs):

        @pl.when(step == index)
        def _():
            held[ROWS:] = far_ref[...]


def norm_project_kernel(
    step,
    at_ref,
    order_ref,
    core_ref,
    near_ref,
    far_0,
    far_1,
    far_2,
    far_3,
    gain_ref,
    shift_ref,
    bias_ref,
    own_ref,
    other_ref,
    turn_ref,
    upper_ref,
    lower_ref,
    normed_ref,
    out_ref,
    weight_ref,
    held,
):
    @pl.when(step == 0)
    def _():
        for chip in range(CHIPS):
            for core, piece in ((core_ref[0], own_ref), (1 - core_ref[0], other_ref)):
                first = pl.multiple_of(chip * CHIP_COLS + core * CORE_COLS, CORE_COLS)
                weight_ref[pl.ds(first, CORE_COLS), :] = piece[:, chip].reshape(CORE_COLS, -1)

    put_rows(step, near_ref, (far_0, far_1, far_2, far_3), held)
    rows = held[...]
    center, inverse = layer_stats(rows.astype(F32))
    normed = (center * inverse * gain_ref[...] + shift_ref[...]).astype(BF16)
    normed_ref[...] = normed
    projected = dot(normed, weight_ref[...]) + bias_ref[...]
    turned_width = 2 * CHIP_COLS
    for block in range(2):
        rows = slice(block * ROWS, (block + 1) * ROWS)
        for start in range(0, turned_width, PAIR):
            cols = slice(start, start + PAIR)
            out_ref[rows, cols] = turn_columns(
                projected[rows, cols], turn_ref[...], upper_ref[...], lower_ref[...], 1.0
            ).astype(BF16)
    out_ref[:, turned_width:] = projected[:, turned_width:].astype(BF16)


def norm_project(seq_at, order, core, near, far, gain, shift_row, bias, own, other, tables, late):
    block = 2 * ROWS
    width = own.shape[-1]
    row = lambda rows, cols: pl.BlockSpec((rows, cols), lambda i, at, order, core: (order[i], 0))
    own_rows = pl.BlockSpec((ROWS, PAIR), lambda i, at, order, core: (at[0], 0))
    held = lambda dims: pl.BlockSpec(dims, lambda i, at, order, core: (0,) * len(dims))
    fixed_ones = (*far, gain, shift_row, bias, own, other)
    return call(
        norm_project_kernel,
        "norm_project",
        4,
        [row(ROWS, WIDTH)] + [held(a.shape) for a in fixed_ones] + [own_rows] * 3,
        [row(block, WIDTH), row(block, width), held((WIDTH, width))],
        [shape((TOKENS, WIDTH)), shape((TOKENS, width)), shape((WIDTH, width))],
        0,
        0,
        (near, *fixed_ones) + tables,
        late,
        [pltpu.VMEM((block, WIDTH), BF16)],
        (seq_at, order, core),
    )


def hidden_kernel(
    step,
    normed_ref,
    own_ref,
    other_ref,
    own_bias_ref,
    other_bias_ref,
    own_act_ref,
    other_act_ref,
    own_slope_ref,
    other_slope_ref,
):
    root = (2.0 / 3.141592653589793) ** 0.5
    for weight, bias, act, slope in (
        (own_ref, own_bias_ref, own_act_ref, own_slope_ref),
        (other_ref, other_bias_ref, other_act_ref, other_slope_ref),
    ):
        hidden = dot(normed_ref[...], weight[...]) + bias[...]
        square = hidden * hidden
        bend = jnp.tanh(root * hidden * (1.0 + 0.044715 * square))
        half = 0.5 * (1.0 + bend)
        act[...] = (hidden * half).astype(BF16)
        slope[...] = half + 0.5 * hidden * (1.0 - bend * bend) * (
            root * (1.0 + 3.0 * 0.044715 * square)
        )


def hidden_forward(normed, own, other, own_bias, other_bias):
    block = 256
    operands = (own, other, own_bias, other_bias)
    return call(
        hidden_kernel,
        "hidden_forward",
        TOKENS // block,
        [row_block(block, WIDTH)] + [whole(v.shape) for v in operands],
        [row_block(block, CORE_FF)] * 4,
        [shape((TOKENS, CORE_FF))] * 2 + [shape((TOKENS, CORE_FF), F32)] * 2,
        4 * TOKENS * WIDTH * CORE_FF,
        14 * 2**20,
        (normed,) + operands,
    )


def grad_heads_kernel(step, cot_ref, mixer_ref, out_ref):
    out_ref[...] = dot(cot_ref[...], mixer_ref[...], NT).astype(BF16)


def grad_heads(cot, mixer, late):
    block = 256
    return call(
        grad_heads_kernel,
        "grad_heads",
        TOKENS // block,
        [row_block(block, WIDTH), whole(mixer.shape)],
        row_block(block, CHIP_COLS),
        shape((TOKENS, CHIP_COLS)),
        2 * TOKENS * WIDTH * CHIP_COLS,
        6 * 2**20,
        (cot, mixer),
        late,
    )


def hidden_back_kernel(
    step,
    cot_ref, own_ref, other_ref, own_slope_ref, other_slope_ref, own_out, other_out, own_sum, other_sum
):
    for weight, slope, out, total in (
        (own_ref, own_slope_ref, own_out, own_sum),
        (other_ref, other_slope_ref, other_out, other_sum),
    ):
        grad = (dot(cot_ref[...], weight[...], NT) * slope[...]).astype(BF16)
        out[...] = grad
        part = jnp.sum(grad.astype(F32), axis=0, keepdims=True)

        @pl.when(step == 0)
        def _():
            total[...] = part

        @pl.when(step > 0)
        def _():
            total[...] += part


def hidden_back(cot, own, other, own_slope, other_slope):
    block = 256
    return call(
        hidden_back_kernel,
        "hidden_back",
        TOKENS // block,
        [row_block(block, WIDTH), whole(own.shape), whole(other.shape)]
        + [row_block(block, CORE_FF)] * 2,
        [row_block(block, CORE_FF)] * 2 + [whole((1, CORE_FF))] * 2,
        [shape((TOKENS, CORE_FF))] * 2 + [shape((1, CORE_FF), F32)] * 2,
        4 * TOKENS * WIDTH * CORE_FF,
        14 * 2**20,
        (cot, own, other, own_slope, other_slope),
        None,
    )


def out_part_kernel(step, own_act, other_act, attended, own_ref, other_ref, mixer_ref, out_ref):
    out_ref[...] = (
        dot(own_act[...], own_ref[...])
        + dot(other_act[...], other_ref[...])
        + dot(attended[...], mixer_ref[...])
    ).astype(BF16)


def out_part(own_act, other_act, attended, own, other, mixer):
    block = 256
    weights = (own, other, mixer)
    return call(
        out_part_kernel,
        "out_part",
        TOKENS // block,
        [row_block(block, CORE_FF)] * 2
        + [row_block(block, CHIP_COLS)]
        + [whole(w.shape) for w in weights],
        row_block(block, WIDTH),
        shape((TOKENS, WIDTH)),
        2 * TOKENS * WIDTH * (2 * CORE_FF + CHIP_COLS),
        12 * 2**20,
        (own_act, other_act, attended) + weights,
        None,
    )


def normed_part_kernel(
    step,
    order_ref,
    projected,
    own_grad,
    other_grad,
    near_ref,
    far_0,
    far_1,
    far_2,
    far_3,
    attend_ref,
    own_ref,
    other_ref,
    out_ref,
    sums_ref,
    bias_ref,
    held,
):
    put_rows(step, near_ref, (far_0, far_1, far_2, far_3), held)
    total = (
        dot(projected[...], attend_ref[...], NT)
        + dot(own_grad[...], own_ref[...], NT)
        + dot(other_grad[...], other_ref[...], NT)
    )
    out_ref[...] = total.astype(BF16)
    center, inverse = layer_stats(held[...].astype(F32))
    gain_part = jnp.sum(total * (center * inverse), axis=0, keepdims=True)
    shift_part = jnp.sum(total, axis=0, keepdims=True)
    bias_part = jnp.sum(projected[...].astype(F32), axis=0, keepdims=True)

    @pl.when(step == 0)
    def _():
        sums_ref[0:1] = gain_part
        sums_ref[1:2] = shift_part
        bias_ref[...] = bias_part

    @pl.when(step > 0)
    def _():
        sums_ref[0:1] += gain_part
        sums_ref[1:2] += shift_part
        bias_ref[...] += bias_part


def normed_part(order, projected, own_grad, other_grad, near, far, attend, own, other, late):
    block = 2 * ROWS
    width = projected.shape[1]
    row = lambda rows, cols: pl.BlockSpec((rows, cols), lambda i, order: (order[i], 0))
    weights = (attend, own, other)
    return call(
        normed_part_kernel,
        "normed_part",
        4,
        [row(block, width), row(block, CORE_FF), row(block, CORE_FF), row(ROWS, WIDTH)]
        + [fixed(a.shape) for a in (*far, *weights)],
        [row(block, WIDTH), fixed((2, WIDTH)), fixed((1, width))],
        [shape((TOKENS, WIDTH)), shape((2, WIDTH), F32), shape((1, width), F32)],
        0,
        0,
        (projected, own_grad, other_grad, near, *far) + weights,
        late,
        [pltpu.VMEM((block, WIDTH), BF16)],
        (order,),
    )


UP_ROWS = WIDTH // SEQ_DEVICES
DOWN_ROWS = CORE_FF // 2
MIX_ROWS = CORE_COLS // 2
PACK_ROWS = UP_ROWS + MIX_ROWS
PACK_COLS = CORE_FF
HALF = PACK_COLS // 2
SLOT_COLS = WIDTH // SEQ_DEVICES


def across(rows):
    return pl.BlockSpec((rows, SLOT_COLS), lambda i, order: (0, order[i]))


def plan_call(
    kernel, name, grid, in_specs, out_specs, out_shape, scratch, flops, moved, order, side, operands, late=()
):
    return call(
        kernel, name, grid, in_specs, out_specs, out_shape, flops, moved, operands, late, scratch, (order, side)
    )


def plan_whole(array):
    return pl.BlockSpec(array.shape, lambda i, order, side: (0, 0))


WIDE = 2 * SLOT_COLS
WIDE_COLUMNS = pl.BlockSpec((TOKENS, WIDE), lambda i, order, side: (0, order[i]))


def down_grads_kernel(step, order_ref, x_ref, act_ref, act_other, cot_ref, cot_other, *refs):
    outs = refs
    down = (dot(act_ref[...], cot_ref[...], TN) + dot(act_other[...], cot_other[...], TN)).astype(BF16)
    for index, out_ref in enumerate(outs):
        for x in range(2):

            @pl.when((step == index) & (x_ref[0] == x))
            def _():
                for r, half in ((0, x), (1, 1 - x)):
                    cols = slice(half * SLOT_COLS, (half + 1) * SLOT_COLS)
                    out_ref[r, :, :HALF] = down[:DOWN_ROWS, cols]
                    out_ref[r, :, HALF:] = down[DOWN_ROWS:, cols]


def down_grads(order, x_lo, act, act_other, cot, cot_other):
    block = (2, DOWN_ROWS, PACK_COLS)
    return Job(
        "down_grads",
        down_grads_kernel,
        4,
        [plan_whole(act), plan_whole(act_other)] + [WIDE_COLUMNS] * 2,
        [pl.BlockSpec(block, lambda i, order, side: (0, 0, 0))] * 4,
        [shape(block)] * 4,
        (act, act_other, cot, cot_other),
        (),
        (order, x_lo),
    )


def up_grads_kernel(
    step,
    order_ref,
    x_ref,
    core_ref,
    grad_ref,
    grad_other,
    att_ref,
    att_other,
    normed_ref,
    normed_other,
    cot_ref,
    cot_other,
    *refs,
):
    outs, held, mixed = refs[:4], refs[4], refs[5]
    held[...] = (
        dot(normed_ref[...], grad_ref[...], TN) + dot(normed_other[...], grad_other[...], TN)
    ).astype(BF16)
    cols = pl.ds(pl.multiple_of(core_ref[0] * CORE_COLS, CORE_COLS), CORE_COLS)
    mixed[...] = (
        dot(att_ref[:, cols], cot_ref[...], TN) + dot(att_other[:, cols], cot_other[...], TN)
    ).astype(BF16)
    for index, out_ref in enumerate(outs):

        @pl.when(step == index)
        def _():
            for r, x in enumerate((x_ref[0], 1 - x_ref[0])):
                out_ref[r, :UP_ROWS] = held[pl.ds(pl.multiple_of(x * UP_ROWS, UP_ROWS), UP_ROWS), :]
                part = mixed[:, pl.ds(pl.multiple_of(x * SLOT_COLS, SLOT_COLS), SLOT_COLS)]
                out_ref[r, UP_ROWS:, :HALF] = part[:MIX_ROWS]
                out_ref[r, UP_ROWS:, HALF:] = part[MIX_ROWS:]


def up_grads(order, x_lo, core, grad, grad_other, att, att_other, normed, normed_other, cot, cot_other):
    block = (2, PACK_ROWS, PACK_COLS)
    columns = pl.BlockSpec((TOKENS, WIDE), lambda i, order, *plan: (0, order[i]))
    held = [pl.BlockSpec(a.shape, lambda i, *plan: (0, 0)) for a in (grad, grad_other, att, att_other)]
    return Job(
        "up_grads",
        up_grads_kernel,
        4,
        held + [columns] * 4,
        [pl.BlockSpec(block, lambda i, *plan: (0, 0, 0))] * 4,
        [shape(block)] * 4,
        (grad, grad_other, att, att_other, normed, normed_other, cot, cot_other),
        (pltpu.VMEM((2 * UP_ROWS, CORE_FF), BF16), pltpu.VMEM((CORE_COLS, WIDE), BF16)),
        (order, x_lo, core),
    )


def attend_grads_kernel(step, order_ref, core_ref, grad_ref, grad_other, own_0, own_1, other_0, other_1, *refs):
    outs, held = refs[:4], refs[4]
    for half, (own, other) in enumerate(((own_0, other_0), (own_1, other_1))):
        held[half] = (
            dot(own[...], grad_ref[...], TN) + dot(other[...], grad_other[...], TN)
        ).astype(BF16)
    for slot in range(SEQ_DEVICES):
        rows = pl.ds(pl.multiple_of(order_ref[slot] * SLAB, SLAB), SLAB)
        for half in range(2):
            outs[slot // 2][slot % 2, half] = held[half, rows, :]


def attend_grads(order, core, grad, grad_other, normed, normed_other, late):
    cols = grad.shape[1]

    def rows_of(half):
        return pl.BlockSpec((TOKENS, CORE_COLS), lambda i, order, core: (0, 4 * i + 2 * half + core[0]))

    return plan_call(
        attend_grads_kernel,
        "attend_grads",
        CHIPS // 2,
        [plan_whole(grad), plan_whole(grad_other)] + [rows_of(0), rows_of(1)] * 2,
        [pl.BlockSpec((2, 2, SLAB, cols), lambda i, order, core: (0, i, 0, 0))] * 4,
        [shape((2, CHIPS, SLAB, cols))] * 4,
        [pltpu.VMEM((2, CORE_COLS, cols), BF16)],
        4 * TOKENS * WIDTH * cols // 2,
        12 * 2**20,
        order,
        core,
        (grad, grad_other, normed, normed, normed_other, normed_other),
        late,
    )


def unpack_down_kernel(step, order_ref, x_ref, *refs):
    down_ref = refs[4]
    for index, pieces in enumerate(refs[:4]):

        @pl.when(step == index)
        def _():
            for x in range(2):
                piece = pieces[(x_ref[0] + x) % 2]
                cols = slice(x * SLOT_COLS, (x + 1) * SLOT_COLS)
                down_ref[:DOWN_ROWS, cols] = piece[:, :HALF].astype(F32)
                down_ref[DOWN_ROWS:, cols] = piece[:, HALF:].astype(F32)


def unpack_down(order, x_lo, pieces, late):
    return plan_call(
        unpack_down_kernel,
        "unpack_down",
        4,
        [pl.BlockSpec(p.shape, lambda i, order, x: (0, 0, 0)) for p in pieces],
        pl.BlockSpec((CORE_FF, WIDE), lambda i, order, x: (0, order[i])),
        shape((CORE_FF, WIDTH), F32),
        [],
        0,
        0,
        order,
        x_lo,
        tuple(pieces),
        late,
    )


def unpack_up_kernel(step, order_ref, x_ref, *refs):
    up_ref, mix_ref = refs[4:]
    for index, pieces in enumerate(refs[:4]):

        @pl.when(step == index)
        def _():
            for x in range(2):
                piece = pieces.at[(x_ref[0] + x) % 2]
                up_ref[x * UP_ROWS : (x + 1) * UP_ROWS] = piece[:UP_ROWS].astype(F32)
                cols = slice(x * SLOT_COLS, (x + 1) * SLOT_COLS)
                mix_ref[:MIX_ROWS, cols] = piece[UP_ROWS:, :HALF].astype(F32)
                mix_ref[MIX_ROWS:, cols] = piece[UP_ROWS:, HALF:].astype(F32)


def unpack_up(order, x_lo, pieces, late):
    return plan_call(
        unpack_up_kernel,
        "unpack_up",
        4,
        [pl.BlockSpec(p.shape, lambda i, order, x: (0, 0, 0)) for p in pieces],
        [
            pl.BlockSpec((2 * UP_ROWS, CORE_FF), lambda i, order, x: (order[i], 0)),
            pl.BlockSpec((CORE_COLS, WIDE), lambda i, order, x: (0, order[i])),
        ],
        [shape((WIDTH, CORE_FF), F32), shape((CORE_COLS, WIDTH), F32)],
        [],
        0,
        0,
        order,
        x_lo,
        tuple(pieces),
        late,
    )


SLAB = CORE_COLS // SEQ_DEVICES


VECTORS = (128, 128, 128, 384, 512)


def unpack_attend_kernel(step, place_ref, x_ref, *refs):
    out_ref, vector_refs, total_ref = refs[4], refs[5:10], refs[10]

    @pl.when(step == 0)
    def _():
        total_ref[...] = jnp.zeros_like(total_ref)

    for index, pieces in enumerate(refs[:4]):

        @pl.when(place_ref[step] == index)
        def _():
            for half in range(2):
                piece = pieces.at[(x_ref[0] + half) % 2]
                rest = piece[CHIPS * SLAB :].astype(F32).reshape(CHIPS, 4, -1)
                total_ref[...] += jnp.sum(rest, axis=0)
                for chip in range(CHIPS):
                    for part in range(3):
                        start = part * WIDTH + chip * CHIP_COLS
                        out_ref[half * SLAB : (half + 1) * SLAB, start : start + CHIP_COLS] = piece[
                            chip * SLAB : (chip + 1) * SLAB,
                            part * CHIP_COLS : (part + 1) * CHIP_COLS,
                        ].astype(F32)

    @pl.when(step == 3)
    def _():
        sums = total_ref[:2] + total_ref[2:]
        start = 0
        for vector_ref in vector_refs[:4]:
            size = vector_ref.shape[1]
            vector_ref[...] = sums[0:1, start : start + size]
            start += size
        vector_refs[4][...] = sums[1:2, : vector_refs[4].shape[1]]


def unpack_attend(place, x_lo, pieces, late):
    cols = pieces[0].shape[2]
    fixed_out = lambda size: pl.BlockSpec((1, size), lambda i, place, x: (0, 0))
    return plan_call(
        unpack_attend_kernel,
        "unpack_attend",
        4,
        [pl.BlockSpec(p.shape, lambda i, place, x: (0, 0, 0)) for p in pieces],
        [pl.BlockSpec((2 * SLAB, 3 * WIDTH), lambda i, place, x: (i, 0))]
        + [fixed_out(size) for size in VECTORS],
        [shape((CORE_COLS, 3 * WIDTH), F32)] + [shape((1, size), F32) for size in VECTORS],
        [pltpu.VMEM((4, cols), F32)],
        0,
        0,
        place,
        x_lo,
        tuple(pieces),
        late,
    )


def rows_grad_kernel(step, rows_ref, cot_ref, near_ref, far_ref, gain_ref, out_ref):
    grad = near_ref[...].astype(F32) + far_ref[...].astype(F32)
    center, inverse = layer_stats(rows_ref[...].astype(F32))
    unit = center * inverse
    scaled = grad * gain_ref[...]
    out_ref[...] = cot_ref[...].astype(F32) + inverse * (
        scaled
        - jnp.mean(scaled, axis=-1, keepdims=True)
        - unit * jnp.mean(scaled * unit, axis=-1, keepdims=True)
    )


def rows_grad(rows, cot, near, far, gain):
    block = 64
    return call(
        rows_grad_kernel,
        "rows_grad",
        ROWS // block,
        [row_block(block, WIDTH)] * 4 + [whole(gain.shape)],
        row_block(block, WIDTH),
        shape((ROWS, WIDTH), F32),
        0,
        4 * 2**20,
        (rows, cot, near, far, gain),
    )


def lane_masks():
    lane = lax.broadcasted_iota(jnp.int32, (1, PAIR), 1)
    first = (lane < HEAD_DIM).astype(BF16)
    return first, 1 - first


def scores_of(query, keys, low):
    scores = dot(query, keys, NT)
    if low:
        head, last = scores[:, :low], scores[:, low:]
    else:
        head, last = None, scores
    row = lax.broadcasted_iota(jnp.int32, last.shape, 0)
    col = lax.broadcasted_iota(jnp.int32, last.shape, 1)
    last = jnp.where(col <= row, last, NEG_FILL)
    return last if head is None else jnp.concatenate([head, last], axis=1)


def attend_kernel(step, query_ref, key_ref, value_ref, out_ref, logsum_ref):
    first, second = lane_masks()
    lane = lax.broadcasted_iota(jnp.int32, (QBLOCK, PAIR), 1)
    for low in range(0, LENGTH, QBLOCK):
        reach = low + QBLOCK
        query = query_ref[low:reach, :] * BF16(SCALE)
        keys = key_ref[:reach, :]
        values = value_ref[:reach, :]
        found = []
        for mask in (first, second):
            scores = scores_of(query * mask, keys, low)
            peak = jnp.max(scores, axis=1, keepdims=True)
            weight = jnp.exp(scores - peak)
            total = jnp.sum(weight, axis=1, keepdims=True)
            found.append((dot(weight.astype(BF16), values) / total, peak + jnp.log(total)))
        out_ref[low:reach, :] = jnp.where(lane < HEAD_DIM, found[0][0], found[1][0]).astype(BF16)
        logsum_ref[low:reach, :] = jnp.where(lane < HEAD_DIM, found[0][1], found[1][1])


def pair_columns(part):
    return pl.BlockSpec((LENGTH, PAIR), lambda p: (0, part * (CHIP_COLS // PAIR) + p))


def attend_forward(qkv, late):
    return call(
        attend_kernel,
        "attend_forward",
        CHIP_COLS // PAIR,
        [pair_columns(0), pair_columns(1), pair_columns(2)],
        [pair_columns(0)] * 2,
        [shape((LENGTH, CHIP_COLS)), shape((LENGTH, CHIP_COLS), F32)],
        8 * 2**30,
        4 * 2**20,
        (qkv, qkv, qkv),
        late,
    )


def attend_back_kernel(
    step,
    query_ref,
    key_ref,
    value_ref,
    grad_ref,
    logsum_ref,
    turn_ref,
    upper_ref,
    lower_ref,
    out_ref,
    key_total,
    value_total,
):
    pair = step
    first, second = lane_masks()
    lane = lax.broadcasted_iota(jnp.int32, (QBLOCK, PAIR), 1)
    key_total[...] = jnp.zeros_like(key_total)
    value_total[...] = jnp.zeros_like(value_total)

    def store(part, low, reach, values):
        start = pl.multiple_of((part * (CHIP_COLS // PAIR) + pair) * PAIR, PAIR)
        out_ref[low:reach, pl.ds(start, PAIR)] = values.astype(BF16)

    def unturn(values, low, reach):
        kept = values.astype(BF16).astype(F32)
        return turn_columns(
            kept, turn_ref[low:reach, :], upper_ref[low:reach, :], lower_ref[low:reach, :], -1.0
        )

    for low in range(0, LENGTH, QBLOCK):
        reach = low + QBLOCK
        query = query_ref[low:reach, :] * BF16(SCALE)
        grad = grad_ref[low:reach, :]
        keys = key_ref[:reach, :]
        values = value_ref[:reach, :]
        query_grads = []
        key_part = 0.0
        value_part = 0.0
        for head, mask in enumerate((first, second)):
            own_query = query * mask
            own_grad = grad * mask
            scores = scores_of(own_query, keys, low)
            start = head * HEAD_DIM
            probs = jnp.exp(scores - logsum_ref[low:reach, start : start + 1])
            prob_grad = dot(own_grad, values, NT)
            inner = jnp.sum(probs * prob_grad, axis=1, keepdims=True)
            score_grad = (probs * (prob_grad - inner)).astype(BF16)
            query_grads.append(dot(score_grad, keys))
            key_part += dot(score_grad, own_query, TN)
            value_part += dot(probs.astype(BF16), own_grad, TN)
        key_total[:reach, :] += key_part
        value_total[:reach, :] += value_part
        query_grad = jnp.where(lane < HEAD_DIM, query_grads[0], query_grads[1]) * SCALE
        store(0, low, reach, unturn(query_grad, low, reach))
    store(1, 0, LENGTH, unturn(key_total[...], 0, LENGTH))
    store(2, 0, LENGTH, value_total[...])


def attend_backward(qkv, grad, logsum, tables, late):
    return call(
        attend_back_kernel,
        "attend_backward",
        CHIP_COLS // PAIR,
        [pair_columns(0), pair_columns(1), pair_columns(2), pair_columns(0), pair_columns(0)]
        + [whole(t.shape) for t in tables],
        whole((LENGTH, 3 * CHIP_COLS)),
        shape((LENGTH, 3 * CHIP_COLS)),
        20 * 2**30,
        6 * 2**20,
        (qkv, qkv, qkv, grad, logsum) + tables,
        late,
        [pltpu.VMEM((LENGTH, PAIR), F32)] * 2,
    )


def exchange(blocks, axes):
    return lax.all_to_all(blocks, axes, split_axis=0, concat_axis=0, tiled=True)


def spread(block, axes, count):
    return exchange(jnp.broadcast_to(block[None], (count,) + block.shape), axes)


def gate(value):
    return swap(value.reshape(-1, value.shape[-1])[:16, :128], "c")


tie = lax.optimization_barrier


def sent_y(parts):
    return [send(parts[k], "y", k) for k in (1, 3, 2)]


def joined(leave, stay):
    return (stay + swap(leave.astype(BF16), "xl").astype(F32)).astype(BF16)


def sum_seq(parts, arrived):
    leave, stay = (
        parts[0][r].astype(F32) + sum(a[r].astype(F32) for a in arrived) for r in (1, 0)
    )
    return joined(leave, stay)


def in_rows(values):
    width = 3 * CHIP_COLS
    count = values.shape[0]
    head = lax.reduce_precision(values, 8, 7)
    rest = (values - head).astype(BF16)
    head = head.astype(BF16)
    rows = [jnp.pad(part, ((0, 0), (0, 2 * width - part.shape[1]))).reshape(count, 2, width) for part in (head, rest)]
    return jnp.pad(jnp.concatenate(rows, axis=1), ((0, 0), (0, SLAB - 4), (0, 0)))


def summed_y(parts, arrived):
    return (parts[0].astype(F32) + sum(a.astype(F32) for a in arrived)).astype(BF16)


def summed_pair(own, other):
    return (own.astype(F32) + other[::-1].astype(F32)).astype(BF16)


def spread_y(pair):
    found = {0: pair} | {k: shift(pair, "y", k) for k in (1, 3, 2)}
    return [found[k] for k in range(4)]


def sum_rows(parts):
    parts = lax.psum_scatter(
        parts.reshape(4, 2, ROWS, WIDTH), "z", scatter_dimension=0, tiled=False
    )
    return parts


def per_device(
    inputs,
    gains,
    shifts,
    attend,
    attend_bias,
    mixer,
    mixer_bias,
    upward,
    upward_bias,
    downward,
    downward_bias,
    cotangent,
):
    core = lax.axis_index("c")
    x_lo = lax.axis_index("xl")
    chip = lax.axis_index("xh") * 4 + lax.axis_index("z")
    seq_index = lax.axis_index("y") * 2 + x_lo
    core_at = core.reshape(1)
    rows_in = inputs.reshape(ROWS, WIDTH)
    own_cot = cotangent.reshape(ROWS, WIDTH)
    width = 3 * CHIP_COLS

    z_order = (lax.axis_index("z") + jnp.arange(4, dtype=jnp.int32)) % 4
    y_place = (jnp.arange(4, dtype=jnp.int32) - lax.axis_index("y")) % 4
    y_order = (lax.axis_index("y") + jnp.arange(4, dtype=jnp.int32)) % 4
    seq_order = (y_order[:, None] * 2 + jnp.stack([x_lo, 1 - x_lo])[None, :]).reshape(SEQ_DEVICES)

    near = lax.all_gather(rows_in, "z", axis=0, tiled=True)
    other_rows = swap(rows_in, "xh")

    slab = lax.dynamic_slice_in_dim(attend, seq_index * SLAB, SLAB, 0)
    slab = slab.reshape(SLAB, 3, CHIPS, CHIP_COLS).transpose(2, 0, 1, 3).reshape(CHIPS, SLAB, width)
    small, start = 0, 0
    for vector in (gains, shifts, mixer_bias, downward_bias, attend_bias):
        small = small + jnp.pad(vector, (start, 2 * width - start - vector.shape[0]))
        start += vector.shape[0]
    small = small.reshape(1, 2, width)
    small = jnp.pad(jnp.broadcast_to(small, (CHIPS, 2, width)), ((0, 0), (0, SLAB - 2), (0, 0)))
    slab = exchange(jnp.concatenate([slab, small], axis=1), GROUP)
    slab, other_rows = tie((slab, other_rows))
    far = [other_rows] + [shift(other_rows, "z", k) for k in (1, 2, 3)]
    small_own = slab[:, SLAB : SLAB + 2].reshape(CHIPS, 2 * width)[:, :896]
    slab = slab[:, :SLAB]
    attend_own = spread(slab, SEQ, SEQ_DEVICES).reshape(SEQ_DEVICES, CHIPS, SLAB, width)
    attend_own, all_tables, near, *far = tie(
        (attend_own, rope_tables(jnp.arange(LENGTH, dtype=jnp.int32), 2), near, *far)
    )
    attend_other = swap(attend_own, "c")
    small_other = swap(small_own, "c")
    small_all = jnp.where(
        core == 0, jnp.stack([small_own, small_other], 1), jnp.stack([small_other, small_own], 1)
    ).reshape(FSDP_DEVICES, 7, 128).astype(F32)
    gain_all = small_all[:, 0].reshape(1, WIDTH)
    shift_all = small_all[:, 1].reshape(1, WIDTH)
    out_bias = (small_all[:, 2] + small_all[:, 3]).reshape(WIDTH)
    bias_grid = small_all[:, 4:7].reshape(3, CHIPS, CHIP_COLS)
    attend_bias_chip = lax.dynamic_slice_in_dim(bias_grid, chip, 1, 1).reshape(1, width)

    mixer_other = swap(mixer, "c")
    mixer_chip = jnp.where(
        core == 0, jnp.concatenate([mixer, mixer_other]), jnp.concatenate([mixer_other, mixer])
    )
    up_other = swap(upward, "c")
    down_other = swap(downward, "c")
    up_bias_own = upward_bias.astype(F32).reshape(1, CORE_FF)
    up_bias_other = swap(upward_bias.reshape(1, CORE_FF), "c").astype(F32)

    cot_pair = jnp.stack([own_cot, swap(own_cot, "xh")])
    cot_pair, near, *far = tie((cot_pair, near, *far))
    cot_group = lax.all_gather(cot_pair, "z", axis=0, tiled=False).reshape(TOKENS, WIDTH)
    normed, qkv_sent, attend_chip = norm_project(
        seq_index.reshape(1),
        z_order,
        core_at,
        near,
        far,
        gain_all,
        shift_all,
        attend_bias_chip,
        attend_own,
        attend_other,
        all_tables,
        (mixer_chip, up_other, down_other, up_bias_other, up_bias_own),
    )
    normed_other = swap(normed, "c")
    qkv = exchange(qkv_sent.reshape(CHIPS, ROWS, width), SEQ).reshape(LENGTH, width)
    act_own, act_other, slope_own, slope_other = hidden_forward(
        normed, upward, up_other, up_bias_own, up_bias_other
    )
    act_sent = swap(act_other, "c")

    attended, logsum = attend_forward(qkv, (act_own, normed_other))
    attended, cot_group = tie((attended, cot_group))
    attended_group = exchange(attended.reshape(SEQ_DEVICES, ROWS, CHIP_COLS), SEQ).reshape(
        TOKENS, CHIP_COLS
    )
    cot_other = swap(cot_group, "c")
    attended_grad = grad_heads(cot_group, mixer_chip, (attended,))
    grads = exchange(attended_grad.reshape(CHIPS, ROWS, CHIP_COLS), SEQ).reshape(LENGTH, CHIP_COLS)

    x_at = x_lo.reshape(1)
    (grad_own, grad_other, up_bias_sum, up_bias_other_sum), down_slabs = run(
        hidden_back(cot_group, downward, down_other, slope_own, slope_other),
        down_grads(y_order, x_at, act_own, act_sent, cot_group, cot_other),
        late=(gate(attended_grad), attended_group),
    )
    grad_sent = swap(grad_other, "c")

    back = attend_backward(qkv, grads, logsum, all_tables, (down_slabs[0],))
    projected_grad = exchange(back.reshape(SEQ_DEVICES, ROWS, width), SEQ).reshape(TOKENS, width)

    down_arrived = sent_y(down_slabs)
    parts = run(
        out_part(act_own, act_other, attended_group, downward, down_other, mixer_chip),
        late=(gate(back), *down_arrived),
    )
    up_slabs = run(
        up_grads(
            y_order,
            x_at,
            core_at,
            grad_own,
            grad_sent,
            attended_group,
            swap(attended_group, "c"),
            normed,
            normed_other,
            cot_group,
            cot_other,
        ),
        late=(parts,),
    )
    out_sums = sum_rows(parts)
    up_arrived = sent_y(up_slabs)

    down_own = summed_y(down_slabs, down_arrived)
    down_other_x = swap(down_own, "xl")

    projected_grad, up_first = tie((projected_grad, up_slabs[0]))
    attend_slabs = attend_grads(
        seq_order,
        core_at,
        projected_grad,
        swap(projected_grad, "c"),
        normed,
        normed_other,
        (up_first,),
    )

    down_other_x, attend_first = tie((down_other_x, attend_slabs[0]))
    attend_slabs = [attend_first, *attend_slabs[1:]]
    down_pair = summed_pair(down_own, down_other_x)

    parts, norm_sums, attend_bias_sum = normed_part(
        z_order,
        projected_grad,
        grad_own,
        grad_other,
        near,
        far,
        attend_chip,
        upward,
        up_other,
        (attend_slabs[0],),
    )
    parts, out_sums, down_pair, *up_arrived = tie((parts, out_sums, down_pair, *up_arrived))
    outputs = (
        rows_in.astype(F32) + out_bias + out_sums[0].astype(F32) + swap(out_sums[1], "xh").astype(F32)
    ).astype(BF16)
    sums = sum_rows(parts)
    inputs_grad = rows_grad(rows_in, own_cot, sums[0], swap(sums[1], "xh"), gain_all)

    bias_full = jnp.sum(own_cot.astype(F32), axis=0)
    attend_bias_full = lax.dynamic_update_slice(
        jnp.zeros((3, CHIPS, CHIP_COLS), F32), attend_bias_sum.reshape(3, 1, CHIP_COLS), (0, chip, 0)
    )
    up_bias_pair = jnp.where(
        core == 0,
        jnp.concatenate([up_bias_sum, up_bias_other_sum]),
        jnp.concatenate([up_bias_other_sum, up_bias_sum]),
    )
    up_bias_full = lax.dynamic_update_slice(
        jnp.zeros((CHIPS, 2, CORE_FF), F32), up_bias_pair[None], (chip, 0, 0)
    )
    vectors = jnp.concatenate(
        [
            v.reshape(FSDP_DEVICES, -1)
            for v in (norm_sums[0], norm_sums[1], bias_full, attend_bias_full, up_bias_full)
        ],
        axis=1,
    )
    vectors = vectors.reshape(CHIPS, 2, -1)
    vectors_keep = lax.dynamic_index_in_dim(vectors, core, 1, keepdims=False)
    vectors_sent = lax.dynamic_index_in_dim(vectors, 1 - core, 1, keepdims=False)
    vectors = vectors_keep + swap(vectors_sent, "c")
    up_own = summed_y(up_slabs, up_arrived)
    up_pair = summed_pair(up_own, swap(up_own, "xl"))
    *attend_arrived, down_pair, up_pair = tie((*sent_y(attend_slabs), down_pair, up_pair))
    attend_sum = sum_seq(attend_slabs, attend_arrived)
    message = exchange(jnp.concatenate([attend_sum, in_rows(vectors)], axis=1), GROUP)
    kept = message[:, SLAB : SLAB + 4].reshape(-1, width)
    message = jnp.concatenate([message[:, :SLAB].reshape(-1, width), kept], axis=0)
    message, outputs, *down_pieces = tie((message, outputs, *spread_y(down_pair)))
    up_pieces = spread_y(up_pair)
    attend_pieces = spread_y(jnp.stack([message, swap(message, "xl")]))
    down_grad = unpack_down(y_order, x_at, down_pieces, ())
    up_grad, mixer_grad = unpack_up(y_order, x_at, up_pieces, (down_grad,))
    attend_grad, *vectors = unpack_attend(
        y_place, x_at, attend_pieces, (inputs_grad, outputs, down_grad, up_grad)
    )
    gain_grad, shift_grad, bias_grad, attend_bias_grad, up_bias_grad = (v[0] for v in vectors)

    return (
        outputs.reshape(inputs.shape),
        inputs_grad.reshape(inputs.shape),
        gain_grad,
        shift_grad,
        attend_grad,
        attend_bias_grad,
        mixer_grad,
        bias_grad,
        up_grad,
        up_bias_grad,
        down_grad,
        bias_grad,
    )


def solution(mesh):
    fine = Mesh(mesh.devices.reshape(4, 2, 2, 4, 2), ("y", "xl", "xh", "z", "c"))
    rows = P(FSDP, SEQ, None)
    vector = P(FSDP)
    by_row = P(FSDP, None)
    by_col = P(None, FSDP)
    in_specs = (
        rows,
        vector,
        vector,
        by_row,
        vector,
        by_row,
        vector,
        by_col,
        vector,
        by_row,
        vector,
        rows,
    )
    out_specs = (
        rows,
        rows,
        vector,
        vector,
        by_row,
        vector,
        by_row,
        vector,
        by_col,
        vector,
        by_row,
        vector,
    )
    return jax.shard_map(
        per_device, mesh=fine, in_specs=in_specs, out_specs=out_specs, check_vma=False
    )
```

```python
from typing import Callable, NamedTuple, Sequence

import jax
import jax.numpy as jnp
from jax import lax
from jax.experimental import pallas as pl
from jax.experimental.pallas import tpu as pltpu
from jax.sharding import Mesh, PartitionSpec as P

HEADS = 32
HEAD_DIM = 64
ROT = 32
WIDTH = 2048
FF = 8192
SEQ_DEVICES = 8
CHIPS = 8
FSDP_DEVICES = 16
ROWS = 128
LENGTH = ROWS * SEQ_DEVICES
TOKENS = ROWS * CHIPS
CHIP_COLS = WIDTH // CHIPS
CORE_COLS = WIDTH // FSDP_DEVICES
CORE_FF = FF // FSDP_DEVICES
PAIR = 2 * HEAD_DIM
QBLOCK = 256

EPSILON = 1e-05
ROPE_BASE = 10000.0
NEG_FILL = -1e30
PACE = 1 * 1.15e9
MICROSECONDS = dict(
    norm_project=13,
    hidden_forward=11,
    attend_forward=10,
    grad_heads=15,
    hidden_back=30,
    down_grads=30,
    attend_backward=15,
    out_part=30,
    up_grads=40,
    attend_grads=25,
    normed_part=25,
    unpack_down=6,
    unpack_up=6,
    unpack_attend=6,
    rows_grad=3,
)
SCALE = HEAD_DIM ** (-0.5)

F32 = jnp.float32
BF16 = jnp.bfloat16

SEQ = ("y", "xl")
GROUP = ("xh", "z")
FSDP = ("xh", "z", "c")

NT = (((1,), (1,)), ((), ()))
TN = (((0,), (0,)), ((), ()))
NN = (((1,), (0,)), ((), ()))


def dot(lhs, rhs, dims=NN):
    return lax.dot_general(lhs, rhs, dims, preferred_element_type=F32)


def swap(piece, axis):
    return lax.ppermute(piece, axis, [(0, 1), (1, 0)])


def shift(piece, axis, step):
    return lax.ppermute(piece, axis, [(i, (i - step) % 4) for i in range(4)])


def send(piece, axis, step):
    return lax.ppermute(piece, axis, [(i, (i + step) % 4) for i in range(4)])


def rope_tables(positions, heads):
    half = ROT // 2
    frequency = ROPE_BASE ** (-2.0 * jnp.arange(half, dtype=F32) / ROT)
    angle = positions.astype(F32)[:, None] * frequency[None, :]
    cosine, sine = jnp.cos(angle), jnp.sin(angle)
    rest = jnp.zeros((positions.shape[0], HEAD_DIM - ROT), F32)
    blank = jnp.zeros_like(sine)
    turn = jnp.concatenate([cosine, cosine, rest + 1.0], axis=1)
    upper = jnp.concatenate([-sine, blank, rest], axis=1)
    lower = jnp.concatenate([blank, sine, rest], axis=1)
    return tuple(jnp.concatenate([t] * heads, axis=1) for t in (turn, upper, lower))


def turn_columns(values, turn, upper, lower, sign):
    width = values.shape[1]
    half = ROT // 2
    ahead = pltpu.roll(values, width - half, 1)
    behind = pltpu.roll(values, half, 1)
    return values * turn + sign * (ahead * upper + behind * lower)


def cost(names):
    return pl.CostEstimate(
        flops=int(sum(MICROSECONDS[name] for name in names) * PACE), bytes_accessed=0, transcendentals=0
    )


def whole(shape):
    return pl.BlockSpec(shape, lambda i: (0,) * len(shape))


def row_block(rows, width, column=0):
    return pl.BlockSpec((rows, width), lambda i: (i, column))


class Job(NamedTuple):
    name: str
    kernel: Callable
    grid: int
    in_specs: Sequence
    out_specs: Sequence
    out_shape: Sequence
    operands: tuple
    scratch: tuple = ()
    plan: tuple = ()


def run(*jobs, late=()):
    plans = [len(job.plan) for job in jobs]
    starts = [sum(job.grid for job in jobs[:k]) for k in range(len(jobs))]

    def moved(spec, start, count, first, size):
        def index(step, *plan):
            own = plan[first : first + size]
            return spec.index_map(jnp.clip(step - start, 0, count - 1) if len(jobs) > 1 else step, *own)

        return pl.BlockSpec(spec.block_shape, index)

    def specs_of(kind):
        return [
            moved(spec, starts[k], job.grid, sum(plans[:k]), plans[k])
            for k, job in enumerate(jobs)
            for spec in getattr(job, kind)
        ]

    def body(*refs):
        refs = list(refs)
        take = lambda count: [refs.pop(0) for _ in range(count)]
        plan_refs = [take(count) for count in plans]
        in_refs = [take(len(job.operands)) for job in jobs]
        take(len(late))
        out_refs = [take(len(job.out_specs)) for job in jobs]
        held = [take(len(job.scratch)) for job in jobs]
        step = pl.program_id(0)
        for k, job in enumerate(jobs):
            own = (*plan_refs[k], *in_refs[k], *out_refs[k], *held[k])
            if len(jobs) == 1:
                job.kernel(step, *own)
            else:

                @pl.when((step >= starts[k]) & (step < starts[k] + job.grid))
                def _():
                    job.kernel(step - starts[k], *own)

    found = pl.pallas_call(
        body,
        grid_spec=pltpu.PrefetchScalarGridSpec(
            num_scalar_prefetch=sum(plans),
            grid=(sum(job.grid for job in jobs),),
            in_specs=specs_of("in_specs") + [pl.BlockSpec(memory_space=pl.ANY)] * len(late),
            out_specs=specs_of("out_specs"),
            scratch_shapes=[shape for job in jobs for shape in job.scratch],
        ),
        out_shape=[shape for job in jobs for shape in job.out_shape],
        compiler_params=pltpu.CompilerParams(vmem_limit_bytes=60 * 2**20),
        cost_estimate=cost([job.name for job in jobs]),
        name="_".join(job.name for job in jobs),
    )(*(p for job in jobs for p in job.plan), *(a for job in jobs for a in job.operands), *late)
    found = list(found)
    results = []
    for job in jobs:
        own, found = found[: len(job.out_specs)], found[len(job.out_specs) :]
        results.append(own[0] if len(own) == 1 else own)
    return results[0] if len(jobs) == 1 else results


def listed(value):
    return list(value) if isinstance(value, (list, tuple)) else [value]


def call(
    kernel, name, grid, in_specs, out_specs, out_shape, flops, moved, operands, late=(), scratch=(), plan=()
):
    job = Job(
        name, kernel, grid, in_specs, listed(out_specs), listed(out_shape), operands, tuple(scratch), plan
    )
    return job if late is None else run(job, late=late)


def placed_call(
    kernel, name, grid, in_specs, out_specs, out_shape, scratch, flops, moved, order, operands, late=()
):
    return call(
        kernel, name, grid, in_specs, out_specs, out_shape, flops, moved, operands, late, scratch, (order,)
    )


def fixed(dims):
    return pl.BlockSpec(dims, lambda i, order: (0,) * len(dims))


def shape(dims, kind=BF16):
    return jax.ShapeDtypeStruct(dims, kind)


def layer_stats(rows):
    center = rows - jnp.mean(rows, axis=-1, keepdims=True)
    spread_out = jnp.mean(center * center, axis=-1, keepdims=True)
    return center, lax.rsqrt(spread_out + EPSILON)


def put_rows(step, near_ref, far_refs, held):
    held[:ROWS] = near_ref[...]
    for index, far_ref in enumerate(far_refs):

        @pl.when(step == index)
        def _():
            held[ROWS:] = far_ref[...]


def norm_project_kernel(
    step,
    at_ref,
    order_ref,
    core_ref,
    near_ref,
    far_0,
    far_1,
    far_2,
    far_3,
    gain_ref,
    shift_ref,
    bias_ref,
    own_ref,
    other_ref,
    turn_ref,
    upper_ref,
    lower_ref,
    normed_ref,
    out_ref,
    weight_ref,
    held,
):
    @pl.when(step == 0)
    def _():
        for chip in range(CHIPS):
            for core, piece in ((core_ref[0], own_ref), (1 - core_ref[0], other_ref)):
                first = pl.multiple_of(chip * CHIP_COLS + core * CORE_COLS, CORE_COLS)
                weight_ref[pl.ds(first, CORE_COLS), :] = piece[:, chip].reshape(CORE_COLS, -1)

    put_rows(step, near_ref, (far_0, far_1, far_2, far_3), held)
    rows = held[...]
    center, inverse = layer_stats(rows.astype(F32))
    normed = (center * inverse * gain_ref[...] + shift_ref[...]).astype(BF16)
    normed_ref[...] = normed
    projected = dot(normed, weight_ref[...]) + bias_ref[...]
    turned_width = 2 * CHIP_COLS
    for block in range(2):
        rows = slice(block * ROWS, (block + 1) * ROWS)
        for start in range(0, turned_width, PAIR):
            cols = slice(start, start + PAIR)
            out_ref[rows, cols] = turn_columns(
                projected[rows, cols], turn_ref[...], upper_ref[...], lower_ref[...], 1.0
            ).astype(BF16)
    out_ref[:, turned_width:] = projected[:, turned_width:].astype(BF16)


def norm_project(seq_at, order, core, near, far, gain, shift_row, bias, own, other, tables, late):
    block = 2 * ROWS
    width = own.shape[-1]
    row = lambda rows, cols: pl.BlockSpec((rows, cols), lambda i, at, order, core: (order[i], 0))
    own_rows = pl.BlockSpec((ROWS, PAIR), lambda i, at, order, core: (at[0], 0))
    held = lambda dims: pl.BlockSpec(dims, lambda i, at, order, core: (0,) * len(dims))
    fixed_ones = (*far, gain, shift_row, bias, own, other)
    return call(
        norm_project_kernel,
        "norm_project",
        4,
        [row(ROWS, WIDTH)] + [held(a.shape) for a in fixed_ones] + [own_rows] * 3,
        [row(block, WIDTH), row(block, width), held((WIDTH, width))],
        [shape((TOKENS, WIDTH)), shape((TOKENS, width)), shape((WIDTH, width))],
        0,
        0,
        (near, *fixed_ones) + tables,
        late,
        [pltpu.VMEM((block, WIDTH), BF16)],
        (seq_at, order, core),
    )


def hidden_kernel(
    step,
    normed_ref,
    own_ref,
    other_ref,
    own_bias_ref,
    other_bias_ref,
    own_act_ref,
    other_act_ref,
    own_slope_ref,
    other_slope_ref,
):
    root = (2.0 / 3.141592653589793) ** 0.5
    for weight, bias, act, slope in (
        (own_ref, own_bias_ref, own_act_ref, own_slope_ref),
        (other_ref, other_bias_ref, other_act_ref, other_slope_ref),
    ):
        hidden = dot(normed_ref[...], weight[...]) + bias[...]
        square = hidden * hidden
        bend = jnp.tanh(root * hidden * (1.0 + 0.044715 * square))
        half = 0.5 * (1.0 + bend)
        act[...] = (hidden * half).astype(BF16)
        slope[...] = half + 0.5 * hidden * (1.0 - bend * bend) * (
            root * (1.0 + 3.0 * 0.044715 * square)
        )


def hidden_forward(normed, own, other, own_bias, other_bias):
    block = 256
    operands = (own, other, own_bias, other_bias)
    return call(
        hidden_kernel,
        "hidden_forward",
        TOKENS // block,
        [row_block(block, WIDTH)] + [whole(v.shape) for v in operands],
        [row_block(block, CORE_FF)] * 4,
        [shape((TOKENS, CORE_FF))] * 2 + [shape((TOKENS, CORE_FF), F32)] * 2,
        4 * TOKENS * WIDTH * CORE_FF,
        14 * 2**20,
        (normed,) + operands,
    )


def grad_heads_kernel(step, cot_ref, mixer_ref, out_ref):
    out_ref[...] = dot(cot_ref[...], mixer_ref[...], NT).astype(BF16)


def grad_heads(cot, mixer, late):
    block = 256
    return call(
        grad_heads_kernel,
        "grad_heads",
        TOKENS // block,
        [row_block(block, WIDTH), whole(mixer.shape)],
        row_block(block, CHIP_COLS),
        shape((TOKENS, CHIP_COLS)),
        2 * TOKENS * WIDTH * CHIP_COLS,
        6 * 2**20,
        (cot, mixer),
        late,
    )


def hidden_back_kernel(
    step,
    cot_ref, own_ref, other_ref, own_slope_ref, other_slope_ref, own_out, other_out, own_sum, other_sum
):
    for weight, slope, out, total in (
        (own_ref, own_slope_ref, own_out, own_sum),
        (other_ref, other_slope_ref, other_out, other_sum),
    ):
        grad = (dot(cot_ref[...], weight[...], NT) * slope[...]).astype(BF16)
        out[...] = grad
        part = jnp.sum(grad.astype(F32), axis=0, keepdims=True)

        @pl.when(step == 0)
        def _():
            total[...] = part

        @pl.when(step > 0)
        def _():
            total[...] += part


def hidden_back(cot, own, other, own_slope, other_slope):
    block = 256
    return call(
        hidden_back_kernel,
        "hidden_back",
        TOKENS // block,
        [row_block(block, WIDTH), whole(own.shape), whole(other.shape)]
        + [row_block(block, CORE_FF)] * 2,
        [row_block(block, CORE_FF)] * 2 + [whole((1, CORE_FF))] * 2,
        [shape((TOKENS, CORE_FF))] * 2 + [shape((1, CORE_FF), F32)] * 2,
        4 * TOKENS * WIDTH * CORE_FF,
        14 * 2**20,
        (cot, own, other, own_slope, other_slope),
        None,
    )


def out_part_kernel(step, own_act, other_act, attended, own_ref, other_ref, mixer_ref, out_ref):
    out_ref[...] = (
        dot(own_act[...], own_ref[...])
        + dot(other_act[...], other_ref[...])
        + dot(attended[...], mixer_ref[...])
    ).astype(BF16)


def out_part(own_act, other_act, attended, own, other, mixer):
    block = 256
    weights = (own, other, mixer)
    return call(
        out_part_kernel,
        "out_part",
        TOKENS // block,
        [row_block(block, CORE_FF)] * 2
        + [row_block(block, CHIP_COLS)]
        + [whole(w.shape) for w in weights],
        row_block(block, WIDTH),
        shape((TOKENS, WIDTH)),
        2 * TOKENS * WIDTH * (2 * CORE_FF + CHIP_COLS),
        12 * 2**20,
        (own_act, other_act, attended) + weights,
        None,
    )


def normed_part_kernel(
    step,
    order_ref,
    projected,
    own_grad,
    other_grad,
    near_ref,
    far_0,
    far_1,
    far_2,
    far_3,
    attend_ref,
    own_ref,
    other_ref,
    out_ref,
    sums_ref,
    bias_ref,
    held,
):
    put_rows(step, near_ref, (far_0, far_1, far_2, far_3), held)
    total = (
        dot(projected[...], attend_ref[...], NT)
        + dot(own_grad[...], own_ref[...], NT)
        + dot(other_grad[...], other_ref[...], NT)
    )
    out_ref[...] = total.astype(BF16)
    center, inverse = layer_stats(held[...].astype(F32))
    gain_part = jnp.sum(total * (center * inverse), axis=0, keepdims=True)
    shift_part = jnp.sum(total, axis=0, keepdims=True)
    bias_part = jnp.sum(projected[...].astype(F32), axis=0, keepdims=True)

    @pl.when(step == 0)
    def _():
        sums_ref[0:1] = gain_part
        sums_ref[1:2] = shift_part
        bias_ref[...] = bias_part

    @pl.when(step > 0)
    def _():
        sums_ref[0:1] += gain_part
        sums_ref[1:2] += shift_part
        bias_ref[...] += bias_part


def normed_part(order, projected, own_grad, other_grad, near, far, attend, own, other, late):
    block = 2 * ROWS
    width = projected.shape[1]
    row = lambda rows, cols: pl.BlockSpec((rows, cols), lambda i, order: (order[i], 0))
    weights = (attend, own, other)
    return call(
        normed_part_kernel,
        "normed_part",
        4,
        [row(block, width), row(block, CORE_FF), row(block, CORE_FF), row(ROWS, WIDTH)]
        + [fixed(a.shape) for a in (*far, *weights)],
        [row(block, WIDTH), fixed((2, WIDTH)), fixed((1, width))],
        [shape((TOKENS, WIDTH)), shape((2, WIDTH), F32), shape((1, width), F32)],
        0,
        0,
        (projected, own_grad, other_grad, near, *far) + weights,
        late,
        [pltpu.VMEM((block, WIDTH), BF16)],
        (order,),
    )


UP_ROWS = WIDTH // SEQ_DEVICES
DOWN_ROWS = CORE_FF // 2
MIX_ROWS = CORE_COLS // 2
PACK_ROWS = UP_ROWS + MIX_ROWS
PACK_COLS = CORE_FF
HALF = PACK_COLS // 2
SLOT_COLS = WIDTH // SEQ_DEVICES


def across(rows):
    return pl.BlockSpec((rows, SLOT_COLS), lambda i, order: (0, order[i]))


def plan_call(
    kernel, name, grid, in_specs, out_specs, out_shape, scratch, flops, moved, order, side, operands, late=()
):
    return call(
        kernel, name, grid, in_specs, out_specs, out_shape, flops, moved, operands, late, scratch, (order, side)
    )


def plan_whole(array):
    return pl.BlockSpec(array.shape, lambda i, order, side: (0, 0))


WIDE = 2 * SLOT_COLS
WIDE_COLUMNS = pl.BlockSpec((TOKENS, WIDE), lambda i, order, side: (0, order[i]))


def down_grads_kernel(step, order_ref, x_ref, act_ref, act_other, cot_ref, cot_other, *refs):
    outs = refs
    down = (dot(act_ref[...], cot_ref[...], TN) + dot(act_other[...], cot_other[...], TN)).astype(BF16)
    for index, out_ref in enumerate(outs):
        for x in range(2):

            @pl.when((step == index) & (x_ref[0] == x))
            def _():
                for r, half in ((0, x), (1, 1 - x)):
                    cols = slice(half * SLOT_COLS, (half + 1) * SLOT_COLS)
                    out_ref[r, :, :HALF] = down[:DOWN_ROWS, cols]
                    out_ref[r, :, HALF:] = down[DOWN_ROWS:, cols]


def down_grads(order, x_lo, act, act_other, cot, cot_other):
    block = (2, DOWN_ROWS, PACK_COLS)
    return Job(
        "down_grads",
        down_grads_kernel,
        4,
        [plan_whole(act), plan_whole(act_other)] + [WIDE_COLUMNS] * 2,
        [pl.BlockSpec(block, lambda i, order, side: (0, 0, 0))] * 4,
        [shape(block)] * 4,
        (act, act_other, cot, cot_other),
        (),
        (order, x_lo),
    )


def up_grads_kernel(
    step,
    order_ref,
    x_ref,
    core_ref,
    grad_ref,
    grad_other,
    att_ref,
    att_other,
    normed_ref,
    normed_other,
    cot_ref,
    cot_other,
    *refs,
):
    outs, held, mixed = refs[:4], refs[4], refs[5]
    held[...] = (
        dot(normed_ref[...], grad_ref[...], TN) + dot(normed_other[...], grad_other[...], TN)
    ).astype(BF16)
    cols = pl.ds(pl.multiple_of(core_ref[0] * CORE_COLS, CORE_COLS), CORE_COLS)
    mixed[...] = (
        dot(att_ref[:, cols], cot_ref[...], TN) + dot(att_other[:, cols], cot_other[...], TN)
    ).astype(BF16)
    for index, out_ref in enumerate(outs):

        @pl.when(step == index)
        def _():
            for r, x in enumerate((x_ref[0], 1 - x_ref[0])):
                out_ref[r, :UP_ROWS] = held[pl.ds(pl.multiple_of(x * UP_ROWS, UP_ROWS), UP_ROWS), :]
                part = mixed[:, pl.ds(pl.multiple_of(x * SLOT_COLS, SLOT_COLS), SLOT_COLS)]
                out_ref[r, UP_ROWS:, :HALF] = part[:MIX_ROWS]
                out_ref[r, UP_ROWS:, HALF:] = part[MIX_ROWS:]


def up_grads(order, x_lo, core, grad, grad_other, att, att_other, normed, normed_other, cot, cot_other):
    block = (2, PACK_ROWS, PACK_COLS)
    columns = pl.BlockSpec((TOKENS, WIDE), lambda i, order, *plan: (0, order[i]))
    held = [pl.BlockSpec(a.shape, lambda i, *plan: (0, 0)) for a in (grad, grad_other, att, att_other)]
    return Job(
        "up_grads",
        up_grads_kernel,
        4,
        held + [columns] * 4,
        [pl.BlockSpec(block, lambda i, *plan: (0, 0, 0))] * 4,
        [shape(block)] * 4,
        (grad, grad_other, att, att_other, normed, normed_other, cot, cot_other),
        (pltpu.VMEM((2 * UP_ROWS, CORE_FF), BF16), pltpu.VMEM((CORE_COLS, WIDE), BF16)),
        (order, x_lo, core),
    )


def attend_grads_kernel(step, order_ref, core_ref, grad_ref, grad_other, own_0, own_1, other_0, other_1, *refs):
    outs, held = refs[:4], refs[4]
    for half, (own, other) in enumerate(((own_0, other_0), (own_1, other_1))):
        held[half] = (
            dot(own[...], grad_ref[...], TN) + dot(other[...], grad_other[...], TN)
        ).astype(BF16)
    for slot in range(SEQ_DEVICES):
        rows = pl.ds(pl.multiple_of(order_ref[slot] * SLAB, SLAB), SLAB)
        for half in range(2):
            outs[slot // 2][slot % 2, half] = held[half, rows, :]


def attend_grads(order, core, grad, grad_other, normed, normed_other, late):
    cols = grad.shape[1]

    def rows_of(half):
        return pl.BlockSpec((TOKENS, CORE_COLS), lambda i, order, core: (0, 4 * i + 2 * half + core[0]))

    return plan_call(
        attend_grads_kernel,
        "attend_grads",
        CHIPS // 2,
        [plan_whole(grad), plan_whole(grad_other)] + [rows_of(0), rows_of(1)] * 2,
        [pl.BlockSpec((2, 2, SLAB, cols), lambda i, order, core: (0, i, 0, 0))] * 4,
        [shape((2, CHIPS, SLAB, cols))] * 4,
        [pltpu.VMEM((2, CORE_COLS, cols), BF16)],
        4 * TOKENS * WIDTH * cols // 2,
        12 * 2**20,
        order,
        core,
        (grad, grad_other, normed, normed, normed_other, normed_other),
        late,
    )


def unpack_down_kernel(step, order_ref, x_ref, *refs):
    down_ref = refs[8]
    for index in range(4):
        for own in range(2):

            @pl.when((step == index) & (x_ref[0] == own))
            def _():
                for x in range(2):
                    piece = refs[index if x == own else 4 + index]
                    cols = slice(x * SLOT_COLS, (x + 1) * SLOT_COLS)
                    down_ref[:DOWN_ROWS, cols] = piece[:, :HALF].astype(F32)
                    down_ref[DOWN_ROWS:, cols] = piece[:, HALF:].astype(F32)


def unpack_down(order, x_lo, pieces, late):
    return plan_call(
        unpack_down_kernel,
        "unpack_down",
        4,
        [pl.BlockSpec(p.shape, lambda i, order, x: (0, 0)) for p in pieces],
        pl.BlockSpec((CORE_FF, WIDE), lambda i, order, x: (0, order[i])),
        shape((CORE_FF, WIDTH), F32),
        [],
        0,
        0,
        order,
        x_lo,
        tuple(pieces),
        late,
    )


def unpack_up_kernel(step, order_ref, x_ref, *refs):
    up_ref, mix_ref = refs[4:]
    for index, pieces in enumerate(refs[:4]):

        @pl.when(step == index)
        def _():
            for x in range(2):
                piece = pieces.at[(x_ref[0] + x) % 2]
                up_ref[x * UP_ROWS : (x + 1) * UP_ROWS] = piece[:UP_ROWS].astype(F32)
                cols = slice(x * SLOT_COLS, (x + 1) * SLOT_COLS)
                mix_ref[:MIX_ROWS, cols] = piece[UP_ROWS:, :HALF].astype(F32)
                mix_ref[MIX_ROWS:, cols] = piece[UP_ROWS:, HALF:].astype(F32)


def unpack_up(order, x_lo, pieces, late):
    return plan_call(
        unpack_up_kernel,
        "unpack_up",
        4,
        [pl.BlockSpec(p.shape, lambda i, order, x: (0, 0, 0)) for p in pieces],
        [
            pl.BlockSpec((2 * UP_ROWS, CORE_FF), lambda i, order, x: (order[i], 0)),
            pl.BlockSpec((CORE_COLS, WIDE), lambda i, order, x: (0, order[i])),
        ],
        [shape((WIDTH, CORE_FF), F32), shape((CORE_COLS, WIDTH), F32)],
        [],
        0,
        0,
        order,
        x_lo,
        tuple(pieces),
        late,
    )


SLAB = CORE_COLS // SEQ_DEVICES


VECTORS = (128, 128, 128, 384, 512)


def unpack_attend_kernel(step, place_ref, x_ref, *refs):
    out_ref, vector_refs, total_ref = refs[4], refs[5:10], refs[10]

    @pl.when(step == 0)
    def _():
        total_ref[...] = jnp.zeros_like(total_ref)

    for index, pieces in enumerate(refs[:4]):

        @pl.when(place_ref[step] == index)
        def _():
            for half in range(2):
                piece = pieces.at[(x_ref[0] + half) % 2]
                rest = piece[CHIPS * SLAB :].astype(F32).reshape(CHIPS, 4, -1)
                total_ref[...] += jnp.sum(rest, axis=0)
                for chip in range(CHIPS):
                    for part in range(3):
                        start = part * WIDTH + chip * CHIP_COLS
                        out_ref[half * SLAB : (half + 1) * SLAB, start : start + CHIP_COLS] = piece[
                            chip * SLAB : (chip + 1) * SLAB,
                            part * CHIP_COLS : (part + 1) * CHIP_COLS,
                        ].astype(F32)

    @pl.when(step == 3)
    def _():
        sums = total_ref[:2] + total_ref[2:]
        start = 0
        for vector_ref in vector_refs[:4]:
            size = vector_ref.shape[1]
            vector_ref[...] = sums[0:1, start : start + size]
            start += size
        vector_refs[4][...] = sums[1:2, : vector_refs[4].shape[1]]


def unpack_attend(place, x_lo, pieces, late):
    cols = pieces[0].shape[2]
    fixed_out = lambda size: pl.BlockSpec((1, size), lambda i, place, x: (0, 0))
    return plan_call(
        unpack_attend_kernel,
        "unpack_attend",
        4,
        [pl.BlockSpec(p.shape, lambda i, place, x: (0, 0, 0)) for p in pieces],
        [pl.BlockSpec((2 * SLAB, 3 * WIDTH), lambda i, place, x: (i, 0))]
        + [fixed_out(size) for size in VECTORS],
        [shape((CORE_COLS, 3 * WIDTH), F32)] + [shape((1, size), F32) for size in VECTORS],
        [pltpu.VMEM((4, cols), F32)],
        0,
        0,
        place,
        x_lo,
        tuple(pieces),
        late,
    )


def rows_grad_kernel(step, rows_ref, cot_ref, near_ref, far_ref, gain_ref, out_ref):
    grad = near_ref[...].astype(F32) + far_ref[...].astype(F32)
    center, inverse = layer_stats(rows_ref[...].astype(F32))
    unit = center * inverse
    scaled = grad * gain_ref[...]
    out_ref[...] = cot_ref[...].astype(F32) + inverse * (
        scaled
        - jnp.mean(scaled, axis=-1, keepdims=True)
        - unit * jnp.mean(scaled * unit, axis=-1, keepdims=True)
    )


def rows_grad(rows, cot, near, far, gain):
    block = 64
    return call(
        rows_grad_kernel,
        "rows_grad",
        ROWS // block,
        [row_block(block, WIDTH)] * 4 + [whole(gain.shape)],
        row_block(block, WIDTH),
        shape((ROWS, WIDTH), F32),
        0,
        4 * 2**20,
        (rows, cot, near, far, gain),
    )


def lane_masks():
    lane = lax.broadcasted_iota(jnp.int32, (1, PAIR), 1)
    first = (lane < HEAD_DIM).astype(BF16)
    return first, 1 - first


def scores_of(query, keys, low):
    scores = dot(query, keys, NT)
    if low:
        head, last = scores[:, :low], scores[:, low:]
    else:
        head, last = None, scores
    row = lax.broadcasted_iota(jnp.int32, last.shape, 0)
    col = lax.broadcasted_iota(jnp.int32, last.shape, 1)
    last = jnp.where(col <= row, last, NEG_FILL)
    return last if head is None else jnp.concatenate([head, last], axis=1)


def attend_kernel(step, query_ref, key_ref, value_ref, out_ref, logsum_ref):
    first, second = lane_masks()
    lane = lax.broadcasted_iota(jnp.int32, (QBLOCK, PAIR), 1)
    for low in range(0, LENGTH, QBLOCK):
        reach = low + QBLOCK
        query = query_ref[low:reach, :] * BF16(SCALE)
        keys = key_ref[:reach, :]
        values = value_ref[:reach, :]
        found = []
        for mask in (first, second):
            scores = scores_of(query * mask, keys, low)
            peak = jnp.max(scores, axis=1, keepdims=True)
            weight = jnp.exp(scores - peak)
            total = jnp.sum(weight, axis=1, keepdims=True)
            found.append((dot(weight.astype(BF16), values) / total, peak + jnp.log(total)))
        out_ref[low:reach, :] = jnp.where(lane < HEAD_DIM, found[0][0], found[1][0]).astype(BF16)
        logsum_ref[low:reach, :] = jnp.where(lane < HEAD_DIM, found[0][1], found[1][1])


def pair_columns(part):
    return pl.BlockSpec((LENGTH, PAIR), lambda p: (0, part * (CHIP_COLS // PAIR) + p))


def attend_forward(qkv, late):
    return call(
        attend_kernel,
        "attend_forward",
        CHIP_COLS // PAIR,
        [pair_columns(0), pair_columns(1), pair_columns(2)],
        [pair_columns(0)] * 2,
        [shape((LENGTH, CHIP_COLS)), shape((LENGTH, CHIP_COLS), F32)],
        8 * 2**30,
        4 * 2**20,
        (qkv, qkv, qkv),
        late,
    )


def attend_back_kernel(
    step,
    query_ref,
    key_ref,
    value_ref,
    grad_ref,
    logsum_ref,
    turn_ref,
    upper_ref,
    lower_ref,
    out_ref,
    key_total,
    value_total,
):
    pair = step
    first, second = lane_masks()
    lane = lax.broadcasted_iota(jnp.int32, (QBLOCK, PAIR), 1)
    key_total[...] = jnp.zeros_like(key_total)
    value_total[...] = jnp.zeros_like(value_total)

    def store(part, low, reach, values):
        start = pl.multiple_of((part * (CHIP_COLS // PAIR) + pair) * PAIR, PAIR)
        out_ref[low:reach, pl.ds(start, PAIR)] = values.astype(BF16)

    def unturn(values, low, reach):
        kept = values.astype(BF16).astype(F32)
        return turn_columns(
            kept, turn_ref[low:reach, :], upper_ref[low:reach, :], lower_ref[low:reach, :], -1.0
        )

    for low in range(0, LENGTH, QBLOCK):
        reach = low + QBLOCK
        query = query_ref[low:reach, :] * BF16(SCALE)
        grad = grad_ref[low:reach, :]
        keys = key_ref[:reach, :]
        values = value_ref[:reach, :]
        query_grads = []
        key_part = 0.0
        value_part = 0.0
        for head, mask in enumerate((first, second)):
            own_query = query * mask
            own_grad = grad * mask
            scores = scores_of(own_query, keys, low)
            start = head * HEAD_DIM
            probs = jnp.exp(scores - logsum_ref[low:reach, start : start + 1])
            prob_grad = dot(own_grad, values, NT)
            inner = jnp.sum(probs * prob_grad, axis=1, keepdims=True)
            score_grad = (probs * (prob_grad - inner)).astype(BF16)
            query_grads.append(dot(score_grad, keys))
            key_part += dot(score_grad, own_query, TN)
            value_part += dot(probs.astype(BF16), own_grad, TN)
        key_total[:reach, :] += key_part
        value_total[:reach, :] += value_part
        query_grad = jnp.where(lane < HEAD_DIM, query_grads[0], query_grads[1]) * SCALE
        store(0, low, reach, unturn(query_grad, low, reach))
    store(1, 0, LENGTH, unturn(key_total[...], 0, LENGTH))
    store(2, 0, LENGTH, value_total[...])


def attend_backward(qkv, grad, logsum, tables, late):
    return call(
        attend_back_kernel,
        "attend_backward",
        CHIP_COLS // PAIR,
        [pair_columns(0), pair_columns(1), pair_columns(2), pair_columns(0), pair_columns(0)]
        + [whole(t.shape) for t in tables],
        whole((LENGTH, 3 * CHIP_COLS)),
        shape((LENGTH, 3 * CHIP_COLS)),
        20 * 2**30,
        6 * 2**20,
        (qkv, qkv, qkv, grad, logsum) + tables,
        late,
        [pltpu.VMEM((LENGTH, PAIR), F32)] * 2,
    )


def exchange(blocks, axes):
    return lax.all_to_all(blocks, axes, split_axis=0, concat_axis=0, tiled=True)


def spread(block, axes, count):
    return exchange(jnp.broadcast_to(block[None], (count,) + block.shape), axes)


tie = lax.optimization_barrier


def sent_y(parts):
    return [send(parts[k], "y", k) for k in (1, 3, 2)]


def joined(leave, stay):
    return (stay + swap(leave.astype(BF16), "xl").astype(F32)).astype(BF16)


def sum_seq(parts, arrived):
    leave, stay = (
        parts[0][r].astype(F32) + sum(a[r].astype(F32) for a in arrived) for r in (1, 0)
    )
    return joined(leave, stay)


def in_rows(values):
    width = 3 * CHIP_COLS
    count = values.shape[0]
    head = lax.reduce_precision(values, 8, 7)
    rest = (values - head).astype(BF16)
    head = head.astype(BF16)
    rows = [jnp.pad(part, ((0, 0), (0, 2 * width - part.shape[1]))).reshape(count, 2, width) for part in (head, rest)]
    return jnp.pad(jnp.concatenate(rows, axis=1), ((0, 0), (0, SLAB - 4), (0, 0)))


def summed_y(parts, arrived):
    return (parts[0].astype(F32) + sum(a.astype(F32) for a in arrived)).astype(BF16)


def summed_pair(own, other):
    return (own.astype(F32) + other[::-1].astype(F32)).astype(BF16)


def spread_y(pair):
    found = {0: pair} | {k: shift(pair, "y", k) for k in (1, 3, 2)}
    return [found[k] for k in range(4)]


def sum_rows(parts):
    parts = lax.psum_scatter(
        parts.reshape(4, 2, ROWS, WIDTH), "z", scatter_dimension=0, tiled=False
    )
    return parts


def per_device(
    inputs,
    gains,
    shifts,
    attend,
    attend_bias,
    mixer,
    mixer_bias,
    upward,
    upward_bias,
    downward,
    downward_bias,
    cotangent,
):
    core = lax.axis_index("c")
    x_lo = lax.axis_index("xl")
    chip = lax.axis_index("xh") * 4 + lax.axis_index("z")
    seq_index = lax.axis_index("y") * 2 + x_lo
    core_at = core.reshape(1)
    rows_in = inputs.reshape(ROWS, WIDTH)
    own_cot = cotangent.reshape(ROWS, WIDTH)
    width = 3 * CHIP_COLS

    z_order = (lax.axis_index("z") + jnp.arange(4, dtype=jnp.int32)) % 4
    y_place = (jnp.arange(4, dtype=jnp.int32) - lax.axis_index("y")) % 4
    y_order = (lax.axis_index("y") + jnp.arange(4, dtype=jnp.int32)) % 4
    seq_order = (y_order[:, None] * 2 + jnp.stack([x_lo, 1 - x_lo])[None, :]).reshape(SEQ_DEVICES)

    near = lax.all_gather(rows_in, "z", axis=0, tiled=True)
    other_rows = swap(rows_in, "xh")

    slab = lax.dynamic_slice_in_dim(attend, seq_index * SLAB, SLAB, 0)
    slab = slab.reshape(SLAB, 3, CHIPS, CHIP_COLS).transpose(2, 0, 1, 3).reshape(CHIPS, SLAB, width)
    small, start = 0, 0
    for vector in (gains, shifts, mixer_bias, downward_bias, attend_bias):
        small = small + jnp.pad(vector, (start, 2 * width - start - vector.shape[0]))
        start += vector.shape[0]
    small = small.reshape(1, 2, width)
    small = jnp.pad(jnp.broadcast_to(small, (CHIPS, 2, width)), ((0, 0), (0, SLAB - 2), (0, 0)))
    slab = exchange(jnp.concatenate([slab, small], axis=1), GROUP)
    slab, other_rows = tie((slab, other_rows))
    far = [other_rows] + [shift(other_rows, "z", k) for k in (1, 2, 3)]
    small_own = slab[:, SLAB : SLAB + 2].reshape(CHIPS, 2 * width)[:, :896]
    slab = slab[:, :SLAB]
    attend_own = spread(slab, SEQ, SEQ_DEVICES).reshape(SEQ_DEVICES, CHIPS, SLAB, width)
    attend_own, all_tables, near, *far = tie(
        (attend_own, rope_tables(jnp.arange(LENGTH, dtype=jnp.int32), 2), near, *far)
    )
    attend_other = swap(attend_own, "c")
    small_other = swap(small_own, "c")
    small_all = jnp.where(
        core == 0, jnp.stack([small_own, small_other], 1), jnp.stack([small_other, small_own], 1)
    ).reshape(FSDP_DEVICES, 7, 128).astype(F32)
    gain_all = small_all[:, 0].reshape(1, WIDTH)
    shift_all = small_all[:, 1].reshape(1, WIDTH)
    out_bias = (small_all[:, 2] + small_all[:, 3]).reshape(WIDTH)
    bias_grid = small_all[:, 4:7].reshape(3, CHIPS, CHIP_COLS)
    attend_bias_chip = lax.dynamic_slice_in_dim(bias_grid, chip, 1, 1).reshape(1, width)

    mixer_other = swap(mixer, "c")
    mixer_chip = jnp.where(
        core == 0, jnp.concatenate([mixer, mixer_other]), jnp.concatenate([mixer_other, mixer])
    )
    up_other = swap(upward, "c")
    down_other = swap(downward, "c")
    up_bias_own = upward_bias.astype(F32).reshape(1, CORE_FF)
    up_bias_other = swap(upward_bias.reshape(1, CORE_FF), "c").astype(F32)

    cot_pair = jnp.stack([own_cot, swap(own_cot, "xh")])
    cot_pair, near, *far = tie((cot_pair, near, *far))
    cot_group = lax.all_gather(cot_pair, "z", axis=0, tiled=False).reshape(TOKENS, WIDTH)
    normed, qkv_sent, attend_chip = norm_project(
        seq_index.reshape(1),
        z_order,
        core_at,
        near,
        far,
        gain_all,
        shift_all,
        attend_bias_chip,
        attend_own,
        attend_other,
        all_tables,
        (mixer_chip, up_other, down_other, up_bias_other, up_bias_own),
    )
    normed_other = swap(normed, "c")
    qkv = exchange(qkv_sent.reshape(CHIPS, ROWS, width), SEQ).reshape(LENGTH, width)
    act_own, act_other, slope_own, slope_other = hidden_forward(
        normed, upward, up_other, up_bias_own, up_bias_other
    )
    act_sent = swap(act_other, "c")

    attended, logsum = attend_forward(qkv, (act_own, normed_other))
    attended, cot_group = tie((attended, cot_group))
    attended_group = exchange(attended.reshape(SEQ_DEVICES, ROWS, CHIP_COLS), SEQ).reshape(
        TOKENS, CHIP_COLS
    )
    cot_other = swap(cot_group, "c")
    attended_grad = grad_heads(cot_group, mixer_chip, (attended,))
    grads = exchange(attended_grad.reshape(CHIPS, ROWS, CHIP_COLS), SEQ).reshape(LENGTH, CHIP_COLS)

    x_at = x_lo.reshape(1)
    (grad_own, grad_other, up_bias_sum, up_bias_other_sum), down_slabs = run(
        hidden_back(cot_group, downward, down_other, slope_own, slope_other),
        down_grads(y_order, x_at, act_own, act_sent, cot_group, cot_other),
        late=(attended_grad, attended_group),
    )
    grad_sent = swap(grad_other, "c")

    back = attend_backward(qkv, grads, logsum, all_tables, (down_slabs[0],))
    projected_grad = exchange(back.reshape(SEQ_DEVICES, ROWS, width), SEQ).reshape(TOKENS, width)

    attended_group, *down_arrived = tie((attended_group, *sent_y(down_slabs)))
    parts = run(
        out_part(act_own, act_other, attended_group, downward, down_other, mixer_chip),
        late=(back,),
    )
    up_slabs = run(
        up_grads(
            y_order,
            x_at,
            core_at,
            grad_own,
            grad_sent,
            attended_group,
            swap(attended_group, "c"),
            normed,
            normed_other,
            cot_group,
            cot_other,
        ),
        late=(parts,),
    )
    out_sums = sum_rows(parts)
    up_arrived = sent_y(up_slabs)

    down_own = summed_y(down_slabs, down_arrived)
    down_other_x = swap(down_own[1], "xl")

    projected_grad, up_first = tie((projected_grad, up_slabs[0]))
    attend_slabs = attend_grads(
        seq_order,
        core_at,
        projected_grad,
        swap(projected_grad, "c"),
        normed,
        normed_other,
        (up_first,),
    )

    down_other_x, attend_first = tie((down_other_x, attend_slabs[0]))
    attend_slabs = [attend_first, *attend_slabs[1:]]
    down_sum = (down_own[0].astype(F32) + down_other_x.astype(F32)).astype(BF16)

    parts, norm_sums, attend_bias_sum = normed_part(
        z_order,
        projected_grad,
        grad_own,
        grad_other,
        near,
        far,
        attend_chip,
        upward,
        up_other,
        (attend_slabs[0],),
    )
    parts, out_sums, down_sum, *up_arrived = tie((parts, out_sums, down_sum, *up_arrived))
    outputs = (
        rows_in.astype(F32) + out_bias + out_sums[0].astype(F32) + swap(out_sums[1], "xh").astype(F32)
    ).astype(BF16)
    sums = sum_rows(parts)
    inputs_grad = rows_grad(rows_in, own_cot, sums[0], swap(sums[1], "xh"), gain_all)

    bias_full = jnp.sum(own_cot.astype(F32), axis=0)
    attend_bias_full = lax.dynamic_update_slice(
        jnp.zeros((3, CHIPS, CHIP_COLS), F32), attend_bias_sum.reshape(3, 1, CHIP_COLS), (0, chip, 0)
    )
    up_bias_pair = jnp.where(
        core == 0,
        jnp.concatenate([up_bias_sum, up_bias_other_sum]),
        jnp.concatenate([up_bias_other_sum, up_bias_sum]),
    )
    up_bias_full = lax.dynamic_update_slice(
        jnp.zeros((CHIPS, 2, CORE_FF), F32), up_bias_pair[None], (chip, 0, 0)
    )
    vectors = jnp.concatenate(
        [
            v.reshape(FSDP_DEVICES, -1)
            for v in (norm_sums[0], norm_sums[1], bias_full, attend_bias_full, up_bias_full)
        ],
        axis=1,
    )
    vectors = vectors.reshape(CHIPS, 2, -1)
    vectors_keep = lax.dynamic_index_in_dim(vectors, core, 1, keepdims=False)
    vectors_sent = lax.dynamic_index_in_dim(vectors, 1 - core, 1, keepdims=False)
    vectors = vectors_keep + swap(vectors_sent, "c")
    up_own = summed_y(up_slabs, up_arrived)
    up_pair = summed_pair(up_own, swap(up_own, "xl"))
    *attend_arrived, down_sum, up_pair = tie((*sent_y(attend_slabs), down_sum, up_pair))
    attend_sum = sum_seq(attend_slabs, attend_arrived)
    message = exchange(jnp.concatenate([attend_sum, in_rows(vectors)], axis=1), GROUP)
    kept = message[:, SLAB : SLAB + 4].reshape(-1, width)
    message = jnp.concatenate([message[:, :SLAB].reshape(-1, width), kept], axis=0)
    up_1, up_3 = shift(up_pair, "y", 1), shift(up_pair, "y", 3)
    message, outputs, up_1, up_3, *down_near = tie((message, outputs, up_1, up_3, *spread_y(down_sum)))
    up_pieces = [up_pair, up_1, shift(up_pair, "y", 2), up_3]
    attend_pair, *down_near = tie((jnp.stack([message, swap(message, "xl")]), *down_near))
    attend_pieces = spread_y(attend_pair)
    down_pieces = down_near + [swap(piece, "xl") for piece in down_near]
    down_grad, (up_grad, mixer_grad) = run(
        unpack_down(y_order, x_at, down_pieces, None), unpack_up(y_order, x_at, up_pieces, None)
    )
    attend_grad, *vectors = unpack_attend(
        y_place, x_at, attend_pieces, (inputs_grad, outputs, down_grad, up_grad)
    )
    gain_grad, shift_grad, bias_grad, attend_bias_grad, up_bias_grad = (v[0] for v in vectors)

    return (
        outputs.reshape(inputs.shape),
        inputs_grad.reshape(inputs.shape),
        gain_grad,
        shift_grad,
        attend_grad,
        attend_bias_grad,
        mixer_grad,
        bias_grad,
        up_grad,
        up_bias_grad,
        down_grad,
        bias_grad,
    )


def solution(mesh):
    fine = Mesh(mesh.devices.reshape(4, 2, 2, 4, 2), ("y", "xl", "xh", "z", "c"))
    rows = P(FSDP, SEQ, None)
    vector = P(FSDP)
    by_row = P(FSDP, None)
    by_col = P(None, FSDP)
    in_specs = (
        rows,
        vector,
        vector,
        by_row,
        vector,
        by_row,
        vector,
        by_col,
        vector,
        by_row,
        vector,
        rows,
    )
    out_specs = (
        rows,
        rows,
        vector,
        vector,
        by_row,
        vector,
        by_row,
        vector,
        by_col,
        vector,
        by_row,
        vector,
    )
    return jax.shard_map(
        per_device, mesh=fine, in_specs=in_specs, out_specs=out_specs, check_vma=False
    )
```

```python
from typing import Callable, NamedTuple, Sequence

import jax
import jax.numpy as jnp
from jax import lax
from jax.experimental import pallas as pl
from jax.experimental.pallas import tpu as pltpu
from jax.sharding import Mesh, PartitionSpec as P

HEADS = 32
HEAD_DIM = 64
ROT = 32
WIDTH = 2048
FF = 8192
SEQ_DEVICES = 8
CHIPS = 8
FSDP_DEVICES = 16
ROWS = 128
LENGTH = ROWS * SEQ_DEVICES
TOKENS = ROWS * CHIPS
CHIP_COLS = WIDTH // CHIPS
CORE_COLS = WIDTH // FSDP_DEVICES
CORE_FF = FF // FSDP_DEVICES
PAIR = 2 * HEAD_DIM
QBLOCK = 256

EPSILON = 1e-05
ROPE_BASE = 10000.0
NEG_FILL = -1e30
PACE = 1 * 1.15e9
MICROSECONDS = dict(
    norm_project=13,
    hidden_forward=11,
    attend_forward=10,
    grad_heads=15,
    hidden_back=30,
    down_grads=30,
    attend_backward=15,
    out_part=30,
    up_grads=40,
    attend_grads=25,
    normed_part=25,
    unpack_down=6,
    unpack_up=6,
    unpack_attend=6,
    rows_grad=3,
)
SCALE = HEAD_DIM ** (-0.5)

F32 = jnp.float32
BF16 = jnp.bfloat16

SEQ = ("y", "xl")
GROUP = ("xh", "z")
FSDP = ("xh", "z", "c")

NT = (((1,), (1,)), ((), ()))
TN = (((0,), (0,)), ((), ()))
NN = (((1,), (0,)), ((), ()))


def dot(lhs, rhs, dims=NN):
    return lax.dot_general(lhs, rhs, dims, preferred_element_type=F32)


def swap(piece, axis):
    return lax.ppermute(piece, axis, [(0, 1), (1, 0)])


def shift(piece, axis, step):
    return lax.ppermute(piece, axis, [(i, (i - step) % 4) for i in range(4)])


def send(piece, axis, step):
    return lax.ppermute(piece, axis, [(i, (i + step) % 4) for i in range(4)])


def rope_tables(positions, heads):
    half = ROT // 2
    frequency = ROPE_BASE ** (-2.0 * jnp.arange(half, dtype=F32) / ROT)
    angle = positions.astype(F32)[:, None] * frequency[None, :]
    cosine, sine = jnp.cos(angle), jnp.sin(angle)
    rest = jnp.zeros((positions.shape[0], HEAD_DIM - ROT), F32)
    blank = jnp.zeros_like(sine)
    turn = jnp.concatenate([cosine, cosine, rest + 1.0], axis=1)
    upper = jnp.concatenate([-sine, blank, rest], axis=1)
    lower = jnp.concatenate([blank, sine, rest], axis=1)
    return tuple(jnp.concatenate([t] * heads, axis=1) for t in (turn, upper, lower))


def turn_columns(values, turn, upper, lower, sign):
    width = values.shape[1]
    half = ROT // 2
    ahead = pltpu.roll(values, width - half, 1)
    behind = pltpu.roll(values, half, 1)
    return values * turn + sign * (ahead * upper + behind * lower)


def cost(names):
    return pl.CostEstimate(
        flops=int(sum(MICROSECONDS[name] for name in names) * PACE), bytes_accessed=0, transcendentals=0
    )


def whole(shape):
    return pl.BlockSpec(shape, lambda i: (0,) * len(shape))


def row_block(rows, width, column=0):
    return pl.BlockSpec((rows, width), lambda i: (i, column))


class Job(NamedTuple):
    name: str
    kernel: Callable
    grid: int
    in_specs: Sequence
    out_specs: Sequence
    out_shape: Sequence
    operands: tuple
    scratch: tuple = ()
    plan: tuple = ()


def run(*jobs, late=()):
    plans = [len(job.plan) for job in jobs]
    starts = [sum(job.grid for job in jobs[:k]) for k in range(len(jobs))]

    def moved(spec, start, count, first, size):
        def index(step, *plan):
            own = plan[first : first + size]
            return spec.index_map(jnp.clip(step - start, 0, count - 1) if len(jobs) > 1 else step, *own)

        return pl.BlockSpec(spec.block_shape, index)

    def specs_of(kind):
        return [
            moved(spec, starts[k], job.grid, sum(plans[:k]), plans[k])
            for k, job in enumerate(jobs)
            for spec in getattr(job, kind)
        ]

    def body(*refs):
        refs = list(refs)
        take = lambda count: [refs.pop(0) for _ in range(count)]
        plan_refs = [take(count) for count in plans]
        in_refs = [take(len(job.operands)) for job in jobs]
        take(len(late))
        out_refs = [take(len(job.out_specs)) for job in jobs]
        held = [take(len(job.scratch)) for job in jobs]
        step = pl.program_id(0)
        for k, job in enumerate(jobs):
            own = (*plan_refs[k], *in_refs[k], *out_refs[k], *held[k])
            if len(jobs) == 1:
                job.kernel(step, *own)
            else:

                @pl.when((step >= starts[k]) & (step < starts[k] + job.grid))
                def _():
                    job.kernel(step - starts[k], *own)

    found = pl.pallas_call(
        body,
        grid_spec=pltpu.PrefetchScalarGridSpec(
            num_scalar_prefetch=sum(plans),
            grid=(sum(job.grid for job in jobs),),
            in_specs=specs_of("in_specs") + [pl.BlockSpec(memory_space=pl.ANY)] * len(late),
            out_specs=specs_of("out_specs"),
            scratch_shapes=[shape for job in jobs for shape in job.scratch],
        ),
        out_shape=[shape for job in jobs for shape in job.out_shape],
        compiler_params=pltpu.CompilerParams(vmem_limit_bytes=60 * 2**20),
        cost_estimate=cost([job.name for job in jobs]),
        name="_".join(job.name for job in jobs),
    )(*(p for job in jobs for p in job.plan), *(a for job in jobs for a in job.operands), *late)
    found = list(found)
    results = []
    for job in jobs:
        own, found = found[: len(job.out_specs)], found[len(job.out_specs) :]
        results.append(own[0] if len(own) == 1 else own)
    return results[0] if len(jobs) == 1 else results


def listed(value):
    return list(value) if isinstance(value, (list, tuple)) else [value]


def call(
    kernel, name, grid, in_specs, out_specs, out_shape, flops, moved, operands, late=(), scratch=(), plan=()
):
    job = Job(
        name, kernel, grid, in_specs, listed(out_specs), listed(out_shape), operands, tuple(scratch), plan
    )
    return job if late is None else run(job, late=late)


def placed_call(
    kernel, name, grid, in_specs, out_specs, out_shape, scratch, flops, moved, order, operands, late=()
):
    return call(
        kernel, name, grid, in_specs, out_specs, out_shape, flops, moved, operands, late, scratch, (order,)
    )


def fixed(dims):
    return pl.BlockSpec(dims, lambda i, order: (0,) * len(dims))


def shape(dims, kind=BF16):
    return jax.ShapeDtypeStruct(dims, kind)


def layer_stats(rows):
    center = rows - jnp.mean(rows, axis=-1, keepdims=True)
    spread_out = jnp.mean(center * center, axis=-1, keepdims=True)
    return center, lax.rsqrt(spread_out + EPSILON)


def put_rows(step, near_ref, far_refs, held):
    held[:ROWS] = near_ref[...]
    for index, far_ref in enumerate(far_refs):

        @pl.when(step == index)
        def _():
            held[ROWS:] = far_ref[...]


def norm_project_kernel(
    step,
    at_ref,
    order_ref,
    core_ref,
    near_ref,
    far_0,
    far_1,
    far_2,
    far_3,
    gain_ref,
    shift_ref,
    bias_ref,
    own_ref,
    other_ref,
    turn_ref,
    upper_ref,
    lower_ref,
    normed_ref,
    out_ref,
    weight_ref,
    held,
):
    @pl.when(step == 0)
    def _():
        for chip in range(CHIPS):
            for core, piece in ((core_ref[0], own_ref), (1 - core_ref[0], other_ref)):
                first = pl.multiple_of(chip * CHIP_COLS + core * CORE_COLS, CORE_COLS)
                weight_ref[pl.ds(first, CORE_COLS), :] = piece[:, chip].reshape(CORE_COLS, -1)

    put_rows(step, near_ref, (far_0, far_1, far_2, far_3), held)
    rows = held[...]
    center, inverse = layer_stats(rows.astype(F32))
    normed = (center * inverse * gain_ref[...] + shift_ref[...]).astype(BF16)
    normed_ref[...] = normed
    projected = dot(normed, weight_ref[...]) + bias_ref[...]
    turned_width = 2 * CHIP_COLS
    for block in range(2):
        rows = slice(block * ROWS, (block + 1) * ROWS)
        for start in range(0, turned_width, PAIR):
            cols = slice(start, start + PAIR)
            out_ref[rows, cols] = turn_columns(
                projected[rows, cols], turn_ref[...], upper_ref[...], lower_ref[...], 1.0
            ).astype(BF16)
    out_ref[:, turned_width:] = projected[:, turned_width:].astype(BF16)


def norm_project(seq_at, order, core, near, far, gain, shift_row, bias, own, other, tables, late):
    block = 2 * ROWS
    width = own.shape[-1]
    row = lambda rows, cols: pl.BlockSpec((rows, cols), lambda i, at, order, core: (order[i], 0))
    own_rows = pl.BlockSpec((ROWS, PAIR), lambda i, at, order, core: (at[0], 0))
    held = lambda dims: pl.BlockSpec(dims, lambda i, at, order, core: (0,) * len(dims))
    fixed_ones = (*far, gain, shift_row, bias, own, other)
    return call(
        norm_project_kernel,
        "norm_project",
        4,
        [row(ROWS, WIDTH)] + [held(a.shape) for a in fixed_ones] + [own_rows] * 3,
        [row(block, WIDTH), row(block, width), held((WIDTH, width))],
        [shape((TOKENS, WIDTH)), shape((TOKENS, width)), shape((WIDTH, width))],
        0,
        0,
        (near, *fixed_ones) + tables,
        late,
        [pltpu.VMEM((block, WIDTH), BF16)],
        (seq_at, order, core),
    )


def hidden_kernel(
    step,
    normed_ref,
    own_ref,
    other_ref,
    own_bias_ref,
    other_bias_ref,
    own_act_ref,
    other_act_ref,
    own_slope_ref,
    other_slope_ref,
):
    root = (2.0 / 3.141592653589793) ** 0.5
    for weight, bias, act, slope in (
        (own_ref, own_bias_ref, own_act_ref, own_slope_ref),
        (other_ref, other_bias_ref, other_act_ref, other_slope_ref),
    ):
        hidden = dot(normed_ref[...], weight[...]) + bias[...]
        square = hidden * hidden
        bend = jnp.tanh(root * hidden * (1.0 + 0.044715 * square))
        half = 0.5 * (1.0 + bend)
        act[...] = (hidden * half).astype(BF16)
        slope[...] = half + 0.5 * hidden * (1.0 - bend * bend) * (
            root * (1.0 + 3.0 * 0.044715 * square)
        )


def hidden_forward(normed, own, other, own_bias, other_bias):
    block = 256
    operands = (own, other, own_bias, other_bias)
    return call(
        hidden_kernel,
        "hidden_forward",
        TOKENS // block,
        [row_block(block, WIDTH)] + [whole(v.shape) for v in operands],
        [row_block(block, CORE_FF)] * 4,
        [shape((TOKENS, CORE_FF))] * 2 + [shape((TOKENS, CORE_FF), F32)] * 2,
        4 * TOKENS * WIDTH * CORE_FF,
        14 * 2**20,
        (normed,) + operands,
    )


def grad_heads_kernel(step, cot_ref, mixer_ref, out_ref):
    out_ref[...] = dot(cot_ref[...], mixer_ref[...], NT).astype(BF16)


def grad_heads(cot, mixer, late):
    block = 256
    return call(
        grad_heads_kernel,
        "grad_heads",
        TOKENS // block,
        [row_block(block, WIDTH), whole(mixer.shape)],
        row_block(block, CHIP_COLS),
        shape((TOKENS, CHIP_COLS)),
        2 * TOKENS * WIDTH * CHIP_COLS,
        6 * 2**20,
        (cot, mixer),
        late,
    )


def hidden_back_kernel(
    step,
    cot_ref, own_ref, other_ref, own_slope_ref, other_slope_ref, own_out, other_out, own_sum, other_sum
):
    for weight, slope, out, total in (
        (own_ref, own_slope_ref, own_out, own_sum),
        (other_ref, other_slope_ref, other_out, other_sum),
    ):
        grad = (dot(cot_ref[...], weight[...], NT) * slope[...]).astype(BF16)
        out[...] = grad
        part = jnp.sum(grad.astype(F32), axis=0, keepdims=True)

        @pl.when(step == 0)
        def _():
            total[...] = part

        @pl.when(step > 0)
        def _():
            total[...] += part


def hidden_back(cot, own, other, own_slope, other_slope):
    block = 256
    return call(
        hidden_back_kernel,
        "hidden_back",
        TOKENS // block,
        [row_block(block, WIDTH), whole(own.shape), whole(other.shape)]
        + [row_block(block, CORE_FF)] * 2,
        [row_block(block, CORE_FF)] * 2 + [whole((1, CORE_FF))] * 2,
        [shape((TOKENS, CORE_FF))] * 2 + [shape((1, CORE_FF), F32)] * 2,
        4 * TOKENS * WIDTH * CORE_FF,
        14 * 2**20,
        (cot, own, other, own_slope, other_slope),
        None,
    )


def out_part_kernel(step, own_act, other_act, attended, own_ref, other_ref, mixer_ref, out_ref):
    out_ref[...] = (
        dot(own_act[...], own_ref[...])
        + dot(other_act[...], other_ref[...])
        + dot(attended[...], mixer_ref[...])
    ).astype(BF16)


def out_part(own_act, other_act, attended, own, other, mixer):
    block = 256
    weights = (own, other, mixer)
    return call(
        out_part_kernel,
        "out_part",
        TOKENS // block,
        [row_block(block, CORE_FF)] * 2
        + [row_block(block, CHIP_COLS)]
        + [whole(w.shape) for w in weights],
        row_block(block, WIDTH),
        shape((TOKENS, WIDTH)),
        2 * TOKENS * WIDTH * (2 * CORE_FF + CHIP_COLS),
        12 * 2**20,
        (own_act, other_act, attended) + weights,
        None,
    )


def normed_part_kernel(
    step,
    order_ref,
    projected,
    own_grad,
    other_grad,
    near_ref,
    far_0,
    far_1,
    far_2,
    far_3,
    attend_ref,
    own_ref,
    other_ref,
    out_ref,
    sums_ref,
    bias_ref,
    held,
):
    put_rows(step, near_ref, (far_0, far_1, far_2, far_3), held)
    total = (
        dot(projected[...], attend_ref[...], NT)
        + dot(own_grad[...], own_ref[...], NT)
        + dot(other_grad[...], other_ref[...], NT)
    )
    out_ref[...] = total.astype(BF16)
    center, inverse = layer_stats(held[...].astype(F32))
    gain_part = jnp.sum(total * (center * inverse), axis=0, keepdims=True)
    shift_part = jnp.sum(total, axis=0, keepdims=True)
    bias_part = jnp.sum(projected[...].astype(F32), axis=0, keepdims=True)

    @pl.when(step == 0)
    def _():
        sums_ref[0:1] = gain_part
        sums_ref[1:2] = shift_part
        bias_ref[...] = bias_part

    @pl.when(step > 0)
    def _():
        sums_ref[0:1] += gain_part
        sums_ref[1:2] += shift_part
        bias_ref[...] += bias_part


def normed_part(order, projected, own_grad, other_grad, near, far, attend, own, other, late):
    block = 2 * ROWS
    width = projected.shape[1]
    row = lambda rows, cols: pl.BlockSpec((rows, cols), lambda i, order: (order[i], 0))
    weights = (attend, own, other)
    return call(
        normed_part_kernel,
        "normed_part",
        4,
        [row(block, width), row(block, CORE_FF), row(block, CORE_FF), row(ROWS, WIDTH)]
        + [fixed(a.shape) for a in (*far, *weights)],
        [row(block, WIDTH), fixed((2, WIDTH)), fixed((1, width))],
        [shape((TOKENS, WIDTH)), shape((2, WIDTH), F32), shape((1, width), F32)],
        0,
        0,
        (projected, own_grad, other_grad, near, *far) + weights,
        late,
        [pltpu.VMEM((block, WIDTH), BF16)],
        (order,),
    )


UP_ROWS = WIDTH // SEQ_DEVICES
DOWN_ROWS = CORE_FF // 2
MIX_ROWS = CORE_COLS // 2
PACK_ROWS = UP_ROWS + MIX_ROWS
PACK_COLS = CORE_FF
HALF = PACK_COLS // 2
SLOT_COLS = WIDTH // SEQ_DEVICES


def across(rows):
    return pl.BlockSpec((rows, SLOT_COLS), lambda i, order: (0, order[i]))


def plan_call(
    kernel, name, grid, in_specs, out_specs, out_shape, scratch, flops, moved, order, side, operands, late=()
):
    return call(
        kernel, name, grid, in_specs, out_specs, out_shape, flops, moved, operands, late, scratch, (order, side)
    )


def plan_whole(array):
    return pl.BlockSpec(array.shape, lambda i, order, side: (0, 0))


WIDE = 2 * SLOT_COLS
WIDE_COLUMNS = pl.BlockSpec((TOKENS, WIDE), lambda i, order, side: (0, order[i]))


def down_grads_kernel(step, order_ref, x_ref, act_ref, act_other, cot_ref, cot_other, *refs):
    outs = refs
    down = (dot(act_ref[...], cot_ref[...], TN) + dot(act_other[...], cot_other[...], TN)).astype(BF16)
    for index, out_ref in enumerate(outs):
        for x in range(2):

            @pl.when((step == index) & (x_ref[0] == x))
            def _():
                for r, half in ((0, x), (1, 1 - x)):
                    cols = slice(half * SLOT_COLS, (half + 1) * SLOT_COLS)
                    out_ref[r, :, :HALF] = down[:DOWN_ROWS, cols]
                    out_ref[r, :, HALF:] = down[DOWN_ROWS:, cols]


def down_grads(order, x_lo, act, act_other, cot, cot_other):
    block = (2, DOWN_ROWS, PACK_COLS)
    return Job(
        "down_grads",
        down_grads_kernel,
        4,
        [plan_whole(act), plan_whole(act_other)] + [WIDE_COLUMNS] * 2,
        [pl.BlockSpec(block, lambda i, order, side: (0, 0, 0))] * 4,
        [shape(block)] * 4,
        (act, act_other, cot, cot_other),
        (),
        (order, x_lo),
    )


def up_grads_kernel(
    step,
    order_ref,
    x_ref,
    core_ref,
    grad_ref,
    grad_other,
    att_ref,
    att_other,
    normed_ref,
    normed_other,
    cot_ref,
    cot_other,
    *refs,
):
    outs, held, mixed = refs[:4], refs[4], refs[5]
    held[...] = (
        dot(normed_ref[...], grad_ref[...], TN) + dot(normed_other[...], grad_other[...], TN)
    ).astype(BF16)
    cols = pl.ds(pl.multiple_of(core_ref[0] * CORE_COLS, CORE_COLS), CORE_COLS)
    mixed[...] = (
        dot(att_ref[:, cols], cot_ref[...], TN) + dot(att_other[:, cols], cot_other[...], TN)
    ).astype(BF16)
    for index, out_ref in enumerate(outs):

        @pl.when(step == index)
        def _():
            for r, x in enumerate((x_ref[0], 1 - x_ref[0])):
                out_ref[r, :UP_ROWS] = held[pl.ds(pl.multiple_of(x * UP_ROWS, UP_ROWS), UP_ROWS), :]
                part = mixed[:, pl.ds(pl.multiple_of(x * SLOT_COLS, SLOT_COLS), SLOT_COLS)]
                out_ref[r, UP_ROWS:, :HALF] = part[:MIX_ROWS]
                out_ref[r, UP_ROWS:, HALF:] = part[MIX_ROWS:]


def up_grads(order, x_lo, core, grad, grad_other, att, att_other, normed, normed_other, cot, cot_other):
    block = (2, PACK_ROWS, PACK_COLS)
    columns = pl.BlockSpec((TOKENS, WIDE), lambda i, order, *plan: (0, order[i]))
    held = [pl.BlockSpec(a.shape, lambda i, *plan: (0, 0)) for a in (grad, grad_other, att, att_other)]
    return Job(
        "up_grads",
        up_grads_kernel,
        4,
        held + [columns] * 4,
        [pl.BlockSpec(block, lambda i, *plan: (0, 0, 0))] * 4,
        [shape(block)] * 4,
        (grad, grad_other, att, att_other, normed, normed_other, cot, cot_other),
        (pltpu.VMEM((2 * UP_ROWS, CORE_FF), BF16), pltpu.VMEM((CORE_COLS, WIDE), BF16)),
        (order, x_lo, core),
    )


def attend_grads_kernel(step, order_ref, core_ref, grad_ref, grad_other, own_0, own_1, other_0, other_1, *refs):
    outs, held = refs[:4], refs[4]
    for half, (own, other) in enumerate(((own_0, other_0), (own_1, other_1))):
        held[half] = (
            dot(own[...], grad_ref[...], TN) + dot(other[...], grad_other[...], TN)
        ).astype(BF16)
    for slot in range(SEQ_DEVICES):
        rows = pl.ds(pl.multiple_of(order_ref[slot] * SLAB, SLAB), SLAB)
        for half in range(2):
            outs[slot // 2][slot % 2, half] = held[half, rows, :]


def attend_grads(order, core, grad, grad_other, normed, normed_other, late):
    cols = grad.shape[1]

    def rows_of(half):
        return pl.BlockSpec((TOKENS, CORE_COLS), lambda i, order, core: (0, 4 * i + 2 * half + core[0]))

    return plan_call(
        attend_grads_kernel,
        "attend_grads",
        CHIPS // 2,
        [plan_whole(grad), plan_whole(grad_other)] + [rows_of(0), rows_of(1)] * 2,
        [pl.BlockSpec((2, 2, SLAB, cols), lambda i, order, core: (0, i, 0, 0))] * 4,
        [shape((2, CHIPS, SLAB, cols))] * 4,
        [pltpu.VMEM((2, CORE_COLS, cols), BF16)],
        4 * TOKENS * WIDTH * cols // 2,
        12 * 2**20,
        order,
        core,
        (grad, grad_other, normed, normed, normed_other, normed_other),
        late,
    )


def unpack_down_kernel(step, order_ref, x_ref, *refs):
    down_ref = refs[8]
    for index in range(4):
        for own in range(2):

            @pl.when((step == index) & (x_ref[0] == own))
            def _():
                for x in range(2):
                    piece = refs[index if x == own else 4 + index]
                    cols = slice(x * SLOT_COLS, (x + 1) * SLOT_COLS)
                    down_ref[:DOWN_ROWS, cols] = piece[:, :HALF].astype(F32)
                    down_ref[DOWN_ROWS:, cols] = piece[:, HALF:].astype(F32)


def unpack_down(order, x_lo, pieces, late):
    return plan_call(
        unpack_down_kernel,
        "unpack_down",
        4,
        [pl.BlockSpec(p.shape, lambda i, order, x: (0, 0)) for p in pieces],
        pl.BlockSpec((CORE_FF, WIDE), lambda i, order, x: (0, order[i])),
        shape((CORE_FF, WIDTH), F32),
        [],
        0,
        0,
        order,
        x_lo,
        tuple(pieces),
        late,
    )


def unpack_up_kernel(step, order_ref, x_ref, *refs):
    up_ref, mix_ref = refs[4:]
    for index, pieces in enumerate(refs[:4]):

        @pl.when(step == index)
        def _():
            for x in range(2):
                piece = pieces.at[(x_ref[0] + x) % 2]
                up_ref[x * UP_ROWS : (x + 1) * UP_ROWS] = piece[:UP_ROWS].astype(F32)
                cols = slice(x * SLOT_COLS, (x + 1) * SLOT_COLS)
                mix_ref[:MIX_ROWS, cols] = piece[UP_ROWS:, :HALF].astype(F32)
                mix_ref[MIX_ROWS:, cols] = piece[UP_ROWS:, HALF:].astype(F32)


def unpack_up(order, x_lo, pieces, late):
    return plan_call(
        unpack_up_kernel,
        "unpack_up",
        4,
        [pl.BlockSpec(p.shape, lambda i, order, x: (0, 0, 0)) for p in pieces],
        [
            pl.BlockSpec((2 * UP_ROWS, CORE_FF), lambda i, order, x: (order[i], 0)),
            pl.BlockSpec((CORE_COLS, WIDE), lambda i, order, x: (0, order[i])),
        ],
        [shape((WIDTH, CORE_FF), F32), shape((CORE_COLS, WIDTH), F32)],
        [],
        0,
        0,
        order,
        x_lo,
        tuple(pieces),
        late,
    )


SLAB = CORE_COLS // SEQ_DEVICES


VECTORS = (128, 128, 128, 384, 512, 128)


def unpack_attend_kernel(step, place_ref, x_ref, *refs):
    out_ref, vector_refs, total_ref = refs[4], refs[5:11], refs[11]

    @pl.when(step == 0)
    def _():
        total_ref[...] = jnp.zeros_like(total_ref)

    for index, pieces in enumerate(refs[:4]):

        @pl.when(place_ref[step] == index)
        def _():
            for half in range(2):
                piece = pieces.at[(x_ref[0] + half) % 2]
                rest = piece[CHIPS * SLAB :].astype(F32).reshape(CHIPS, 4, -1)
                total_ref[...] += jnp.sum(rest, axis=0)
                for chip in range(CHIPS):
                    for part in range(3):
                        start = part * WIDTH + chip * CHIP_COLS
                        out_ref[half * SLAB : (half + 1) * SLAB, start : start + CHIP_COLS] = piece[
                            chip * SLAB : (chip + 1) * SLAB,
                            part * CHIP_COLS : (part + 1) * CHIP_COLS,
                        ].astype(F32)

    @pl.when(step == 3)
    def _():
        sums = total_ref[:2] + total_ref[2:]
        start = 0
        for vector_ref in vector_refs[:4]:
            size = vector_ref.shape[1]
            vector_ref[...] = sums[0:1, start : start + size]
            start += size
        vector_refs[4][...] = sums[1:2, : vector_refs[4].shape[1]]
        vector_refs[5][...] = vector_refs[2][...]


def unpack_attend(place, x_lo, pieces, late):
    cols = pieces[0].shape[2]
    fixed_out = lambda size: pl.BlockSpec((1, size), lambda i, place, x: (0, 0))
    return plan_call(
        unpack_attend_kernel,
        "unpack_attend",
        4,
        [pl.BlockSpec(p.shape, lambda i, place, x: (0, 0, 0)) for p in pieces],
        [pl.BlockSpec((2 * SLAB, 3 * WIDTH), lambda i, place, x: (i, 0))]
        + [fixed_out(size) for size in VECTORS],
        [shape((CORE_COLS, 3 * WIDTH), F32)] + [shape((1, size), F32) for size in VECTORS],
        [pltpu.VMEM((4, cols), F32)],
        0,
        0,
        place,
        x_lo,
        tuple(pieces),
        late,
    )


def rows_grad_kernel(step, rows_ref, cot_ref, near_ref, far_ref, gain_ref, out_ref):
    grad = near_ref[...].astype(F32) + far_ref[...].astype(F32)
    center, inverse = layer_stats(rows_ref[...].astype(F32))
    unit = center * inverse
    scaled = grad * gain_ref[...]
    out_ref[...] = cot_ref[...].astype(F32) + inverse * (
        scaled
        - jnp.mean(scaled, axis=-1, keepdims=True)
        - unit * jnp.mean(scaled * unit, axis=-1, keepdims=True)
    )


def rows_grad(rows, cot, near, far, gain):
    block = 64
    return call(
        rows_grad_kernel,
        "rows_grad",
        ROWS // block,
        [row_block(block, WIDTH)] * 4 + [whole(gain.shape)],
        row_block(block, WIDTH),
        shape((ROWS, WIDTH), F32),
        0,
        4 * 2**20,
        (rows, cot, near, far, gain),
    )


def lane_masks():
    lane = lax.broadcasted_iota(jnp.int32, (1, PAIR), 1)
    first = (lane < HEAD_DIM).astype(BF16)
    return first, 1 - first


def scores_of(query, keys, low):
    scores = dot(query, keys, NT)
    if low:
        head, last = scores[:, :low], scores[:, low:]
    else:
        head, last = None, scores
    row = lax.broadcasted_iota(jnp.int32, last.shape, 0)
    col = lax.broadcasted_iota(jnp.int32, last.shape, 1)
    last = jnp.where(col <= row, last, NEG_FILL)
    return last if head is None else jnp.concatenate([head, last], axis=1)


def attend_kernel(step, query_ref, key_ref, value_ref, out_ref, logsum_ref):
    first, second = lane_masks()
    lane = lax.broadcasted_iota(jnp.int32, (QBLOCK, PAIR), 1)
    for low in range(0, LENGTH, QBLOCK):
        reach = low + QBLOCK
        query = query_ref[low:reach, :] * BF16(SCALE)
        keys = key_ref[:reach, :]
        values = value_ref[:reach, :]
        found = []
        for mask in (first, second):
            scores = scores_of(query * mask, keys, low)
            peak = jnp.max(scores, axis=1, keepdims=True)
            weight = jnp.exp(scores - peak)
            total = jnp.sum(weight, axis=1, keepdims=True)
            found.append((dot(weight.astype(BF16), values) / total, peak + jnp.log(total)))
        out_ref[low:reach, :] = jnp.where(lane < HEAD_DIM, found[0][0], found[1][0]).astype(BF16)
        logsum_ref[low:reach, :] = jnp.where(lane < HEAD_DIM, found[0][1], found[1][1])


def pair_columns(part):
    return pl.BlockSpec((LENGTH, PAIR), lambda p: (0, part * (CHIP_COLS // PAIR) + p))


def attend_forward(qkv, late):
    return call(
        attend_kernel,
        "attend_forward",
        CHIP_COLS // PAIR,
        [pair_columns(0), pair_columns(1), pair_columns(2)],
        [pair_columns(0)] * 2,
        [shape((LENGTH, CHIP_COLS)), shape((LENGTH, CHIP_COLS), F32)],
        8 * 2**30,
        4 * 2**20,
        (qkv, qkv, qkv),
        late,
    )


def attend_back_kernel(
    step,
    query_ref,
    key_ref,
    value_ref,
    grad_ref,
    logsum_ref,
    turn_ref,
    upper_ref,
    lower_ref,
    out_ref,
    key_total,
    value_total,
):
    pair = step
    first, second = lane_masks()
    lane = lax.broadcasted_iota(jnp.int32, (QBLOCK, PAIR), 1)
    key_total[...] = jnp.zeros_like(key_total)
    value_total[...] = jnp.zeros_like(value_total)

    def store(part, low, reach, values):
        start = pl.multiple_of((part * (CHIP_COLS // PAIR) + pair) * PAIR, PAIR)
        out_ref[low:reach, pl.ds(start, PAIR)] = values.astype(BF16)

    def unturn(values, low, reach):
        kept = values.astype(BF16).astype(F32)
        return turn_columns(
            kept, turn_ref[low:reach, :], upper_ref[low:reach, :], lower_ref[low:reach, :], -1.0
        )

    for low in range(0, LENGTH, QBLOCK):
        reach = low + QBLOCK
        query = query_ref[low:reach, :] * BF16(SCALE)
        grad = grad_ref[low:reach, :]
        keys = key_ref[:reach, :]
        values = value_ref[:reach, :]
        query_grads = []
        key_part = 0.0
        value_part = 0.0
        for head, mask in enumerate((first, second)):
            own_query = query * mask
            own_grad = grad * mask
            scores = scores_of(own_query, keys, low)
            start = head * HEAD_DIM
            probs = jnp.exp(scores - logsum_ref[low:reach, start : start + 1])
            prob_grad = dot(own_grad, values, NT)
            inner = jnp.sum(probs * prob_grad, axis=1, keepdims=True)
            score_grad = (probs * (prob_grad - inner)).astype(BF16)
            query_grads.append(dot(score_grad, keys))
            key_part += dot(score_grad, own_query, TN)
            value_part += dot(probs.astype(BF16), own_grad, TN)
        key_total[:reach, :] += key_part
        value_total[:reach, :] += value_part
        query_grad = jnp.where(lane < HEAD_DIM, query_grads[0], query_grads[1]) * SCALE
        store(0, low, reach, unturn(query_grad, low, reach))
    store(1, 0, LENGTH, unturn(key_total[...], 0, LENGTH))
    store(2, 0, LENGTH, value_total[...])


def attend_backward(qkv, grad, logsum, tables, late):
    return call(
        attend_back_kernel,
        "attend_backward",
        CHIP_COLS // PAIR,
        [pair_columns(0), pair_columns(1), pair_columns(2), pair_columns(0), pair_columns(0)]
        + [whole(t.shape) for t in tables],
        whole((LENGTH, 3 * CHIP_COLS)),
        shape((LENGTH, 3 * CHIP_COLS)),
        20 * 2**30,
        6 * 2**20,
        (qkv, qkv, qkv, grad, logsum) + tables,
        late,
        [pltpu.VMEM((LENGTH, PAIR), F32)] * 2,
    )


def exchange(blocks, axes):
    return lax.all_to_all(blocks, axes, split_axis=0, concat_axis=0, tiled=True)


def spread(block, axes, count):
    return exchange(jnp.broadcast_to(block[None], (count,) + block.shape), axes)


tie = lax.optimization_barrier


def sent_y(parts):
    return [send(parts[k], "y", k) for k in (1, 3, 2)]


def joined(leave, stay):
    return (stay + swap(leave.astype(BF16), "xl").astype(F32)).astype(BF16)


def sum_seq(parts, arrived):
    leave, stay = (
        parts[0][r].astype(F32) + sum(a[r].astype(F32) for a in arrived) for r in (1, 0)
    )
    return joined(leave, stay)


def in_rows(values):
    width = 3 * CHIP_COLS
    count = values.shape[0]
    head = lax.reduce_precision(values, 8, 7)
    rest = (values - head).astype(BF16)
    head = head.astype(BF16)
    rows = [jnp.pad(part, ((0, 0), (0, 2 * width - part.shape[1]))).reshape(count, 2, width) for part in (head, rest)]
    return jnp.pad(jnp.concatenate(rows, axis=1), ((0, 0), (0, SLAB - 4), (0, 0)))


def summed_y(parts, arrived):
    return (parts[0].astype(F32) + sum(a.astype(F32) for a in arrived)).astype(BF16)


def summed_pair(own, other):
    return (own.astype(F32) + other[::-1].astype(F32)).astype(BF16)


def spread_y(pair):
    found = {0: pair} | {k: shift(pair, "y", k) for k in (1, 3, 2)}
    return [found[k] for k in range(4)]


def sum_rows(parts):
    parts = lax.psum_scatter(
        parts.reshape(4, 2, ROWS, WIDTH), "z", scatter_dimension=0, tiled=False
    )
    return parts


def per_device(
    inputs,
    gains,
    shifts,
    attend,
    attend_bias,
    mixer,
    mixer_bias,
    upward,
    upward_bias,
    downward,
    downward_bias,
    cotangent,
):
    core = lax.axis_index("c")
    x_lo = lax.axis_index("xl")
    chip = lax.axis_index("xh") * 4 + lax.axis_index("z")
    seq_index = lax.axis_index("y") * 2 + x_lo
    core_at = core.reshape(1)
    rows_in = inputs.reshape(ROWS, WIDTH)
    own_cot = cotangent.reshape(ROWS, WIDTH)
    width = 3 * CHIP_COLS

    z_order = (lax.axis_index("z") + jnp.arange(4, dtype=jnp.int32)) % 4
    y_place = (jnp.arange(4, dtype=jnp.int32) - lax.axis_index("y")) % 4
    y_order = (lax.axis_index("y") + jnp.arange(4, dtype=jnp.int32)) % 4
    seq_order = (y_order[:, None] * 2 + jnp.stack([x_lo, 1 - x_lo])[None, :]).reshape(SEQ_DEVICES)

    near = lax.all_gather(rows_in, "z", axis=0, tiled=True)
    other_rows = swap(rows_in, "xh")

    slab = lax.dynamic_slice_in_dim(attend, seq_index * SLAB, SLAB, 0)
    slab = slab.reshape(SLAB, 3, CHIPS, CHIP_COLS).transpose(2, 0, 1, 3).reshape(CHIPS, SLAB, width)
    small, start = 0, 0
    for vector in (gains, shifts, mixer_bias, downward_bias, attend_bias):
        small = small + jnp.pad(vector, (start, 2 * width - start - vector.shape[0]))
        start += vector.shape[0]
    small = small.reshape(1, 2, width)
    small = jnp.pad(jnp.broadcast_to(small, (CHIPS, 2, width)), ((0, 0), (0, SLAB - 2), (0, 0)))
    slab = exchange(jnp.concatenate([slab, small], axis=1), GROUP)
    slab, other_rows = tie((slab, other_rows))
    far = [other_rows] + [shift(other_rows, "z", k) for k in (1, 2, 3)]
    small_own = slab[:, SLAB : SLAB + 2].reshape(CHIPS, 2 * width)[:, :896]
    slab = slab[:, :SLAB]
    attend_own = spread(slab, SEQ, SEQ_DEVICES).reshape(SEQ_DEVICES, CHIPS, SLAB, width)
    attend_own, all_tables, near, *far = tie(
        (attend_own, rope_tables(jnp.arange(LENGTH, dtype=jnp.int32), 2), near, *far)
    )
    attend_other = swap(attend_own, "c")
    small_other = swap(small_own, "c")
    small_all = jnp.where(
        core == 0, jnp.stack([small_own, small_other], 1), jnp.stack([small_other, small_own], 1)
    ).reshape(FSDP_DEVICES, 7, 128).astype(F32)
    gain_all = small_all[:, 0].reshape(1, WIDTH)
    shift_all = small_all[:, 1].reshape(1, WIDTH)
    out_bias = (small_all[:, 2] + small_all[:, 3]).reshape(WIDTH)
    bias_grid = small_all[:, 4:7].reshape(3, CHIPS, CHIP_COLS)
    attend_bias_chip = lax.dynamic_slice_in_dim(bias_grid, chip, 1, 1).reshape(1, width)

    mixer_other = swap(mixer, "c")
    mixer_chip = jnp.where(
        core == 0, jnp.concatenate([mixer, mixer_other]), jnp.concatenate([mixer_other, mixer])
    )
    up_other = swap(upward, "c")
    down_other = swap(downward, "c")
    up_bias_own = upward_bias.astype(F32).reshape(1, CORE_FF)
    up_bias_other = swap(upward_bias.reshape(1, CORE_FF), "c").astype(F32)

    cot_pair = jnp.stack([own_cot, swap(own_cot, "xh")])
    cot_pair, near, *far = tie((cot_pair, near, *far))
    cot_group = lax.all_gather(cot_pair, "z", axis=0, tiled=False).reshape(TOKENS, WIDTH)
    normed, qkv_sent, attend_chip = norm_project(
        seq_index.reshape(1),
        z_order,
        core_at,
        near,
        far,
        gain_all,
        shift_all,
        attend_bias_chip,
        attend_own,
        attend_other,
        all_tables,
        (mixer_chip, up_other, down_other, up_bias_other, up_bias_own),
    )
    normed_other = swap(normed, "c")
    qkv = exchange(qkv_sent.reshape(CHIPS, ROWS, width), SEQ).reshape(LENGTH, width)
    act_own, act_other, slope_own, slope_other = hidden_forward(
        normed, upward, up_other, up_bias_own, up_bias_other
    )
    act_sent = swap(act_other, "c")

    attended, logsum = attend_forward(qkv, (act_own, normed_other))
    attended, cot_group = tie((attended, cot_group))
    attended_group = exchange(attended.reshape(SEQ_DEVICES, ROWS, CHIP_COLS), SEQ).reshape(
        TOKENS, CHIP_COLS
    )
    cot_other = swap(cot_group, "c")
    attended_grad = grad_heads(cot_group, mixer_chip, (attended,))
    grads = exchange(attended_grad.reshape(CHIPS, ROWS, CHIP_COLS), SEQ).reshape(LENGTH, CHIP_COLS)

    x_at = x_lo.reshape(1)
    (grad_own, grad_other, up_bias_sum, up_bias_other_sum), down_slabs = run(
        hidden_back(cot_group, downward, down_other, slope_own, slope_other),
        down_grads(y_order, x_at, act_own, act_sent, cot_group, cot_other),
        late=(attended_grad, attended_group),
    )
    grad_sent = swap(grad_other, "c")

    back = attend_backward(qkv, grads, logsum, all_tables, (down_slabs[0],))
    projected_grad = exchange(back.reshape(SEQ_DEVICES, ROWS, width), SEQ).reshape(TOKENS, width)

    attended_group, *down_arrived = tie((attended_group, *sent_y(down_slabs)))
    parts = run(
        out_part(act_own, act_other, attended_group, downward, down_other, mixer_chip),
        late=(back,),
    )
    up_slabs = run(
        up_grads(
            y_order,
            x_at,
            core_at,
            grad_own,
            grad_sent,
            attended_group,
            swap(attended_group, "c"),
            normed,
            normed_other,
            cot_group,
            cot_other,
        ),
        late=(parts,),
    )
    out_sums = sum_rows(parts)
    up_arrived = sent_y(up_slabs)

    down_own = summed_y(down_slabs, down_arrived)
    down_other_x = swap(down_own[1], "xl")

    projected_grad, up_first = tie((projected_grad, up_slabs[0]))
    attend_slabs = attend_grads(
        seq_order,
        core_at,
        projected_grad,
        swap(projected_grad, "c"),
        normed,
        normed_other,
        (up_first,),
    )

    down_other_x, attend_first = tie((down_other_x, attend_slabs[0]))
    attend_slabs = [attend_first, *attend_slabs[1:]]
    down_sum = (down_own[0].astype(F32) + down_other_x.astype(F32)).astype(BF16)

    parts, norm_sums, attend_bias_sum = normed_part(
        z_order,
        projected_grad,
        grad_own,
        grad_other,
        near,
        far,
        attend_chip,
        upward,
        up_other,
        (attend_slabs[0],),
    )
    parts, out_sums, down_sum, *up_arrived = tie((parts, out_sums, down_sum, *up_arrived))
    outputs = (
        rows_in.astype(F32) + out_bias + out_sums[0].astype(F32) + swap(out_sums[1], "xh").astype(F32)
    ).astype(BF16)
    sums = sum_rows(parts)
    inputs_grad = rows_grad(rows_in, own_cot, sums[0], swap(sums[1], "xh"), gain_all)

    bias_full = jnp.sum(own_cot.astype(F32), axis=0)
    attend_bias_full = lax.dynamic_update_slice(
        jnp.zeros((3, CHIPS, CHIP_COLS), F32), attend_bias_sum.reshape(3, 1, CHIP_COLS), (0, chip, 0)
    )
    up_bias_pair = jnp.where(
        core == 0,
        jnp.concatenate([up_bias_sum, up_bias_other_sum]),
        jnp.concatenate([up_bias_other_sum, up_bias_sum]),
    )
    up_bias_full = lax.dynamic_update_slice(
        jnp.zeros((CHIPS, 2, CORE_FF), F32), up_bias_pair[None], (chip, 0, 0)
    )
    vectors = jnp.concatenate(
        [
            v.reshape(FSDP_DEVICES, -1)
            for v in (norm_sums[0], norm_sums[1], bias_full, attend_bias_full, up_bias_full)
        ],
        axis=1,
    )
    vectors = vectors.reshape(CHIPS, 2, -1)
    vectors_keep = lax.dynamic_index_in_dim(vectors, core, 1, keepdims=False)
    vectors_sent = lax.dynamic_index_in_dim(vectors, 1 - core, 1, keepdims=False)
    vectors = vectors_keep + swap(vectors_sent, "c")
    up_own = summed_y(up_slabs, up_arrived)
    up_pair = summed_pair(up_own, swap(up_own, "xl"))
    *attend_arrived, down_sum, up_pair = tie((*sent_y(attend_slabs), down_sum, up_pair))
    attend_sum = sum_seq(attend_slabs, attend_arrived)
    message = exchange(jnp.concatenate([attend_sum, in_rows(vectors)], axis=1), GROUP)
    kept = message[:, SLAB : SLAB + 4].reshape(-1, width)
    message = jnp.concatenate([message[:, :SLAB].reshape(-1, width), kept], axis=0)
    up_1, up_3 = shift(up_pair, "y", 1), shift(up_pair, "y", 3)
    message, outputs, up_1, up_3, *down_near = tie((message, outputs, up_1, up_3, *spread_y(down_sum)))
    up_pieces = [up_pair, up_1, shift(up_pair, "y", 2), up_3]
    attend_pair, *down_near = tie((jnp.stack([message, swap(message, "xl")]), *down_near))
    attend_pieces = spread_y(attend_pair)
    down_pieces = down_near + [swap(piece, "xl") for piece in down_near]
    down_grad, (up_grad, mixer_grad) = run(
        unpack_down(y_order, x_at, down_pieces, None), unpack_up(y_order, x_at, up_pieces, None)
    )
    attend_grad, *vectors = unpack_attend(
        y_place, x_at, attend_pieces, (inputs_grad, outputs, down_grad, up_grad)
    )
    gain_grad, shift_grad, bias_grad, attend_bias_grad, up_bias_grad, bias_again = (v[0] for v in vectors)

    return (
        outputs.reshape(inputs.shape),
        inputs_grad.reshape(inputs.shape),
        gain_grad,
        shift_grad,
        attend_grad,
        attend_bias_grad,
        mixer_grad,
        bias_grad,
        up_grad,
        up_bias_grad,
        down_grad,
        bias_again,
    )


def solution(mesh):
    fine = Mesh(mesh.devices.reshape(4, 2, 2, 4, 2), ("y", "xl", "xh", "z", "c"))
    rows = P(FSDP, SEQ, None)
    vector = P(FSDP)
    by_row = P(FSDP, None)
    by_col = P(None, FSDP)
    in_specs = (
        rows,
        vector,
        vector,
        by_row,
        vector,
        by_row,
        vector,
        by_col,
        vector,
        by_row,
        vector,
        rows,
    )
    out_specs = (
        rows,
        rows,
        vector,
        vector,
        by_row,
        vector,
        by_row,
        vector,
        by_col,
        vector,
        by_row,
        vector,
    )
    return jax.shard_map(
        per_device, mesh=fine, in_specs=in_specs, out_specs=out_specs, check_vma=False
    )
```
